128 devices in a mesh: section: 2 (over core), ctx: 4 (over x), fsdp: 16 (over z, y).
Axes of the slice: x: 4, y: 4, z: 4, core: 2. Of those that a mesh axis runs over, the one named last changes fastest.
Arguments:
- inputs: bfloat16 [32, 1024, 768], P('fsdp', 'ctx'), may hold values from -6 to 6
- cotangent: bfloat16 [32, 1024, 768], P('fsdp', 'ctx'), may hold values from -6 to 6
- lengths: int32 [32], P('fsdp'), may hold values from 256 to 1024, as said below
- routes: int32 [2, 32, 1024, 2], P('section', 'fsdp', 'ctx'), may hold values from 0 to 2, all different within a row; in each aligned block of 256 rows (0 to 255, 256 to 511, ..., all dimensions but the last counted through in order) at most 208 rows name the same one
- step_count: int32 [1], replicated, may hold values from 1 to 20
- norm_gains: float32 [2, 2, 768], P('section', None, 'fsdp'), may hold values from 0.5 to 1.5
- gains_mean: float32 [2, 2, 768], P('section', None, 'fsdp'), may hold values from -0.0390625 to 0.0390625
- gains_square: float32 [2, 2, 768], P('section', None, 'fsdp'), may hold values from 3.4244793e-05 to 0.00013704428
- attn_weight: float32 [2, 768, 3072], P('section', 'fsdp')
- attn_mean: float32 [2, 768, 3072], P('section', 'fsdp'), may hold values from -0.0009765625 to 0.0009765625
- attn_square: float32 [2, 768, 3072], P('section', 'fsdp'), may hold values from 2.2294786e-08 to 8.922153e-08
- router_weight: float32 [2, 768, 3], P('section', 'fsdp'), may hold values from -0.4375 to 0.4375
- router_mean: float32 [2, 768, 3], P('section', 'fsdp'), may hold values from -0.03125 to 0.03125
- router_square: float32 [2, 768, 3], P('section', 'fsdp'), may hold values from 2.2829861e-05 to 9.136285e-05
- expert_in: float32 [2, 4, 768, 2, 2048], P('section', None, None, None, 'fsdp'), may hold values from -0.21875 to 0.21875
- in_mean: float32 [2, 4, 768, 2, 2048], P('section', None, None, None, 'fsdp'), may hold values from -0.00048828125 to 0.00048828125
- in_square: float32 [2, 4, 768, 2, 2048], P('section', None, None, None, 'fsdp'), may hold values from 4.1802726e-09 to 1.6729038e-08
- expert_out: float32 [2, 4, 2048, 768], P('section', None, 'fsdp'), may hold values from -0.125 to 0.125
- out_mean: float32 [2, 4, 2048, 768], P('section', None, 'fsdp'), may hold values from -0.00061035156 to 0.00061035156
- out_square: float32 [2, 4, 2048, 768], P('section', None, 'fsdp'), may hold values from 8.360545e-09 to 3.3458075e-08
Outputs:
- layer_outputs: bfloat16 [2, 32, 1024, 768], P('section', 'fsdp', 'ctx')
- input_grads: float32 [2, 32, 1024, 768], P('section', 'fsdp', 'ctx')
- gains_grad: float32 [2, 2, 768], P('section', None, 'fsdp')
- gains_mean_new: float32 [2, 2, 768], P('section', None, 'fsdp')
- gains_square_new: float32 [2, 2, 768], P('section', None, 'fsdp')
- gains_master: float32 [2, 2, 768], P('section', None, 'fsdp')
- gains_copy: bfloat16 [2, 2, 768], P('section', None, 'fsdp')
- attn_grad: float32 [2, 768, 3072], P('section', 'fsdp')
- attn_mean_new: float32 [2, 768, 3072], P('section', 'fsdp')
- attn_square_new: float32 [2, 768, 3072], P('section', 'fsdp')
- attn_master: float32 [2, 768, 3072], P('section', 'fsdp')
- attn_copy: bfloat16 [2, 768, 3072], P('section', 'fsdp')
- router_grad: float32 [2, 768, 3], P('section', 'fsdp')
- router_mean_new: float32 [2, 768, 3], P('section', 'fsdp')
- router_square_new: float32 [2, 768, 3], P('section', 'fsdp')
- router_master: float32 [2, 768, 3], P('section', 'fsdp')
- router_copy: bfloat16 [2, 768, 3], P('section', 'fsdp')
- in_grad: float32 [2, 4, 768, 2, 2048], P('section', None, None, None, 'fsdp')
- in_mean_new: float32 [2, 4, 768, 2, 2048], P('section', None, None, None, 'fsdp')
- in_square_new: float32 [2, 4, 768, 2, 2048], P('section', None, None, None, 'fsdp')
- in_master: float32 [2, 4, 768, 2, 2048], P('section', None, None, None, 'fsdp')
- in_copy: bfloat16 [2, 4, 768, 2, 2048], P('section', None, None, None, 'fsdp')
- out_grad: float32 [2, 4, 2048, 768], P('section', None, 'fsdp')
- out_mean_new: float32 [2, 4, 2048, 768], P('section', None, 'fsdp')
- out_square_new: float32 [2, 4, 2048, 768], P('section', None, 'fsdp')
- out_master: float32 [2, 4, 2048, 768], P('section', None, 'fsdp')
- out_copy: bfloat16 [2, 4, 2048, 768], P('section', None, 'fsdp')
- clip_norms: float32 [2, 5], P('section')
The draws below stay inside these ranges and needn't reach their ends.
Inputs may be any that keep to these rules, and one draw needn't show every extreme that they name: One of the 32 lengths is 1024 in every draw. `routes`: each position names two different experts; among the 256 positions of one aligned block of a sequence row in one layer, no expert is named more than 208 times.
All inputs are finite; a program needn't handle non-finite values.
Results may differ from the reference program's by a relative error of at most 0.03.
Values may be sent and summed in bfloat16 or wider, within the bound.
A program may use at most 512 MiB of HBM per device.

```python
import math
import jax
import jax.numpy as jnp
import numpy as np
from jax import lax

D = 768
HEADS = 12
HEAD_DIM = 64
FFN = 2048
EXPERTS = 3
SEQ_DEV = 256
SLOT = 1024
SEQS = 32
CAP = 208


def draw_lengths(key, part):
    values = jax.random.randint(key, (SEQS,), SLOT // 4, SLOT + 1, dtype=jnp.int32)
    chosen = jax.random.randint(jax.random.fold_in(key, 7), (), 0, SEQS, dtype=jnp.int32)
    return values.at[chosen].set(SLOT)


def draw_attn_weight(key, part):
    column = jnp.arange(4 * D)
    factor = jnp.where(column < 3 * D, 1.0, 12.0) * D ** (-0.5)
    values = jnp.clip(jax.random.normal(key, (2, D, 4 * D), jnp.float32), -6.0, 6.0)
    return values * factor[None, None, :]


def steps_of(key, shape, shards, low, high):
    def one(position, blocks):
        heights = jax.random.uniform(jax.random.fold_in(jax.random.fold_in(key, 6), position), (blocks,), jnp.float32, low / len(shards), high / len(shards))
        return jnp.repeat(jnp.exp(heights), shape[position] // blocks).reshape((-1,) + (1,) * (len(shape) - position - 1))

    loudness = one(*shards[0])
    for cut in shards[1:]:
        loudness = loudness * one(*cut)
    return loudness


def routed_block(own_key, own, number, rows, count, top, bound, slope):
    order = jax.random.permutation(own_key, count)
    heavy_load, ordinary = shares(count, rows * top, bound, slope, True), shares(count, rows * top, bound, slope, False)
    places = jnp.arange(count)

    def named(sizes, offset_by):
        used = int((sizes > 0).sum())
        fixed = max(1, used // 4)
        shifted = fixed + (places - fixed + offset_by * (used - fixed)) % max(1, count - fixed)
        return jnp.zeros((count,), jnp.int32).at[order[jnp.where(places < fixed, places, shifted)]].set(jnp.asarray(sizes, jnp.int32))

    sizes = jnp.where(number % 4 == 0, named(heavy_load, number // 4), named(ordinary, number - number // 4 - 1))
    mixed = jax.random.permutation(jax.random.fold_in(own, 3), count)
    donor, receiver = mixed[0:count // 2 * 2:2], mixed[1:count // 2 * 2:2]
    slack = jnp.minimum(sizes[donor] - 1, bound - sizes[receiver]) // 2
    slack = jnp.where((donor == order[0]) | (receiver == order[0]) | (sizes[receiver] == 0), 0, jnp.maximum(slack, 0))
    shifted = jax.random.randint(jax.random.fold_in(own, 4), (count // 2,), 0, 1 << 20) % (slack + 1)
    sizes = sizes.at[donor].add(-shifted).at[receiver].add(shifted)
    items = jnp.searchsorted(jnp.cumsum(sizes), jnp.arange(rows * top), side="right").astype(jnp.int32)
    listing = items.reshape(top, rows).T
    listing = listing[jax.random.permutation(jax.random.fold_in(own, 1), rows)]
    offset_by = jax.random.randint(jax.random.fold_in(own, 2), (rows, 1), 0, top)
    return jnp.take_along_axis(listing, (jnp.arange(top)[None, :] + offset_by) % top, axis=1)


def shares(number_of, total, limit, skew, full):
    loads = [(1 << 20) // math.isqrt(grade ** skew) + 1 for grade in range(1, number_of + 1)]
    largest = limit if full else min(limit, max(-(-total // number_of), total * loads[0] // sum(loads)))
    least = 1 if total - largest >= number_of - 1 else 0
    holding, spare = [largest] + [least] * (number_of - 1), total - largest - least * (number_of - 1)
    while spare > 0:
        movable = [i for i in range(1, number_of) if holding[i] < largest] or [i for i in range(1, number_of) if holding[i] < limit]
        mass, budget = sum([loads[i] for i in movable]), spare
        for i in movable:
            extra = min(limit - holding[i], max(1, budget * loads[i] // mass), spare)
            holding[i] = holding[i] + extra
            spare = spare - extra
    return np.array(holding)


def bell_draw(rng, dims, deviation, reach, pieces=(), held_as=jnp.bfloat16):
    values = jax.random.normal(rng, dims, jnp.float32) * deviation
    if len(pieces) > 0:
        values = steps_of(rng, dims, pieces, -0.22, 0.18) * values
    return jnp.clip(values, min=-reach, max=reach).astype(held_as)


def setup_inputs(seed: int = 0) -> dict:
    streams_of = jax.random.split(jax.random.key(seed), 21)
    inputs = bell_draw(streams_of[0], (SEQS, SLOT, D), 1.0, 6.0, ((0, 16), (1, 4)))
    cotangent = bell_draw(streams_of[1], (SEQS, SLOT, D), 1.0, 6.0, ((0, 16), (1, 4)))
    lengths = draw_lengths(jax.random.fold_in(streams_of[20], 71), 0)
    routes_keys = jax.random.split(jax.random.fold_in(streams_of[3], 1), 2 * SEQS * SLOT // SEQ_DEV)
    routes_turns = jax.random.permutation(jax.random.fold_in(streams_of[3], 3), 2 * SEQS * SLOT // SEQ_DEV)
    routes = jax.vmap(lambda own, number: routed_block(jax.random.fold_in(streams_of[3], 2), own, number, SEQ_DEV, EXPERTS, 2, CAP, 0))(routes_keys, routes_turns).reshape((2, SEQS, SLOT, 2))
    step_count = jax.random.randint(streams_of[4], (1,), 1, 21).astype(jnp.int32)
    norm_gains = jnp.clip(1.0 + 0.1 * jax.random.normal(streams_of[5], (2, 2, D), jnp.float32), 0.5, 1.5)
    gains_mean = bell_draw(streams_of[6], (2, 2, D), (0.111 * (2 * D) ** -0.5), 0.0390625, ((0, 2), (2, 16)), jnp.float32)
    gains_square = jnp.clip(jnp.exp(math.log(0.00013704428) - 1.3867695 * jax.random.uniform(streams_of[7], (2, 2, D), jnp.float32) ** steps_of(streams_of[7], (2, 2, D), ((0, 2), (2, 16)), -0.2, 0.2)), 3.4244792914250866e-05, 0.00013704428)
    attn_weight = draw_attn_weight(jax.random.fold_in(streams_of[20], 71), 0)
    attn_mean = bell_draw(streams_of[9], (2, D, 4 * D), (0.111 * (4 * D * D) ** -0.5), 0.0009765625, ((0, 2), (1, 16)), jnp.float32)
    attn_square = jnp.clip(jnp.exp(math.log(8.922152971990727e-08) - 1.3867695 * jax.random.uniform(streams_of[10], (2, D, 4 * D), jnp.float32) ** steps_of(streams_of[10], (2, D, 4 * D), ((0, 2), (1, 16)), -0.2, 0.2)), 2.2294786461429794e-08, 8.922152971990727e-08)
    router_weight = bell_draw(streams_of[11], (2, D, EXPERTS), (D // 4) ** -0.5, 0.4375, ((0, 2), (1, 16)), jnp.float32)
    router_mean = bell_draw(streams_of[12], (2, D, EXPERTS), (0.111 * (D * EXPERTS) ** -0.5), 0.03125, ((0, 2), (1, 16)), jnp.float32)
    router_square = jnp.clip(jnp.exp(math.log(9.136284643318504e-05) - 1.3867695 * jax.random.uniform(streams_of[13], (2, D, EXPERTS), jnp.float32) ** steps_of(streams_of[13], (2, D, EXPERTS), ((0, 2), (1, 16)), -0.2, 0.2)), 2.282986133650411e-05, 9.136284643318504e-05)
    expert_in = bell_draw(streams_of[14], (2, EXPERTS + 1, D, 2, FFN), D ** -0.5, 0.21875, ((0, 2), (4, 16)), jnp.float32)
    in_mean = bell_draw(streams_of[15], (2, EXPERTS + 1, D, 2, FFN), (0.111 * (2 * (EXPERTS + 1) * D * FFN) ** -0.5), 0.00048828125, ((0, 2), (4, 16)), jnp.float32)
    in_square = jnp.clip(jnp.exp(math.log(1.6729037710661032e-08) - 1.3867695 * jax.random.uniform(streams_of[16], (2, EXPERTS + 1, D, 2, FFN), jnp.float32) ** steps_of(streams_of[16], (2, EXPERTS + 1, D, 2, FFN), ((0, 2), (4, 16)), -0.2, 0.2)), 4.180272572540389e-09, 1.6729037710661032e-08)
    expert_out = bell_draw(streams_of[17], (2, EXPERTS + 1, FFN, D), FFN ** -0.5, 0.125, ((0, 2), (2, 16)), jnp.float32)
    out_mean = bell_draw(streams_of[18], (2, EXPERTS + 1, FFN, D), (0.111 * ((EXPERTS + 1) * D * FFN) ** -0.5), 0.00061035156, ((0, 2), (2, 16)), jnp.float32)
    out_square = jnp.clip(jnp.exp(math.log(3.3458075421322064e-08) - 1.3867695 * jax.random.uniform(streams_of[19], (2, EXPERTS + 1, FFN, D), jnp.float32) ** steps_of(streams_of[19], (2, EXPERTS + 1, FFN, D), ((0, 2), (2, 16)), -0.2, 0.2)), 8.360545145080778e-09, 3.3458075421322064e-08)
    return {"inputs": inputs, "cotangent": cotangent, "lengths": lengths, "routes": routes, "step_count": step_count, "norm_gains": norm_gains, "gains_mean": gains_mean, "gains_square": gains_square, "attn_weight": attn_weight, "attn_mean": attn_mean, "attn_square": attn_square, "router_weight": router_weight, "router_mean": router_mean, "router_square": router_square, "expert_in": expert_in, "in_mean": in_mean, "in_square": in_square, "expert_out": expert_out, "out_mean": out_mean, "out_square": out_square}


@jax.custom_vjp
def low(v):
    return lax.optimization_barrier(v.astype(jnp.bfloat16)).astype(jnp.float32)

@jax.custom_vjp
def low_back(v):
    return v

def low_keep(v):
    return (low(v), None)

def low_pass(kept, grad):
    return (grad,)

def back_keep(v):
    return (v, None)

def back_low(kept, grad):
    return (low(grad),)
low.defvjp(low_keep, low_pass)
low_back.defvjp(back_keep, back_low)
EPS_NORM = 1e-06
BETA_ONE = 0.9
BETA_TWO = 0.95
RATE_FACTOR = 3.0
GAIN_RATE = 0.3
DECAY_RATE = 0.1
ADAM_EPS = 1e-08
CLIP_LIMIT = 1.0
MASK_VALUE = -1e+30
HIGHEST_MODE = lax.Precision.HIGHEST

def matmul(left, right):
    return jnp.dot(left, right, precision=HIGHEST_MODE, preferred_element_type=jnp.float32)

def softmax_rows(values, axis_index):
    top_value = lax.optimization_barrier(jnp.max(values, axis=axis_index, keepdims=True))
    raised = jnp.exp(values - top_value)
    return raised / lax.optimization_barrier(jnp.sum(raised, axis=axis_index, keepdims=True))

def rotate(values, positions, direction):
    half_dim = HEAD_DIM // 2
    frequency = jnp.exp(-jnp.log(10000.0) * (2.0 * jnp.arange(half_dim, dtype=jnp.float32) / HEAD_DIM))
    angles = positions.astype(jnp.float32)[:, None] * frequency[None, :]
    cosine = jnp.cos(angles)[:, None, :]
    sine_part = direction * jnp.sin(angles)[:, None, :]
    first_half = values[:, :, :half_dim]
    second_half = values[:, :, half_dim:]
    return jnp.concatenate([first_half * cosine - second_half * sine_part, second_half * cosine + first_half * sine_part], axis=2)

def slot_index(route_rows):
    flat_routes = route_rows.reshape(-1).astype(jnp.int32)
    onehot = (flat_routes[:, None] == jnp.arange(EXPERTS, dtype=jnp.int32)[None, :]).astype(jnp.int32)
    before = jnp.cumsum(onehot, axis=0) - onehot
    return (flat_routes * CAP + lax.optimization_barrier(jnp.sum(before * onehot, axis=1))).astype(jnp.int32)

def sequence_layer(weights, inputs):
    gain_pair, attn_w, router_w, weight_in, weight_out = weights
    tokens_in, length, route_rows = inputs
    total_rows = tokens_in.shape[0]
    positions = jnp.arange(total_rows, dtype=jnp.int32)
    scale_one = lax.rsqrt(lax.optimization_barrier(jnp.mean(tokens_in * tokens_in, axis=1, keepdims=True)) + EPS_NORM)
    normed = low(tokens_in * scale_one * gain_pair[0])
    mixed_rows = low_back(matmul(normed, attn_w[:, :3 * D]))
    queries = low(rotate(mixed_rows[:, :D].reshape(total_rows, HEADS, HEAD_DIM), positions, 1.0))
    keys_low = low(rotate(mixed_rows[:, D:2 * D].reshape(total_rows, HEADS, HEAD_DIM), positions, 1.0))
    values_low = low(mixed_rows[:, 2 * D:].reshape(total_rows, HEADS, HEAD_DIM))
    scores = low_back(jnp.einsum('qhd,khd->hqk', queries, keys_low, precision=HIGHEST_MODE) * HEAD_DIM ** (-0.5))
    allowed = (positions[None, :] <= positions[:, None]) & (positions[None, :] < length)
    scores = jnp.where(allowed[None], scores, MASK_VALUE)
    probs_low = low(softmax_rows(scores, 2))
    attended = low(low_back(jnp.einsum('hqk,khd->qhd', probs_low, values_low, precision=HIGHEST_MODE).reshape(total_rows, D)))
    residual = tokens_in + low_back(matmul(attended, attn_w[:, 3 * D:]))
    scale_two = lax.rsqrt(lax.optimization_barrier(jnp.mean(residual * residual, axis=1, keepdims=True)) + EPS_NORM)
    second = low(residual * scale_two * gain_pair[1])
    logits = low_back(matmul(second, router_w))
    gate_probs = softmax_rows(jnp.take_along_axis(logits, route_rows, axis=1), 1)
    blocks = total_rows // SEQ_DEV

    def expert_block(block_rows, block_routes, block_gates):
        slot_ids = slot_index(block_routes)
        buffer = jnp.zeros((EXPERTS * CAP, D), jnp.float32).at[slot_ids].set(jnp.repeat(block_rows, 2, axis=0))
        buffer = buffer.reshape(EXPERTS, CAP, D)
        hidden_pre = low_back(jnp.einsum('ecd,edgf->ecgf', buffer, weight_in[:EXPERTS], precision=HIGHEST_MODE))
        acted = low(jax.nn.silu(hidden_pre[:, :, 0]) * hidden_pre[:, :, 1])
        slot_out = low_back(jnp.einsum('ecf,efd->ecd', acted, weight_out[:EXPERTS], precision=HIGHEST_MODE))
        picked = slot_out.reshape(EXPERTS * CAP, D)[slot_ids].reshape(SEQ_DEV, 2, D)
        return lax.optimization_barrier(jnp.sum(picked * block_gates[:, :, None], axis=1))
    mixture = jax.vmap(expert_block)(second.reshape(blocks, SEQ_DEV, D), route_rows.reshape(blocks, SEQ_DEV, 2), gate_probs.reshape(blocks, SEQ_DEV, 2)).reshape(total_rows, D)
    shared_pre = low_back(jnp.einsum('nd,dgf->ngf', second, weight_in[EXPERTS], precision=HIGHEST_MODE))
    shared_act = low(jax.nn.silu(shared_pre[:, 0]) * shared_pre[:, 1])
    shared_out = low_back(matmul(shared_act, weight_out[EXPERTS]))
    return residual + mixture + shared_out

def layer_all(masters, tokens_all, lengths, routes):
    weights = (low(masters[0]), low(masters[1]), low(masters[2]), low(masters[3]), low(masters[4]))
    checked = jax.checkpoint(sequence_layer)

    def one_sequence(inputs):
        return checked(weights, inputs)
    return lax.map(one_sequence, (tokens_all, lengths, routes))

def clip_layers(gradient):
    squares = lax.optimization_barrier(jnp.sum((gradient * gradient).reshape(2, -1), axis=1))
    norms = jnp.sqrt(squares)
    factor = jnp.minimum(1.0, CLIP_LIMIT / norms)
    shaped = factor.reshape((2,) + (1,) * (gradient.ndim - 1))
    return (norms, gradient * shaped)

def adam_update(gradient, clipped, master, mean_old, square_old, step_value, learn_rate):
    mean_new = BETA_ONE * mean_old + (1.0 - BETA_ONE) * clipped
    square_new = BETA_TWO * square_old + (1.0 - BETA_TWO) * clipped * clipped
    fix_one = 1.0 - BETA_ONE ** step_value
    fix_two = 1.0 - BETA_TWO ** step_value
    master_new = master - learn_rate * (mean_new / fix_one / (jnp.sqrt(square_new / fix_two) + ADAM_EPS) + DECAY_RATE * master)
    return (gradient, mean_new, square_new, master_new, master_new.astype(jnp.bfloat16))

def reference(inputs, cotangent, lengths, routes, step_count, norm_gains, gains_mean, gains_square, attn_weight, attn_mean, attn_square, router_weight, router_mean, router_square, expert_in, in_mean, in_square, expert_out, out_mean, out_square):
    first_layer = (norm_gains[0], attn_weight[0], router_weight[0], expert_in[0], expert_out[0])
    second_layer = (norm_gains[1], attn_weight[1], router_weight[1], expert_in[1], expert_out[1])

    def run_first(weights, tokens_all):
        return layer_all(weights, tokens_all, lengths, routes[0])

    def run_second(weights, tokens_all):
        return layer_all(weights, tokens_all, lengths, routes[1])
    first_out, first_pull = jax.vjp(run_first, first_layer, inputs.astype(jnp.float32))
    hidden = low(first_out)
    second_out, second_pull = jax.vjp(run_second, second_layer, hidden)
    valid_rows = (jnp.arange(SLOT, dtype=jnp.int32)[None, :] < lengths[:, None]).astype(jnp.float32)
    second_grads, hidden_grad = second_pull(cotangent.astype(jnp.float32) * valid_rows[:, :, None])
    first_grads, input_grad = first_pull(low(hidden_grad))
    layer_outputs = jnp.stack([hidden, second_out]).astype(jnp.bfloat16)
    input_grads = jnp.stack([input_grad, hidden_grad])
    step_value = step_count[0].astype(jnp.float32)
    wide_rate = RATE_FACTOR / D ** 0.5
    router_rate = RATE_FACTOR / (D // 4) ** 0.5
    down_rate = RATE_FACTOR / FFN ** 0.5
    gains_full = jnp.stack([first_grads[0], second_grads[0]])
    attn_full = jnp.stack([first_grads[1], second_grads[1]])
    router_full = jnp.stack([first_grads[2], second_grads[2]])
    in_full = jnp.stack([first_grads[3], second_grads[3]])
    out_full = jnp.stack([first_grads[4], second_grads[4]])
    gains_norm, gains_clip = clip_layers(gains_full)
    attn_norm, attn_clip = clip_layers(attn_full)
    router_norm, router_clip = clip_layers(router_full)
    in_norm, in_clip = clip_layers(in_full)
    out_norm, out_clip = clip_layers(out_full)
    clip_norms = jnp.stack([gains_norm, attn_norm, router_norm, in_norm, out_norm], axis=1)
    gains_grad, gains_mean_new, gains_square_new, gains_master, gains_copy = adam_update(gains_full, gains_clip, norm_gains, gains_mean, gains_square, step_value, GAIN_RATE)
    attn_grad, attn_mean_new, attn_square_new, attn_master, attn_copy = adam_update(attn_full, attn_clip, attn_weight, attn_mean, attn_square, step_value, wide_rate)
    router_grad, router_mean_new, router_square_new, router_master, router_copy = adam_update(router_full, router_clip, router_weight, router_mean, router_square, step_value, router_rate)
    in_grad, in_mean_new, in_square_new, in_master, in_copy = adam_update(in_full, in_clip, expert_in, in_mean, in_square, step_value, wide_rate)
    out_grad, out_mean_new, out_square_new, out_master, out_copy = adam_update(out_full, out_clip, expert_out, out_mean, out_square, step_value, down_rate)
    return (layer_outputs, input_grads, gains_grad, gains_mean_new, gains_square_new, gains_master, gains_copy, attn_grad, attn_mean_new, attn_square_new, attn_master, attn_copy, router_grad, router_mean_new, router_square_new, router_master, router_copy, in_grad, in_mean_new, in_square_new, in_master, in_copy, out_grad, out_mean_new, out_square_new, out_master, out_copy, clip_norms)
```

```python
import functools

import jax
import jax.numpy as jnp
from jax import lax
from jax.experimental import pallas as pl
from jax.experimental.pallas import tpu as pltpu
from jax.sharding import PartitionSpec as P

D = 768
HEADS = 12
HEAD_DIM = 64
FFN = 2048
EXPERTS = 3
ROWS = 256
CTX = 4
SEQ = ROWS * CTX
HEADS_DEV = HEADS // CTX
WIDE = 128
EXT = 3 * HEADS_DEV * WIDE
COLS = HEADS_DEV * HEAD_DIM

EPS_NORM = 1e-06
BETA_ONE = 0.9
BETA_TWO = 0.95
RATE_FACTOR = 3.0
GAIN_RATE = 0.3
DECAY_RATE = 0.1
ADAM_EPS = 1e-08
CLIP_LIMIT = 1.0
MASK_VALUE = -1e30
SCORE_SCALE = HEAD_DIM ** (-0.5) / 2.0
BF16 = jnp.bfloat16
F32 = jnp.float32
VMEM_LIMIT = 56 * 1024 * 1024
NT = (((1,), (1,)), ((), ()))
TN = (((0,), (0,)), ((), ()))
HALF = ROWS // 2
LANES = 128
MESH = pl.DeviceIdType.MESH
EXACT = lax.Precision.HIGHEST


def dot(left, right):
    return jnp.dot(left, right, preferred_element_type=F32)


def dot_nt(left, right):
    return lax.dot_general(left, right, NT, preferred_element_type=F32)


def dot_tn(left, right):
    return lax.dot_general(left, right, TN, preferred_element_type=F32)


def params(collective_id):
    return pltpu.CompilerParams(
        vmem_limit_bytes=VMEM_LIMIT, collective_id=collective_id, has_side_effects=True
    )


def whole(shape):
    return pl.BlockSpec(shape, lambda *_: (0,) * len(shape))


def allowed_keys(block, keys, length):
    key_pos = lax.broadcasted_iota(jnp.int32, (ROWS, keys), 1)
    query_pos = lax.broadcasted_iota(jnp.int32, (ROWS, keys), 0) + block * ROWS
    return (key_pos <= query_pos) & (key_pos < length)


VMEM = pl.BlockSpec(memory_space=pltpu.VMEM)
SMEM = pl.BlockSpec(memory_space=pltpu.SMEM)


def ring():
    me = lax.axis_index("ctx")
    return me, lax.rem(me + 1, CTX), lax.rem(me + 3, CTX), lax.rem(me + 2, CTX)


def greet(peers):
    barrier = pltpu.get_barrier_semaphore()
    for peer in peers:
        pl.semaphore_signal(barrier, inc=1, device_id={"ctx": peer}, device_id_type=MESH)


def met(count):
    pl.semaphore_wait(pltpu.get_barrier_semaphore(), count)


def remote(source, target, send, recv, peer):
    return pltpu.make_async_remote_copy(
        src_ref=source,
        dst_ref=target,
        send_sem=send,
        recv_sem=recv,
        device_id={"ctx": peer},
        device_id_type=MESH,
    )


def rows_of(block, half=None):
    if half is None:
        return pl.ds(pl.multiple_of(block * ROWS, ROWS), ROWS)
    return pl.ds(pl.multiple_of(block * ROWS + half * HALF, HALF), HALF)


def gather_rows(all_ref, send, recv):
    me, right, left, _ = ring()

    def piece(index, block, half, peer):
        spot = all_ref.at[rows_of(block, half)]
        return remote(spot, spot, send.at[index], recv.at[index], peer)

    copies = [
        piece(0, me, 0, right),
        piece(1, me, 1, left),
        piece(2, me, 1, right),
        piece(3, me, 0, left),
    ]
    for copy in copies:
        copy.start()
    copies[0].wait_recv()
    copies.append(piece(4, left, 0, right))
    copies[4].start()
    copies[1].wait_recv()
    copies.append(piece(5, right, 1, left))
    copies[5].start()
    for index in range(2, 6):
        copies[index].wait_recv()
    for copy in copies:
        copy.wait_send()


def reduce_rows(make, part, across_in, from_left, from_right, send, recv, beside=None):
    me, right, left, across = ring()
    top, bottom = pl.ds(0, HALF), pl.ds(HALF, HALF)

    def piece(index, block, half, target, peer):
        return remote(part.at[rows_of(block, half)], target, send.at[index], recv.at[index], peer)

    make(across)
    copies = [
        piece(0, across, 0, across_in.at[0], right),
        piece(1, across, 1, across_in.at[1], left),
    ]
    copies[0].start()
    copies[1].start()
    make(right)
    copies.append(piece(2, right, 1, from_left.at[bottom], right))
    copies[2].start()
    make(left)
    copies.append(piece(3, left, 0, from_right.at[top], left))
    copies[3].start()
    copies[0].wait_recv()
    spot = rows_of(right, 0)
    part[spot, :] = (part[spot, :].astype(F32) + across_in[0].astype(F32)).astype(BF16)
    copies.append(piece(4, right, 0, from_left.at[top], right))
    copies[4].start()
    copies[1].wait_recv()
    spot = rows_of(left, 1)
    part[spot, :] = (part[spot, :].astype(F32) + across_in[1].astype(F32)).astype(BF16)
    copies.append(piece(5, left, 1, from_right.at[bottom], left))
    copies[5].start()
    make(me)
    if beside is not None:
        beside()
    for index in range(2, 6):
        copies[index].wait_recv()
    for copy in copies:
        copy.wait_send()
    return (
        part[rows_of(me), :].astype(F32) + from_left[...].astype(F32) + from_right[...].astype(F32)
    )


REDUCE_SCRATCH = [
    pltpu.VMEM((SEQ, D), BF16),
    pltpu.VMEM((2, HALF, D), BF16),
    pltpu.VMEM((ROWS, D), BF16),
    pltpu.VMEM((ROWS, D), BF16),
    pltpu.SemaphoreType.DMA((6,)),
    pltpu.SemaphoreType.DMA((6,)),
]


def inverse_size(values):
    return lax.rsqrt(jnp.mean(values * values, axis=1, keepdims=True) + EPS_NORM)


def attn_forward_kernel(
    length_ref, u_ref, gains_ref, router_ref, routes_ref, w_ref, back_ref, table_ref,
    a_ref, qkv_ref, mass_ref, attended_ref, residual_ref, b_ref, gates_ref, gate_ref,
    heads_out, send_a, recv_a, send_o, recv_o, send_b, recv_b,
):
    me, right, left, across = ring()
    greet((right, left, across))
    length = length_ref[0]
    tokens = u_ref[...].astype(F32)
    a_ref[rows_of(me), :] = (tokens * inverse_size(tokens) * gains_ref[0:1, :]).astype(BF16)
    met(3)
    gather_rows(a_ref, send_a, recv_a)
    for block in range(CTX):
        rows = pl.ds(block * ROWS, ROWS)
        table = table_ref[rows, :]
        mixed = dot(a_ref[rows, :], w_ref[...])
        for part in range(3 * HEADS_DEV):
            lanes = slice(part * WIDE, (part + 1) * WIDE)
            piece = mixed[:, lanes]
            if part < 2 * HEADS_DEV:
                turned = piece * table
                piece = turned + pltpu.roll(turned, WIDE // 2, 1)
            qkv_ref[rows, lanes] = piece.astype(BF16)

    def handed(block):
        step = lax.rem(block - me + CTX, CTX)
        return remote(
            heads_out.at[block], attended_ref.at[me], send_o.at[step], recv_o.at[step], block
        )

    for block in reversed(range(CTX)):
        rows = pl.ds(block * ROWS, ROWS)
        keys = (block + 1) * ROWS
        allowed = allowed_keys(block, keys, length)
        outs = []
        for head in range(HEADS_DEV):
            queries = qkv_ref[rows, head * WIDE : (head + 1) * WIDE]
            key_lanes = slice((HEADS_DEV + head) * WIDE, (HEADS_DEV + head + 1) * WIDE)
            value_lanes = slice((2 * HEADS_DEV + head) * WIDE, (2 * HEADS_DEV + head + 1) * WIDE)
            scores = dot_nt(queries, qkv_ref[:keys, key_lanes]) * SCORE_SCALE
            scores = jnp.where(allowed, scores, MASK_VALUE)
            top = jnp.max(scores, axis=1, keepdims=True)
            raw = jnp.exp(scores - top)
            total = jnp.sum(raw, axis=1, keepdims=True)
            probs = (raw * (1.0 / total)).astype(BF16)
            outs.append(dot(probs, qkv_ref[:keys, value_lanes]))
            mass_ref[head, rows, :] = top + jnp.log(total)
        first = (outs[0] + pltpu.roll(outs[1], WIDE // 2, 1)).astype(BF16)
        second = outs[2][:, : WIDE // 2].astype(BF16)
        heads_out[block, :, :WIDE] = first
        heads_out[block, :, WIDE:] = second

        @pl.when(block != me)
        def _():
            handed(block).start()

    attended_ref[me] = heads_out[me]
    for step in range(1, CTX):
        pltpu.make_async_copy(heads_out.at[0], attended_ref.at[0], recv_o.at[step]).wait()
    residual = tokens
    for block in range(CTX):
        residual = residual + dot(attended_ref[block], back_ref[block * COLS : (block + 1) * COLS, :])
    residual_ref[...] = residual
    b_ref[rows_of(me), :] = (residual * inverse_size(residual) * gains_ref[1:2, :]).astype(BF16)
    for step in range(1, CTX):
        pltpu.make_async_copy(heads_out.at[0], attended_ref.at[0], send_o.at[step]).wait()
    gather_rows(b_ref, send_b, recv_b)
    lanes = lax.broadcasted_iota(jnp.int32, (ROWS, LANES), 1)
    for block in range(CTX):
        rows = pl.ds(block * ROWS, ROWS)
        logits = dot(b_ref[rows, :], router_ref[...])
        named = (lanes == routes_ref[rows, 0:1]) | (lanes == routes_ref[rows, 1:2])
        chosen = jnp.where(named, logits, MASK_VALUE)
        raw = jnp.where(named, jnp.exp(chosen - jnp.max(chosen, axis=1, keepdims=True)), 0.0)
        gates = raw / jnp.sum(raw, axis=1, keepdims=True)
        gates_ref[rows, :] = gates
        gates = jnp.where(lanes == EXPERTS, 1.0, gates)
        gate_ref[rows, :] = jnp.sum(jnp.where(lanes == me, gates, 0.0), axis=1, keepdims=True)


def attn_forward(length, u, gains, router, routes, w_ext, w_back, table):
    sems = pltpu.SemaphoreType.DMA
    return pl.pallas_call(
        attn_forward_kernel,
        out_shape=(
            jax.ShapeDtypeStruct((SEQ, D), BF16),
            jax.ShapeDtypeStruct((SEQ, EXT), BF16),
            jax.ShapeDtypeStruct((HEADS_DEV, SEQ, 1), F32),
            jax.ShapeDtypeStruct((CTX, ROWS, COLS), BF16),
            jax.ShapeDtypeStruct((ROWS, D), F32),
            jax.ShapeDtypeStruct((SEQ, D), BF16),
            jax.ShapeDtypeStruct((SEQ, LANES), F32),
            jax.ShapeDtypeStruct((SEQ, 1), F32),
        ),
        in_specs=[SMEM] + [VMEM] * 7,
        out_specs=[VMEM] * 8,
        scratch_shapes=[pltpu.VMEM((CTX, ROWS, COLS), BF16)]
        + [sems((6,)), sems((6,)), sems((CTX,)), sems((CTX,)), sems((6,)), sems((6,))],
        compiler_params=params(1),
        name="attn_forward",
    )(length, u, gains, router, routes, w_ext, w_back, table)


def attn_backward_kernel(
    last, length_ref, u_ref, gains_ref, router_ref, w_ref, back_ref, table_ref,
    a_ref, qkv_ref, mass_ref, attended_ref, residual_ref, second_ref, gates_ref,
    delta_ref, db_ref, gate_grad_ref, *rest,
):
    if last:
        input_ref, dheads_ref, dback_ref, small_ref = rest[:4]
        rest = rest[4:]
    else:
        input_ref, lower_ref, dheads_ref, dback_ref, small_ref = rest[:5]
        rest = rest[5:]
    key_acc, value_acc, dz, grads_out, grads_in, send_o, recv_o = rest[:7]
    part, across_in, from_left, from_right, send_r, recv_r = rest[7:13]
    me, right, left, across = ring()
    greet((right, left, across))
    length = length_ref[0]
    lanes = lax.broadcasted_iota(jnp.int32, (ROWS, LANES), 1)
    gates = gates_ref[...]
    gate_grads = jnp.where(lanes < EXPERTS, gate_grad_ref[...], 0.0)
    logit_grad = gates * (gate_grads - jnp.sum(gates * gate_grads, axis=1, keepdims=True))
    logit_grad = logit_grad.astype(BF16)
    second_grad = db_ref[...] + dot_nt(logit_grad, router_ref[...])
    residual = residual_ref[...]
    scale_two = inverse_size(residual)
    normal_two = residual * scale_two
    gain_two_terms = second_grad * normal_two
    scaled_two = second_grad * gains_ref[1:2, :]
    residual_grad = delta_ref[...].astype(F32) + scale_two * (
        scaled_two - normal_two * jnp.mean(scaled_two * normal_two, axis=1, keepdims=True)
    )
    input_ref[...] = residual_grad
    branch_grad = residual_grad.astype(BF16)
    met(3)

    for block in range(CTX):
        grads_out[block] = dot_nt(branch_grad, back_ref[block * COLS : (block + 1) * COLS, :]).astype(
            BF16
        )

        @pl.when(block != me)
        def _():
            step = lax.rem(block - me + CTX, CTX)
            remote(
                grads_out.at[block], grads_in.at[me], send_o.at[step], recv_o.at[step], block
            ).start()

    grads_in[me] = grads_out[me]
    for block in range(CTX):
        dback_ref[block * COLS : (block + 1) * COLS, :] = dot_tn(
            attended_ref[block], branch_grad
        ).astype(BF16)
    router_terms = dot_tn(second_ref[...], logit_grad)
    ones = jnp.ones((ROWS, LANES), F32)
    gain_two_column = lax.dot_general(
        gain_two_terms, ones, TN, precision=EXACT, preferred_element_type=F32
    )
    key_acc[...] = jnp.zeros_like(key_acc)
    value_acc[...] = jnp.zeros_like(value_acc)
    for step in range(1, CTX):
        pltpu.make_async_copy(grads_out.at[0], grads_in.at[0], recv_o.at[step]).wait()
    for step in range(1, CTX):
        pltpu.make_async_copy(grads_out.at[0], grads_in.at[0], send_o.at[step]).wait()
    for block in range(CTX):
        rows = pl.ds(block * ROWS, ROWS)
        keys = (block + 1) * ROWS
        allowed = allowed_keys(block, keys, length)
        pair = grads_in[block, :, :WIDE]
        tail = grads_in[block, :, WIDE:]
        head_grads = (
            pair,
            pltpu.roll(pair.astype(F32), WIDE // 2, 1).astype(BF16),
            jnp.concatenate([tail, jnp.zeros_like(tail)], axis=1),
        )
        for head in range(HEADS_DEV):
            queries = qkv_ref[rows, head * WIDE : (head + 1) * WIDE]
            keys_all = qkv_ref[:keys, (HEADS_DEV + head) * WIDE : (HEADS_DEV + head + 1) * WIDE]
            values_all = qkv_ref[
                :keys, (2 * HEADS_DEV + head) * WIDE : (2 * HEADS_DEV + head + 1) * WIDE
            ]
            grads = head_grads[head]
            scores = dot_nt(queries, keys_all) * SCORE_SCALE
            probs = jnp.where(allowed, jnp.exp(scores - mass_ref[head, rows, :]), 0.0)
            prob_grad = dot_nt(grads, values_all)
            row_sum = jnp.sum(probs * prob_grad, axis=1, keepdims=True)
            score_grad = (probs * (prob_grad - row_sum)).astype(BF16)
            query_grad = dot(score_grad, keys_all) * (HEAD_DIM**-0.5)
            dz[rows, head * WIDE : (head + 1) * WIDE] = (query_grad * table_ref[rows, :]).astype(BF16)
            spot = slice(head * WIDE, (head + 1) * WIDE)
            key_acc[:keys, spot] += dot_tn(score_grad, queries)
            value_acc[:keys, spot] += dot_tn(probs.astype(BF16), grads)
    for block in range(CTX):
        rows = pl.ds(block * ROWS, ROWS)
        table = table_ref[rows, :] * (HEAD_DIM**-0.5)
        for head in range(HEADS_DEV):
            spot = slice(head * WIDE, (head + 1) * WIDE)
            at = (HEADS_DEV + head) * WIDE
            dz[rows, at : at + WIDE] = (key_acc[rows, spot] * table).astype(BF16)
            at = (2 * HEADS_DEV + head) * WIDE
            dz[rows, at : at + WIDE] = value_acc[rows, spot].astype(BF16)

    def make(block):
        part[rows_of(block), :] = dot_nt(dz[rows_of(block), :], w_ref[...]).astype(BF16)

    def beside():
        wide_lanes = lax.broadcasted_iota(jnp.int32, (D, WIDE), 1)
        pieces = []
        for piece in range(3):
            spot = slice(piece * HEADS_DEV * WIDE, (piece + 1) * HEADS_DEV * WIDE)
            terms = dot_tn(a_ref[...], dz[:, spot])
            for head in range(HEADS_DEV):
                term = terms[:, head * WIDE : (head + 1) * WIDE]
                if piece < 2:
                    term = term + jnp.where(
                        wide_lanes < HEAD_DIM // 2,
                        pltpu.roll(term, HEAD_DIM // 2, 1),
                        -pltpu.roll(term, WIDE - HEAD_DIM // 2, 1),
                    )
                pieces.append(term)
        for pair in range(4):
            joined = jnp.where(
                wide_lanes < HEAD_DIM,
                pieces[2 * pair],
                pltpu.roll(pieces[2 * pair + 1], HEAD_DIM, 1),
            )
            dheads_ref[:, pair * WIDE : (pair + 1) * WIDE] = joined.astype(BF16)
        dheads_ref[:, 4 * WIDE :] = pieces[8][:, :HEAD_DIM].astype(BF16)

    normed_grad = reduce_rows(make, part, across_in, from_left, from_right, send_r, recv_r, beside)
    tokens = u_ref[...].astype(F32)
    scale_one = inverse_size(tokens)
    normal_one = tokens * scale_one
    gain_one_column = lax.dot_general(
        normed_grad * normal_one, ones, TN, precision=EXACT, preferred_element_type=F32
    )
    scaled_one = normed_grad * gains_ref[0:1, :]
    input_grad = input_ref[...] + scale_one * (
        scaled_one - normal_one * jnp.mean(scaled_one * normal_one, axis=1, keepdims=True)
    )
    input_ref[...] = input_grad
    small_lanes = lax.broadcasted_iota(jnp.int32, (D, LANES), 1)
    small_ref[...] = jnp.where(
        small_lanes == EXPERTS,
        gain_one_column,
        jnp.where(small_lanes == EXPERTS + 1, gain_two_column, router_terms),
    ).astype(BF16)
    if not last:
        lower_ref[rows_of(me), :] = input_grad.astype(BF16)
        gather_rows(lower_ref, *rest[13:])


def attn_backward(last, length, *arrays):
    sems = pltpu.SemaphoreType.DMA
    out_shape = [jax.ShapeDtypeStruct((ROWS, D), F32)]
    if not last:
        out_shape.append(jax.ShapeDtypeStruct((SEQ, D), BF16))
    out_shape += [
        jax.ShapeDtypeStruct((D, 3 * COLS), BF16),
        jax.ShapeDtypeStruct((D, D), BF16),
        jax.ShapeDtypeStruct((D, LANES), BF16),
    ]
    scratch = [
        pltpu.VMEM((SEQ, HEADS_DEV * WIDE), F32),
        pltpu.VMEM((SEQ, HEADS_DEV * WIDE), F32),
        pltpu.VMEM((SEQ, EXT), BF16),
        pltpu.VMEM((CTX, ROWS, COLS), BF16),
        pltpu.VMEM((CTX, ROWS, COLS), BF16),
        sems((CTX,)),
        sems((CTX,)),
    ] + REDUCE_SCRATCH
    if not last:
        scratch += [sems((6,)), sems((6,))]
    return pl.pallas_call(
        functools.partial(attn_backward_kernel, last),
        out_shape=tuple(out_shape),
        in_specs=[SMEM] + [VMEM] * len(arrays),
        out_specs=[VMEM] * len(out_shape),
        scratch_shapes=scratch,
        compiler_params=params(3 if last else 4),
        name="attn_backward",
    )(length, *arrays)


SHARDS_STEP = 4
IN_ROWS = D
HALF_ROWS = (D + D * 128 // 256) // 2


def assemble(w_ref, win, wout):
    shards, units = win.shape[0], LANES
    width = 2 * units
    split = HALF_ROWS
    for shard in range(shards):
        win[shard, :split, :] = w_ref[0, shard]
        win[shard, split:, :] = w_ref[1, shard, : D - split, :]
        for piece in range(D // width):
            at = D - split + piece * units
            wout[shard * units : (shard + 1) * units, piece * width : (piece + 1) * width] = w_ref[
                1, shard, at : at + units, :
            ]


def ffn_forward_kernel(
    b_ref, gate_ref, residual_ref, w_ref, y_ref, kept_ref, acc, win, wout,
    part, across_in, from_left, from_right, send, recv,
):
    step = pl.program_id(0)
    final = pl.num_programs(0) - 1
    shards, units = win.shape[0], LANES

    @pl.when(step == 0)
    def _():
        _, right, left, _ = ring()
        greet((right, left))
        acc[...] = jnp.zeros_like(acc)

    assemble(w_ref, win, wout)

    def terms(block):
        rows = rows_of(block)
        b_rows = b_ref[rows, :]
        acted = []
        for shard in range(shards):
            hidden = dot(b_rows, win[shard])
            kept_ref[shard, rows, :] = hidden.astype(BF16)
            gate_part = hidden[:, :units]
            acted.append(
                (gate_part / (1.0 + jnp.exp(-gate_part)) * hidden[:, units:]).astype(BF16)
            )
        return acc[rows, :] + dot(jnp.concatenate(acted, axis=1), wout[...])

    @pl.when(step < final)
    def _():
        for block in range(CTX):
            acc[pl.ds(block * ROWS, ROWS), :] = terms(block)

    @pl.when(step == final)
    def _():
        met(2)

        def make(block):
            rows = rows_of(block)
            part[rows, :] = (terms(block) * gate_ref[rows, :]).astype(BF16)

        total = reduce_rows(make, part, across_in, from_left, from_right, send, recv)
        y_ref[...] = (residual_ref[...] + total).astype(BF16)


def ffn_forward(b_all, gate_col, residual, weights):
    _, count, half_rows, double = weights.shape
    shards = SHARDS_STEP
    return pl.pallas_call(
        ffn_forward_kernel,
        grid=(count // shards,),
        out_shape=(
            jax.ShapeDtypeStruct((ROWS, D), BF16),
            jax.ShapeDtypeStruct((count, SEQ, double), BF16),
        ),
        in_specs=[
            whole((SEQ, D)),
            whole((SEQ, 1)),
            whole((ROWS, D)),
            pl.BlockSpec((2, shards, half_rows, double), lambda i: (0, i, 0, 0)),
        ],
        out_specs=[whole((ROWS, D)), pl.BlockSpec((shards, SEQ, double), lambda i: (i, 0, 0))],
        scratch_shapes=[
            pltpu.VMEM((SEQ, D), F32),
            pltpu.VMEM((shards, D, double), BF16),
            pltpu.VMEM((shards * double // 2, D), BF16),
        ]
        + REDUCE_SCRATCH,
        compiler_params=params(5),
        name="ffn_forward",
    )(b_all, gate_col, residual, weights)


def ffn_backward_kernel(
    b_ref, gate_ref, delta_ref, kept_ref, w_ref, db_ref, gate_grad_ref, dw_ref,
    acc, gate_acc, b_turned, slot_grad, hidden_grad, acted, win, wout, rows_out, rows_in, send_g, recv_g,
    part, across_in, from_left, from_right, send, recv,
):
    step = pl.program_id(0)
    final = pl.num_programs(0) - 1
    shards, units = win.shape[0], LANES
    width = 2 * units

    @pl.when(step == 0)
    def _():
        _, right, left, across = ring()
        greet((right, left, across))
        acc[...] = jnp.zeros_like(acc)
        gate_acc[...] = jnp.zeros_like(gate_acc)
        b_turned[...] = b_ref[...].T
        slot_grad[...] = (delta_ref[...].astype(F32) * gate_ref[...]).astype(BF16)

    assemble(w_ref, win, wout)

    def terms(block):
        rows = rows_of(block)
        gate = gate_ref[rows, :]
        act_grad_all = dot_nt(delta_ref[rows, :], wout[...])
        gate_sum = gate_acc[rows, :]
        second_grad = acc[rows, :]
        for shard in range(shards):
            hidden = kept_ref[shard, rows, :].astype(F32)
            gate_part = hidden[:, :units]
            up_part = hidden[:, units:]
            act_grad = act_grad_all[:, shard * units : (shard + 1) * units]
            sigmoid = 1.0 / (1.0 + jnp.exp(-gate_part))
            silu = gate_part * sigmoid
            act = (silu * up_part).astype(BF16)
            acted[rows, shard * units : (shard + 1) * units] = act
            gate_sum += act.astype(F32) * act_grad
            act_grad = act_grad * gate
            gate_grad = act_grad * up_part * (sigmoid * (1.0 + gate_part * (1.0 - sigmoid)))
            pair = jnp.concatenate([gate_grad, act_grad * silu], axis=1).astype(BF16)
            hidden_grad[shard, rows, :] = pair
            second_grad += dot_nt(pair, win[shard])
        gate_acc[rows, :] = gate_sum
        return second_grad

    def weight_terms():
        split = HALF_ROWS
        for shard in range(shards):
            whole_in = dot(b_turned[...], hidden_grad[shard]).astype(BF16)
            dw_ref[0, shard] = whole_in[:split]
            dw_ref[1, shard, : D - split, :] = whole_in[split:]
        whole_out = dot_tn(acted[...], slot_grad[...]).astype(BF16)
        for shard in range(shards):
            for piece in range(D // width):
                at = D - split + piece * units
                dw_ref[1, shard, at : at + units, :] = whole_out[
                    shard * units : (shard + 1) * units, piece * width : (piece + 1) * width
                ]

    @pl.when(step < final)
    def _():
        for block in range(CTX):
            acc[pl.ds(block * ROWS, ROWS), :] = terms(block)
        weight_terms()

    @pl.when(step == final)
    def _():
        met(3)
        me, right, left, across = ring()

        def make(block):
            part[rows_of(block), :] = terms(block).astype(BF16)

        def handed(step_to, peer):
            return remote(
                rows_out.at[peer], rows_in.at[step_to], send_g.at[step_to], recv_g.at[step_to], peer
            )

        def beside():
            own_row = lax.broadcasted_iota(jnp.int32, (8, LANES), 0) == me
            picker = jnp.where(own_row, 1.0, 0.0)
            for block in range(CTX):
                rows_out[block] = lax.dot_general(
                    picker,
                    gate_acc[pl.ds(block * ROWS, ROWS), :],
                    NT,
                    precision=EXACT,
                    preferred_element_type=F32,
                )
            for step_to, peer in ((0, right), (1, left), (2, across)):
                handed(step_to, peer).start()
            weight_terms()

        db_ref[...] = reduce_rows(
            make, part, across_in, from_left, from_right, send, recv, beside
        )
        for step_to, peer in ((0, right), (1, left), (2, across)):
            handed(step_to, peer).wait()
        rows_all = rows_out[me] + rows_in[0] + rows_in[1] + rows_in[2]
        picker = jnp.where(
            lax.broadcasted_iota(jnp.int32, (8, LANES), 0)
            == lax.broadcasted_iota(jnp.int32, (8, LANES), 1),
            1.0,
            0.0,
        )
        gate_grad_ref[...] = lax.dot_general(
            rows_all, picker, TN, precision=EXACT, preferred_element_type=F32
        )


def ffn_backward(b_all, gate_col, delta_all, kept, weights):
    _, count, half_rows, double = weights.shape
    shards = SHARDS_STEP
    units = double // 2
    sems = pltpu.SemaphoreType.DMA
    return pl.pallas_call(
        ffn_backward_kernel,
        grid=(count // shards,),
        out_shape=(
            jax.ShapeDtypeStruct((ROWS, D), F32),
            jax.ShapeDtypeStruct((ROWS, LANES), F32),
            jax.ShapeDtypeStruct(weights.shape, BF16),
        ),
        in_specs=[
            whole((SEQ, D)),
            whole((SEQ, 1)),
            whole((SEQ, D)),
            pl.BlockSpec((shards, SEQ, double), lambda i: (i, 0, 0)),
            pl.BlockSpec((2, shards, half_rows, double), lambda i: (0, i, 0, 0)),
        ],
        out_specs=[
            whole((ROWS, D)),
            whole((ROWS, LANES)),
            pl.BlockSpec((2, shards, half_rows, double), lambda i: (0, i, 0, 0)),
        ],
        scratch_shapes=[
            pltpu.VMEM((SEQ, D), F32),
            pltpu.VMEM((SEQ, units), F32),
            pltpu.VMEM((D, SEQ), BF16),
            pltpu.VMEM((SEQ, D), BF16),
            pltpu.VMEM((shards, SEQ, double), BF16),
            pltpu.VMEM((SEQ, shards * units), BF16),
            pltpu.VMEM((shards, D, double), BF16),
            pltpu.VMEM((shards * units, D), BF16),
            pltpu.VMEM((CTX, 8, ROWS), F32),
            pltpu.VMEM((3, 8, ROWS), F32),
            sems((3,)),
            sems((3,)),
        ]
        + REDUCE_SCRATCH,
        compiler_params=params(6),
        name="ffn_backward",
    )(b_all, gate_col, delta_all, kept, weights)

def rotary_table():
    half_dim = HEAD_DIM // 2
    frequency = jnp.exp(
        -jnp.log(10000.0) * (2.0 * jnp.arange(half_dim, dtype=F32) / HEAD_DIM)
    )
    angles = jnp.arange(SEQ, dtype=jnp.int32).astype(F32)[:, None] * frequency[None, :]
    cosine, sine = jnp.cos(angles), jnp.sin(angles)
    return jnp.concatenate([cosine, cosine, sine, sine], axis=1)


def extended(w_heads):
    half_dim = HEAD_DIM // 2
    turning = w_heads[:, : 2 * COLS].reshape(D, 2 * HEADS_DEV, 2, half_dim)
    first, second = turning[:, :, 0], turning[:, :, 1]
    turning = jnp.concatenate([first, second, -second, first], axis=2)
    values = w_heads[:, 2 * COLS :].reshape(D, HEADS_DEV, HEAD_DIM)
    values = jnp.concatenate([values, jnp.zeros_like(values)], axis=2)
    return jnp.concatenate(
        [turning.reshape(D, 2 * HEADS_DEV * WIDE), values.reshape(D, HEADS_DEV * WIDE)], axis=1
    )


def layer_forward(weights, tokens_in, length, routes_all, table):
    gains, router, w_ext, w_back, experts = weights
    a_all, qkv, mass, attended, residual, b_all, gates, gate_col = attn_forward(
        length, tokens_in, gains, router, routes_all, w_ext, w_back, table
    )
    output, kept = ffn_forward(b_all, gate_col, residual, experts)
    return output, (tokens_in, a_all, qkv, mass, attended, residual, b_all, gates, gate_col, kept)


def layer_backward(weights, saved, delta_all, delta_own, length, table, ctx_index, last):
    gains, router, w_ext, w_back, experts = weights
    tokens_in, a_all, qkv, mass, attended, residual, b_all, gates, gate_col, kept = saved
    db, gate_grads, dexperts = ffn_backward(b_all, gate_col, delta_all, kept, experts)
    second = lax.dynamic_slice_in_dim(b_all, ctx_index * ROWS, ROWS, 0)
    own_gates = lax.dynamic_slice_in_dim(gates, ctx_index * ROWS, ROWS, 0)
    results = attn_backward(
        last, length, tokens_in, gains, router, w_ext, w_back, table, a_all, qkv, mass,
        attended, residual, second, own_gates, delta_own, db, gate_grads,
    )
    return dexperts, results

def adam_update(gradient, clipped, master, mean_old, square_old, step_value, learn_rate):
    mean_new = BETA_ONE * mean_old + (1.0 - BETA_ONE) * clipped
    square_new = BETA_TWO * square_old + (1.0 - BETA_TWO) * clipped * clipped
    fix_one = 1.0 - BETA_ONE**step_value
    fix_two = 1.0 - BETA_TWO**step_value
    master_new = master - learn_rate * (
        mean_new / fix_one / (jnp.sqrt(square_new / fix_two) + ADAM_EPS) + DECAY_RATE * master
    )
    return (gradient, mean_new, square_new, master_new, master_new.astype(BF16))


def on_device(
    inputs, cotangent, lengths, routes, step_count,
    norm_gains, gains_mean, gains_square,
    attn_weight, attn_mean, attn_square,
    router_weight, router_mean, router_square,
    expert_in, in_mean, in_square,
    expert_out, out_mean, out_square,
):
    section = lax.axis_index("section")
    ctx_index = lax.axis_index("ctx")
    fsdp = lax.axis_size("fsdp")
    everyone = ("section", "fsdp")
    shard_rows = attn_weight.shape[1]
    units = expert_in.shape[4]
    first_core = section == 0

    def own_columns(matrix, part):
        return lax.dynamic_slice_in_dim(matrix, part * D + ctx_index * COLS, COLS, 1)

    def swap(block):
        return lax.ppermute(block, "section", [(0, 1), (1, 0)])

    attn_shard = jnp.concatenate(
        [own_columns(attn_weight[0], part) for part in range(3)]
        + [attn_weight[0][:, 3 * D :], norm_gains[0].T, router_weight[0]],
        axis=1,
    ).astype(BF16)
    in_shard = (
        lax.dynamic_index_in_dim(expert_in[0], ctx_index, 0, keepdims=False)
        .astype(BF16)
        .reshape(D, 2 * units)
    )
    out_shard = lax.dynamic_index_in_dim(expert_out[0], ctx_index, 0, keepdims=False).astype(BF16)
    halves = jnp.concatenate(
        [in_shard] + [out_shard[:, at : at + 2 * units] for at in range(0, D, 2 * units)], axis=0
    ).reshape(2, HALF_ROWS, 2 * units)
    other = swap(jnp.where(first_core, halves[1], halves[0]))
    attn_full = lax.all_gather(attn_shard, everyone, tiled=True).reshape(2, D, -1)
    pieces = (jnp.where(first_core, halves[0], other), jnp.where(first_core, other, halves[1]))
    experts = [
        lax.all_gather(piece, everyone).reshape(2, fsdp, HALF_ROWS, 2 * units) for piece in pieces
    ]
    routes_all = lax.all_gather(routes[0], ("section", "ctx")).reshape((2, CTX) + routes.shape[1:])
    routes_all = lax.dynamic_index_in_dim(routes_all, section, 2, keepdims=False).reshape(2, SEQ, 2)
    length = lax.dynamic_slice_in_dim(lengths, section, 1, 0)
    tokens = lax.dynamic_index_in_dim(inputs, section, 0, keepdims=False)
    positions = ctx_index * ROWS + jnp.arange(ROWS, dtype=jnp.int32)
    seed = lax.dynamic_index_in_dim(cotangent, section, 0, keepdims=False)
    seed = jnp.where((positions < length[0])[:, None], seed, jnp.zeros_like(seed))
    seed_all = lax.all_gather(seed, "ctx", tiled=True)
    table = rotary_table()

    layers = []
    for layer in range(2):
        full = attn_full[layer]
        small_at = 3 * COLS + D
        gains = full[:, small_at : small_at + 2].astype(F32).T
        router = jnp.pad(full[:, small_at + 2 :], ((0, 0), (0, LANES - EXPERTS)))
        layers.append(
            (
                jnp.pad(gains, ((0, 6), (0, 0))),
                router,
                extended(full[:, : 3 * COLS]),
                full[:, 3 * COLS : small_at],
                experts[layer],
            )
        )
    lower_out, lower_saved = layer_forward(layers[0], tokens, length, routes_all[0], table)
    upper_out, upper_saved = layer_forward(layers[1], lower_out, length, routes_all[1], table)

    def scattered(terms):
        return lax.psum_scatter(
            terms.reshape((2 * fsdp,) + terms.shape[2:]), everyone, scatter_dimension=0, tiled=True
        )[0]

    upper_experts, (upper_grad, lower_seed, *upper_rest) = layer_backward(
        layers[1], upper_saved, seed_all, seed, length, table, ctx_index, False
    )
    upper_half = scattered(upper_experts)
    own_seed = upper_grad.astype(BF16)
    lower_experts, (lower_grad, *lower_rest) = layer_backward(
        layers[0], lower_saved, lower_seed, own_seed, length, table, ctx_index, True
    )
    lower_half = scattered(lower_experts)

    def paired(first, second):
        kept = jnp.where(first_core, first, second)
        other = swap(jnp.where(first_core, second, first))
        return jnp.stack(
            [jnp.where(first_core, kept, other), jnp.where(first_core, other, kept)]
        )

    layer_outputs = paired(lower_out, upper_out)[None]
    input_grads = paired(lower_grad, upper_grad)[None]
    expert_part = paired(lower_half, upper_half).reshape(2 * HALF_ROWS, 2 * units)
    attn_terms = jnp.stack([jnp.concatenate(lower_rest, axis=1), jnp.concatenate(upper_rest, axis=1)])
    attn_part = scattered(attn_terms.reshape(2, fsdp, shard_rows, -1))
    expert_all = lax.all_gather(expert_part, "ctx")
    attn_all = lax.all_gather(attn_part, "ctx")
    in_sum = expert_all[:, :D].astype(F32).reshape(1, CTX, D, 2, units)
    out_sum = jnp.concatenate(
        [expert_all[:, at : at + units] for at in range(D, 2 * HALF_ROWS, units)], axis=2
    ).astype(F32)[None]
    heads_sum = attn_all[:, :, : 3 * COLS].astype(F32)
    heads_sum = (
        heads_sum.reshape(CTX, shard_rows, 3, COLS).transpose(1, 2, 0, 3).reshape(shard_rows, 3 * D)
    )
    rest_sum = jnp.sum(attn_all[:, :, 3 * COLS :].astype(F32), axis=0)
    attn_sum = jnp.concatenate([heads_sum, rest_sum[:, :D]], axis=1)[None]
    router_sum = rest_sum[:, D : D + EXPERTS][None]
    gain_sum = rest_sum[:, D + EXPERTS : D + EXPERTS + 2].T[None]
    sums = (gain_sum, attn_sum, router_sum, in_sum, out_sum)
    squares = lax.psum(jnp.stack([jnp.sum(total * total) for total in sums]), "fsdp")
    norms = jnp.sqrt(squares)
    factors = jnp.minimum(1.0, CLIP_LIMIT / norms)
    step_value = step_count[0].astype(F32)
    wide_rate = RATE_FACTOR / D**0.5
    router_rate = RATE_FACTOR / (D // 4) ** 0.5
    down_rate = RATE_FACTOR / FFN**0.5
    olds = (
        (norm_gains, gains_mean, gains_square, GAIN_RATE),
        (attn_weight, attn_mean, attn_square, wide_rate),
        (router_weight, router_mean, router_square, router_rate),
        (expert_in, in_mean, in_square, wide_rate),
        (expert_out, out_mean, out_square, down_rate),
    )
    results = [layer_outputs, input_grads]
    for index, (total, (master, mean_old, square_old, rate)) in enumerate(zip(sums, olds)):
        results.extend(
            adam_update(total, total * factors[index], master, mean_old, square_old, step_value, rate)
        )
    return tuple(results) + (norms[None],)


def solution(mesh):
    gains = P("section", None, "fsdp")
    rows = P("section", "fsdp", None)
    wide = P("section", None, None, None, "fsdp")
    down = P("section", None, "fsdp", None)
    tokens = P("section", "fsdp", "ctx", None)
    return jax.shard_map(
        on_device,
        mesh=mesh,
        in_specs=(
            P("fsdp", "ctx", None),
            P("fsdp", "ctx", None),
            P("fsdp"),
            tokens,
            P(),
        )
        + (gains,) * 3
        + (rows,) * 6
        + (wide,) * 3
        + (down,) * 3,
        out_specs=(tokens, tokens)
        + (gains,) * 5
        + (rows,) * 10
        + (wide,) * 5
        + (down,) * 5
        + (P("section", None),),
        check_vma=False,
    )
```

```python
import functools

import jax
import jax.numpy as jnp
from jax import lax
from jax.experimental import pallas as pl
from jax.experimental.pallas import tpu as pltpu
from jax.sharding import PartitionSpec as P

D = 768
HEADS = 12
HEAD_DIM = 64
FFN = 2048
EXPERTS = 3
ROWS = 256
CTX = 4
SEQ = ROWS * CTX
HEADS_DEV = HEADS // CTX
WIDE = 128
EXT = 3 * HEADS_DEV * WIDE
COLS = HEADS_DEV * HEAD_DIM

EPS_NORM = 1e-06
BETA_ONE = 0.9
BETA_TWO = 0.95
RATE_FACTOR = 3.0
GAIN_RATE = 0.3
DECAY_RATE = 0.1
ADAM_EPS = 1e-08
CLIP_LIMIT = 1.0
MASK_VALUE = -1e30
SCORE_SCALE = HEAD_DIM ** (-0.5) / 2.0
BF16 = jnp.bfloat16
F32 = jnp.float32
VMEM_LIMIT = 56 * 1024 * 1024
NT = (((1,), (1,)), ((), ()))
TN = (((0,), (0,)), ((), ()))
HALF = ROWS // 2
LANES = 128
MESH = pl.DeviceIdType.MESH
EXACT = lax.Precision.HIGHEST


def dot(left, right):
    return jnp.dot(left, right, preferred_element_type=F32)


def dot_nt(left, right):
    return lax.dot_general(left, right, NT, preferred_element_type=F32)


def dot_tn(left, right):
    return lax.dot_general(left, right, TN, preferred_element_type=F32)


def params(collective_id):
    return pltpu.CompilerParams(
        vmem_limit_bytes=VMEM_LIMIT, collective_id=collective_id, has_side_effects=True
    )


def whole(shape):
    return pl.BlockSpec(shape, lambda *_: (0,) * len(shape))


def allowed_keys(block, keys, length):
    key_pos = lax.broadcasted_iota(jnp.int32, (ROWS, keys), 1)
    query_pos = lax.broadcasted_iota(jnp.int32, (ROWS, keys), 0) + block * ROWS
    return (key_pos <= query_pos) & (key_pos < length)


VMEM = pl.BlockSpec(memory_space=pltpu.VMEM)
SMEM = pl.BlockSpec(memory_space=pltpu.SMEM)


def ring():
    me = lax.axis_index("ctx")
    return me, lax.rem(me + 1, CTX), lax.rem(me + 3, CTX), lax.rem(me + 2, CTX)


def greet(peers):
    barrier = pltpu.get_barrier_semaphore()
    for peer in peers:
        pl.semaphore_signal(barrier, inc=1, device_id={"ctx": peer}, device_id_type=MESH)


def met(count):
    pl.semaphore_wait(pltpu.get_barrier_semaphore(), count)


def remote(source, target, send, recv, peer):
    return pltpu.make_async_remote_copy(
        src_ref=source,
        dst_ref=target,
        send_sem=send,
        recv_sem=recv,
        device_id={"ctx": peer},
        device_id_type=MESH,
    )


def rows_of(block, half=None):
    if half is None:
        return pl.ds(pl.multiple_of(block * ROWS, ROWS), ROWS)
    return pl.ds(pl.multiple_of(block * ROWS + half * HALF, HALF), HALF)


def gather_rows(all_ref, send, recv, beside=None):
    me, right, left, _ = ring()

    def piece(index, block, half, peer):
        spot = all_ref.at[rows_of(block, half)]
        return remote(spot, spot, send.at[index], recv.at[index], peer)

    copies = [
        piece(0, me, 0, right),
        piece(1, me, 1, left),
        piece(2, me, 1, right),
        piece(3, me, 0, left),
    ]
    for copy in copies:
        copy.start()
    if beside is not None:
        beside()
    copies[0].wait_recv()
    copies.append(piece(4, left, 0, right))
    copies[4].start()
    copies[1].wait_recv()
    copies.append(piece(5, right, 1, left))
    copies[5].start()
    for index in range(2, 6):
        copies[index].wait_recv()
    for copy in copies:
        copy.wait_send()


def reduce_rows(make, part, across_in, from_left, from_right, send, recv, beside=None):
    me, right, left, across = ring()
    top, bottom = pl.ds(0, HALF), pl.ds(HALF, HALF)

    def piece(index, block, half, target, peer):
        return remote(part.at[rows_of(block, half)], target, send.at[index], recv.at[index], peer)

    make(across)
    copies = [
        piece(0, across, 0, across_in.at[0], right),
        piece(1, across, 1, across_in.at[1], left),
    ]
    copies[0].start()
    copies[1].start()
    make(right)
    copies.append(piece(2, right, 1, from_left.at[bottom], right))
    copies[2].start()
    make(left)
    copies.append(piece(3, left, 0, from_right.at[top], left))
    copies[3].start()
    copies[0].wait_recv()
    spot = rows_of(right, 0)
    part[spot, :] = (part[spot, :].astype(F32) + across_in[0].astype(F32)).astype(BF16)
    copies.append(piece(4, right, 0, from_left.at[top], right))
    copies[4].start()
    copies[1].wait_recv()
    spot = rows_of(left, 1)
    part[spot, :] = (part[spot, :].astype(F32) + across_in[1].astype(F32)).astype(BF16)
    copies.append(piece(5, left, 1, from_right.at[bottom], left))
    copies[5].start()
    make(me)
    if beside is not None:
        beside()
    for index in range(2, 6):
        copies[index].wait_recv()
    for copy in copies:
        copy.wait_send()
    return (
        part[rows_of(me), :].astype(F32) + from_left[...].astype(F32) + from_right[...].astype(F32)
    )


REDUCE_SCRATCH = [
    pltpu.VMEM((SEQ, D), BF16),
    pltpu.VMEM((2, HALF, D), BF16),
    pltpu.VMEM((ROWS, D), BF16),
    pltpu.VMEM((ROWS, D), BF16),
    pltpu.SemaphoreType.DMA((6,)),
    pltpu.SemaphoreType.DMA((6,)),
]


def greet_ids(peers):
    barrier = pltpu.get_barrier_semaphore()
    for peer in peers:
        pl.semaphore_signal(barrier, inc=1, device_id=peer, device_id_type=MESH)


class Ring:
    def __init__(self, axis):
        if axis == "x":
            self.me = lax.axis_index("ctx")
            self.place = lambda index: {"ctx": index}
        else:
            shard = lax.axis_index("fsdp")
            inner, outer = lax.rem(shard, CTX), lax.div(shard, CTX)
            if axis == "y":
                self.me = inner
                self.place = lambda index: {"fsdp": outer * CTX + index}
            else:
                self.me = outer
                self.place = lambda index: {"fsdp": index * CTX + inner}
        self.right = lax.rem(self.me + 1, CTX)
        self.left = lax.rem(self.me + 3, CTX)
        self.across = lax.rem(self.me + 2, CTX)

    def order(self):
        return (self.across, self.right, self.left, self.me)

    def near(self):
        return [self.place(self.right), self.place(self.left)]

    def copy(self, source, target, send, recv, index):
        return pltpu.make_async_remote_copy(
            src_ref=source,
            dst_ref=target,
            send_sem=send,
            recv_sem=recv,
            device_id=self.place(index),
            device_id_type=MESH,
        )


class RingGather:
    def __init__(self, ring, at, send, recv):
        self.ring, self.at, self.send, self.recv = ring, at, send, recv
        self.copies = []

    def go(self, block, half, to):
        spot = self.at(block, half)
        index = len(self.copies)
        self.copies.append(
            self.ring.copy(spot, spot, self.send.at[index], self.recv.at[index], to)
        )
        self.copies[-1].start()

    def start(self):
        ring = self.ring
        self.go(ring.me, 0, ring.right)
        self.go(ring.me, 1, ring.left)
        self.go(ring.me, 1, ring.right)
        self.go(ring.me, 0, ring.left)

    def forward(self):
        ring = self.ring
        spot = self.at(ring.left, 0)
        ring.copy(spot, spot, self.send.at[0], self.recv.at[0], ring.right).wait_recv()
        self.go(ring.left, 0, ring.right)
        spot = self.at(ring.right, 1)
        ring.copy(spot, spot, self.send.at[1], self.recv.at[1], ring.left).wait_recv()
        self.go(ring.right, 1, ring.left)

    def finish(self):
        ring = self.ring
        for index, block, half in (
            (2, ring.left, 1), (3, ring.right, 0), (4, ring.across, 0), (5, ring.across, 1),
        ):
            spot = self.at(block, half)
            ring.copy(spot, spot, self.send.at[index], self.recv.at[index], ring.right).wait_recv()
        for copy in self.copies:
            copy.wait_send()


class RingSum:
    def __init__(self, ring, part, across_in, from_left, from_right, send, recv, cut, make):
        self.ring, self.part, self.across_in = ring, part, across_in
        self.from_left, self.from_right, self.send, self.recv = from_left, from_right, send, recv
        size = part.shape[1]
        self.halves = (pl.ds(0, cut), pl.ds(cut, size - cut))
        self.make = make
        self.copies = []

    def go(self, block, half, target, to):
        index = len(self.copies)
        self.copies.append(
            self.ring.copy(
                self.part.at[block, self.halves[half]], target, self.send.at[index], self.recv.at[index], to
            )
        )
        self.copies[-1].start()

    def arrived(self, half, block):
        self.copies[half].wait_recv()
        incoming = self.across_in[half]
        if len(self.part.shape) == 3:
            spot = (block, self.halves[half])
            self.part[spot] = (self.part[spot].astype(F32) + incoming[...].astype(F32)).astype(BF16)
            return
        start = (0, self.part.shape[1] - incoming.shape[0])[half]
        for index in range(incoming.shape[0]):
            self.part[block, start + index] = (
                self.part[block, start + index].astype(F32) + incoming[index].astype(F32)
            ).astype(BF16)

    def stage(self, number):
        ring = self.ring
        if number == 0:
            self.make(0, ring.across)
            self.go(ring.across, 0, self.across_in[0], ring.right)
            self.go(ring.across, 1, self.across_in[1], ring.left)
        elif number == 1:
            self.make(1, ring.right)
            self.go(ring.right, 1, self.from_left.at[self.halves[1]], ring.right)
        elif number == 2:
            self.make(2, ring.left)
            self.go(ring.left, 0, self.from_right.at[self.halves[0]], ring.left)
        elif number == 3:
            self.arrived(0, ring.right)
            self.go(ring.right, 0, self.from_left.at[self.halves[0]], ring.right)
            self.arrived(1, ring.left)
            self.go(ring.left, 1, self.from_right.at[self.halves[1]], ring.left)
        elif number == 4:
            self.make(3, ring.me)
        else:
            for copy in self.copies[2:]:
                copy.wait_recv()
            for copy in self.copies:
                copy.wait_send()

    def total(self, index=None):
        spot = (self.ring.me,) if index is None else (self.ring.me, index)
        tail = () if index is None else (index,)
        return (
            self.part[spot].astype(F32)
            + self.from_left[tail or ...].astype(F32)
            + self.from_right[tail or ...].astype(F32)
        )


UNIT = 256
EXPERT_ROWS = D + D // 2
ATTN_ROWS = 288
SHARD_ROWS = EXPERT_ROWS + ATTN_ROWS
FIRST = SHARD_ROWS // 2
KEPT = EXPERT_ROWS - FIRST
CUT = 352
SEMS = pltpu.SemaphoreType.DMA


def gather_shards_kernel(shard_ref, out_ref, *sems):
    section = lax.axis_index("section")
    sibling = {"section": 1 - section}
    ring_y, ring_z = Ring("y"), Ring("z")
    y, z = ring_y.me, ring_z.me
    greet_ids([sibling] + ring_y.near() + ring_z.near())
    out_ref[section, z, y] = shard_ref[...]
    met(5)
    half = ATTN_ROWS // 2
    low = (pl.ds(0, 64), pl.ds(64, half - 64))
    high = (pl.ds(half, 64), pl.ds(half + 64, half - 64))
    pair = (pl.ds(0, 2), pl.ds(2, 2))
    near_y = RingGather(ring_y, lambda b, h: out_ref.at[section, z, b, low[h]], sems[0], sems[1])
    near_z = RingGather(ring_z, lambda b, h: out_ref.at[section, b, y, high[h]], sems[2], sems[3])
    far_z = RingGather(
        ring_z, lambda b, h: out_ref.at[section, b, pair[h], pl.ds(0, half)], sems[4], sems[5]
    )
    far_y = RingGather(
        ring_y, lambda b, h: out_ref.at[section, pair[h], b, pl.ds(half, half)], sems[6], sems[7]
    )
    for rings in ((near_y, near_z), (far_z, far_y)):
        for one in rings:
            one.start()
        for one in rings:
            one.forward()
        for one in rings:
            one.finish()
    across = pltpu.make_async_remote_copy(
        src_ref=out_ref.at[section],
        dst_ref=out_ref.at[section],
        send_sem=sems[8],
        recv_sem=sems[9],
        device_id=sibling,
        device_id_type=MESH,
    )
    across.start()
    across.wait()


def gather_shards(shard):
    return pl.pallas_call(
        gather_shards_kernel,
        out_shape=jax.ShapeDtypeStruct((2, CTX, CTX, ATTN_ROWS, UNIT), BF16),
        in_specs=[VMEM],
        out_specs=VMEM,
        scratch_shapes=[SEMS((6,))] * 8 + [SEMS, SEMS],
        compiler_params=params(7),
        name="gather_shards",
    )(shard)


def sum_shards_kernel(
    lower_e, lower_a, upper_e, upper_a, out_ref,
    part_y, in_y, part_z, in_z, top_y, bottom_y, left_y, right_y, top_z, bottom_z, left_z, right_z,
    more_z, more_y, top_zz, bottom_zz, left_zz, right_zz, top_yy, bottom_yy, left_yy, right_yy, *sems,
):
    section = lax.axis_index("section")
    sibling = {"section": 1 - section}
    ring_y, ring_z = Ring("y"), Ring("z")
    greet_ids([sibling] + ring_y.near() + ring_z.near())
    local, send_s, recv_s = sems[:3]

    def pieces(index, experts, attn, target_y, target_z):
        b_y, b_z = ring_y.order()[index], ring_z.order()[index]
        return (
            (experts.at[:, b_y, pl.ds(0, FIRST), :], target_y.at[b_y]),
            (experts.at[b_z, :, pl.ds(FIRST, KEPT), :], target_z.at[b_z, :, pl.ds(0, KEPT), :]),
            (attn.at[b_z], target_z.at[b_z, :, pl.ds(KEPT, ATTN_ROWS), :]),
        )

    def fetch(index, number, source, target):
        return pltpu.make_async_copy(source, target, local.at[index * 3 + number])

    def pass_on(index, number, source, target):
        at = index * 3 + number
        return pltpu.make_async_remote_copy(
            src_ref=source,
            dst_ref=target,
            send_sem=send_s.at[at],
            recv_sem=recv_s.at[at],
            device_id=sibling,
            device_id_type=MESH,
        )

    def begin(own_e, own_a, other_e, other_a):
        for index in range(CTX):
            for number, (source, target) in enumerate(pieces(index, own_e, own_a, part_y, part_z)):
                fetch(index, number, source, target).start()

    def lend(other_e, other_a):
        for index in range(CTX):
            for number, (source, target) in enumerate(pieces(index, other_e, other_a, in_y, in_z)):
                pass_on(index, number, source, target).start()

    @pl.when(section == 0)
    def _():
        begin(lower_e, lower_a, upper_e, upper_a)

    @pl.when(section == 1)
    def _():
        begin(upper_e, upper_a, lower_e, lower_a)

    met(5)

    @pl.when(section == 0)
    def _():
        lend(upper_e, upper_a)

    @pl.when(section == 1)
    def _():
        lend(lower_e, lower_a)

    def ready(index, number):
        source, target = pieces(index, lower_e, lower_a, part_y, part_z)[number]
        fetch(index, number, source, target).wait()
        source, target = pieces(index, lower_e, lower_a, in_y, in_z)[number]
        pass_on(index, number, source, target).wait_recv()

    def make_y(index, block):
        ready(index, 0)
        for other in range(CTX):
            part_y[block, other] = (
                part_y[block, other].astype(F32) + in_y[block, other].astype(F32)
            ).astype(BF16)

    def make_z(index, block):
        ready(index, 1)
        ready(index, 2)
        for other in range(CTX):
            part_z[block, other] = (
                part_z[block, other].astype(F32) + in_z[block, other].astype(F32)
            ).astype(BF16)

    first_y = RingSum(ring_y, part_y, (top_y, bottom_y), left_y, right_y, sems[3], sems[4], 2, make_y)
    first_z = RingSum(ring_z, part_z, (top_z, bottom_z), left_z, right_z, sems[5], sems[6], 2, make_z)

    def make_zz(index, block):
        more_z[block] = first_y.total(block).astype(BF16)

    def make_yy(index, block):
        more_y[block] = first_z.total(block).astype(BF16)

    then_z = RingSum(
        ring_z, more_z, (top_zz, bottom_zz), left_zz, right_zz, sems[7], sems[8], CUT, make_zz
    )
    then_y = RingSum(
        ring_y, more_y, (top_yy, bottom_yy), left_yy, right_yy, sems[9], sems[10], CUT, make_yy
    )
    for number in range(6):
        first_y.stage(number)
        first_z.stage(number)
    for number in range(6):
        then_z.stage(number)
        then_y.stage(number)
    out_ref[:FIRST, :] = then_z.total().astype(BF16)
    out_ref[FIRST:, :] = then_y.total().astype(BF16)
    for index in range(CTX):
        for number, (source, target) in enumerate(pieces(index, lower_e, lower_a, in_y, in_z)):
            pass_on(index, number, source, target).wait_send()


def sum_shards(lower_e, lower_a, upper_e, upper_a):
    block = pltpu.VMEM((CTX, FIRST, UNIT), BF16)
    pair = pltpu.VMEM((2, FIRST, UNIT), BF16)
    one = pltpu.VMEM((FIRST, UNIT), BF16)
    top, bottom = pltpu.VMEM((CUT, UNIT), BF16), pltpu.VMEM((FIRST - CUT, UNIT), BF16)
    full = pltpu.VMEM((CTX, CTX, FIRST, UNIT), BF16)
    anywhere = pl.BlockSpec(memory_space=pl.ANY)
    return pl.pallas_call(
        sum_shards_kernel,
        out_shape=jax.ShapeDtypeStruct((SHARD_ROWS, UNIT), BF16),
        in_specs=[anywhere] * 4,
        out_specs=VMEM,
        scratch_shapes=[full] * 4
        + [pair, pair, block, block] * 2
        + [block, block]
        + [top, bottom, one, one] * 2
        + [SEMS((12,))] * 3
        + [SEMS((6,))] * 8,
        compiler_params=params(8),
        name="sum_shards",
    )(*(
        array.reshape((CTX, CTX) + array.shape[1:])
        for array in (lower_e, lower_a, upper_e, upper_a)
    ))


def spread_sums_kernel(shard_ref, all_ref, squares_ref, from_y, from_z, *sems):
    ring_x, ring_y, ring_z = Ring("x"), Ring("y"), Ring("z")
    far = [
        one.place(index)
        for one in (ring_y, ring_z)
        for index in (one.right, one.left, one.across)
    ]
    greet_ids(ring_x.near() + far)
    all_ref[ring_x.me] = shard_ref[...]
    met(8)
    halves = (pl.ds(0, FIRST), pl.ds(FIRST, FIRST))
    rows = RingGather(ring_x, lambda b, h: all_ref.at[b, halves[h]], sems[0], sems[1])
    rows.start()
    rows.forward()
    rows.finish()

    def folded(values):
        squared = values * values
        return jnp.sum(squared, axis=0, keepdims=True)

    in_row = jnp.zeros((1, UNIT), F32)
    out_row = jnp.zeros((1, UNIT), F32)
    attn_row = jnp.zeros((1, UNIT), F32)
    back = jnp.zeros((ATTN_ROWS // 2, UNIT), F32)
    small = jnp.zeros((48, UNIT), F32)
    lanes = lax.broadcasted_iota(jnp.int32, (1, UNIT), 1)
    for block in range(CTX):
        in_row += folded(all_ref[block, :D, :].astype(F32))
        out_row += folded(all_ref[block, D:EXPERT_ROWS, :].astype(F32))
        middle = EXPERT_ROWS + ATTN_ROWS // 2
        back += all_ref[block, EXPERT_ROWS:middle, :].astype(F32)
        attn_row += folded(all_ref[block, middle : middle + 96, :].astype(F32))
        final = all_ref[block, middle + 96 :, :].astype(F32)
        attn_row += jnp.where(lanes < HEAD_DIM, folded(final), 0.0)
        small += final
    attn_row += folded(back)
    small_row = folded(small)
    is_router = (lanes >= LANES) & (lanes < LANES + EXPERTS)
    is_gain = (lanes >= LANES + EXPERTS) & (lanes < LANES + EXPERTS + 2)
    sums = [
        jnp.where(is_gain, small_row, 0.0),
        attn_row,
        jnp.where(is_router, small_row, 0.0),
        in_row,
        out_row,
    ]
    places = lax.broadcasted_iota(jnp.int32, (8, LANES), 1)
    tile = jnp.zeros((8, LANES), F32)
    for index, row in enumerate(sums):
        tile = jnp.where(places == index, jnp.sum(row, axis=1, keepdims=True), tile)

    def shared(one, slots, send, recv, tile):
        slots[one.me] = tile
        copies = []
        for index, peer in enumerate((one.right, one.left, one.across)):
            spot = slots.at[one.me]
            copies.append(one.copy(spot, spot, send.at[index], recv.at[index], peer))
            copies[-1].start()
        for copy in copies:
            copy.wait()
        return (slots[0] + slots[1]) + (slots[2] + slots[3])

    tile = shared(ring_y, from_y, sems[2], sems[3], tile)
    squares_ref[...] = shared(ring_z, from_z, sems[4], sems[5], tile)


def spread_sums(shard):
    slots = pltpu.VMEM((CTX, 8, LANES), F32)
    return pl.pallas_call(
        spread_sums_kernel,
        out_shape=(
            jax.ShapeDtypeStruct((CTX, SHARD_ROWS, UNIT), BF16),
            jax.ShapeDtypeStruct((8, LANES), F32),
        ),
        in_specs=[VMEM],
        out_specs=[VMEM, VMEM],
        scratch_shapes=[slots, slots, SEMS((6,)), SEMS((6,))] + [SEMS((3,))] * 4,
        compiler_params=params(9),
        name="spread_sums",
    )(shard)


def inverse_size(values):
    return lax.rsqrt(jnp.mean(values * values, axis=1, keepdims=True) + EPS_NORM)


def unpack(pack_ref, back_ref, heads_ref):
    def body(index, _):
        rows = pl.ds(pl.multiple_of(index * 48, 16), 48)
        for piece in range(6):
            target = back_ref if piece < 3 else heads_ref
            at = (piece % 3) * UNIT
            target[rows, at : at + UNIT] = pack_ref[index, piece * 48 : (piece + 1) * 48, :]
        return 0

    lax.fori_loop(0, 16, body, 0)


def repack(back_ref, heads_ref, pack_ref):
    def body(index, _):
        rows = pl.ds(pl.multiple_of(index * 48, 16), 48)
        for piece in range(6):
            source = back_ref if piece < 3 else heads_ref
            at = (piece % 3) * UNIT
            pack_ref[index, piece * 48 : (piece + 1) * 48, :] = source[rows, at : at + UNIT]
        return 0

    lax.fori_loop(0, 16, body, 0)


def extend(heads_ref, w_ref):
    lanes = lax.broadcasted_iota(jnp.int32, (D, WIDE), 1)
    for head in range(3 * HEADS_DEV):
        at = head // 2 * WIDE
        values = heads_ref[:, at : at + WIDE].astype(F32)
        if head % 2:
            values = pltpu.roll(values, HEAD_DIM, 1)
        if head < 2 * HEADS_DEV:
            upper = jnp.where(
                lanes < 96, -pltpu.roll(values, 32, 1), pltpu.roll(values, 96, 1)
            )
        else:
            upper = jnp.zeros_like(values)
        w_ref[:, head * WIDE : (head + 1) * WIDE] = jnp.where(
            lanes < HEAD_DIM, values, upper
        ).astype(BF16)


def attn_forward_kernel(
    length_ref, u_ref, routes_ref, pack_ref, table_ref,
    a_ref, qkv_ref, mass_ref, attended_ref, residual_ref, b_ref, gates_ref, gate_ref,
    gains_ref, router_ref, w_ref, back_ref,
    heads_out, heads_w, send_a, recv_a, send_o, recv_o, send_b, recv_b,
):
    me, right, left, across = ring()
    greet((right, left, across))
    length = length_ref[0]
    tokens = u_ref[...].astype(F32)
    unpack(pack_ref, back_ref, heads_w)
    router_ref[...] = heads_w[:, D - LANES :]
    places = lax.broadcasted_iota(jnp.int32, (8, LANES), 0) + EXPERTS
    picker = jnp.where(places == lax.broadcasted_iota(jnp.int32, (8, LANES), 1), 1.0, 0.0)
    gains_ref[...] = dot_nt(picker.astype(BF16), router_ref[...])
    a_ref[rows_of(me), :] = (tokens * inverse_size(tokens) * gains_ref[0:1, :]).astype(BF16)
    met(3)
    gather_rows(a_ref, send_a, recv_a, lambda: extend(heads_w, w_ref))
    for block in range(CTX):
        rows = pl.ds(block * ROWS, ROWS)
        table = table_ref[rows, :]
        mixed = dot(a_ref[rows, :], w_ref[...])
        for part in range(3 * HEADS_DEV):
            lanes = slice(part * WIDE, (part + 1) * WIDE)
            piece = mixed[:, lanes]
            if part < 2 * HEADS_DEV:
                turned = piece * table
                piece = turned + pltpu.roll(turned, WIDE // 2, 1)
            qkv_ref[rows, lanes] = piece.astype(BF16)

    def handed(block):
        step = lax.rem(block - me + CTX, CTX)
        return remote(
            heads_out.at[block], attended_ref.at[me], send_o.at[step], recv_o.at[step], block
        )

    for block in reversed(range(CTX)):
        rows = pl.ds(block * ROWS, ROWS)
        keys = (block + 1) * ROWS
        allowed = allowed_keys(block, keys, length)
        outs = []
        for head in range(HEADS_DEV):
            queries = qkv_ref[rows, head * WIDE : (head + 1) * WIDE]
            key_lanes = slice((HEADS_DEV + head) * WIDE, (HEADS_DEV + head + 1) * WIDE)
            value_lanes = slice((2 * HEADS_DEV + head) * WIDE, (2 * HEADS_DEV + head + 1) * WIDE)
            scores = dot_nt(queries, qkv_ref[:keys, key_lanes]) * SCORE_SCALE
            scores = jnp.where(allowed, scores, MASK_VALUE)
            top = jnp.max(scores, axis=1, keepdims=True)
            raw = jnp.exp(scores - top)
            total = jnp.sum(raw, axis=1, keepdims=True)
            probs = (raw * (1.0 / total)).astype(BF16)
            outs.append(dot(probs, qkv_ref[:keys, value_lanes]))
            mass_ref[head, rows, :] = top + jnp.log(total)
        first = (outs[0] + pltpu.roll(outs[1], WIDE // 2, 1)).astype(BF16)
        second = outs[2][:, : WIDE // 2].astype(BF16)
        heads_out[block, :, :WIDE] = first
        heads_out[block, :, WIDE:] = second

        @pl.when(block != me)
        def _():
            handed(block).start()

    attended_ref[me] = heads_out[me]
    for step in range(1, CTX):
        pltpu.make_async_copy(heads_out.at[0], attended_ref.at[0], recv_o.at[step]).wait()
    residual = tokens
    for block in range(CTX):
        residual = residual + dot(attended_ref[block], back_ref[block * COLS : (block + 1) * COLS, :])
    residual_ref[...] = residual
    b_ref[rows_of(me), :] = (residual * inverse_size(residual) * gains_ref[1:2, :]).astype(BF16)
    for step in range(1, CTX):
        pltpu.make_async_copy(heads_out.at[0], attended_ref.at[0], send_o.at[step]).wait()
    gather_rows(b_ref, send_b, recv_b)
    lanes = lax.broadcasted_iota(jnp.int32, (ROWS, LANES), 1)
    for block in range(CTX):
        rows = pl.ds(block * ROWS, ROWS)
        logits = dot(b_ref[rows, :], router_ref[...])
        named = (lanes == routes_ref[rows, 0:1]) | (lanes == routes_ref[rows, 1:2])
        chosen = jnp.where(named, logits, MASK_VALUE)
        raw = jnp.where(named, jnp.exp(chosen - jnp.max(chosen, axis=1, keepdims=True)), 0.0)
        gates = raw / jnp.sum(raw, axis=1, keepdims=True)
        gates_ref[rows, :] = gates
        gates = jnp.where(lanes == EXPERTS, 1.0, gates)
        gate_ref[rows, :] = jnp.sum(jnp.where(lanes == me, gates, 0.0), axis=1, keepdims=True)


def attn_forward(length, u, routes, pack, table):
    sems = pltpu.SemaphoreType.DMA
    return pl.pallas_call(
        attn_forward_kernel,
        out_shape=(
            jax.ShapeDtypeStruct((SEQ, D), BF16),
            jax.ShapeDtypeStruct((SEQ, EXT), BF16),
            jax.ShapeDtypeStruct((HEADS_DEV, SEQ, 1), F32),
            jax.ShapeDtypeStruct((CTX, ROWS, COLS), BF16),
            jax.ShapeDtypeStruct((ROWS, D), F32),
            jax.ShapeDtypeStruct((SEQ, D), BF16),
            jax.ShapeDtypeStruct((SEQ, LANES), F32),
            jax.ShapeDtypeStruct((SEQ, 1), F32),
            jax.ShapeDtypeStruct((8, D), F32),
            jax.ShapeDtypeStruct((D, LANES), BF16),
            jax.ShapeDtypeStruct((D, EXT), BF16),
            jax.ShapeDtypeStruct((D, D), BF16),
        ),
        in_specs=[SMEM] + [VMEM] * 4,
        out_specs=[VMEM] * 12,
        scratch_shapes=[pltpu.VMEM((CTX, ROWS, COLS), BF16), pltpu.VMEM((D, D), BF16)]
        + [sems((6,)), sems((6,)), sems((CTX,)), sems((CTX,)), sems((6,)), sems((6,))],
        compiler_params=params(1),
        name="attn_forward",
    )(length, u, routes, pack, table)


def attn_backward_kernel(
    last, length_ref, u_ref, gains_ref, router_ref, w_ref, back_ref, table_ref,
    a_ref, qkv_ref, mass_ref, attended_ref, residual_ref, second_ref, gates_ref,
    delta_ref, db_ref, gate_grad_ref, *rest,
):
    if last:
        input_ref, pack_ref = rest[:2]
        rest = rest[2:]
    else:
        input_ref, pack_ref, lower_ref = rest[:3]
        rest = rest[3:]
    dheads_ref, dback_ref = rest[:2]
    rest = rest[2:]
    key_acc, value_acc, dz, grads_out, grads_in, send_o, recv_o = rest[:7]
    part, across_in, from_left, from_right, send_r, recv_r = rest[7:13]
    me, right, left, across = ring()
    greet((right, left, across))
    length = length_ref[0]
    lanes = lax.broadcasted_iota(jnp.int32, (ROWS, LANES), 1)
    gates = gates_ref[...]
    gate_grads = jnp.where(lanes < EXPERTS, gate_grad_ref[...], 0.0)
    logit_grad = gates * (gate_grads - jnp.sum(gates * gate_grads, axis=1, keepdims=True))
    logit_grad = logit_grad.astype(BF16)
    second_grad = db_ref[...] + dot_nt(logit_grad, router_ref[...])
    residual = residual_ref[...]
    scale_two = inverse_size(residual)
    normal_two = residual * scale_two
    gain_two_terms = second_grad * normal_two
    scaled_two = second_grad * gains_ref[1:2, :]
    residual_grad = delta_ref[...].astype(F32) + scale_two * (
        scaled_two - normal_two * jnp.mean(scaled_two * normal_two, axis=1, keepdims=True)
    )
    input_ref[...] = residual_grad
    branch_grad = residual_grad.astype(BF16)
    met(3)

    for block in range(CTX):
        grads_out[block] = dot_nt(branch_grad, back_ref[block * COLS : (block + 1) * COLS, :]).astype(
            BF16
        )

        @pl.when(block != me)
        def _():
            step = lax.rem(block - me + CTX, CTX)
            remote(
                grads_out.at[block], grads_in.at[me], send_o.at[step], recv_o.at[step], block
            ).start()

    grads_in[me] = grads_out[me]
    for block in range(CTX):
        dback_ref[block * COLS : (block + 1) * COLS, :] = dot_tn(
            attended_ref[block], branch_grad
        ).astype(BF16)
    router_terms = dot_tn(second_ref[...], logit_grad)
    ones = jnp.ones((ROWS, LANES), F32)
    gain_two_column = lax.dot_general(
        gain_two_terms, ones, TN, precision=EXACT, preferred_element_type=F32
    )
    key_acc[...] = jnp.zeros_like(key_acc)
    value_acc[...] = jnp.zeros_like(value_acc)
    for step in range(1, CTX):
        pltpu.make_async_copy(grads_out.at[0], grads_in.at[0], recv_o.at[step]).wait()
    for step in range(1, CTX):
        pltpu.make_async_copy(grads_out.at[0], grads_in.at[0], send_o.at[step]).wait()
    for block in range(CTX):
        rows = pl.ds(block * ROWS, ROWS)
        keys = (block + 1) * ROWS
        allowed = allowed_keys(block, keys, length)
        pair = grads_in[block, :, :WIDE]
        tail = grads_in[block, :, WIDE:]
        head_grads = (
            pair,
            pltpu.roll(pair.astype(F32), WIDE // 2, 1).astype(BF16),
            jnp.concatenate([tail, jnp.zeros_like(tail)], axis=1),
        )
        for head in range(HEADS_DEV):
            queries = qkv_ref[rows, head * WIDE : (head + 1) * WIDE]
            keys_all = qkv_ref[:keys, (HEADS_DEV + head) * WIDE : (HEADS_DEV + head + 1) * WIDE]
            values_all = qkv_ref[
                :keys, (2 * HEADS_DEV + head) * WIDE : (2 * HEADS_DEV + head + 1) * WIDE
            ]
            grads = head_grads[head]
            scores = dot_nt(queries, keys_all) * SCORE_SCALE
            probs = jnp.where(allowed, jnp.exp(scores - mass_ref[head, rows, :]), 0.0)
            prob_grad = dot_nt(grads, values_all)
            row_sum = jnp.sum(probs * prob_grad, axis=1, keepdims=True)
            score_grad = (probs * (prob_grad - row_sum)).astype(BF16)
            query_grad = dot(score_grad, keys_all) * (HEAD_DIM**-0.5)
            dz[rows, head * WIDE : (head + 1) * WIDE] = (query_grad * table_ref[rows, :]).astype(BF16)
            spot = slice(head * WIDE, (head + 1) * WIDE)
            key_acc[:keys, spot] += dot_tn(score_grad, queries)
            value_acc[:keys, spot] += dot_tn(probs.astype(BF16), grads)
    for block in range(CTX):
        rows = pl.ds(block * ROWS, ROWS)
        table = table_ref[rows, :] * (HEAD_DIM**-0.5)
        for head in range(HEADS_DEV):
            spot = slice(head * WIDE, (head + 1) * WIDE)
            at = (HEADS_DEV + head) * WIDE
            dz[rows, at : at + WIDE] = (key_acc[rows, spot] * table).astype(BF16)
            at = (2 * HEADS_DEV + head) * WIDE
            dz[rows, at : at + WIDE] = value_acc[rows, spot].astype(BF16)

    def make(block):
        part[rows_of(block), :] = dot_nt(dz[rows_of(block), :], w_ref[...]).astype(BF16)

    def beside():
        wide_lanes = lax.broadcasted_iota(jnp.int32, (D, WIDE), 1)
        pieces = []
        for piece in range(3):
            spot = slice(piece * HEADS_DEV * WIDE, (piece + 1) * HEADS_DEV * WIDE)
            terms = dot_tn(a_ref[...], dz[:, spot])
            for head in range(HEADS_DEV):
                term = terms[:, head * WIDE : (head + 1) * WIDE]
                if piece < 2:
                    term = term + jnp.where(
                        wide_lanes < HEAD_DIM // 2,
                        pltpu.roll(term, HEAD_DIM // 2, 1),
                        -pltpu.roll(term, WIDE - HEAD_DIM // 2, 1),
                    )
                pieces.append(term)
        for pair in range(4):
            joined = jnp.where(
                wide_lanes < HEAD_DIM,
                pieces[2 * pair],
                pltpu.roll(pieces[2 * pair + 1], HEAD_DIM, 1),
            )
            dheads_ref[:, pair * WIDE : (pair + 1) * WIDE] = joined.astype(BF16)
        dheads_ref[:, 4 * WIDE : 5 * WIDE] = jnp.where(
            wide_lanes < HEAD_DIM, pieces[8], 0.0
        ).astype(BF16)

    normed_grad = reduce_rows(make, part, across_in, from_left, from_right, send_r, recv_r, beside)
    tokens = u_ref[...].astype(F32)
    scale_one = inverse_size(tokens)
    normal_one = tokens * scale_one
    gain_one_column = lax.dot_general(
        normed_grad * normal_one, ones, TN, precision=EXACT, preferred_element_type=F32
    )
    scaled_one = normed_grad * gains_ref[0:1, :]
    input_grad = input_ref[...] + scale_one * (
        scaled_one - normal_one * jnp.mean(scaled_one * normal_one, axis=1, keepdims=True)
    )
    input_ref[...] = input_grad
    small_lanes = lax.broadcasted_iota(jnp.int32, (D, LANES), 1)
    dheads_ref[:, D - LANES :] = jnp.where(
        small_lanes == EXPERTS,
        gain_one_column,
        jnp.where(small_lanes == EXPERTS + 1, gain_two_column, router_terms),
    ).astype(BF16)
    repack(dback_ref, dheads_ref, pack_ref)
    if not last:
        lower_ref[rows_of(me), :] = input_grad.astype(BF16)
        gather_rows(lower_ref, *rest[13:])


def attn_backward(last, length, *arrays):
    sems = pltpu.SemaphoreType.DMA
    out_shape = [
        jax.ShapeDtypeStruct((ROWS, D), F32),
        jax.ShapeDtypeStruct((16, ATTN_ROWS, UNIT), BF16),
    ]
    if not last:
        out_shape.append(jax.ShapeDtypeStruct((SEQ, D), BF16))
    scratch = [
        pltpu.VMEM((D, D), BF16),
        pltpu.VMEM((D, D), BF16),
        pltpu.VMEM((SEQ, HEADS_DEV * WIDE), F32),
        pltpu.VMEM((SEQ, HEADS_DEV * WIDE), F32),
        pltpu.VMEM((SEQ, EXT), BF16),
        pltpu.VMEM((CTX, ROWS, COLS), BF16),
        pltpu.VMEM((CTX, ROWS, COLS), BF16),
        sems((CTX,)),
        sems((CTX,)),
    ] + REDUCE_SCRATCH
    if not last:
        scratch += [sems((6,)), sems((6,))]
    return pl.pallas_call(
        functools.partial(attn_backward_kernel, last),
        out_shape=tuple(out_shape),
        in_specs=[SMEM] + [VMEM] * len(arrays),
        out_specs=[VMEM] * len(out_shape),
        scratch_shapes=scratch,
        compiler_params=params(3 if last else 4),
        name="attn_backward",
    )(length, *arrays)


SHARDS_STEP = 4
IN_ROWS = D
HALF_ROWS = (D + D * 128 // 256) // 2


def assemble(w_ref, win, wout):
    shards, units = win.shape[0], LANES
    width = 2 * units
    split = HALF_ROWS
    for shard in range(shards):
        win[shard, :split, :] = w_ref[0, shard]
        win[shard, split:, :] = w_ref[1, shard, : D - split, :]
        for piece in range(D // width):
            at = D - split + piece * units
            wout[shard * units : (shard + 1) * units, piece * width : (piece + 1) * width] = w_ref[
                1, shard, at : at + units, :
            ]


def ffn_forward_kernel(
    b_ref, gate_ref, residual_ref, w_ref, y_ref, kept_ref, acc, win, wout,
    part, across_in, from_left, from_right, send, recv,
):
    step = pl.program_id(0)
    final = pl.num_programs(0) - 1
    shards, units = win.shape[0], LANES

    @pl.when(step == 0)
    def _():
        _, right, left, _ = ring()
        greet((right, left))
        acc[...] = jnp.zeros_like(acc)

    assemble(w_ref, win, wout)

    def terms(block):
        rows = rows_of(block)
        b_rows = b_ref[rows, :]
        acted = []
        for shard in range(shards):
            hidden = dot(b_rows, win[shard])
            kept_ref[shard, rows, :] = hidden.astype(BF16)
            gate_part = hidden[:, :units]
            acted.append(
                (gate_part / (1.0 + jnp.exp(-gate_part)) * hidden[:, units:]).astype(BF16)
            )
        return acc[rows, :] + dot(jnp.concatenate(acted, axis=1), wout[...])

    @pl.when(step < final)
    def _():
        for block in range(CTX):
            acc[pl.ds(block * ROWS, ROWS), :] = terms(block)

    @pl.when(step == final)
    def _():
        met(2)

        def make(block):
            rows = rows_of(block)
            part[rows, :] = (terms(block) * gate_ref[rows, :]).astype(BF16)

        total = reduce_rows(make, part, across_in, from_left, from_right, send, recv)
        y_ref[...] = (residual_ref[...] + total).astype(BF16)


def ffn_forward(b_all, gate_col, residual, weights):
    _, count, half_rows, double = weights.shape
    shards = SHARDS_STEP
    return pl.pallas_call(
        ffn_forward_kernel,
        grid=(count // shards,),
        out_shape=(
            jax.ShapeDtypeStruct((ROWS, D), BF16),
            jax.ShapeDtypeStruct((count, SEQ, double), BF16),
        ),
        in_specs=[
            whole((SEQ, D)),
            whole((SEQ, 1)),
            whole((ROWS, D)),
            pl.BlockSpec((2, shards, half_rows, double), lambda i: (0, i, 0, 0)),
        ],
        out_specs=[whole((ROWS, D)), pl.BlockSpec((shards, SEQ, double), lambda i: (i, 0, 0))],
        scratch_shapes=[
            pltpu.VMEM((SEQ, D), F32),
            pltpu.VMEM((shards, D, double), BF16),
            pltpu.VMEM((shards * double // 2, D), BF16),
        ]
        + REDUCE_SCRATCH,
        compiler_params=params(5),
        name="ffn_forward",
    )(b_all, gate_col, residual, weights)


def ffn_backward_kernel(
    b_ref, gate_ref, delta_ref, kept_ref, w_ref, db_ref, gate_grad_ref, dw_ref,
    acc, gate_acc, b_turned, slot_grad, hidden_grad, acted, win, wout, rows_out, rows_in, send_g, recv_g,
    part, across_in, from_left, from_right, send, recv,
):
    step = pl.program_id(0)
    final = pl.num_programs(0) - 1
    shards, units = win.shape[0], LANES
    width = 2 * units

    @pl.when(step == 0)
    def _():
        _, right, left, across = ring()
        greet((right, left, across))
        acc[...] = jnp.zeros_like(acc)
        gate_acc[...] = jnp.zeros_like(gate_acc)
        b_turned[...] = b_ref[...].T
        slot_grad[...] = (delta_ref[...].astype(F32) * gate_ref[...]).astype(BF16)

    assemble(w_ref, win, wout)

    def terms(block):
        rows = rows_of(block)
        gate = gate_ref[rows, :]
        act_grad_all = dot_nt(delta_ref[rows, :], wout[...])
        gate_sum = gate_acc[rows, :]
        second_grad = acc[rows, :]
        for shard in range(shards):
            hidden = kept_ref[shard, rows, :].astype(F32)
            gate_part = hidden[:, :units]
            up_part = hidden[:, units:]
            act_grad = act_grad_all[:, shard * units : (shard + 1) * units]
            sigmoid = 1.0 / (1.0 + jnp.exp(-gate_part))
            silu = gate_part * sigmoid
            act = (silu * up_part).astype(BF16)
            acted[rows, shard * units : (shard + 1) * units] = act
            gate_sum += act.astype(F32) * act_grad
            act_grad = act_grad * gate
            gate_grad = act_grad * up_part * (sigmoid * (1.0 + gate_part * (1.0 - sigmoid)))
            pair = jnp.concatenate([gate_grad, act_grad * silu], axis=1).astype(BF16)
            hidden_grad[shard, rows, :] = pair
            second_grad += dot_nt(pair, win[shard])
        gate_acc[rows, :] = gate_sum
        return second_grad

    def weight_terms():
        for shard in range(shards):
            dw_ref[shard, :D, :] = dot(b_turned[...], hidden_grad[shard]).astype(BF16)
        whole_out = dot_tn(acted[...], slot_grad[...]).astype(BF16)
        for shard in range(shards):
            for piece in range(D // width):
                at = D + piece * units
                dw_ref[shard, at : at + units, :] = whole_out[
                    shard * units : (shard + 1) * units, piece * width : (piece + 1) * width
                ]

    @pl.when(step < final)
    def _():
        for block in range(CTX):
            acc[pl.ds(block * ROWS, ROWS), :] = terms(block)
        weight_terms()

    @pl.when(step == final)
    def _():
        met(3)
        me, right, left, across = ring()

        def make(block):
            part[rows_of(block), :] = terms(block).astype(BF16)

        def handed(step_to, peer):
            return remote(
                rows_out.at[peer], rows_in.at[step_to], send_g.at[step_to], recv_g.at[step_to], peer
            )

        def beside():
            own_row = lax.broadcasted_iota(jnp.int32, (8, LANES), 0) == me
            picker = jnp.where(own_row, 1.0, 0.0)
            for block in range(CTX):
                rows_out[block] = lax.dot_general(
                    picker,
                    gate_acc[pl.ds(block * ROWS, ROWS), :],
                    NT,
                    precision=EXACT,
                    preferred_element_type=F32,
                )
            for step_to, peer in ((0, right), (1, left), (2, across)):
                handed(step_to, peer).start()
            weight_terms()

        db_ref[...] = reduce_rows(
            make, part, across_in, from_left, from_right, send, recv, beside
        )
        for step_to, peer in ((0, right), (1, left), (2, across)):
            handed(step_to, peer).wait()
        rows_all = rows_out[me] + rows_in[0] + rows_in[1] + rows_in[2]
        picker = jnp.where(
            lax.broadcasted_iota(jnp.int32, (8, LANES), 0)
            == lax.broadcasted_iota(jnp.int32, (8, LANES), 1),
            1.0,
            0.0,
        )
        gate_grad_ref[...] = lax.dot_general(
            rows_all, picker, TN, precision=EXACT, preferred_element_type=F32
        )


def ffn_backward(b_all, gate_col, delta_all, kept, weights):
    _, count, half_rows, double = weights.shape
    shards = SHARDS_STEP
    units = double // 2
    sems = pltpu.SemaphoreType.DMA
    return pl.pallas_call(
        ffn_backward_kernel,
        grid=(count // shards,),
        out_shape=(
            jax.ShapeDtypeStruct((ROWS, D), F32),
            jax.ShapeDtypeStruct((ROWS, LANES), F32),
            jax.ShapeDtypeStruct((count, 2 * half_rows, double), BF16),
        ),
        in_specs=[
            whole((SEQ, D)),
            whole((SEQ, 1)),
            whole((SEQ, D)),
            pl.BlockSpec((shards, SEQ, double), lambda i: (i, 0, 0)),
            pl.BlockSpec((2, shards, half_rows, double), lambda i: (0, i, 0, 0)),
        ],
        out_specs=[
            whole((ROWS, D)),
            whole((ROWS, LANES)),
            pl.BlockSpec((shards, 2 * half_rows, double), lambda i: (i, 0, 0)),
        ],
        scratch_shapes=[
            pltpu.VMEM((SEQ, D), F32),
            pltpu.VMEM((SEQ, units), F32),
            pltpu.VMEM((D, SEQ), BF16),
            pltpu.VMEM((SEQ, D), BF16),
            pltpu.VMEM((shards, SEQ, double), BF16),
            pltpu.VMEM((SEQ, shards * units), BF16),
            pltpu.VMEM((shards, D, double), BF16),
            pltpu.VMEM((shards * units, D), BF16),
            pltpu.VMEM((CTX, 8, ROWS), F32),
            pltpu.VMEM((3, 8, ROWS), F32),
            sems((3,)),
            sems((3,)),
        ]
        + REDUCE_SCRATCH,
        compiler_params=params(6),
        name="ffn_backward",
    )(b_all, gate_col, delta_all, kept, weights)

def rotary_table():
    half_dim = HEAD_DIM // 2
    frequency = jnp.exp(
        -jnp.log(10000.0) * (2.0 * jnp.arange(half_dim, dtype=F32) / HEAD_DIM)
    )
    angles = jnp.arange(SEQ, dtype=jnp.int32).astype(F32)[:, None] * frequency[None, :]
    cosine, sine = jnp.cos(angles), jnp.sin(angles)
    return jnp.concatenate([cosine, cosine, sine, sine], axis=1)


def layer_forward(weights, tokens_in, length, routes_all, table):
    pack, experts = weights
    a_all, qkv, mass, attended, residual, b_all, gates, gate_col, *unpacked = attn_forward(
        length, tokens_in, routes_all, pack, table
    )
    output, kept = ffn_forward(b_all, gate_col, residual, experts)
    return output, (
        tokens_in, a_all, qkv, mass, attended, residual, b_all, gates, gate_col, kept, unpacked,
    )


def layer_backward(weights, saved, delta_all, delta_own, length, table, ctx_index, last):
    _, experts = weights
    tokens_in, a_all, qkv, mass, attended, residual, b_all, gates, gate_col, kept, unpacked = saved
    db, gate_grads, dexperts = ffn_backward(b_all, gate_col, delta_all, kept, experts)
    second = lax.dynamic_slice_in_dim(b_all, ctx_index * ROWS, ROWS, 0)
    own_gates = lax.dynamic_slice_in_dim(gates, ctx_index * ROWS, ROWS, 0)
    results = attn_backward(
        last, length, tokens_in, *unpacked, table, a_all, qkv, mass,
        attended, residual, second, own_gates, delta_own, db, gate_grads,
    )
    return dexperts, results

def adam_update(gradient, clipped, master, mean_old, square_old, step_value, learn_rate):
    mean_new = BETA_ONE * mean_old + (1.0 - BETA_ONE) * clipped
    square_new = BETA_TWO * square_old + (1.0 - BETA_TWO) * clipped * clipped
    fix_one = 1.0 - BETA_ONE**step_value
    fix_two = 1.0 - BETA_TWO**step_value
    master_new = master - learn_rate * (
        mean_new / fix_one / (jnp.sqrt(square_new / fix_two) + ADAM_EPS) + DECAY_RATE * master
    )
    return (gradient, mean_new, square_new, master_new, master_new.astype(BF16))


def on_device(
    inputs, cotangent, lengths, routes, step_count,
    norm_gains, gains_mean, gains_square,
    attn_weight, attn_mean, attn_square,
    router_weight, router_mean, router_square,
    expert_in, in_mean, in_square,
    expert_out, out_mean, out_square,
):
    section = lax.axis_index("section")
    ctx_index = lax.axis_index("ctx")
    fsdp = lax.axis_size("fsdp")
    everyone = ("section", "fsdp")
    shard_rows = attn_weight.shape[1]
    units = expert_in.shape[4]
    first_core = section == 0

    def own_columns(matrix, part):
        return lax.dynamic_slice_in_dim(matrix, part * D + ctx_index * COLS, COLS, 1)

    def swap(block):
        return lax.ppermute(block, "section", [(0, 1), (1, 0)])

    attn_shard = jnp.concatenate(
        [attn_weight[0][:, 3 * D :]]
        + [own_columns(attn_weight[0], part) for part in range(3)]
        + [jnp.zeros((shard_rows, HEAD_DIM), F32), router_weight[0], norm_gains[0].T]
        + [jnp.zeros((shard_rows, LANES - EXPERTS - 2), F32)],
        axis=1,
    ).astype(BF16)
    attn_shard = attn_shard.reshape(shard_rows, 6, UNIT).transpose(1, 0, 2).reshape(-1, UNIT)
    packs = gather_shards(attn_shard).reshape(2, fsdp, ATTN_ROWS, UNIT)
    in_shard = (
        lax.dynamic_index_in_dim(expert_in[0], ctx_index, 0, keepdims=False)
        .astype(BF16)
        .reshape(D, 2 * units)
    )
    out_shard = lax.dynamic_index_in_dim(expert_out[0], ctx_index, 0, keepdims=False).astype(BF16)
    halves = jnp.concatenate(
        [in_shard] + [out_shard[:, at : at + 2 * units] for at in range(0, D, 2 * units)], axis=0
    ).reshape(2, HALF_ROWS, 2 * units)
    other = swap(jnp.where(first_core, halves[1], halves[0]))
    pieces = (jnp.where(first_core, halves[0], other), jnp.where(first_core, other, halves[1]))
    experts = [
        lax.all_gather(piece, everyone).reshape(2, fsdp, HALF_ROWS, 2 * units) for piece in pieces
    ]
    routes_all = lax.all_gather(routes[0], ("section", "ctx")).reshape((2, CTX) + routes.shape[1:])
    routes_all = lax.dynamic_index_in_dim(routes_all, section, 2, keepdims=False).reshape(2, SEQ, 2)
    length = lax.dynamic_slice_in_dim(lengths, section, 1, 0)
    tokens = lax.dynamic_index_in_dim(inputs, section, 0, keepdims=False)
    positions = ctx_index * ROWS + jnp.arange(ROWS, dtype=jnp.int32)
    seed = lax.dynamic_index_in_dim(cotangent, section, 0, keepdims=False)
    seed = jnp.where((positions < length[0])[:, None], seed, jnp.zeros_like(seed))
    seed_all = lax.all_gather(seed, "ctx", tiled=True)
    table = rotary_table()

    layers = [(packs[layer], experts[layer]) for layer in range(2)]
    lower_out, lower_saved = layer_forward(layers[0], tokens, length, routes_all[0], table)
    upper_out, upper_saved = layer_forward(layers[1], lower_out, length, routes_all[1], table)

    upper_experts, (upper_grad, upper_attn, lower_seed) = layer_backward(
        layers[1], upper_saved, seed_all, seed, length, table, ctx_index, False
    )
    own_seed = upper_grad.astype(BF16)
    lower_experts, (lower_grad, lower_attn) = layer_backward(
        layers[0], lower_saved, lower_seed, own_seed, length, table, ctx_index, True
    )

    def paired(first, second):
        kept = jnp.where(first_core, first, second)
        other = swap(jnp.where(first_core, second, first))
        return jnp.stack(
            [jnp.where(first_core, kept, other), jnp.where(first_core, other, kept)]
        )

    layer_outputs = paired(lower_out, upper_out)[None]
    input_grads = paired(lower_grad, upper_grad)[None]
    shard_sum = sum_shards(lower_experts, lower_attn, upper_experts, upper_attn)
    sums_all, squares = spread_sums(shard_sum)
    in_sum = sums_all[:, :D].astype(F32).reshape(1, CTX, D, 2, units)
    out_sum = jnp.concatenate(
        [sums_all[:, at : at + units] for at in range(D, EXPERT_ROWS, units)], axis=2
    ).astype(F32)[None]
    attn_all = sums_all[:, EXPERT_ROWS:].astype(F32).reshape(CTX, 6, shard_rows, UNIT)
    back_sum = jnp.sum(attn_all[:, :3], axis=0).transpose(1, 0, 2).reshape(shard_rows, D)
    heads_sum = attn_all[:, 3:].transpose(0, 2, 1, 3).reshape(CTX, shard_rows, D)
    small_sum = jnp.sum(heads_sum[:, :, D - LANES :], axis=0)
    heads_sum = heads_sum[:, :, : 3 * COLS].reshape(CTX, shard_rows, 3, COLS)
    heads_sum = heads_sum.transpose(1, 2, 0, 3).reshape(shard_rows, 3 * D)
    attn_sum = jnp.concatenate([heads_sum, back_sum], axis=1)[None]
    router_sum = small_sum[:, :EXPERTS][None]
    gain_sum = small_sum[:, EXPERTS : EXPERTS + 2].T[None]
    sums = (gain_sum, attn_sum, router_sum, in_sum, out_sum)
    norms = jnp.sqrt(squares[0, : len(sums)])
    factors = jnp.minimum(1.0, CLIP_LIMIT / norms)
    step_value = step_count[0].astype(F32)
    wide_rate = RATE_FACTOR / D**0.5
    router_rate = RATE_FACTOR / (D // 4) ** 0.5
    down_rate = RATE_FACTOR / FFN**0.5
    olds = (
        (norm_gains, gains_mean, gains_square, GAIN_RATE),
        (attn_weight, attn_mean, attn_square, wide_rate),
        (router_weight, router_mean, router_square, router_rate),
        (expert_in, in_mean, in_square, wide_rate),
        (expert_out, out_mean, out_square, down_rate),
    )
    results = [layer_outputs, input_grads]
    for index, (total, (master, mean_old, square_old, rate)) in enumerate(zip(sums, olds)):
        results.extend(
            adam_update(total, total * factors[index], master, mean_old, square_old, step_value, rate)
        )
    return tuple(results) + (norms[None],)


def solution(mesh):
    gains = P("section", None, "fsdp")
    rows = P("section", "fsdp", None)
    wide = P("section", None, None, None, "fsdp")
    down = P("section", None, "fsdp", None)
    tokens = P("section", "fsdp", "ctx", None)
    return jax.shard_map(
        on_device,
        mesh=mesh,
        in_specs=(
            P("fsdp", "ctx", None),
            P("fsdp", "ctx", None),
            P("fsdp"),
            tokens,
            P(),
        )
        + (gains,) * 3
        + (rows,) * 6
        + (wide,) * 3
        + (down,) * 3,
        out_specs=(tokens, tokens)
        + (gains,) * 5
        + (rows,) * 10
        + (wide,) * 5
        + (down,) * 5
        + (P("section", None),),
        check_vma=False,
    )
```

```python
import functools

import jax
import jax.numpy as jnp
from jax import lax
from jax.experimental import pallas as pl
from jax.experimental.pallas import tpu as pltpu
from jax.sharding import PartitionSpec as P

D = 768
HEADS = 12
HEAD_DIM = 64
FFN = 2048
EXPERTS = 3
ROWS = 256
CTX = 4
SEQ = ROWS * CTX
HEADS_DEV = HEADS // CTX
WIDE = 128
EXT = 3 * HEADS_DEV * WIDE
COLS = HEADS_DEV * HEAD_DIM

EPS_NORM = 1e-06
BETA_ONE = 0.9
BETA_TWO = 0.95
RATE_FACTOR = 3.0
GAIN_RATE = 0.3
DECAY_RATE = 0.1
ADAM_EPS = 1e-08
CLIP_LIMIT = 1.0
MASK_VALUE = -1e30
SCORE_SCALE = HEAD_DIM ** (-0.5) / 2.0
BF16 = jnp.bfloat16
F32 = jnp.float32
VMEM_LIMIT = 56 * 1024 * 1024
NT = (((1,), (1,)), ((), ()))
TN = (((0,), (0,)), ((), ()))
HALF = ROWS // 2
LANES = 128
MESH = pl.DeviceIdType.MESH
EXACT = lax.Precision.HIGHEST


def dot(left, right):
    return jnp.dot(left, right, preferred_element_type=F32)


def dot_nt(left, right):
    return lax.dot_general(left, right, NT, preferred_element_type=F32)


def dot_tn(left, right):
    return lax.dot_general(left, right, TN, preferred_element_type=F32)


def params(collective_id):
    return pltpu.CompilerParams(
        vmem_limit_bytes=VMEM_LIMIT, collective_id=collective_id, has_side_effects=True
    )


def whole(shape):
    return pl.BlockSpec(shape, lambda *_: (0,) * len(shape))


def allowed_keys(block, keys, length):
    key_pos = lax.broadcasted_iota(jnp.int32, (ROWS, keys), 1)
    query_pos = lax.broadcasted_iota(jnp.int32, (ROWS, keys), 0) + block * ROWS
    return (key_pos <= query_pos) & (key_pos < length)


VMEM = pl.BlockSpec(memory_space=pltpu.VMEM)
SMEM = pl.BlockSpec(memory_space=pltpu.SMEM)


def ring():
    me = lax.axis_index("ctx")
    return me, lax.rem(me + 1, CTX), lax.rem(me + 3, CTX), lax.rem(me + 2, CTX)


def greet(peers):
    barrier = pltpu.get_barrier_semaphore()
    for peer in peers:
        pl.semaphore_signal(barrier, inc=1, device_id={"ctx": peer}, device_id_type=MESH)


def met(count):
    pl.semaphore_wait(pltpu.get_barrier_semaphore(), count)


def remote(source, target, send, recv, peer):
    return pltpu.make_async_remote_copy(
        src_ref=source,
        dst_ref=target,
        send_sem=send,
        recv_sem=recv,
        device_id={"ctx": peer},
        device_id_type=MESH,
    )


def rows_of(block, half=None):
    if half is None:
        return pl.ds(pl.multiple_of(block * ROWS, ROWS), ROWS)
    return pl.ds(pl.multiple_of(block * ROWS + half * HALF, HALF), HALF)


def gather_rows(all_ref, send, recv, beside=None):
    me, right, left, _ = ring()

    def piece(index, block, half, peer):
        spot = all_ref.at[rows_of(block, half)]
        return remote(spot, spot, send.at[index], recv.at[index], peer)

    copies = [
        piece(0, me, 0, right),
        piece(1, me, 1, left),
        piece(2, me, 1, right),
        piece(3, me, 0, left),
    ]
    for copy in copies:
        copy.start()
    if beside is not None:
        beside()
    copies[0].wait_recv()
    copies.append(piece(4, left, 0, right))
    copies[4].start()
    copies[1].wait_recv()
    copies.append(piece(5, right, 1, left))
    copies[5].start()
    for index in range(2, 6):
        copies[index].wait_recv()
    for copy in copies:
        copy.wait_send()


def reduce_rows(make, part, across_in, from_left, from_right, send, recv, beside=None):
    me, right, left, across = ring()
    top, bottom = pl.ds(0, HALF), pl.ds(HALF, HALF)

    def piece(index, block, half, target, peer):
        return remote(part.at[rows_of(block, half)], target, send.at[index], recv.at[index], peer)

    make(across)
    copies = [
        piece(0, across, 0, across_in.at[0], right),
        piece(1, across, 1, across_in.at[1], left),
    ]
    copies[0].start()
    copies[1].start()
    make(right)
    copies.append(piece(2, right, 1, from_left.at[bottom], right))
    copies[2].start()
    make(left)
    copies.append(piece(3, left, 0, from_right.at[top], left))
    copies[3].start()
    copies[0].wait_recv()
    spot = rows_of(right, 0)
    part[spot, :] = (part[spot, :].astype(F32) + across_in[0].astype(F32)).astype(BF16)
    copies.append(piece(4, right, 0, from_left.at[top], right))
    copies[4].start()
    copies[1].wait_recv()
    spot = rows_of(left, 1)
    part[spot, :] = (part[spot, :].astype(F32) + across_in[1].astype(F32)).astype(BF16)
    copies.append(piece(5, left, 1, from_right.at[bottom], left))
    copies[5].start()
    make(me)
    if beside is not None:
        beside()
    for index in range(2, 6):
        copies[index].wait_recv()
    for copy in copies:
        copy.wait_send()
    return (
        part[rows_of(me), :].astype(F32) + from_left[...].astype(F32) + from_right[...].astype(F32)
    )


REDUCE_SCRATCH = [
    pltpu.VMEM((SEQ, D), BF16),
    pltpu.VMEM((2, HALF, D), BF16),
    pltpu.VMEM((ROWS, D), BF16),
    pltpu.VMEM((ROWS, D), BF16),
    pltpu.SemaphoreType.DMA((6,)),
    pltpu.SemaphoreType.DMA((6,)),
]


def greet_ids(peers):
    barrier = pltpu.get_barrier_semaphore()
    for peer in peers:
        pl.semaphore_signal(barrier, inc=1, device_id=peer, device_id_type=MESH)


class Ring:
    def __init__(self, axis):
        if axis == "x":
            self.me = lax.axis_index("ctx")
            self.place = lambda index: {"ctx": index}
        else:
            shard = lax.axis_index("fsdp")
            inner, outer = lax.rem(shard, CTX), lax.div(shard, CTX)
            if axis == "y":
                self.me = inner
                self.place = lambda index: {"fsdp": outer * CTX + index}
            else:
                self.me = outer
                self.place = lambda index: {"fsdp": index * CTX + inner}
        self.right = lax.rem(self.me + 1, CTX)
        self.left = lax.rem(self.me + 3, CTX)
        self.across = lax.rem(self.me + 2, CTX)

    def order(self):
        return (self.across, self.right, self.left, self.me)

    def near(self):
        return [self.place(self.right), self.place(self.left)]

    def copy(self, source, target, send, recv, index):
        return pltpu.make_async_remote_copy(
            src_ref=source,
            dst_ref=target,
            send_sem=send,
            recv_sem=recv,
            device_id=self.place(index),
            device_id_type=MESH,
        )


class RingGather:
    def __init__(self, ring, at, send, recv):
        self.ring, self.at, self.send, self.recv = ring, at, send, recv
        self.copies = []

    def go(self, block, half, to):
        spot = self.at(block, half)
        index = len(self.copies)
        self.copies.append(
            self.ring.copy(spot, spot, self.send.at[index], self.recv.at[index], to)
        )
        self.copies[-1].start()

    def start(self):
        ring = self.ring
        self.go(ring.me, 0, ring.right)
        self.go(ring.me, 1, ring.left)
        self.go(ring.me, 1, ring.right)
        self.go(ring.me, 0, ring.left)

    def forward(self):
        ring = self.ring
        spot = self.at(ring.left, 0)
        ring.copy(spot, spot, self.send.at[0], self.recv.at[0], ring.right).wait_recv()
        self.go(ring.left, 0, ring.right)
        spot = self.at(ring.right, 1)
        ring.copy(spot, spot, self.send.at[1], self.recv.at[1], ring.left).wait_recv()
        self.go(ring.right, 1, ring.left)

    def landed(self, index, block, half):
        spot = self.at(block, half)
        self.ring.copy(
            spot, spot, self.send.at[index], self.recv.at[index], self.ring.right
        ).wait_recv()

    def near(self):
        self.landed(2, self.ring.left, 1)
        self.landed(3, self.ring.right, 0)

    def far(self):
        self.landed(4, self.ring.across, 0)
        self.landed(5, self.ring.across, 1)

    def sent(self):
        for copy in self.copies:
            copy.wait_send()

    def finish(self):
        self.near()
        self.far()
        self.sent()


class RingSum:
    def __init__(self, ring, part, across_in, from_left, from_right, send, recv, cut, make):
        self.ring, self.part, self.across_in = ring, part, across_in
        self.from_left, self.from_right, self.send, self.recv = from_left, from_right, send, recv
        size = part.shape[1]
        self.halves = (pl.ds(0, cut), pl.ds(cut, size - cut))
        self.make = make
        self.copies = {}

    def go(self, index, block, half, target, to):
        self.copies[index] = self.ring.copy(
            self.part.at[block, self.halves[half]], target, self.send.at[index], self.recv.at[index], to
        )
        self.copies[index].start()

    def arrived(self, half, block):
        self.copies[half].wait_recv()
        incoming = self.across_in[half]
        if len(self.part.shape) == 3:
            spot = (block, self.halves[half])
            self.part[spot] = (self.part[spot].astype(F32) + incoming[...].astype(F32)).astype(BF16)
            return
        start = (0, self.part.shape[1] - incoming.shape[0])[half]
        for index in range(incoming.shape[0]):
            self.part[block, start + index] = (
                self.part[block, start + index].astype(F32) + incoming[index].astype(F32)
            ).astype(BF16)

    def stage(self, number):
        ring = self.ring
        if number == 0:
            self.make(0, ring.across)
            self.go(0, ring.across, 0, self.across_in[0], ring.right)
            self.go(1, ring.across, 1, self.across_in[1], ring.left)
        elif number == 1:
            self.make(1, ring.right)
            self.go(2, ring.right, 1, self.from_left.at[self.halves[1]], ring.right)
        elif number == 2:
            self.make(2, ring.left)
            self.go(3, ring.left, 0, self.from_right.at[self.halves[0]], ring.left)
        elif number == 3:
            self.arrived(0, ring.right)
            self.go(4, ring.right, 0, self.from_left.at[self.halves[0]], ring.right)
            self.arrived(1, ring.left)
            self.go(5, ring.left, 1, self.from_right.at[self.halves[1]], ring.left)
        elif number == 4:
            self.make(3, ring.me)
        else:
            for index in range(2, 6):
                self.copies[index].wait_recv()
            for index in range(6):
                self.copies[index].wait_send()

    def total(self, index=None):
        spot = (self.ring.me,) if index is None else (self.ring.me, index)
        tail = () if index is None else (index,)
        return (
            self.part[spot].astype(F32)
            + self.from_left[tail or ...].astype(F32)
            + self.from_right[tail or ...].astype(F32)
        )


UNIT = 256
EXPERT_ROWS = D + D // 2
ATTN_ROWS = 288
SHARD_ROWS = EXPERT_ROWS + ATTN_ROWS
FIRST = SHARD_ROWS // 2
KEPT = EXPERT_ROWS - FIRST
CUT = 352
SEMS = pltpu.SemaphoreType.DMA


def gather_shards_kernel(shard_ref, code_ref, out_ref, codes_ref, *sems):
    section = lax.axis_index("section")
    sibling = {"section": 1 - section}
    ring_y, ring_z = Ring("y"), Ring("z")
    y, z = ring_y.me, ring_z.me
    ring_x = Ring("x")
    x_peers = (ring_x.right, ring_x.left, ring_x.across)
    greet_ids(
        [sibling] + ring_y.near() + ring_z.near() + [ring_x.place(peer) for peer in x_peers]
    )
    out_ref[section, z, y] = shard_ref[...]
    codes_ref[section, ring_x.me] = code_ref[...]
    met(8)
    spot = codes_ref.at[section, ring_x.me]
    code_copies = [
        ring_x.copy(spot, spot, sems[10].at[index], sems[11].at[index], peer)
        for index, peer in enumerate(x_peers)
    ]
    for copy in code_copies:
        copy.start()
    half = ATTN_ROWS // 2
    low = (pl.ds(0, 64), pl.ds(64, half - 64))
    high = (pl.ds(half, 64), pl.ds(half + 64, half - 64))
    pair = (pl.ds(0, 2), pl.ds(2, 2))
    near_y = RingGather(ring_y, lambda b, h: out_ref.at[section, z, b, low[h]], sems[0], sems[1])
    near_z = RingGather(ring_z, lambda b, h: out_ref.at[section, b, y, high[h]], sems[2], sems[3])
    far_z = RingGather(
        ring_z, lambda b, h: out_ref.at[section, b, pair[h], pl.ds(0, half)], sems[4], sems[5]
    )
    far_y = RingGather(
        ring_y, lambda b, h: out_ref.at[section, pair[h], b, pl.ds(half, half)], sems[6], sems[7]
    )
    for rings in ((near_y, near_z), (far_z, far_y)):
        for one in rings:
            one.start()
        for one in rings:
            one.forward()
        for one in rings:
            one.finish()
    across = pltpu.make_async_remote_copy(
        src_ref=out_ref.at[section],
        dst_ref=out_ref.at[section],
        send_sem=sems[8],
        recv_sem=sems[9],
        device_id=sibling,
        device_id_type=MESH,
    )
    across.start()
    for copy in code_copies:
        copy.wait()
    codes_across = pltpu.make_async_remote_copy(
        src_ref=codes_ref.at[section],
        dst_ref=codes_ref.at[section],
        send_sem=sems[12],
        recv_sem=sems[13],
        device_id=sibling,
        device_id_type=MESH,
    )
    codes_across.start()
    codes_across.wait()
    across.wait()


def gather_shards(shard, codes):
    return pl.pallas_call(
        gather_shards_kernel,
        out_shape=(
            jax.ShapeDtypeStruct((2, CTX, CTX, ATTN_ROWS, UNIT), BF16),
            jax.ShapeDtypeStruct((2, CTX, 8, ROWS), F32),
        ),
        in_specs=[VMEM, VMEM],
        out_specs=[VMEM, VMEM],
        scratch_shapes=[SEMS((6,))] * 8 + [SEMS, SEMS, SEMS((3,)), SEMS((3,)), SEMS, SEMS],
        compiler_params=params(7),
        name="gather_shards",
    )(shard, codes)


def sum_shards_kernel(
    lower_e, lower_a, upper_e, upper_a, out_ref,
    part_y, in_y, part_z, in_z, top_y, bottom_y, left_y, right_y, top_z, bottom_z, left_z, right_z,
    more_z, more_y, top_zz, bottom_zz, left_zz, right_zz, top_yy, bottom_yy, left_yy, right_yy, *sems,
):
    section = lax.axis_index("section")
    sibling = {"section": 1 - section}
    ring_y, ring_z = Ring("y"), Ring("z")
    greet_ids([sibling] + ring_y.near() + ring_z.near())
    local, send_s, recv_s = sems[:3]

    def pieces(index, experts, attn, target_y, target_z):
        b_y, b_z = ring_y.order()[index], ring_z.order()[index]
        return (
            (experts.at[:, b_y, pl.ds(0, FIRST), :], target_y.at[b_y]),
            (experts.at[b_z, :, pl.ds(FIRST, KEPT), :], target_z.at[b_z, :, pl.ds(0, KEPT), :]),
            (attn.at[b_z], target_z.at[b_z, :, pl.ds(KEPT, ATTN_ROWS), :]),
        )

    def fetch(index, number, source, target):
        return pltpu.make_async_copy(source, target, local.at[index * 3 + number])

    def pass_on(index, number, source, target):
        at = index * 3 + number
        return pltpu.make_async_remote_copy(
            src_ref=source,
            dst_ref=target,
            send_sem=send_s.at[at],
            recv_sem=recv_s.at[at],
            device_id=sibling,
            device_id_type=MESH,
        )

    def begin(own_e, own_a, other_e, other_a):
        for index in range(CTX):
            for number, (source, target) in enumerate(pieces(index, own_e, own_a, part_y, part_z)):
                fetch(index, number, source, target).start()

    def lend(other_e, other_a):
        for index in range(CTX):
            for number, (source, target) in enumerate(pieces(index, other_e, other_a, in_y, in_z)):
                pass_on(index, number, source, target).start()

    @pl.when(section == 0)
    def _():
        begin(lower_e, lower_a, upper_e, upper_a)

    @pl.when(section == 1)
    def _():
        begin(upper_e, upper_a, lower_e, lower_a)

    met(5)

    @pl.when(section == 0)
    def _():
        lend(upper_e, upper_a)

    @pl.when(section == 1)
    def _():
        lend(lower_e, lower_a)

    def ready(index, number):
        source, target = pieces(index, lower_e, lower_a, part_y, part_z)[number]
        fetch(index, number, source, target).wait()
        source, target = pieces(index, lower_e, lower_a, in_y, in_z)[number]
        pass_on(index, number, source, target).wait_recv()

    def make_y(index, block):
        ready(index, 0)
        for other in range(CTX):
            part_y[block, other] = (
                part_y[block, other].astype(F32) + in_y[block, other].astype(F32)
            ).astype(BF16)

    def make_z(index, block):
        ready(index, 1)
        ready(index, 2)
        for other in range(CTX):
            part_z[block, other] = (
                part_z[block, other].astype(F32) + in_z[block, other].astype(F32)
            ).astype(BF16)

    first_y = RingSum(ring_y, part_y, (top_y, bottom_y), left_y, right_y, sems[3], sems[4], 2, make_y)
    first_z = RingSum(ring_z, part_z, (top_z, bottom_z), left_z, right_z, sems[5], sems[6], 2, make_z)

    def make_zz(index, block):
        more_z[block] = first_y.total(block).astype(BF16)

    def make_yy(index, block):
        more_y[block] = first_z.total(block).astype(BF16)

    then_z = RingSum(
        ring_z, more_z, (top_zz, bottom_zz), left_zz, right_zz, sems[7], sems[8], CUT, make_zz
    )
    then_y = RingSum(
        ring_y, more_y, (top_yy, bottom_yy), left_yy, right_yy, sems[9], sems[10], CUT, make_yy
    )
    for number in range(6):
        first_y.stage(number)
        first_z.stage(number)
    for number in range(6):
        then_z.stage(number)
        then_y.stage(number)
    out_ref[:FIRST, :] = then_z.total().astype(BF16)
    out_ref[FIRST:, :] = then_y.total().astype(BF16)
    for index in range(CTX):
        for number, (source, target) in enumerate(pieces(index, lower_e, lower_a, in_y, in_z)):
            pass_on(index, number, source, target).wait_send()


def sum_shards(lower_e, lower_a, upper_e, upper_a):
    block = pltpu.VMEM((CTX, FIRST, UNIT), BF16)
    pair = pltpu.VMEM((2, FIRST, UNIT), BF16)
    one = pltpu.VMEM((FIRST, UNIT), BF16)
    top, bottom = pltpu.VMEM((CUT, UNIT), BF16), pltpu.VMEM((FIRST - CUT, UNIT), BF16)
    full = pltpu.VMEM((CTX, CTX, FIRST, UNIT), BF16)
    anywhere = pl.BlockSpec(memory_space=pl.ANY)
    return pl.pallas_call(
        sum_shards_kernel,
        out_shape=jax.ShapeDtypeStruct((SHARD_ROWS, UNIT), BF16),
        in_specs=[anywhere] * 4,
        out_specs=VMEM,
        scratch_shapes=[full] * 4
        + [pair, pair, block, block] * 2
        + [block, block]
        + [top, bottom, one, one] * 2
        + [SEMS((12,))] * 3
        + [SEMS((6,))] * 8,
        compiler_params=params(8),
        name="sum_shards",
    )(*(
        array.reshape((CTX, CTX) + array.shape[1:])
        for array in (lower_e, lower_a, upper_e, upper_a)
    ))


def spread_sums_kernel(shard_ref, all_ref, squares_ref, from_y, from_z, *sems):
    ring_x, ring_y, ring_z = Ring("x"), Ring("y"), Ring("z")
    far = [
        one.place(index)
        for one in (ring_y, ring_z)
        for index in (one.right, one.left, one.across)
    ]
    greet_ids(ring_x.near() + far)
    all_ref[ring_x.me] = shard_ref[...]
    met(8)
    halves = (pl.ds(0, FIRST), pl.ds(FIRST, FIRST))
    rows = RingGather(ring_x, lambda b, h: all_ref.at[b, halves[h]], sems[0], sems[1])
    rows.start()
    rows.forward()
    rows.finish()

    def folded(values):
        squared = values * values
        return jnp.sum(squared, axis=0, keepdims=True)

    in_row = jnp.zeros((1, UNIT), F32)
    out_row = jnp.zeros((1, UNIT), F32)
    attn_row = jnp.zeros((1, UNIT), F32)
    back = jnp.zeros((ATTN_ROWS // 2, UNIT), F32)
    small = jnp.zeros((48, UNIT), F32)
    lanes = lax.broadcasted_iota(jnp.int32, (1, UNIT), 1)
    for block in range(CTX):
        in_row += folded(all_ref[block, :D, :].astype(F32))
        out_row += folded(all_ref[block, D:EXPERT_ROWS, :].astype(F32))
        middle = EXPERT_ROWS + ATTN_ROWS // 2
        back += all_ref[block, EXPERT_ROWS:middle, :].astype(F32)
        attn_row += folded(all_ref[block, middle : middle + 96, :].astype(F32))
        final = all_ref[block, middle + 96 :, :].astype(F32)
        attn_row += jnp.where(lanes < HEAD_DIM, folded(final), 0.0)
        small += final
    attn_row += folded(back)
    small_row = folded(small)
    is_router = (lanes >= LANES) & (lanes < LANES + EXPERTS)
    is_gain = (lanes >= LANES + EXPERTS) & (lanes < LANES + EXPERTS + 2)
    sums = [
        jnp.where(is_gain, small_row, 0.0),
        attn_row,
        jnp.where(is_router, small_row, 0.0),
        in_row,
        out_row,
    ]
    places = lax.broadcasted_iota(jnp.int32, (8, LANES), 1)
    tile = jnp.zeros((8, LANES), F32)
    for index, row in enumerate(sums):
        tile = jnp.where(places == index, jnp.sum(row, axis=1, keepdims=True), tile)

    def shared(one, slots, send, recv, tile):
        slots[one.me] = tile
        copies = []
        for index, peer in enumerate((one.right, one.left, one.across)):
            spot = slots.at[one.me]
            copies.append(one.copy(spot, spot, send.at[index], recv.at[index], peer))
            copies[-1].start()
        for copy in copies:
            copy.wait()
        return (slots[0] + slots[1]) + (slots[2] + slots[3])

    tile = shared(ring_y, from_y, sems[2], sems[3], tile)
    squares_ref[...] = shared(ring_z, from_z, sems[4], sems[5], tile)


def spread_sums(shard):
    slots = pltpu.VMEM((CTX, 8, LANES), F32)
    return pl.pallas_call(
        spread_sums_kernel,
        out_shape=(
            jax.ShapeDtypeStruct((CTX, SHARD_ROWS, UNIT), BF16),
            jax.ShapeDtypeStruct((8, LANES), F32),
        ),
        in_specs=[VMEM],
        out_specs=[VMEM, VMEM],
        scratch_shapes=[slots, slots, SEMS((6,)), SEMS((6,))] + [SEMS((3,))] * 4,
        compiler_params=params(9),
        name="spread_sums",
    )(shard)


def inverse_size(values):
    return lax.rsqrt(jnp.mean(values * values, axis=1, keepdims=True) + EPS_NORM)


def unpack(pack_ref, back_ref, heads_ref):
    def body(index, _):
        rows = pl.ds(pl.multiple_of(index * 48, 16), 48)
        for piece in range(6):
            target = back_ref if piece < 3 else heads_ref
            at = (piece % 3) * UNIT
            target[rows, at : at + UNIT] = pack_ref[index, piece * 48 : (piece + 1) * 48, :]
        return 0

    lax.fori_loop(0, 16, body, 0)


def repack(back_ref, heads_ref, pack_ref):
    def body(index, _):
        rows = pl.ds(pl.multiple_of(index * 48, 16), 48)
        for piece in range(6):
            source = back_ref if piece < 3 else heads_ref
            at = (piece % 3) * UNIT
            pack_ref[index, piece * 48 : (piece + 1) * 48, :] = source[rows, at : at + UNIT]
        return 0

    lax.fori_loop(0, 16, body, 0)


def extend(heads_ref, w_ref):
    lanes = lax.broadcasted_iota(jnp.int32, (D, WIDE), 1)
    for head in range(3 * HEADS_DEV):
        at = head // 2 * WIDE
        values = heads_ref[:, at : at + WIDE].astype(F32)
        if head % 2:
            values = pltpu.roll(values, HEAD_DIM, 1)
        if head < 2 * HEADS_DEV:
            upper = jnp.where(
                lanes < 96, -pltpu.roll(values, 32, 1), pltpu.roll(values, 96, 1)
            )
        else:
            upper = jnp.zeros_like(values)
        w_ref[:, head * WIDE : (head + 1) * WIDE] = jnp.where(
            lanes < HEAD_DIM, values, upper
        ).astype(BF16)


def attn_forward_kernel(
    length_ref, u_ref, pack_ref, table_ref,
    a_ref, qkv_ref, mass_ref, attended_ref, residual_ref, b_ref,
    gains_ref, router_ref, w_ref, back_ref,
    heads_out, heads_w, send_a, recv_a, send_o, recv_o,
):
    me, right, left, across = ring()
    greet((right, left, across))
    length = length_ref[0]
    tokens = u_ref[...].astype(F32)
    unpack(pack_ref, back_ref, heads_w)
    router_ref[...] = heads_w[:, D - LANES :]
    places = lax.broadcasted_iota(jnp.int32, (8, LANES), 0) + EXPERTS
    picker = jnp.where(places == lax.broadcasted_iota(jnp.int32, (8, LANES), 1), 1.0, 0.0)
    gains_ref[...] = dot_nt(picker.astype(BF16), router_ref[...])
    a_ref[rows_of(me), :] = (tokens * inverse_size(tokens) * gains_ref[0:1, :]).astype(BF16)
    met(3)
    gather_rows(a_ref, send_a, recv_a, lambda: extend(heads_w, w_ref))
    for block in range(CTX):
        rows = pl.ds(block * ROWS, ROWS)
        table = table_ref[rows, :]
        mixed = dot(a_ref[rows, :], w_ref[...])
        for part in range(3 * HEADS_DEV):
            lanes = slice(part * WIDE, (part + 1) * WIDE)
            piece = mixed[:, lanes]
            if part < 2 * HEADS_DEV:
                turned = piece * table
                piece = turned + pltpu.roll(turned, WIDE // 2, 1)
            qkv_ref[rows, lanes] = piece.astype(BF16)

    def handed(block):
        step = lax.rem(block - me + CTX, CTX)
        return remote(
            heads_out.at[block], attended_ref.at[me], send_o.at[step], recv_o.at[step], block
        )

    for block in reversed(range(CTX)):
        rows = pl.ds(block * ROWS, ROWS)
        keys = (block + 1) * ROWS
        allowed = allowed_keys(block, keys, length)
        outs = []
        for head in range(HEADS_DEV):
            queries = qkv_ref[rows, head * WIDE : (head + 1) * WIDE]
            key_lanes = slice((HEADS_DEV + head) * WIDE, (HEADS_DEV + head + 1) * WIDE)
            value_lanes = slice((2 * HEADS_DEV + head) * WIDE, (2 * HEADS_DEV + head + 1) * WIDE)
            scores = dot_nt(queries, qkv_ref[:keys, key_lanes]) * SCORE_SCALE
            scores = jnp.where(allowed, scores, MASK_VALUE)
            top = jnp.max(scores, axis=1, keepdims=True)
            raw = jnp.exp(scores - top)
            total = jnp.sum(raw, axis=1, keepdims=True)
            probs = (raw * (1.0 / total)).astype(BF16)
            outs.append(dot(probs, qkv_ref[:keys, value_lanes]))
            mass_ref[head, rows, :] = top + jnp.log(total)
        first = (outs[0] + pltpu.roll(outs[1], WIDE // 2, 1)).astype(BF16)
        second = outs[2][:, : WIDE // 2].astype(BF16)
        heads_out[block, :, :WIDE] = first
        heads_out[block, :, WIDE:] = second

        @pl.when(block != me)
        def _():
            handed(block).start()

    attended_ref[me] = heads_out[me]
    for step in range(1, CTX):
        pltpu.make_async_copy(heads_out.at[0], attended_ref.at[0], recv_o.at[step]).wait()
    residual = tokens
    for block in range(CTX):
        residual = residual + dot(attended_ref[block], back_ref[block * COLS : (block + 1) * COLS, :])
    residual_ref[...] = residual
    b_ref[...] = (residual * inverse_size(residual) * gains_ref[1:2, :]).astype(BF16)
    for step in range(1, CTX):
        pltpu.make_async_copy(heads_out.at[0], attended_ref.at[0], send_o.at[step]).wait()


def attn_forward(length, u, pack, table):
    sems = pltpu.SemaphoreType.DMA
    return pl.pallas_call(
        attn_forward_kernel,
        out_shape=(
            jax.ShapeDtypeStruct((SEQ, D), BF16),
            jax.ShapeDtypeStruct((SEQ, EXT), BF16),
            jax.ShapeDtypeStruct((HEADS_DEV, SEQ, 1), F32),
            jax.ShapeDtypeStruct((CTX, ROWS, COLS), BF16),
            jax.ShapeDtypeStruct((ROWS, D), F32),
            jax.ShapeDtypeStruct((ROWS, D), BF16),
            jax.ShapeDtypeStruct((8, D), F32),
            jax.ShapeDtypeStruct((D, LANES), BF16),
            jax.ShapeDtypeStruct((D, EXT), BF16),
            jax.ShapeDtypeStruct((D, D), BF16),
        ),
        in_specs=[SMEM] + [VMEM] * 3,
        out_specs=[VMEM] * 10,
        scratch_shapes=[pltpu.VMEM((CTX, ROWS, COLS), BF16), pltpu.VMEM((D, D), BF16)]
        + [sems((6,)), sems((6,)), sems((CTX,)), sems((CTX,))],
        compiler_params=params(1),
        name="attn_forward",
    )(length, u, pack, table)


def attn_backward_kernel(
    length_ref, u_ref, gains_ref, router_ref, w_ref, back_ref, table_ref,
    a_ref, qkv_ref, mass_ref, attended_ref, residual_ref, second_ref, gates_ref,
    delta_ref, db_ref, gate_grad_ref, *rest,
):
    input_ref, pack_ref, lower_ref = rest[:3]
    rest = rest[3:]
    dheads_ref, dback_ref = rest[:2]
    rest = rest[2:]
    key_acc, value_acc, dz, grads_out, grads_in, send_o, recv_o = rest[:7]
    part, across_in, from_left, from_right, send_r, recv_r = rest[7:13]
    me, right, left, across = ring()
    greet((right, left, across))
    length = length_ref[0]
    lanes = lax.broadcasted_iota(jnp.int32, (ROWS, LANES), 1)
    gates = gates_ref[...]
    gate_grads = jnp.where(lanes < EXPERTS, gate_grad_ref[...], 0.0)
    logit_grad = gates * (gate_grads - jnp.sum(gates * gate_grads, axis=1, keepdims=True))
    logit_grad = logit_grad.astype(BF16)
    second_grad = db_ref[...] + dot_nt(logit_grad, router_ref[...])
    residual = residual_ref[...]
    scale_two = inverse_size(residual)
    normal_two = residual * scale_two
    gain_two_terms = second_grad * normal_two
    scaled_two = second_grad * gains_ref[1:2, :]
    residual_grad = delta_ref[...].astype(F32) + scale_two * (
        scaled_two - normal_two * jnp.mean(scaled_two * normal_two, axis=1, keepdims=True)
    )
    input_ref[...] = residual_grad
    branch_grad = residual_grad.astype(BF16)
    met(3)

    for block in range(CTX):
        grads_out[block] = dot_nt(branch_grad, back_ref[block * COLS : (block + 1) * COLS, :]).astype(
            BF16
        )

        @pl.when(block != me)
        def _():
            step = lax.rem(block - me + CTX, CTX)
            remote(
                grads_out.at[block], grads_in.at[me], send_o.at[step], recv_o.at[step], block
            ).start()

    grads_in[me] = grads_out[me]
    for block in range(CTX):
        dback_ref[block * COLS : (block + 1) * COLS, :] = dot_tn(
            attended_ref[block], branch_grad
        ).astype(BF16)
    router_terms = dot_tn(second_ref[...], logit_grad)
    ones = jnp.ones((ROWS, LANES), F32)
    gain_two_column = lax.dot_general(
        gain_two_terms, ones, TN, precision=EXACT, preferred_element_type=F32
    )
    key_acc[...] = jnp.zeros_like(key_acc)
    value_acc[...] = jnp.zeros_like(value_acc)
    for step in range(1, CTX):
        pltpu.make_async_copy(grads_out.at[0], grads_in.at[0], recv_o.at[step]).wait()
    for step in range(1, CTX):
        pltpu.make_async_copy(grads_out.at[0], grads_in.at[0], send_o.at[step]).wait()
    for block in range(CTX):
        rows = pl.ds(block * ROWS, ROWS)
        keys = (block + 1) * ROWS
        allowed = allowed_keys(block, keys, length)
        pair = grads_in[block, :, :WIDE]
        tail = grads_in[block, :, WIDE:]
        head_grads = (
            pair,
            pltpu.roll(pair.astype(F32), WIDE // 2, 1).astype(BF16),
            jnp.concatenate([tail, jnp.zeros_like(tail)], axis=1),
        )
        for head in range(HEADS_DEV):
            queries = qkv_ref[rows, head * WIDE : (head + 1) * WIDE]
            keys_all = qkv_ref[:keys, (HEADS_DEV + head) * WIDE : (HEADS_DEV + head + 1) * WIDE]
            values_all = qkv_ref[
                :keys, (2 * HEADS_DEV + head) * WIDE : (2 * HEADS_DEV + head + 1) * WIDE
            ]
            grads = head_grads[head]
            scores = dot_nt(queries, keys_all) * SCORE_SCALE
            probs = jnp.where(allowed, jnp.exp(scores - mass_ref[head, rows, :]), 0.0)
            prob_grad = dot_nt(grads, values_all)
            row_sum = jnp.sum(probs * prob_grad, axis=1, keepdims=True)
            score_grad = (probs * (prob_grad - row_sum)).astype(BF16)
            query_grad = dot(score_grad, keys_all) * (HEAD_DIM**-0.5)
            dz[rows, head * WIDE : (head + 1) * WIDE] = (query_grad * table_ref[rows, :]).astype(BF16)
            spot = slice(head * WIDE, (head + 1) * WIDE)
            key_acc[:keys, spot] += dot_tn(score_grad, queries)
            value_acc[:keys, spot] += dot_tn(probs.astype(BF16), grads)
    for block in range(CTX):
        rows = pl.ds(block * ROWS, ROWS)
        table = table_ref[rows, :] * (HEAD_DIM**-0.5)
        for head in range(HEADS_DEV):
            spot = slice(head * WIDE, (head + 1) * WIDE)
            at = (HEADS_DEV + head) * WIDE
            dz[rows, at : at + WIDE] = (key_acc[rows, spot] * table).astype(BF16)
            at = (2 * HEADS_DEV + head) * WIDE
            dz[rows, at : at + WIDE] = value_acc[rows, spot].astype(BF16)

    def make(block):
        part[rows_of(block), :] = dot_nt(dz[rows_of(block), :], w_ref[...]).astype(BF16)

    def beside():
        wide_lanes = lax.broadcasted_iota(jnp.int32, (D, WIDE), 1)
        pieces = []
        for piece in range(3):
            spot = slice(piece * HEADS_DEV * WIDE, (piece + 1) * HEADS_DEV * WIDE)
            terms = dot_tn(a_ref[...], dz[:, spot])
            for head in range(HEADS_DEV):
                term = terms[:, head * WIDE : (head + 1) * WIDE]
                if piece < 2:
                    term = term + jnp.where(
                        wide_lanes < HEAD_DIM // 2,
                        pltpu.roll(term, HEAD_DIM // 2, 1),
                        -pltpu.roll(term, WIDE - HEAD_DIM // 2, 1),
                    )
                pieces.append(term)
        for pair in range(4):
            joined = jnp.where(
                wide_lanes < HEAD_DIM,
                pieces[2 * pair],
                pltpu.roll(pieces[2 * pair + 1], HEAD_DIM, 1),
            )
            dheads_ref[:, pair * WIDE : (pair + 1) * WIDE] = joined.astype(BF16)
        dheads_ref[:, 4 * WIDE : 5 * WIDE] = jnp.where(
            wide_lanes < HEAD_DIM, pieces[8], 0.0
        ).astype(BF16)

    normed_grad = reduce_rows(make, part, across_in, from_left, from_right, send_r, recv_r, beside)
    tokens = u_ref[...].astype(F32)
    scale_one = inverse_size(tokens)
    normal_one = tokens * scale_one
    gain_one_column = lax.dot_general(
        normed_grad * normal_one, ones, TN, precision=EXACT, preferred_element_type=F32
    )
    scaled_one = normed_grad * gains_ref[0:1, :]
    input_grad = input_ref[...] + scale_one * (
        scaled_one - normal_one * jnp.mean(scaled_one * normal_one, axis=1, keepdims=True)
    )
    input_ref[...] = input_grad
    small_lanes = lax.broadcasted_iota(jnp.int32, (D, LANES), 1)
    dheads_ref[:, D - LANES :] = jnp.where(
        small_lanes == EXPERTS,
        gain_one_column,
        jnp.where(small_lanes == EXPERTS + 1, gain_two_column, router_terms),
    ).astype(BF16)
    repack(dback_ref, dheads_ref, pack_ref)
    lower_ref[...] = input_grad.astype(BF16)


def attn_backward(length, *arrays):
    sems = pltpu.SemaphoreType.DMA
    out_shape = [
        jax.ShapeDtypeStruct((ROWS, D), F32),
        jax.ShapeDtypeStruct((16, ATTN_ROWS, UNIT), BF16),
        jax.ShapeDtypeStruct((ROWS, D), BF16),
    ]
    scratch = [
        pltpu.VMEM((D, D), BF16),
        pltpu.VMEM((D, D), BF16),
        pltpu.VMEM((SEQ, HEADS_DEV * WIDE), F32),
        pltpu.VMEM((SEQ, HEADS_DEV * WIDE), F32),
        pltpu.VMEM((SEQ, EXT), BF16),
        pltpu.VMEM((CTX, ROWS, COLS), BF16),
        pltpu.VMEM((CTX, ROWS, COLS), BF16),
        sems((CTX,)),
        sems((CTX,)),
    ] + REDUCE_SCRATCH
    return pl.pallas_call(
        attn_backward_kernel,
        out_shape=tuple(out_shape),
        in_specs=[SMEM] + [VMEM] * len(arrays),
        out_specs=[VMEM] * len(out_shape),
        scratch_shapes=scratch,
        compiler_params=params(3),
        name="attn_backward",
    )(length, *arrays)


GROUP = 4
GROUPS = 16 // GROUP
GROUP_UNITS = GROUP * LANES
SPLIT = EXPERT_ROWS // 2
ANY = pl.BlockSpec(memory_space=pl.ANY)
SUM_SCRATCH = [
    pltpu.VMEM((CTX, ROWS, D), BF16),
    pltpu.VMEM((HALF, D), BF16),
    pltpu.VMEM((HALF, D), BF16),
    pltpu.VMEM((ROWS, D), BF16),
    pltpu.VMEM((ROWS, D), BF16),
    SEMS((6,)),
    SEMS((6,)),
]


def weight_copies(w_ref, win, wout, sem):
    groups = []
    for group in range(GROUPS):
        shards = pl.ds(group * GROUP, GROUP)
        pairs = [
            (w_ref.at[0, shards], win.at[shards, pl.ds(0, SPLIT), :]),
            (w_ref.at[1, shards, pl.ds(0, D - SPLIT), :], win.at[shards, pl.ds(SPLIT, D - SPLIT), :]),
        ]
        for piece in range(D // UNIT):
            pairs.append(
                (
                    w_ref.at[1, shards, pl.ds(D - SPLIT + piece * LANES, LANES), :],
                    wout.at[shards, :, pl.ds(piece * UNIT, UNIT)],
                )
            )
        groups.append(
            [
                pltpu.make_async_copy(source, target, sem.at[group * 5 + index])
                for index, (source, target) in enumerate(pairs)
            ]
        )
    return groups


def wout_group(wout, group):
    return wout[group * GROUP : (group + 1) * GROUP].reshape(GROUP_UNITS, D)


def ffn_forward_kernel(
    b_own_ref, residual_ref, codes_ref, router_ref, w_ref,
    y_ref, b_ref, gates_ref, gate_ref, kept_ref,
    win, wout, kept_out, acc, w_sem, kept_sem, send_b, recv_b,
    part, top_in, bottom_in, from_left, from_right, send, recv,
):
    ring = Ring("x")
    greet_ids(ring.near())
    loads = weight_copies(w_ref, win, wout, w_sem)
    for group in loads:
        for copy in group:
            copy.start()
    b_ref[ring.me] = b_own_ref[...]
    met(2)
    halves = (pl.ds(0, HALF), pl.ds(HALF, HALF))
    rows = RingGather(ring, lambda b, h: b_ref.at[b, halves[h]], send_b, recv_b)
    rows.start()
    section = lax.axis_index("section")
    lanes = lax.broadcasted_iota(jnp.int32, (ROWS, LANES), 1)
    picker = jnp.where(lax.broadcasted_iota(jnp.int32, (8, LANES), 0) == section, 1.0, 0.0)
    stores = []

    def make(index, block):
        b_rows = b_ref[block]
        slot = index % 2
        for shard in range(16):
            if index == 0 and shard % GROUP == 0:
                for copy in loads[shard // GROUP]:
                    copy.wait()
            if index >= 2 and shard == 0:
                stores[index - 2].wait()
            hidden = dot(b_rows, win[shard])
            kept_out[slot, shard] = hidden.astype(BF16)
            gate_part = hidden[:, :LANES]
            at = shard % GROUP * LANES
            acc_act = (gate_part / (1.0 + jnp.exp(-gate_part)) * hidden[:, LANES:]).astype(BF16)
            if shard % GROUP == 0:
                acted = []
            acted.append(acc_act)
            if shard % GROUP == GROUP - 1:
                terms = dot(jnp.concatenate(acted, axis=1), wout_group(wout, shard // GROUP))
                acc[...] = terms if shard < GROUP else acc[...] + terms
        stores.append(pltpu.make_async_copy(kept_out.at[slot], kept_ref.at[block], kept_sem.at[slot]))
        stores[-1].start()
        logits = dot(b_rows, router_ref[...])
        codes = lax.dot_general(
            codes_ref[block], picker, TN, precision=EXACT, preferred_element_type=F32
        )
        named = (lanes < EXPERTS) & (lanes != jnp.round(codes).astype(jnp.int32))
        chosen = jnp.where(named, logits, MASK_VALUE)
        raw = jnp.where(named, jnp.exp(chosen - jnp.max(chosen, axis=1, keepdims=True)), 0.0)
        gates = raw / jnp.sum(raw, axis=1, keepdims=True)
        if index == 0:
            gates_ref[...] = gates
        gates = jnp.where(lanes == EXPERTS, 1.0, gates)
        gate = jnp.sum(jnp.where(lanes == ring.me, gates, 0.0), axis=1, keepdims=True)
        gate_ref[block] = gate
        part[block] = (acc[...] * gate).astype(BF16)

    order = {ring_index: number for number, ring_index in enumerate(("me", "right", "left", "across"))}

    def from_sum(position, block):
        make({0: order["across"], 1: order["right"], 2: order["left"], 3: order["me"]}[position], block)

    sums = RingSum(
        ring, part, (top_in, bottom_in), from_left, from_right, send, recv, HALF, from_sum
    )
    sums.stage(4)
    rows.forward()
    rows.near()
    sums.stage(1)
    sums.stage(2)
    rows.far()
    sums.stage(0)
    sums.stage(3)
    sums.stage(5)
    y_ref[...] = (residual_ref[...] + sums.total()).astype(BF16)
    rows.sent()
    stores[2].wait()
    stores[3].wait()


def ffn_forward(b_own, residual, codes, router, weights):
    return pl.pallas_call(
        ffn_forward_kernel,
        out_shape=(
            jax.ShapeDtypeStruct((ROWS, D), BF16),
            jax.ShapeDtypeStruct((CTX, ROWS, D), BF16),
            jax.ShapeDtypeStruct((ROWS, LANES), F32),
            jax.ShapeDtypeStruct((CTX, ROWS, 1), F32),
            jax.ShapeDtypeStruct((CTX, 16, ROWS, UNIT), BF16),
        ),
        in_specs=[VMEM] * 4 + [ANY],
        out_specs=[VMEM] * 4 + [ANY],
        scratch_shapes=[
            pltpu.VMEM((16, D, UNIT), BF16),
            pltpu.VMEM((16, LANES, D), BF16),
            pltpu.VMEM((2, 16, ROWS, UNIT), BF16),
            pltpu.VMEM((ROWS, D), F32),
            SEMS((5 * GROUPS,)),
            SEMS((2,)),
            SEMS((6,)),
            SEMS((6,)),
        ]
        + SUM_SCRATCH,
        compiler_params=params(5),
        name="ffn_forward",
    )(b_own, residual, codes, router, weights)


def ffn_backward_kernel(
    b_ref, gate_ref, delta_own_ref, kept_ref, w_ref, db_ref, gate_grad_ref, dw_ref,
    delta, acc, gate_acc, slot_grad, hidden, acted, win, wout, staged, rows_out, rows_in,
    w_sem, kept_sem, dw_sem, send_d, recv_d, send_g, recv_g,
    part, top_in, bottom_in, from_left, from_right, send, recv,
):
    ring = Ring("x")
    peers = (ring.right, ring.left, ring.across)
    greet_ids([ring.place(peer) for peer in peers])
    blocks = (ring.me, ring.right, ring.left, ring.across)
    kept_loads = [
        pltpu.make_async_copy(
            kept_ref.at[block], hidden.at[:, rows_of(block), :], kept_sem.at[index]
        )
        for index, block in enumerate(blocks)
    ]
    loads = weight_copies(w_ref, win, wout, w_sem)
    kept_loads[0].start()
    for group in loads:
        for copy in group:
            copy.start()
    for copy in kept_loads[1:]:
        copy.start()
    delta[ring.me] = delta_own_ref[...]
    met(3)
    halves = (pl.ds(0, HALF), pl.ds(HALF, HALF))
    rows = RingGather(ring, lambda b, h: delta.at[b, halves[h]], send_d, recv_d)
    rows.start()
    own_row = lax.broadcasted_iota(jnp.int32, (8, LANES), 0) == ring.me
    picker = jnp.where(own_row, 1.0, 0.0)
    handed = [
        ring.copy(rows_out.at[peer], rows_in.at[index], send_g.at[index], recv_g.at[index], peer)
        for index, peer in enumerate(peers)
    ]

    def make(index, block):
        kept_loads[index].wait()
        at = rows_of(block)
        gate = gate_ref[block]
        delta_rows = delta[block]
        slot_grad[at, :] = (delta_rows.astype(F32) * gate).astype(BF16)
        gate_sum = jnp.zeros((ROWS, LANES), F32)
        for group in range(GROUPS):
            if index == 0:
                for copy in loads[group]:
                    copy.wait()
            act_grad_all = dot_nt(delta_rows, wout_group(wout, group))
            second_grad = None
            for inner in range(GROUP):
                shard = group * GROUP + inner
                values = hidden[shard, at, :].astype(F32)
                gate_part = values[:, :LANES]
                up_part = values[:, LANES:]
                act_grad = act_grad_all[:, inner * LANES : (inner + 1) * LANES]
                sigmoid = 1.0 / (1.0 + jnp.exp(-gate_part))
                silu = gate_part * sigmoid
                act = (silu * up_part).astype(BF16)
                acted[at, shard * LANES : (shard + 1) * LANES] = act
                gate_sum += act.astype(F32) * act_grad
                act_grad = act_grad * gate
                gate_grad = act_grad * up_part * (sigmoid * (1.0 + gate_part * (1.0 - sigmoid)))
                pair = jnp.concatenate([gate_grad, act_grad * silu], axis=1).astype(BF16)
                hidden[shard, at, :] = pair
                term = dot_nt(pair, win[shard])
                second_grad = term if second_grad is None else second_grad + term
            acc[...] = second_grad if group == 0 else acc[...] + second_grad
        part[block] = acc[...].astype(BF16)
        rows_out[block] = lax.dot_general(
            picker, gate_sum, NT, precision=EXACT, preferred_element_type=F32
        )
        if index > 0:
            handed[index - 1].start()

    def from_sum(position, block):
        make((3, 1, 2, 0)[position], block)

    sums = RingSum(
        ring, part, (top_in, bottom_in), from_left, from_right, send, recv, HALF, from_sum
    )
    sums.stage(4)
    rows.forward()
    rows.near()
    sums.stage(1)
    sums.stage(2)
    rows.far()
    sums.stage(0)
    stores = []
    b_all = b_ref[...].reshape(SEQ, D)
    for group in range(GROUPS):
        slot = group % 2
        if group == 1:
            sums.stage(3)
        if group >= 2:
            stores[group - 2].wait()
        for inner in range(GROUP):
            staged[slot, inner, :D, :] = dot_tn(b_all, hidden[group * GROUP + inner]).astype(BF16)
        whole_out = dot_tn(
            acted[:, group * GROUP_UNITS : (group + 1) * GROUP_UNITS], slot_grad[...]
        ).astype(BF16)
        for inner in range(GROUP):
            for piece in range(D // UNIT):
                at = D + piece * LANES
                staged[slot, inner, at : at + LANES, :] = whole_out[
                    inner * LANES : (inner + 1) * LANES, piece * UNIT : (piece + 1) * UNIT
                ]
        stores.append(
            pltpu.make_async_copy(
                staged.at[slot], dw_ref.at[pl.ds(group * GROUP, GROUP)], dw_sem.at[slot]
            )
        )
        stores[-1].start()
    sums.stage(5)
    db_ref[...] = sums.total()
    for copy in handed:
        copy.wait()
    rows_all = rows_out[ring.me] + rows_in[0] + rows_in[1] + rows_in[2]
    diagonal = jnp.where(
        lax.broadcasted_iota(jnp.int32, (8, LANES), 0)
        == lax.broadcasted_iota(jnp.int32, (8, LANES), 1),
        1.0,
        0.0,
    )
    gate_grad_ref[...] = lax.dot_general(
        rows_all, diagonal, TN, precision=EXACT, preferred_element_type=F32
    )
    rows.sent()
    stores[2].wait()
    stores[3].wait()


def ffn_backward(b_all, gate_col, delta_own, kept, weights):
    return pl.pallas_call(
        ffn_backward_kernel,
        out_shape=(
            jax.ShapeDtypeStruct((ROWS, D), F32),
            jax.ShapeDtypeStruct((ROWS, LANES), F32),
            jax.ShapeDtypeStruct((16, EXPERT_ROWS, UNIT), BF16),
        ),
        in_specs=[VMEM] * 3 + [ANY] * 2,
        out_specs=[VMEM] * 2 + [ANY],
        scratch_shapes=[
            pltpu.VMEM((CTX, ROWS, D), BF16),
            pltpu.VMEM((ROWS, D), F32),
            pltpu.VMEM((8, LANES), F32),
            pltpu.VMEM((SEQ, D), BF16),
            pltpu.VMEM((16, SEQ, UNIT), BF16),
            pltpu.VMEM((SEQ, FFN), BF16),
            pltpu.VMEM((16, D, UNIT), BF16),
            pltpu.VMEM((16, LANES, D), BF16),
            pltpu.VMEM((2, GROUP, EXPERT_ROWS, UNIT), BF16),
            pltpu.VMEM((CTX, 8, ROWS), F32),
            pltpu.VMEM((3, 8, ROWS), F32),
            SEMS((5 * GROUPS,)),
            SEMS((CTX,)),
            SEMS((2,)),
            SEMS((6,)),
            SEMS((6,)),
            SEMS((3,)),
            SEMS((3,)),
        ]
        + SUM_SCRATCH,
        compiler_params=params(6),
        name="ffn_backward",
    )(b_all, gate_col, delta_own, kept, weights)


def rotary_table():
    half_dim = HEAD_DIM // 2
    frequency = jnp.exp(
        -jnp.log(10000.0) * (2.0 * jnp.arange(half_dim, dtype=F32) / HEAD_DIM)
    )
    angles = jnp.arange(SEQ, dtype=jnp.int32).astype(F32)[:, None] * frequency[None, :]
    cosine, sine = jnp.cos(angles), jnp.sin(angles)
    return jnp.concatenate([cosine, cosine, sine, sine], axis=1)


def layer_forward(weights, tokens_in, length, codes, table):
    pack, experts = weights
    a_all, qkv, mass, attended, residual, second, *unpacked = attn_forward(
        length, tokens_in, pack, table
    )
    output, b_all, gates, gate_col, kept = ffn_forward(
        second, residual, codes, unpacked[1], experts
    )
    return output, (
        tokens_in, a_all, qkv, mass, attended, residual, second, b_all, gates, gate_col, kept, unpacked,
    )


def layer_backward(weights, saved, delta_own, length, table):
    _, experts = weights
    (
        tokens_in, a_all, qkv, mass, attended, residual, second, b_all, gates, gate_col, kept, unpacked,
    ) = saved
    db, gate_grads, dexperts = ffn_backward(b_all, gate_col, delta_own, kept, experts)
    return dexperts, attn_backward(
        length, tokens_in, *unpacked, table, a_all, qkv, mass,
        attended, residual, second, gates, delta_own, db, gate_grads,
    )


def adam_update(gradient, clipped, master, mean_old, square_old, step_value, learn_rate):
    mean_new = BETA_ONE * mean_old + (1.0 - BETA_ONE) * clipped
    square_new = BETA_TWO * square_old + (1.0 - BETA_TWO) * clipped * clipped
    fix_one = 1.0 - BETA_ONE**step_value
    fix_two = 1.0 - BETA_TWO**step_value
    master_new = master - learn_rate * (
        mean_new / fix_one / (jnp.sqrt(square_new / fix_two) + ADAM_EPS) + DECAY_RATE * master
    )
    return (gradient, mean_new, square_new, master_new, master_new.astype(BF16))


def factor_of(squares_ref, index):
    return jnp.minimum(1.0, CLIP_LIMIT / jnp.sqrt(squares_ref[0:1, index : index + 1]))


def updated(fixes_ref, gradient, factor, old, new, learn_rate, at=...):
    master_ref, mean_ref, square_ref = old
    gradient_ref, mean_new_ref, square_new_ref, master_new_ref, copy_ref = new
    clipped = gradient * factor
    master = master_ref[at]
    mean_new = BETA_ONE * mean_ref[at] + (1.0 - BETA_ONE) * clipped
    square_new = BETA_TWO * square_ref[at] + (1.0 - BETA_TWO) * clipped * clipped
    master_new = master - learn_rate * (
        mean_new / fixes_ref[0] / (jnp.sqrt(square_new / fixes_ref[1]) + ADAM_EPS) + DECAY_RATE * master
    )
    gradient_ref[at] = gradient
    mean_new_ref[at] = mean_new
    square_new_ref[at] = square_new
    master_new_ref[at] = master_new
    copy_ref[at] = master_new.astype(BF16)


def update_kernel(
    fixes_ref, squares_ref, in_sum_ref, out_sum_ref, attn_sum_ref, *refs,
):
    in_old, out_old, attn_old = refs[0:3], refs[3:6], refs[6:9]
    in_new, out_new, attn_new = refs[9:14], refs[14:19], refs[19:24]
    small_ref, turned, wide = refs[24:]
    turned[pl.ds(0, D, 2), :] = in_sum_ref[0, :, :LANES].astype(F32)
    turned[pl.ds(1, D, 2), :] = in_sum_ref[0, :, LANES:].astype(F32)
    updated(
        fixes_ref, turned[...], factor_of(squares_ref, 3), in_old, in_new, RATE_FACTOR / D**0.5
    )
    pieces = [
        out_sum_ref[0, piece * LANES : (piece + 1) * LANES, :].astype(F32)
        for piece in range(D // UNIT)
    ]
    updated(
        fixes_ref,
        jnp.concatenate(pieces, axis=1),
        factor_of(squares_ref, 4),
        out_old,
        out_new,
        RATE_FACTOR / FFN**0.5,
        0,
    )

    @pl.when(pl.program_id(0) == 0)
    def _():
        back = [jnp.zeros((48, UNIT), F32) for _ in range(3)]
        small = jnp.zeros((48, UNIT), F32)
        for block in range(CTX):
            rows = [
                attn_sum_ref[block, piece * 48 : (piece + 1) * 48, :].astype(F32) for piece in range(6)
            ]
            back = [left + right for left, right in zip(back, rows[:3])]
            small = small + rows[5]
            heads = jnp.concatenate(rows[3:], axis=1)
            for part in range(3):
                at = part * D + block * COLS
                wide[:, at : at + COLS] = heads[:, part * COLS : (part + 1) * COLS]
        wide[:, 3 * D :] = jnp.concatenate(back, axis=1)
        small_ref[...] = small[:, LANES:]
        for part in range(4):
            lanes = (slice(None), slice(part * D, (part + 1) * D))
            updated(
                fixes_ref,
                wide[lanes],
                factor_of(squares_ref, 1),
                attn_old,
                attn_new,
                RATE_FACTOR / D**0.5,
                lanes,
            )


def update(fixes, squares, sums_all, in_old, out_old, attn_old):
    in_rows, units = 2 * D, LANES
    in_shape, out_shape, attn_shape = (CTX * in_rows, units), (CTX, units, D), (48, 4 * D)
    in_spec = pl.BlockSpec((in_rows, units), lambda i: (i, 0))
    out_spec = pl.BlockSpec((1, units, D), lambda i: (i, 0, 0))
    attn_spec = whole(attn_shape)

    def five(shape):
        return [jax.ShapeDtypeStruct(shape, F32)] * 4 + [jax.ShapeDtypeStruct(shape, BF16)]

    return pl.pallas_call(
        update_kernel,
        grid=(CTX,),
        out_shape=five(in_shape)
        + five(out_shape)
        + five(attn_shape)
        + [jax.ShapeDtypeStruct((48, LANES), F32)],
        in_specs=[
            SMEM,
            whole((8, LANES)),
            pl.BlockSpec((1, D, UNIT), lambda i: (i, 0, 0)),
            pl.BlockSpec((1, D // 2, UNIT), lambda i: (i, 2, 0)),
            pl.BlockSpec((CTX, ATTN_ROWS, UNIT), lambda i: (0, EXPERT_ROWS // ATTN_ROWS, 0)),
        ]
        + [in_spec] * 3
        + [out_spec] * 3
        + [attn_spec] * 3,
        out_specs=[in_spec] * 5 + [out_spec] * 5 + [attn_spec] * 5 + [whole((48, LANES))],
        scratch_shapes=[pltpu.VMEM((in_rows, units), F32), pltpu.VMEM(attn_shape, F32)],
        compiler_params=pltpu.CompilerParams(vmem_limit_bytes=VMEM_LIMIT),
        name="update",
    )(
        fixes, squares, sums_all, sums_all, sums_all,
        *(array.reshape(in_shape) for array in in_old),
        *(array.reshape(out_shape) for array in out_old),
        *(array.reshape(attn_shape) for array in attn_old),
    )


def on_device(
    inputs, cotangent, lengths, routes, step_count,
    norm_gains, gains_mean, gains_square,
    attn_weight, attn_mean, attn_square,
    router_weight, router_mean, router_square,
    expert_in, in_mean, in_square,
    expert_out, out_mean, out_square,
):
    section = lax.axis_index("section")
    ctx_index = lax.axis_index("ctx")
    fsdp = lax.axis_size("fsdp")
    everyone = ("section", "fsdp")
    shard_rows = attn_weight.shape[1]
    units = expert_in.shape[4]
    first_core = section == 0

    def own_columns(matrix, part):
        return lax.dynamic_slice_in_dim(matrix, part * D + ctx_index * COLS, COLS, 1)

    def swap(block):
        return lax.ppermute(block, "section", [(0, 1), (1, 0)])

    attn_shard = jnp.concatenate(
        [attn_weight[0][:, 3 * D :]]
        + [own_columns(attn_weight[0], part) for part in range(3)]
        + [jnp.zeros((shard_rows, HEAD_DIM), F32), router_weight[0], norm_gains[0].T]
        + [jnp.zeros((shard_rows, LANES - EXPERTS - 2), F32)],
        axis=1,
    ).astype(BF16)
    attn_shard = attn_shard.reshape(shard_rows, 6, UNIT).transpose(1, 0, 2).reshape(-1, UNIT)
    left_out = (3 - routes[0, :, :, 0] - routes[0, :, :, 1]).astype(F32)
    packs, codes = gather_shards(attn_shard, jnp.pad(left_out, ((0, 8 - left_out.shape[0]), (0, 0))))
    packs = packs.reshape(2, fsdp, ATTN_ROWS, UNIT)
    in_shard = (
        lax.dynamic_index_in_dim(expert_in[0], ctx_index, 0, keepdims=False)
        .astype(BF16)
        .reshape(D, 2 * units)
    )
    out_shard = lax.dynamic_index_in_dim(expert_out[0], ctx_index, 0, keepdims=False).astype(BF16)
    halves = jnp.concatenate(
        [in_shard] + [out_shard[:, at : at + 2 * units] for at in range(0, D, 2 * units)], axis=0
    ).reshape(2, SPLIT, 2 * units)
    other = swap(jnp.where(first_core, halves[1], halves[0]))
    pieces = (jnp.where(first_core, halves[0], other), jnp.where(first_core, other, halves[1]))
    experts = [
        lax.all_gather(piece, everyone).reshape(2, fsdp, SPLIT, 2 * units) for piece in pieces
    ]
    length = lax.dynamic_slice_in_dim(lengths, section, 1, 0)
    tokens = lax.dynamic_index_in_dim(inputs, section, 0, keepdims=False)
    positions = ctx_index * ROWS + jnp.arange(ROWS, dtype=jnp.int32)
    seed = lax.dynamic_index_in_dim(cotangent, section, 0, keepdims=False)
    seed = jnp.where((positions < length[0])[:, None], seed, jnp.zeros_like(seed))
    table = rotary_table()

    layers = [(packs[layer], experts[layer]) for layer in range(2)]
    lower_out, lower_saved = layer_forward(layers[0], tokens, length, codes[0], table)
    upper_out, upper_saved = layer_forward(layers[1], lower_out, length, codes[1], table)

    upper_experts, (upper_grad, upper_attn, lower_seed) = layer_backward(
        layers[1], upper_saved, seed, length, table
    )
    lower_experts, (lower_grad, lower_attn, _) = layer_backward(
        layers[0], lower_saved, lower_seed, length, table
    )

    def paired(first, second):
        kept = jnp.where(first_core, first, second)
        other = swap(jnp.where(first_core, second, first))
        return jnp.stack(
            [jnp.where(first_core, kept, other), jnp.where(first_core, other, kept)]
        )

    layer_outputs = paired(lower_out, upper_out)[None]
    input_grads = paired(lower_grad, upper_grad)[None]
    shard_sum = sum_shards(lower_experts, lower_attn, upper_experts, upper_attn)
    sums_all, squares = spread_sums(shard_sum)
    step_value = step_count[0].astype(F32)
    fixes = jnp.stack([1.0 - BETA_ONE**step_value, 1.0 - BETA_TWO**step_value])
    changed = update(
        fixes,
        squares,
        sums_all,
        (expert_in, in_mean, in_square),
        (expert_out, out_mean, out_square),
        (attn_weight, attn_mean, attn_square),
    )
    small_sum = changed[15]
    norms = jnp.sqrt(squares[0, :5])
    factors = jnp.minimum(1.0, CLIP_LIMIT / norms)
    router_sum = small_sum[:, :EXPERTS][None]
    gain_sum = small_sum[:, EXPERTS : EXPERTS + 2].T[None]
    gains_new = adam_update(
        gain_sum, gain_sum * factors[0], norm_gains, gains_mean, gains_square, step_value, GAIN_RATE
    )
    router_new = adam_update(
        router_sum,
        router_sum * factors[2],
        router_weight,
        router_mean,
        router_square,
        step_value,
        RATE_FACTOR / (D // 4) ** 0.5,
    )
    return (
        (layer_outputs, input_grads)
        + gains_new
        + tuple(array.reshape(attn_weight.shape) for array in changed[10:15])
        + router_new
        + tuple(array.reshape(expert_in.shape) for array in changed[:5])
        + tuple(array.reshape(expert_out.shape) for array in changed[5:10])
        + (norms[None],)
    )


def solution(mesh):
    gains = P("section", None, "fsdp")
    rows = P("section", "fsdp", None)
    wide = P("section", None, None, None, "fsdp")
    down = P("section", None, "fsdp", None)
    tokens = P("section", "fsdp", "ctx", None)
    return jax.shard_map(
        on_device,
        mesh=mesh,
        in_specs=(
            P("fsdp", "ctx", None),
            P("fsdp", "ctx", None),
            P("fsdp"),
            tokens,
            P(),
        )
        + (gains,) * 3
        + (rows,) * 6
        + (wide,) * 3
        + (down,) * 3,
        out_specs=(tokens, tokens)
        + (gains,) * 5
        + (rows,) * 10
        + (wide,) * 5
        + (down,) * 5
        + (P("section", None),),
        check_vma=False,
    )
```

```python
import functools

import jax
import jax.numpy as jnp
import numpy as np
from jax import lax
from jax.experimental import pallas as pl
from jax.experimental.pallas import tpu as pltpu
from jax.sharding import PartitionSpec as P

D = 768
HEADS = 12
HEAD_DIM = 64
FFN = 2048
EXPERTS = 3
ROWS = 256
CTX = 4
SEQ = ROWS * CTX
HEADS_DEV = HEADS // CTX
WIDE = 128
EXT = 3 * HEADS_DEV * WIDE
COLS = HEADS_DEV * HEAD_DIM

EPS_NORM = 1e-06
BETA_ONE = 0.9
BETA_TWO = 0.95
RATE_FACTOR = 3.0
GAIN_RATE = 0.3
DECAY_RATE = 0.1
ADAM_EPS = 1e-08
CLIP_LIMIT = 1.0
MASK_VALUE = -1e30
SCORE_SCALE = HEAD_DIM ** (-0.5) / 2.0
BF16 = jnp.bfloat16
F32 = jnp.float32
VMEM_LIMIT = 56 * 1024 * 1024
NT = (((1,), (1,)), ((), ()))
TN = (((0,), (0,)), ((), ()))
HALF = ROWS // 2
LANES = 128
MESH = pl.DeviceIdType.MESH
EXACT = lax.Precision.HIGHEST


def dot(left, right):
    return jnp.dot(left, right, preferred_element_type=F32)


def dot_nt(left, right):
    return lax.dot_general(left, right, NT, preferred_element_type=F32)


def dot_tn(left, right):
    return lax.dot_general(left, right, TN, preferred_element_type=F32)


def params(collective_id):
    return pltpu.CompilerParams(
        vmem_limit_bytes=VMEM_LIMIT, collective_id=collective_id, has_side_effects=True
    )


def whole(shape):
    return pl.BlockSpec(shape, lambda *_: (0,) * len(shape))


def allowed_keys(block, keys, length):
    key_pos = lax.broadcasted_iota(jnp.int32, (ROWS, keys), 1)
    query_pos = lax.broadcasted_iota(jnp.int32, (ROWS, keys), 0) + block * ROWS
    return (key_pos <= query_pos) & (key_pos < length)


VMEM = pl.BlockSpec(memory_space=pltpu.VMEM)
SMEM = pl.BlockSpec(memory_space=pltpu.SMEM)
ANY = pl.BlockSpec(memory_space=pl.ANY)


def ring():
    me = lax.axis_index("ctx")
    return me, lax.rem(me + 1, CTX), lax.rem(me + 3, CTX), lax.rem(me + 2, CTX)


def greet(peers):
    barrier = pltpu.get_barrier_semaphore()
    for peer in peers:
        pl.semaphore_signal(barrier, inc=1, device_id={"ctx": peer}, device_id_type=MESH)


def met(count):
    pl.semaphore_wait(pltpu.get_barrier_semaphore(), count)


def remote(source, target, send, recv, peer):
    return pltpu.make_async_remote_copy(
        src_ref=source,
        dst_ref=target,
        send_sem=send,
        recv_sem=recv,
        device_id={"ctx": peer},
        device_id_type=MESH,
    )


def rows_of(block, half=None):
    if half is None:
        return pl.ds(pl.multiple_of(block * ROWS, ROWS), ROWS)
    return pl.ds(pl.multiple_of(block * ROWS + half * HALF, HALF), HALF)


def gather_rows(all_ref, send, recv, beside=None):
    me, right, left, _ = ring()

    def piece(index, block, half, peer):
        spot = all_ref.at[rows_of(block, half)]
        return remote(spot, spot, send.at[index], recv.at[index], peer)

    copies = [
        piece(0, me, 0, right),
        piece(1, me, 1, left),
        piece(2, me, 1, right),
        piece(3, me, 0, left),
    ]
    for copy in copies:
        copy.start()
    if beside is not None:
        beside()
    copies[0].wait_recv()
    copies.append(piece(4, left, 0, right))
    copies[4].start()
    copies[1].wait_recv()
    copies.append(piece(5, right, 1, left))
    copies[5].start()
    for index in range(2, 6):
        copies[index].wait_recv()
    for copy in copies:
        copy.wait_send()


def reduce_rows(make, part, across_in, from_left, from_right, send, recv, beside=None):
    me, right, left, across = ring()
    top, bottom = pl.ds(0, HALF), pl.ds(HALF, HALF)

    def piece(index, block, half, target, peer):
        return remote(part.at[rows_of(block, half)], target, send.at[index], recv.at[index], peer)

    make(across)
    copies = [
        piece(0, across, 0, across_in.at[0], right),
        piece(1, across, 1, across_in.at[1], left),
    ]
    copies[0].start()
    copies[1].start()
    make(right)
    copies.append(piece(2, right, 1, from_left.at[bottom], right))
    copies[2].start()
    make(left)
    copies.append(piece(3, left, 0, from_right.at[top], left))
    copies[3].start()
    copies[0].wait_recv()
    spot = rows_of(right, 0)
    part[spot, :] = (part[spot, :].astype(F32) + across_in[0].astype(F32)).astype(BF16)
    copies.append(piece(4, right, 0, from_left.at[top], right))
    copies[4].start()
    copies[1].wait_recv()
    spot = rows_of(left, 1)
    part[spot, :] = (part[spot, :].astype(F32) + across_in[1].astype(F32)).astype(BF16)
    copies.append(piece(5, left, 1, from_right.at[bottom], left))
    copies[5].start()
    make(me)
    if beside is not None:
        beside()
    for index in range(2, 6):
        copies[index].wait_recv()
    for copy in copies:
        copy.wait_send()
    return (
        part[rows_of(me), :].astype(F32) + from_left[...].astype(F32) + from_right[...].astype(F32)
    )


REDUCE_SCRATCH = [
    pltpu.VMEM((SEQ, D), BF16),
    pltpu.VMEM((2, HALF, D), BF16),
    pltpu.VMEM((ROWS, D), BF16),
    pltpu.VMEM((ROWS, D), BF16),
    pltpu.SemaphoreType.DMA((6,)),
    pltpu.SemaphoreType.DMA((6,)),
]


def greet_ids(peers):
    barrier = pltpu.get_barrier_semaphore()
    for peer in peers:
        pl.semaphore_signal(barrier, inc=1, device_id=peer, device_id_type=MESH)


class Ring:
    def __init__(self, axis):
        if axis == "x":
            self.me = lax.axis_index("ctx")
            self.place = lambda index: {"ctx": index}
        else:
            shard = lax.axis_index("fsdp")
            inner, outer = lax.rem(shard, CTX), lax.div(shard, CTX)
            if axis == "y":
                self.me = inner
                self.place = lambda index: {"fsdp": outer * CTX + index}
            else:
                self.me = outer
                self.place = lambda index: {"fsdp": index * CTX + inner}
        self.right = lax.rem(self.me + 1, CTX)
        self.left = lax.rem(self.me + 3, CTX)
        self.across = lax.rem(self.me + 2, CTX)

    def order(self):
        return (self.across, self.right, self.left, self.me)

    def near(self):
        return [self.place(self.right), self.place(self.left)]

    def copy(self, source, target, send, recv, index):
        return pltpu.make_async_remote_copy(
            src_ref=source,
            dst_ref=target,
            send_sem=send,
            recv_sem=recv,
            device_id=self.place(index),
            device_id_type=MESH,
        )


class RingGather:
    def __init__(self, ring, at, send, recv):
        self.ring, self.at, self.send, self.recv = ring, at, send, recv
        self.copies = []

    def go(self, block, half, to):
        spot = self.at(block, half)
        index = len(self.copies)
        self.copies.append(
            self.ring.copy(spot, spot, self.send.at[index], self.recv.at[index], to)
        )
        self.copies[-1].start()

    def start(self):
        ring = self.ring
        self.go(ring.me, 0, ring.right)
        self.go(ring.me, 1, ring.left)
        self.go(ring.me, 1, ring.right)
        self.go(ring.me, 0, ring.left)

    def forward(self):
        ring = self.ring
        spot = self.at(ring.left, 0)
        ring.copy(spot, spot, self.send.at[0], self.recv.at[0], ring.right).wait_recv()
        self.go(ring.left, 0, ring.right)
        spot = self.at(ring.right, 1)
        ring.copy(spot, spot, self.send.at[1], self.recv.at[1], ring.left).wait_recv()
        self.go(ring.right, 1, ring.left)

    def landed(self, index, block, half):
        spot = self.at(block, half)
        self.ring.copy(
            spot, spot, self.send.at[index], self.recv.at[index], self.ring.right
        ).wait_recv()

    def near(self):
        self.landed(2, self.ring.left, 1)
        self.landed(3, self.ring.right, 0)

    def far(self):
        self.landed(4, self.ring.across, 0)
        self.landed(5, self.ring.across, 1)

    def sent(self):
        for copy in self.copies:
            copy.wait_send()

    def finish(self):
        self.near()
        self.far()
        self.sent()


class RingSum:
    def __init__(self, ring, part, across_in, from_left, from_right, send, recv, cut, make):
        self.ring, self.part, self.across_in = ring, part, across_in
        self.from_left, self.from_right, self.send, self.recv = from_left, from_right, send, recv
        size = part.shape[1]
        self.halves = (pl.ds(0, cut), pl.ds(cut, size - cut))
        self.make = make
        self.copies = {}

    def go(self, index, block, half, target, to):
        self.copies[index] = self.ring.copy(
            self.part.at[block, self.halves[half]], target, self.send.at[index], self.recv.at[index], to
        )
        self.copies[index].start()

    def arrived(self, half, block):
        self.copies[half].wait_recv()
        incoming = self.across_in[half]
        if len(self.part.shape) == 3:
            spot = (block, self.halves[half])
            self.part[spot] = (self.part[spot].astype(F32) + incoming[...].astype(F32)).astype(BF16)
            return
        start = (0, self.part.shape[1] - incoming.shape[0])[half]
        for index in range(incoming.shape[0]):
            self.part[block, start + index] = (
                self.part[block, start + index].astype(F32) + incoming[index].astype(F32)
            ).astype(BF16)

    def stage(self, number):
        ring = self.ring
        if number == 0:
            self.make(0, ring.across)
            self.go(0, ring.across, 0, self.across_in[0], ring.right)
            self.go(1, ring.across, 1, self.across_in[1], ring.left)
        elif number == 1:
            self.make(1, ring.right)
            self.go(2, ring.right, 1, self.from_left.at[self.halves[1]], ring.right)
        elif number == 2:
            self.make(2, ring.left)
            self.go(3, ring.left, 0, self.from_right.at[self.halves[0]], ring.left)
        elif number == 3:
            self.arrived(0, ring.right)
            self.go(4, ring.right, 0, self.from_left.at[self.halves[0]], ring.right)
            self.arrived(1, ring.left)
            self.go(5, ring.left, 1, self.from_right.at[self.halves[1]], ring.left)
        elif number == 4:
            self.make(3, ring.me)
        else:
            for index in range(2, 6):
                self.copies[index].wait_recv()
            for index in range(6):
                self.copies[index].wait_send()

    def total(self, index=None):
        spot = (self.ring.me,) if index is None else (self.ring.me, index)
        tail = () if index is None else (index,)
        return (
            self.part[spot].astype(F32)
            + self.from_left[tail or ...].astype(F32)
            + self.from_right[tail or ...].astype(F32)
        )


UNIT = 256
EXPERT_ROWS = D + D // 2
ATTN_ROWS = 288
SHARD_ROWS = EXPERT_ROWS + ATTN_ROWS
FIRST = SHARD_ROWS // 2
KEPT = EXPERT_ROWS - FIRST
CUT = 352
SEMS = pltpu.SemaphoreType.DMA


def gather_shards_kernel(shard_ref, code_ref, out_ref, codes_ref, *sems):
    section = lax.axis_index("section")
    sibling = {"section": 1 - section}
    ring_y, ring_z = Ring("y"), Ring("z")
    y, z = ring_y.me, ring_z.me
    ring_x = Ring("x")
    x_peers = (ring_x.right, ring_x.left, ring_x.across)
    greet_ids(
        [sibling] + ring_y.near() + ring_z.near() + [ring_x.place(peer) for peer in x_peers]
    )
    out_ref[section, z, y] = shard_ref[...]
    codes_ref[section, ring_x.me] = code_ref[...]
    met(8)
    spot = codes_ref.at[section, ring_x.me]
    code_copies = [
        ring_x.copy(spot, spot, sems[10].at[index], sems[11].at[index], peer)
        for index, peer in enumerate(x_peers)
    ]
    for copy in code_copies:
        copy.start()
    half = ATTN_ROWS // 2
    low = (pl.ds(0, 64), pl.ds(64, half - 64))
    high = (pl.ds(half, 64), pl.ds(half + 64, half - 64))
    pair = (pl.ds(0, 2), pl.ds(2, 2))
    near_y = RingGather(ring_y, lambda b, h: out_ref.at[section, z, b, low[h]], sems[0], sems[1])
    near_z = RingGather(ring_z, lambda b, h: out_ref.at[section, b, y, high[h]], sems[2], sems[3])
    far_z = RingGather(
        ring_z, lambda b, h: out_ref.at[section, b, pair[h], pl.ds(0, half)], sems[4], sems[5]
    )
    far_y = RingGather(
        ring_y, lambda b, h: out_ref.at[section, pair[h], b, pl.ds(half, half)], sems[6], sems[7]
    )
    for rings in ((near_y, near_z), (far_z, far_y)):
        for one in rings:
            one.start()
        for one in rings:
            one.forward()
        for one in rings:
            one.finish()
    across = pltpu.make_async_remote_copy(
        src_ref=out_ref.at[section],
        dst_ref=out_ref.at[section],
        send_sem=sems[8],
        recv_sem=sems[9],
        device_id=sibling,
        device_id_type=MESH,
    )
    across.start()
    for copy in code_copies:
        copy.wait()
    codes_across = pltpu.make_async_remote_copy(
        src_ref=codes_ref.at[section],
        dst_ref=codes_ref.at[section],
        send_sem=sems[12],
        recv_sem=sems[13],
        device_id=sibling,
        device_id_type=MESH,
    )
    codes_across.start()
    codes_across.wait()
    across.wait()


def gather_shards(shard, codes):
    return pl.pallas_call(
        gather_shards_kernel,
        out_shape=(
            jax.ShapeDtypeStruct((2, CTX, CTX, ATTN_ROWS, UNIT), BF16),
            jax.ShapeDtypeStruct((2, CTX, 8, ROWS), F32),
        ),
        in_specs=[VMEM, VMEM],
        out_specs=[VMEM, VMEM],
        scratch_shapes=[SEMS((6,))] * 8 + [SEMS, SEMS, SEMS((3,)), SEMS((3,)), SEMS, SEMS],
        compiler_params=params(7),
        name="gather_shards",
    )(shard, codes)


HALF_SHARD = SHARD_ROWS // 2
Y_ROWS, Z_ROWS = 352, 368
Z_CUT = Z_ROWS - ATTN_ROWS


def half_sources(half, experts, attn):
    if half == 0:
        return (
            experts.at[:, :, pl.ds(0, Y_ROWS), :],
            experts.at[:, :, pl.ds(Y_ROWS, Z_CUT), :],
            experts.at[:, :, pl.ds(Y_ROWS + Z_CUT, ATTN_ROWS), :],
        )
    return (
        experts.at[:, :, pl.ds(HALF_SHARD, Y_ROWS), :],
        experts.at[:, :, pl.ds(HALF_SHARD + Y_ROWS, Z_CUT), :],
        attn,
    )


class HalfSums:
    def __init__(self, refs, sems, make_y, make_z):
        (
            self.part_y, self.part_z, top_y, bottom_y, left_y, right_y, top_z, bottom_z, left_z, right_z,
            more_z, more_y, top_zz, bottom_zz, left_zz, right_zz, top_yy, bottom_yy, left_yy, right_yy,
        ) = refs
        ring_y, ring_z = Ring("y"), Ring("z")
        self.ring_y, self.ring_z = ring_y, ring_z
        self.first_y = RingSum(
            ring_y, self.part_y, (top_y, bottom_y), left_y, right_y, sems[0], sems[1], 2, make_y
        )
        self.first_z = RingSum(
            ring_z, self.part_z, (top_z, bottom_z), left_z, right_z, sems[2], sems[3], 2, make_z
        )

        def make_zz(index, block):
            more_z[block] = self.first_y.total(block).astype(BF16)

        def make_yy(index, block):
            more_y[block] = self.first_z.total(block).astype(BF16)

        self.then_z = RingSum(
            ring_z, more_z, (top_zz, bottom_zz), left_zz, right_zz, sems[4], sems[5], Y_ROWS // 2, make_zz
        )
        self.then_y = RingSum(
            ring_y, more_y, (top_yy, bottom_yy), left_yy, right_yy, sems[6], sems[7], 176, make_yy
        )

    def first(self, number):
        self.first_y.stage(number)
        self.first_z.stage(number)

    def then(self, number):
        self.then_z.stage(number)
        self.then_y.stage(number)

    def result(self, out_ref):
        out_ref[pl.ds(0, Y_ROWS), :] = self.then_z.total().astype(BF16)
        out_ref[pl.ds(Y_ROWS, Z_ROWS), :] = self.then_y.total().astype(BF16)


def half_scratch():
    shapes = [(CTX, CTX, Y_ROWS, UNIT), (CTX, CTX, Z_ROWS, UNIT)]
    for rows in (Y_ROWS, Z_ROWS):
        shapes += [(2, rows, UNIT)] * 2 + [(CTX, rows, UNIT)] * 2
    shapes += [(CTX, Y_ROWS, UNIT), (CTX, Z_ROWS, UNIT)]
    for rows in (Y_ROWS, Z_ROWS):
        shapes += [(176, UNIT), (rows - 176, UNIT)] + [(rows, UNIT)] * 2
    return [pltpu.VMEM(shape, BF16) for shape in shapes]


HALF_REFS = 20


def add_block(part, incoming, block):
    for other in range(CTX):
        part[block, other] = (part[block, other].astype(F32) + incoming[block, other].astype(F32)).astype(
            BF16
        )


def sum_shards_kernel(
    experts, attn, upper_half_ref, lower_out_ref, upper_out_ref, lower_grad_ref, upper_grad_ref,
    out_ref, outputs_ref, grads_ref, *rest,
):
    halves, rest = rest[:HALF_REFS], rest[HALF_REFS:]
    in_y, in_z, sent_out, sent_grad, local, send_s, recv_s, send_w, recv_w = rest[:9]
    section = lax.axis_index("section")
    sibling = {"section": 1 - section}
    first_core = section == 0
    part_y, part_z = halves[:2]

    def make_y(index, block):
        ready(index, 0)
        add_block(part_y, in_y, block)

    def make_z(index, block):
        ready(index, 1)
        ready(index, 2)
        add_block(part_z, in_z, block)

    sums = HalfSums(halves, rest[9:], make_y, make_z)
    ring_y, ring_z = sums.ring_y, sums.ring_z
    greet_ids([sibling] + ring_y.near() + ring_z.near())

    def pieces(index, half, target_y, target_z):
        b_y, b_z = ring_y.order()[index], ring_z.order()[index]
        sources = half_sources(half, experts, attn)
        return (
            (sources[0].at[:, b_y], target_y.at[b_y]),
            (sources[1].at[b_z], target_z.at[b_z, :, pl.ds(0, Z_CUT), :]),
            (sources[2].at[b_z], target_z.at[b_z, :, pl.ds(Z_CUT, ATTN_ROWS), :]),
        )

    def fetch(index, number, source, target):
        return pltpu.make_async_copy(source, target, local.at[index * 3 + number])

    def pass_on(source, target, send, recv):
        return pltpu.make_async_remote_copy(
            src_ref=source,
            dst_ref=target,
            send_sem=send,
            recv_sem=recv,
            device_id=sibling,
            device_id_type=MESH,
        )

    def lend(index, number, source, target):
        at = index * 3 + number
        return pass_on(source, target, send_s.at[at], recv_s.at[at])

    def ready(index, number):
        source, target = pieces(index, 0, part_y, part_z)[number]
        fetch(index, number, source, target).wait()
        source, target = pieces(index, 0, in_y, in_z)[number]
        lend(index, number, source, target).wait_recv()

    def start(kept):
        for index in range(CTX):
            for number, pair in enumerate(pieces(index, kept, part_y, part_z)):
                fetch(index, number, *pair).start()

    def hand(given):
        for index in range(CTX):
            for number, pair in enumerate(pieces(index, given, in_y, in_z)):
                lend(index, number, *pair).start()

    for core in range(2):

        @pl.when(section == core)
        def _():
            start(core)

    met(5)
    for core in range(2):

        @pl.when(section == core)
        def _():
            hand(1 - core)

    lower_out, upper_out = lower_out_ref[...], upper_out_ref[...]
    outputs_ref[section] = jnp.where(first_core, lower_out, upper_out)
    sent_out[...] = jnp.where(first_core, upper_out, lower_out)
    lower_grad, upper_grad = lower_grad_ref[...], upper_grad_ref[...]
    grads_ref[section] = jnp.where(first_core, lower_grad, upper_grad)
    sent_grad[...] = jnp.where(first_core, upper_grad, lower_grad)
    swaps = [
        pass_on(sent_out, outputs_ref.at[section], send_w.at[0], recv_w.at[0]),
        pass_on(sent_grad, grads_ref.at[section], send_w.at[1], recv_w.at[1]),
    ]
    for number in range(3):
        sums.first(number)
    for copy in swaps:
        copy.start()
    for number in range(3, 6):
        sums.first(number)
    for number in range(6):
        sums.then(number)
    own = out_ref.at[pl.ds(pl.multiple_of(section * HALF_SHARD, HALF_SHARD), HALF_SHARD)]

    @pl.when(first_core)
    def _():
        sums.result(own)
        copy = pass_on(upper_half_ref, own, send_w.at[2], recv_w.at[2])
        copy.start()
        copy.wait()

    @pl.when(section == 1)
    def _():
        sums.result(sent_half := rest[8 + 9])
        own[...] = upper_half_ref[...]
        copy = pass_on(sent_half, own, send_w.at[2], recv_w.at[2])
        copy.start()
        copy.wait()

    for copy in swaps:
        copy.wait()
    for index in range(CTX):
        for number, pair in enumerate(pieces(index, 0, in_y, in_z)):
            lend(index, number, *pair).wait_send()


def by_place(array):
    return array.reshape((CTX, CTX) + array.shape[1:])


def sum_shards(lower_e, lower_a, upper_half, lower_out, upper_out, lower_grad, upper_grad):
    return pl.pallas_call(
        sum_shards_kernel,
        out_shape=(
            jax.ShapeDtypeStruct((SHARD_ROWS, UNIT), BF16),
            jax.ShapeDtypeStruct((2, ROWS, D), BF16),
            jax.ShapeDtypeStruct((2, ROWS, D), F32),
        ),
        in_specs=[ANY] * 2 + [VMEM] * 5,
        out_specs=[VMEM] * 3,
        scratch_shapes=half_scratch()
        + [
            pltpu.VMEM((CTX, CTX, Y_ROWS, UNIT), BF16),
            pltpu.VMEM((CTX, CTX, Z_ROWS, UNIT), BF16),
            pltpu.VMEM((ROWS, D), BF16),
            pltpu.VMEM((ROWS, D), F32),
        ]
        + [SEMS((12,))] * 3
        + [SEMS((3,))] * 2
        + [SEMS((6,))] * 8
        + [pltpu.VMEM((HALF_SHARD, UNIT), BF16)],
        compiler_params=params(8),
        name="sum_shards",
    )(by_place(lower_e), by_place(lower_a), upper_half, lower_out, upper_out, lower_grad, upper_grad)


def spread_sums_kernel(shard_ref, all_ref, squares_ref, from_y, from_z, *sems):
    ring_x, ring_y, ring_z = Ring("x"), Ring("y"), Ring("z")
    far = [
        one.place(index)
        for one in (ring_y, ring_z)
        for index in (one.right, one.left, one.across)
    ]
    greet_ids(ring_x.near() + far)
    all_ref[ring_x.me] = shard_ref[...]
    met(8)
    halves = (pl.ds(0, FIRST), pl.ds(FIRST, FIRST))
    rows = RingGather(ring_x, lambda b, h: all_ref.at[b, halves[h]], sems[0], sems[1])
    rows.start()
    rows.forward()
    rows.finish()

    def folded(values):
        squared = values * values
        return jnp.sum(squared, axis=0, keepdims=True)

    in_row = jnp.zeros((1, UNIT), F32)
    out_row = jnp.zeros((1, UNIT), F32)
    attn_row = jnp.zeros((1, UNIT), F32)
    back = jnp.zeros((ATTN_ROWS // 2, UNIT), F32)
    small = jnp.zeros((48, UNIT), F32)
    lanes = lax.broadcasted_iota(jnp.int32, (1, UNIT), 1)
    for block in range(CTX):
        in_row += folded(all_ref[block, :D, :].astype(F32))
        out_row += folded(all_ref[block, D:EXPERT_ROWS, :].astype(F32))
        middle = EXPERT_ROWS + ATTN_ROWS // 2
        back += all_ref[block, EXPERT_ROWS:middle, :].astype(F32)
        attn_row += folded(all_ref[block, middle : middle + 96, :].astype(F32))
        final = all_ref[block, middle + 96 :, :].astype(F32)
        attn_row += jnp.where(lanes < HEAD_DIM, folded(final), 0.0)
        small += final
    attn_row += folded(back)
    small_row = folded(small)
    is_router = (lanes >= LANES) & (lanes < LANES + EXPERTS)
    is_gain = (lanes >= LANES + EXPERTS) & (lanes < LANES + EXPERTS + 2)
    sums = [
        jnp.where(is_gain, small_row, 0.0),
        attn_row,
        jnp.where(is_router, small_row, 0.0),
        in_row,
        out_row,
    ]
    places = lax.broadcasted_iota(jnp.int32, (8, LANES), 1)
    tile = jnp.zeros((8, LANES), F32)
    for index, row in enumerate(sums):
        tile = jnp.where(places == index, jnp.sum(row, axis=1, keepdims=True), tile)

    def shared(one, slots, send, recv, tile):
        slots[one.me] = tile
        copies = []
        for index, peer in enumerate((one.right, one.left, one.across)):
            spot = slots.at[one.me]
            copies.append(one.copy(spot, spot, send.at[index], recv.at[index], peer))
            copies[-1].start()
        for copy in copies:
            copy.wait()
        return (slots[0] + slots[1]) + (slots[2] + slots[3])

    tile = shared(ring_y, from_y, sems[2], sems[3], tile)
    squares_ref[...] = shared(ring_z, from_z, sems[4], sems[5], tile)


def spread_sums(shard):
    slots = pltpu.VMEM((CTX, 8, LANES), F32)
    return pl.pallas_call(
        spread_sums_kernel,
        out_shape=(
            jax.ShapeDtypeStruct((CTX, SHARD_ROWS, UNIT), BF16),
            jax.ShapeDtypeStruct((8, LANES), F32),
        ),
        in_specs=[VMEM],
        out_specs=[VMEM, VMEM],
        scratch_shapes=[slots, slots, SEMS((6,)), SEMS((6,))] + [SEMS((3,))] * 4,
        compiler_params=params(9),
        name="spread_sums",
    )(shard)


def inverse_size(values):
    return lax.rsqrt(jnp.mean(values * values, axis=1, keepdims=True) + EPS_NORM)


def unpack(pack_ref, back_ref, heads_ref):
    def body(index, _):
        rows = pl.ds(pl.multiple_of(index * 48, 16), 48)
        for piece in range(6):
            target = back_ref if piece < 3 else heads_ref
            at = (piece % 3) * UNIT
            target[rows, at : at + UNIT] = pack_ref[index, piece * 48 : (piece + 1) * 48, :]
        return 0

    lax.fori_loop(0, 16, body, 0)


def repack(back_ref, heads_ref, pack_ref):
    def body(index, _):
        rows = pl.ds(pl.multiple_of(index * 48, 16), 48)
        for piece in range(6):
            source = back_ref if piece < 3 else heads_ref
            at = (piece % 3) * UNIT
            pack_ref[index, piece * 48 : (piece + 1) * 48, :] = source[rows, at : at + UNIT]
        return 0

    lax.fori_loop(0, 16, body, 0)


def extend(heads_ref, w_ref):
    lanes = lax.broadcasted_iota(jnp.int32, (D, WIDE), 1)
    for head in range(3 * HEADS_DEV):
        at = head // 2 * WIDE
        values = heads_ref[:, at : at + WIDE].astype(F32)
        if head % 2:
            values = pltpu.roll(values, HEAD_DIM, 1)
        if head < 2 * HEADS_DEV:
            upper = jnp.where(
                lanes < 96, -pltpu.roll(values, 32, 1), pltpu.roll(values, 96, 1)
            )
        else:
            upper = jnp.zeros_like(values)
        w_ref[:, head * WIDE : (head + 1) * WIDE] = jnp.where(
            lanes < HEAD_DIM, values, upper
        ).astype(BF16)


def attn_forward_kernel(
    layer, length_ref, u_ref, packs_ref, table_ref,
    a_ref, qkv_ref, mass_ref, attended_ref, residual_ref, b_ref,
    gains_ref, router_ref, w_ref, back_ref,
    heads_out, heads_w, pack_ref, pack_sem, send_a, recv_a, send_o, recv_o,
):
    me, right, left, across = ring()
    load = pltpu.make_async_copy(packs_ref.at[layer], pack_ref, pack_sem)
    load.start()
    greet((right, left, across))
    length = length_ref[0]
    tokens = u_ref[...].astype(F32)
    load.wait()
    unpack(pack_ref, back_ref, heads_w)
    router_ref[...] = heads_w[:, D - LANES :]
    places = lax.broadcasted_iota(jnp.int32, (8, LANES), 0) + EXPERTS
    picker = jnp.where(places == lax.broadcasted_iota(jnp.int32, (8, LANES), 1), 1.0, 0.0)
    gains_ref[...] = dot_nt(picker.astype(BF16), router_ref[...])
    a_ref[rows_of(me), :] = (tokens * inverse_size(tokens) * gains_ref[0:1, :]).astype(BF16)
    met(3)
    gather_rows(a_ref, send_a, recv_a, lambda: extend(heads_w, w_ref))
    for block in range(CTX):
        rows = pl.ds(block * ROWS, ROWS)
        table = table_ref[rows, :]
        mixed = dot(a_ref[rows, :], w_ref[...])
        for part in range(3 * HEADS_DEV):
            lanes = slice(part * WIDE, (part + 1) * WIDE)
            piece = mixed[:, lanes]
            if part < 2 * HEADS_DEV:
                turned = piece * table
                piece = turned + pltpu.roll(turned, WIDE // 2, 1)
            qkv_ref[rows, lanes] = piece.astype(BF16)

    def handed(block):
        step = lax.rem(block - me + CTX, CTX)
        return remote(
            heads_out.at[block], attended_ref.at[me], send_o.at[step], recv_o.at[step], block
        )

    for block in reversed(range(CTX)):
        rows = pl.ds(block * ROWS, ROWS)
        keys = (block + 1) * ROWS
        allowed = allowed_keys(block, keys, length)
        outs = []
        for head in range(HEADS_DEV):
            queries = qkv_ref[rows, head * WIDE : (head + 1) * WIDE]
            key_lanes = slice((HEADS_DEV + head) * WIDE, (HEADS_DEV + head + 1) * WIDE)
            value_lanes = slice((2 * HEADS_DEV + head) * WIDE, (2 * HEADS_DEV + head + 1) * WIDE)
            scores = dot_nt(queries, qkv_ref[:keys, key_lanes]) * SCORE_SCALE
            scores = jnp.where(allowed, scores, MASK_VALUE)
            top = jnp.max(scores, axis=1, keepdims=True)
            raw = jnp.exp(scores - top)
            total = jnp.sum(raw, axis=1, keepdims=True)
            probs = (raw * (1.0 / total)).astype(BF16)
            outs.append(dot(probs, qkv_ref[:keys, value_lanes]))
            mass_ref[head, rows, :] = top + jnp.log(total)
        first = (outs[0] + pltpu.roll(outs[1], WIDE // 2, 1)).astype(BF16)
        second = outs[2][:, : WIDE // 2].astype(BF16)
        heads_out[block, :, :WIDE] = first
        heads_out[block, :, WIDE:] = second

        @pl.when(block != me)
        def _():
            handed(block).start()

    attended_ref[me] = heads_out[me]
    for step in range(1, CTX):
        pltpu.make_async_copy(heads_out.at[0], attended_ref.at[0], recv_o.at[step]).wait()
    residual = tokens
    for block in range(CTX):
        residual = residual + dot(attended_ref[block], back_ref[block * COLS : (block + 1) * COLS, :])
    residual_ref[...] = residual
    b_ref[...] = (residual * inverse_size(residual) * gains_ref[1:2, :]).astype(BF16)
    for step in range(1, CTX):
        pltpu.make_async_copy(heads_out.at[0], attended_ref.at[0], send_o.at[step]).wait()


def attn_forward(layer, length, u, packs, table):
    sems = pltpu.SemaphoreType.DMA
    return pl.pallas_call(
        functools.partial(attn_forward_kernel, layer),
        out_shape=(
            jax.ShapeDtypeStruct((SEQ, D), BF16),
            jax.ShapeDtypeStruct((SEQ, EXT), BF16),
            jax.ShapeDtypeStruct((HEADS_DEV, SEQ, 1), F32),
            jax.ShapeDtypeStruct((CTX, ROWS, COLS), BF16),
            jax.ShapeDtypeStruct((ROWS, D), F32),
            jax.ShapeDtypeStruct((ROWS, D), BF16),
            jax.ShapeDtypeStruct((8, D), F32),
            jax.ShapeDtypeStruct((D, LANES), BF16),
            jax.ShapeDtypeStruct((D, EXT), BF16),
            jax.ShapeDtypeStruct((D, D), BF16),
        ),
        in_specs=[
            SMEM,
            VMEM,
            ANY,
            VMEM,
        ],
        out_specs=[VMEM] * 10,
        scratch_shapes=[
            pltpu.VMEM((CTX, ROWS, COLS), BF16),
            pltpu.VMEM((D, D), BF16),
            pltpu.VMEM((16, ATTN_ROWS, UNIT), BF16),
            sems,
        ]
        + [sems((6,)), sems((6,)), sems((CTX,)), sems((CTX,))],
        compiler_params=params(1 + 10 * layer),
        name="attn_forward",
    )(length, u, packs, table)


def attn_backward_kernel(
    hosting, length_ref, u_ref, gains_ref, router_ref, w_ref, back_ref, table_ref,
    a_ref, qkv_ref, mass_ref, attended_ref, residual_ref, second_ref, gates_ref,
    delta_ref, db_ref, gate_grad_ref, *rest,
):
    if hosting:
        upper_e, upper_a, lent, *rest = rest
    input_ref, pack_ref, lower_ref = rest[:3]
    rest = rest[3:]
    if hosting:
        half_ref, *rest = rest
        rest, hosted = rest[:15], rest[15:]
    dheads_ref, dback_ref = rest[:2]
    rest = rest[2:]
    key_acc, value_acc, dz, grads_out, grads_in, send_o, recv_o = rest[:7]
    part, across_in, from_left, from_right, send_r, recv_r = rest[7:13]
    me, right, left, across = ring()
    greet((right, left, across))
    if hosting:
        refs, (in_y, in_z, local, *sems) = hosted[:HALF_REFS], hosted[HALF_REFS:]
        part_y, part_z = refs[:2]
        section = lax.axis_index("section")
        sums = HalfSums(
            refs,
            sems,
            lambda index, block: add_block(part_y, in_y, block),
            lambda index, block: add_block(part_z, in_z, block),
        )
        greet_ids(sums.ring_y.near() + sums.ring_z.near())

        def loads(half):
            sources = half_sources(half, upper_e, upper_a)
            pairs = [
                (sources[1], part_z.at[:, :, pl.ds(0, Z_CUT), :]),
                (sources[2], part_z.at[:, :, pl.ds(Z_CUT, ATTN_ROWS), :]),
                (lent.at[:, :, pl.ds(Y_ROWS, Z_ROWS), :], in_z),
            ]
            for block in range(CTX):
                pairs.append((sources[0].at[:, block], part_y.at[block]))
                pairs.append((lent.at[:, block, pl.ds(0, Y_ROWS), :], in_y.at[block]))
            return [
                pltpu.make_async_copy(source, target, local.at[index])
                for index, (source, target) in enumerate(pairs)
            ]

        for core in range(2):

            @pl.when(section == core)
            def _():
                for copy in loads(core):
                    copy.start()

    length = length_ref[0]
    lanes = lax.broadcasted_iota(jnp.int32, (ROWS, LANES), 1)
    gates = gates_ref[...]
    gate_grads = jnp.where(lanes < EXPERTS, gate_grad_ref[...], 0.0)
    logit_grad = gates * (gate_grads - jnp.sum(gates * gate_grads, axis=1, keepdims=True))
    logit_grad = logit_grad.astype(BF16)
    second_grad = db_ref[...] + dot_nt(logit_grad, router_ref[...])
    residual = residual_ref[...]
    scale_two = inverse_size(residual)
    normal_two = residual * scale_two
    gain_two_terms = second_grad * normal_two
    scaled_two = second_grad * gains_ref[1:2, :]
    residual_grad = delta_ref[...].astype(F32) + scale_two * (
        scaled_two - normal_two * jnp.mean(scaled_two * normal_two, axis=1, keepdims=True)
    )
    input_ref[...] = residual_grad
    branch_grad = residual_grad.astype(BF16)
    met(7 if hosting else 3)

    for block in range(CTX):
        grads_out[block] = dot_nt(branch_grad, back_ref[block * COLS : (block + 1) * COLS, :]).astype(
            BF16
        )

        @pl.when(block != me)
        def _():
            step = lax.rem(block - me + CTX, CTX)
            remote(
                grads_out.at[block], grads_in.at[me], send_o.at[step], recv_o.at[step], block
            ).start()

    grads_in[me] = grads_out[me]
    if hosting:
        for copy in loads(0):
            copy.wait()
        for number in range(3):
            sums.first(number)
    for block in range(CTX):
        dback_ref[block * COLS : (block + 1) * COLS, :] = dot_tn(
            attended_ref[block], branch_grad
        ).astype(BF16)
    router_terms = dot_tn(second_ref[...], logit_grad)
    ones = jnp.ones((ROWS, LANES), F32)
    gain_two_column = lax.dot_general(
        gain_two_terms, ones, TN, precision=EXACT, preferred_element_type=F32
    )
    key_acc[...] = jnp.zeros_like(key_acc)
    value_acc[...] = jnp.zeros_like(value_acc)
    for step in range(1, CTX):
        pltpu.make_async_copy(grads_out.at[0], grads_in.at[0], recv_o.at[step]).wait()
    for step in range(1, CTX):
        pltpu.make_async_copy(grads_out.at[0], grads_in.at[0], send_o.at[step]).wait()
    for block in range(CTX):
        rows = pl.ds(block * ROWS, ROWS)
        keys = (block + 1) * ROWS
        allowed = allowed_keys(block, keys, length)
        pair = grads_in[block, :, :WIDE]
        tail = grads_in[block, :, WIDE:]
        head_grads = (
            pair,
            pltpu.roll(pair.astype(F32), WIDE // 2, 1).astype(BF16),
            jnp.concatenate([tail, jnp.zeros_like(tail)], axis=1),
        )
        for head in range(HEADS_DEV):
            queries = qkv_ref[rows, head * WIDE : (head + 1) * WIDE]
            keys_all = qkv_ref[:keys, (HEADS_DEV + head) * WIDE : (HEADS_DEV + head + 1) * WIDE]
            values_all = qkv_ref[
                :keys, (2 * HEADS_DEV + head) * WIDE : (2 * HEADS_DEV + head + 1) * WIDE
            ]
            grads = head_grads[head]
            scores = dot_nt(queries, keys_all) * SCORE_SCALE
            probs = jnp.where(allowed, jnp.exp(scores - mass_ref[head, rows, :]), 0.0)
            prob_grad = dot_nt(grads, values_all)
            row_sum = jnp.sum(probs * prob_grad, axis=1, keepdims=True)
            score_grad = (probs * (prob_grad - row_sum)).astype(BF16)
            query_grad = dot(score_grad, keys_all) * (HEAD_DIM**-0.5)
            dz[rows, head * WIDE : (head + 1) * WIDE] = (query_grad * table_ref[rows, :]).astype(BF16)
            spot = slice(head * WIDE, (head + 1) * WIDE)
            key_acc[:keys, spot] += dot_tn(score_grad, queries)
            value_acc[:keys, spot] += dot_tn(probs.astype(BF16), grads)
        if hosting and block == 2:
            sums.first(3)
            sums.first(4)
    for block in range(CTX):
        rows = pl.ds(block * ROWS, ROWS)
        table = table_ref[rows, :] * (HEAD_DIM**-0.5)
        for head in range(HEADS_DEV):
            spot = slice(head * WIDE, (head + 1) * WIDE)
            at = (HEADS_DEV + head) * WIDE
            dz[rows, at : at + WIDE] = (key_acc[rows, spot] * table).astype(BF16)
            at = (2 * HEADS_DEV + head) * WIDE
            dz[rows, at : at + WIDE] = value_acc[rows, spot].astype(BF16)

    if hosting:
        sums.first(5)
        for number in range(3):
            sums.then(number)

    def make(block):
        part[rows_of(block), :] = dot_nt(dz[rows_of(block), :], w_ref[...]).astype(BF16)

    def beside():
        wide_lanes = lax.broadcasted_iota(jnp.int32, (D, WIDE), 1)
        pieces = []
        for piece in range(3):
            spot = slice(piece * HEADS_DEV * WIDE, (piece + 1) * HEADS_DEV * WIDE)
            terms = dot_tn(a_ref[...], dz[:, spot])
            for head in range(HEADS_DEV):
                term = terms[:, head * WIDE : (head + 1) * WIDE]
                if piece < 2:
                    term = term + jnp.where(
                        wide_lanes < HEAD_DIM // 2,
                        pltpu.roll(term, HEAD_DIM // 2, 1),
                        -pltpu.roll(term, WIDE - HEAD_DIM // 2, 1),
                    )
                pieces.append(term)
        for pair in range(4):
            joined = jnp.where(
                wide_lanes < HEAD_DIM,
                pieces[2 * pair],
                pltpu.roll(pieces[2 * pair + 1], HEAD_DIM, 1),
            )
            dheads_ref[:, pair * WIDE : (pair + 1) * WIDE] = joined.astype(BF16)
        dheads_ref[:, 4 * WIDE : 5 * WIDE] = jnp.where(
            wide_lanes < HEAD_DIM, pieces[8], 0.0
        ).astype(BF16)
        if hosting:
            sums.then(3)
            sums.then(4)

    normed_grad = reduce_rows(make, part, across_in, from_left, from_right, send_r, recv_r, beside)
    tokens = u_ref[...].astype(F32)
    scale_one = inverse_size(tokens)
    normal_one = tokens * scale_one
    gain_one_column = lax.dot_general(
        normed_grad * normal_one, ones, TN, precision=EXACT, preferred_element_type=F32
    )
    scaled_one = normed_grad * gains_ref[0:1, :]
    input_grad = input_ref[...] + scale_one * (
        scaled_one - normal_one * jnp.mean(scaled_one * normal_one, axis=1, keepdims=True)
    )
    input_ref[...] = input_grad
    small_lanes = lax.broadcasted_iota(jnp.int32, (D, LANES), 1)
    dheads_ref[:, D - LANES :] = jnp.where(
        small_lanes == EXPERTS,
        gain_one_column,
        jnp.where(small_lanes == EXPERTS + 1, gain_two_column, router_terms),
    ).astype(BF16)
    repack(dback_ref, dheads_ref, pack_ref)
    lower_ref[...] = input_grad.astype(BF16)
    if hosting:
        sums.then(5)
        sums.result(half_ref)


def attn_backward(length, arrays, upper=()):
    sems = pltpu.SemaphoreType.DMA
    out_shape = [
        jax.ShapeDtypeStruct((ROWS, D), F32),
        jax.ShapeDtypeStruct((16, ATTN_ROWS, UNIT), BF16),
        jax.ShapeDtypeStruct((ROWS, D), BF16),
    ]
    if upper:
        out_shape.append(jax.ShapeDtypeStruct((HALF_SHARD, UNIT), BF16))
    scratch = [
        pltpu.VMEM((D, D), BF16),
        pltpu.VMEM((D, D), BF16),
        pltpu.VMEM((SEQ, HEADS_DEV * WIDE), F32),
        pltpu.VMEM((SEQ, HEADS_DEV * WIDE), F32),
        pltpu.VMEM((SEQ, EXT), BF16),
        pltpu.VMEM((CTX, ROWS, COLS), BF16),
        pltpu.VMEM((CTX, ROWS, COLS), BF16),
        sems((CTX,)),
        sems((CTX,)),
    ] + REDUCE_SCRATCH
    if upper:
        scratch += half_scratch()
        scratch += [
            pltpu.VMEM((CTX, CTX, Y_ROWS, UNIT), BF16),
            pltpu.VMEM((CTX, CTX, Z_ROWS, UNIT), BF16),
            sems((11,)),
        ] + [sems((6,))] * 8
    return pl.pallas_call(
        functools.partial(attn_backward_kernel, bool(upper)),
        out_shape=tuple(out_shape),
        in_specs=[SMEM] + [VMEM] * len(arrays) + [ANY] * len(upper),
        out_specs=[VMEM] * len(out_shape),
        scratch_shapes=scratch,
        compiler_params=params(4 if upper else 3),
        name="attn_backward",
    )(length, *arrays, *(by_place(array) for array in upper))


GROUP = 4
GROUPS = 16 // GROUP
GROUP_UNITS = GROUP * LANES
SPLIT = EXPERT_ROWS // 2
SUM_SCRATCH = [
    pltpu.VMEM((CTX, ROWS, D), BF16),
    pltpu.VMEM((HALF, D), BF16),
    pltpu.VMEM((HALF, D), BF16),
    pltpu.VMEM((ROWS, D), BF16),
    pltpu.VMEM((ROWS, D), BF16),
    SEMS((6,)),
    SEMS((6,)),
]


def weight_copies(w_ref, win, wout, sem):
    groups = []
    for group in range(GROUPS):
        shards = pl.ds(group * GROUP, GROUP)
        pairs = [
            (w_ref.at[0, shards], win.at[shards, pl.ds(0, SPLIT), :]),
            (w_ref.at[1, shards, pl.ds(0, D - SPLIT), :], win.at[shards, pl.ds(SPLIT, D - SPLIT), :]),
        ]
        for piece in range(D // UNIT):
            pairs.append(
                (
                    w_ref.at[1, shards, pl.ds(D - SPLIT + piece * LANES, LANES), :],
                    wout.at[shards, :, pl.ds(piece * UNIT, UNIT)],
                )
            )
        groups.append(
            [
                pltpu.make_async_copy(source, target, sem.at[group * 5 + index])
                for index, (source, target) in enumerate(pairs)
            ]
        )
    return groups


def wout_group(wout, group):
    return wout[group * GROUP : (group + 1) * GROUP].reshape(GROUP_UNITS, D)


def ffn_forward_kernel(
    b_own_ref, residual_ref, codes_ref, router_ref, w_ref,
    y_ref, b_ref, gates_ref, gate_ref, kept_ref,
    win, wout, kept_out, acc, w_sem, kept_sem, send_b, recv_b,
    part, top_in, bottom_in, from_left, from_right, send, recv,
):
    ring = Ring("x")
    greet_ids(ring.near())
    loads = weight_copies(w_ref, win, wout, w_sem)
    for group in loads:
        for copy in group:
            copy.start()
    b_ref[ring.me] = b_own_ref[...]
    met(2)
    halves = (pl.ds(0, HALF), pl.ds(HALF, HALF))
    rows = RingGather(ring, lambda b, h: b_ref.at[b, halves[h]], send_b, recv_b)
    rows.start()
    section = lax.axis_index("section")
    lanes = lax.broadcasted_iota(jnp.int32, (ROWS, LANES), 1)
    picker = jnp.where(lax.broadcasted_iota(jnp.int32, (8, LANES), 0) == section, 1.0, 0.0)
    stores = []

    def make(index, block):
        b_rows = b_ref[block]
        slot = index % 2
        for shard in range(16):
            if index == 0 and shard % GROUP == 0:
                for copy in loads[shard // GROUP]:
                    copy.wait()
            if index >= 2 and shard == 0:
                stores[index - 2].wait()
            hidden = dot(b_rows, win[shard])
            kept_out[slot, shard] = hidden.astype(BF16)
            gate_part = hidden[:, :LANES]
            at = shard % GROUP * LANES
            acc_act = (gate_part / (1.0 + jnp.exp(-gate_part)) * hidden[:, LANES:]).astype(BF16)
            if shard % GROUP == 0:
                acted = []
            acted.append(acc_act)
            if shard % GROUP == GROUP - 1:
                terms = dot(jnp.concatenate(acted, axis=1), wout_group(wout, shard // GROUP))
                acc[...] = terms if shard < GROUP else acc[...] + terms
        stores.append(pltpu.make_async_copy(kept_out.at[slot], kept_ref.at[block], kept_sem.at[slot]))
        stores[-1].start()
        logits = dot(b_rows, router_ref[...])
        codes = lax.dot_general(
            codes_ref[block], picker, TN, precision=EXACT, preferred_element_type=F32
        )
        named = (lanes < EXPERTS) & (lanes != jnp.round(codes).astype(jnp.int32))
        chosen = jnp.where(named, logits, MASK_VALUE)
        raw = jnp.where(named, jnp.exp(chosen - jnp.max(chosen, axis=1, keepdims=True)), 0.0)
        gates = raw / jnp.sum(raw, axis=1, keepdims=True)
        if index == 0:
            gates_ref[...] = gates
        gates = jnp.where(lanes == EXPERTS, 1.0, gates)
        gate = jnp.sum(jnp.where(lanes == ring.me, gates, 0.0), axis=1, keepdims=True)
        gate_ref[block] = gate
        part[block] = (acc[...] * gate).astype(BF16)

    order = {ring_index: number for number, ring_index in enumerate(("me", "right", "left", "across"))}

    def from_sum(position, block):
        make({0: order["across"], 1: order["right"], 2: order["left"], 3: order["me"]}[position], block)

    sums = RingSum(
        ring, part, (top_in, bottom_in), from_left, from_right, send, recv, HALF, from_sum
    )
    sums.stage(4)
    rows.forward()
    rows.near()
    sums.stage(1)
    sums.stage(2)
    rows.far()
    sums.stage(0)
    sums.stage(3)
    sums.stage(5)
    y_ref[...] = (residual_ref[...] + sums.total()).astype(BF16)
    rows.sent()
    stores[2].wait()
    stores[3].wait()


def ffn_forward(b_own, residual, codes, router, weights):
    return pl.pallas_call(
        ffn_forward_kernel,
        out_shape=(
            jax.ShapeDtypeStruct((ROWS, D), BF16),
            jax.ShapeDtypeStruct((CTX, ROWS, D), BF16),
            jax.ShapeDtypeStruct((ROWS, LANES), F32),
            jax.ShapeDtypeStruct((CTX, ROWS, 1), F32),
            jax.ShapeDtypeStruct((CTX, 16, ROWS, UNIT), BF16),
        ),
        in_specs=[VMEM] * 4 + [ANY],
        out_specs=[VMEM] * 4 + [ANY],
        scratch_shapes=[
            pltpu.VMEM((16, D, UNIT), BF16),
            pltpu.VMEM((16, LANES, D), BF16),
            pltpu.VMEM((2, 16, ROWS, UNIT), BF16),
            pltpu.VMEM((ROWS, D), F32),
            SEMS((5 * GROUPS,)),
            SEMS((2,)),
            SEMS((6,)),
            SEMS((6,)),
        ]
        + SUM_SCRATCH,
        compiler_params=params(5),
        name="ffn_forward",
    )(b_own, residual, codes, router, weights)


def ffn_backward_kernel(
    lending, b_ref, gate_ref, delta_own_ref, kept_ref, w_ref, *rest,
):
    if lending:
        upper_e, upper_a, db_ref, gate_grad_ref, dw_ref, lent_ref, *rest = rest
        *rest, send_l, recv_l = rest
    else:
        db_ref, gate_grad_ref, dw_ref, *rest = rest
    (
    delta, acc, gate_acc, slot_grad, hidden, acted, win, wout, staged, rows_out, rows_in,
    w_sem, kept_sem, dw_sem, send_d, recv_d, send_g, recv_g,
    part, top_in, bottom_in, from_left, from_right, send, recv,
    ) = rest
    ring = Ring("x")
    peers = (ring.right, ring.left, ring.across)
    section = lax.axis_index("section")
    sibling = {"section": 1 - section}
    greet_ids([ring.place(peer) for peer in peers] + ([sibling] if lending else []))
    blocks = (ring.me, ring.right, ring.left, ring.across)
    kept_loads = [
        pltpu.make_async_copy(
            kept_ref.at[block], hidden.at[:, rows_of(block), :], kept_sem.at[index]
        )
        for index, block in enumerate(blocks)
    ]
    loads = weight_copies(w_ref, win, wout, w_sem)
    kept_loads[0].start()
    for group in loads:
        for copy in group:
            copy.start()
    for copy in kept_loads[1:]:
        copy.start()
    delta[ring.me] = delta_own_ref[...]
    met(4 if lending else 3)
    if lending:
        first_rows = pl.ds(0, KEPT)
        last_rows = pl.ds(KEPT, ATTN_ROWS)

        def lends(given):
            sources = (
                (upper_e.at[:, first_rows, :], upper_e.at[:, last_rows, :])
                if given == 0
                else (upper_e.at[:, pl.ds(HALF_SHARD, KEPT), :], upper_a)
            )
            return [
                pltpu.make_async_remote_copy(
                    src_ref=source,
                    dst_ref=lent_ref.at[:, target, :],
                    send_sem=send_l.at[index],
                    recv_sem=recv_l.at[index],
                    device_id=sibling,
                    device_id_type=MESH,
                )
                for index, (source, target) in enumerate(zip(sources, (first_rows, last_rows)))
            ]

        for core in range(2):

            @pl.when(section == core)
            def _():
                for copy in lends(1 - core):
                    copy.start()

    halves = (pl.ds(0, HALF), pl.ds(HALF, HALF))
    rows = RingGather(ring, lambda b, h: delta.at[b, halves[h]], send_d, recv_d)
    rows.start()
    own_row = lax.broadcasted_iota(jnp.int32, (8, LANES), 0) == ring.me
    picker = jnp.where(own_row, 1.0, 0.0)
    handed = [
        ring.copy(rows_out.at[peer], rows_in.at[index], send_g.at[index], recv_g.at[index], peer)
        for index, peer in enumerate(peers)
    ]

    def make(index, block):
        kept_loads[index].wait()
        at = rows_of(block)
        gate = gate_ref[block]
        delta_rows = delta[block]
        slot_grad[at, :] = (delta_rows.astype(F32) * gate).astype(BF16)
        gate_sum = jnp.zeros((ROWS, LANES), F32)
        for group in range(GROUPS):
            if index == 0:
                for copy in loads[group]:
                    copy.wait()
            act_grad_all = dot_nt(delta_rows, wout_group(wout, group))
            second_grad = None
            for inner in range(GROUP):
                shard = group * GROUP + inner
                values = hidden[shard, at, :].astype(F32)
                gate_part = values[:, :LANES]
                up_part = values[:, LANES:]
                act_grad = act_grad_all[:, inner * LANES : (inner + 1) * LANES]
                sigmoid = 1.0 / (1.0 + jnp.exp(-gate_part))
                silu = gate_part * sigmoid
                act = (silu * up_part).astype(BF16)
                acted[at, shard * LANES : (shard + 1) * LANES] = act
                gate_sum += act.astype(F32) * act_grad
                act_grad = act_grad * gate
                gate_grad = act_grad * up_part * (sigmoid * (1.0 + gate_part * (1.0 - sigmoid)))
                pair = jnp.concatenate([gate_grad, act_grad * silu], axis=1).astype(BF16)
                hidden[shard, at, :] = pair
                term = dot_nt(pair, win[shard])
                second_grad = term if second_grad is None else second_grad + term
            acc[...] = second_grad if group == 0 else acc[...] + second_grad
        part[block] = acc[...].astype(BF16)
        rows_out[block] = lax.dot_general(
            picker, gate_sum, NT, precision=EXACT, preferred_element_type=F32
        )
        if index > 0:
            handed[index - 1].start()

    def from_sum(position, block):
        make((3, 1, 2, 0)[position], block)

    sums = RingSum(
        ring, part, (top_in, bottom_in), from_left, from_right, send, recv, HALF, from_sum
    )
    sums.stage(4)
    rows.forward()
    rows.near()
    sums.stage(1)
    sums.stage(2)
    rows.far()
    sums.stage(0)
    stores = []
    b_all = b_ref[...].reshape(SEQ, D)
    for group in range(GROUPS):
        slot = group % 2
        if group == 1:
            sums.stage(3)
        if group >= 2:
            stores[group - 2].wait()
        for inner in range(GROUP):
            staged[slot, inner, :D, :] = dot_tn(b_all, hidden[group * GROUP + inner]).astype(BF16)
        whole_out = dot_tn(
            acted[:, group * GROUP_UNITS : (group + 1) * GROUP_UNITS], slot_grad[...]
        ).astype(BF16)
        for inner in range(GROUP):
            for piece in range(D // UNIT):
                at = D + piece * LANES
                staged[slot, inner, at : at + LANES, :] = whole_out[
                    inner * LANES : (inner + 1) * LANES, piece * UNIT : (piece + 1) * UNIT
                ]
        stores.append(
            pltpu.make_async_copy(
                staged.at[slot], dw_ref.at[pl.ds(group * GROUP, GROUP)], dw_sem.at[slot]
            )
        )
        stores[-1].start()
    sums.stage(5)
    db_ref[...] = sums.total()
    for copy in handed:
        copy.wait()
    rows_all = rows_out[ring.me] + rows_in[0] + rows_in[1] + rows_in[2]
    diagonal = jnp.where(
        lax.broadcasted_iota(jnp.int32, (8, LANES), 0)
        == lax.broadcasted_iota(jnp.int32, (8, LANES), 1),
        1.0,
        0.0,
    )
    gate_grad_ref[...] = lax.dot_general(
        rows_all, diagonal, TN, precision=EXACT, preferred_element_type=F32
    )
    rows.sent()
    stores[2].wait()
    stores[3].wait()
    if lending:
        for copy in lends(0):
            copy.wait()


def ffn_backward(b_all, gate_col, delta_own, kept, weights, upper=()):
    out_shape = [
        jax.ShapeDtypeStruct((ROWS, D), F32),
        jax.ShapeDtypeStruct((ROWS, LANES), F32),
        jax.ShapeDtypeStruct((16, EXPERT_ROWS, UNIT), BF16),
    ]
    if upper:
        out_shape.append(jax.ShapeDtypeStruct((16, HALF_SHARD, UNIT), BF16))
    return pl.pallas_call(
        functools.partial(ffn_backward_kernel, bool(upper)),
        out_shape=out_shape,
        in_specs=[VMEM] * 3 + [ANY] * (2 + len(upper)),
        out_specs=[VMEM] * 2 + [ANY] * (len(out_shape) - 2),
        scratch_shapes=[
            pltpu.VMEM((CTX, ROWS, D), BF16),
            pltpu.VMEM((ROWS, D), F32),
            pltpu.VMEM((8, LANES), F32),
            pltpu.VMEM((SEQ, D), BF16),
            pltpu.VMEM((16, SEQ, UNIT), BF16),
            pltpu.VMEM((SEQ, FFN), BF16),
            pltpu.VMEM((16, D, UNIT), BF16),
            pltpu.VMEM((16, LANES, D), BF16),
            pltpu.VMEM((2, GROUP, EXPERT_ROWS, UNIT), BF16),
            pltpu.VMEM((CTX, 8, ROWS), F32),
            pltpu.VMEM((3, 8, ROWS), F32),
            SEMS((5 * GROUPS,)),
            SEMS((CTX,)),
            SEMS((2,)),
            SEMS((6,)),
            SEMS((6,)),
            SEMS((3,)),
            SEMS((3,)),
        ]
        + SUM_SCRATCH
        + ([SEMS((2,)), SEMS((2,))] if upper else []),
        compiler_params=params(10 if upper else 6),
        name="ffn_backward",
    )(b_all, gate_col, delta_own, kept, weights, *upper)


def rotary_table():
    half_dim = HEAD_DIM // 2
    steps = 2.0 * np.arange(half_dim, dtype=np.float32) / np.float32(HEAD_DIM)
    frequency = np.exp(-np.log(np.float32(10000.0)) * steps)
    angles = np.arange(SEQ, dtype=np.float32)[:, None] * frequency[None, :]
    cosine, sine = np.cos(angles), np.sin(angles)
    return jnp.asarray(np.concatenate([cosine, cosine, sine, sine], axis=1), F32)


def layer_forward(layer, packs, experts, tokens_in, length, codes, table):
    a_all, qkv, mass, attended, residual, second, *unpacked = attn_forward(
        layer, length, tokens_in, packs, table
    )
    output, b_all, gates, gate_col, kept = ffn_forward(
        second, residual, codes, unpacked[1], experts
    )
    return output, (
        tokens_in, a_all, qkv, mass, attended, residual, second, b_all, gates, gate_col, kept, unpacked,
    )


def layer_backward(experts, saved, delta_own, length, table, upper=()):
    (
        tokens_in, a_all, qkv, mass, attended, residual, second, b_all, gates, gate_col, kept, unpacked,
    ) = saved
    db, gate_grads, dexperts, *lent = ffn_backward(b_all, gate_col, delta_own, kept, experts, upper)
    results = attn_backward(
        length,
        (
            tokens_in, *unpacked, table, a_all, qkv, mass,
            attended, residual, second, gates, delta_own, db, gate_grads,
        ),
        tuple(upper) + tuple(lent),
    )
    return dexperts, results


def factor_of(squares_ref, index):
    return jnp.minimum(1.0, CLIP_LIMIT / jnp.sqrt(squares_ref[0:1, index : index + 1]))


def updated(fixes_ref, gradient, factor, old, new, learn_rate, at=...):
    master_ref, mean_ref, square_ref = old
    gradient_ref, mean_new_ref, square_new_ref, master_new_ref, copy_ref = new
    clipped = gradient * factor
    master = master_ref[at]
    mean_new = BETA_ONE * mean_ref[at] + (1.0 - BETA_ONE) * clipped
    square_new = BETA_TWO * square_ref[at] + (1.0 - BETA_TWO) * clipped * clipped
    master_new = master - learn_rate * (
        mean_new / fixes_ref[0] / (jnp.sqrt(square_new / fixes_ref[1]) + ADAM_EPS) + DECAY_RATE * master
    )
    gradient_ref[at] = gradient
    mean_new_ref[at] = mean_new
    square_new_ref[at] = square_new
    master_new_ref[at] = master_new
    copy_ref[at] = master_new.astype(BF16)


def update_kernel(
    fixes_ref, squares_ref, in_sum_ref, out_sum_ref, attn_sum_ref, *refs,
):
    in_old, out_old, attn_old, gain_old, router_old = (refs[at : at + 3] for at in range(0, 15, 3))
    in_new, out_new, attn_new, gain_new, router_new = (refs[at : at + 5] for at in range(15, 40, 5))
    norms_ref, turned, wide = refs[40:]
    turned[pl.ds(0, D, 2), :] = in_sum_ref[0, :, :LANES].astype(F32)
    turned[pl.ds(1, D, 2), :] = in_sum_ref[0, :, LANES:].astype(F32)
    updated(
        fixes_ref, turned[...], factor_of(squares_ref, 3), in_old, in_new, RATE_FACTOR / D**0.5
    )
    pieces = [
        out_sum_ref[0, piece * LANES : (piece + 1) * LANES, :].astype(F32)
        for piece in range(D // UNIT)
    ]
    updated(
        fixes_ref,
        jnp.concatenate(pieces, axis=1),
        factor_of(squares_ref, 4),
        out_old,
        out_new,
        RATE_FACTOR / FFN**0.5,
        0,
    )

    @pl.when(pl.program_id(0) == 0)
    def _():
        back = [jnp.zeros((48, UNIT), F32) for _ in range(3)]
        small = jnp.zeros((48, UNIT), F32)
        for block in range(CTX):
            rows = [
                attn_sum_ref[block, piece * 48 : (piece + 1) * 48, :].astype(F32) for piece in range(6)
            ]
            back = [left + right for left, right in zip(back, rows[:3])]
            small = small + rows[5]
            heads = jnp.concatenate(rows[3:], axis=1)
            for part in range(3):
                at = part * D + block * COLS
                wide[:, at : at + COLS] = heads[:, part * COLS : (part + 1) * COLS]
        wide[:, 3 * D :] = jnp.concatenate(back, axis=1)
        small = small[:, LANES:]
        places = lax.broadcasted_iota(jnp.int32, (8, LANES), 0) + EXPERTS
        picker = jnp.where(places == lax.broadcasted_iota(jnp.int32, (8, LANES), 1), 1.0, 0.0)
        gain_rows = lax.dot_general(
            picker, small, NT, precision=EXACT, preferred_element_type=F32
        )
        updated(fixes_ref, gain_rows[:2], factor_of(squares_ref, 0), gain_old, gain_new, GAIN_RATE)
        updated(
            fixes_ref,
            small[:, :EXPERTS],
            factor_of(squares_ref, 2),
            router_old,
            router_new,
            RATE_FACTOR / (D // 4) ** 0.5,
        )
        norms_ref[...] = jnp.sqrt(squares_ref[...])
        for part in range(4):
            lanes = (slice(None), slice(part * D, (part + 1) * D))
            updated(
                fixes_ref,
                wide[lanes],
                factor_of(squares_ref, 1),
                attn_old,
                attn_new,
                RATE_FACTOR / D**0.5,
                lanes,
            )


def update(fixes, squares, sums_all, in_old, out_old, attn_old, gain_old, router_old):
    in_rows, units = 2 * D, LANES
    in_shape, out_shape, attn_shape = (CTX * in_rows, units), (CTX, units, D), (48, 4 * D)
    in_spec = pl.BlockSpec((in_rows, units), lambda i: (i, 0))
    out_spec = pl.BlockSpec((1, units, D), lambda i: (i, 0, 0))
    attn_spec = whole(attn_shape)
    gain_shape, router_shape = (2, 48), (48, EXPERTS)

    def five(shape):
        return [jax.ShapeDtypeStruct(shape, F32)] * 4 + [jax.ShapeDtypeStruct(shape, BF16)]

    return pl.pallas_call(
        update_kernel,
        grid=(CTX,),
        out_shape=five(in_shape)
        + five(out_shape)
        + five(attn_shape)
        + five(gain_shape)
        + five(router_shape)
        + [jax.ShapeDtypeStruct((8, LANES), F32)],
        in_specs=[
            SMEM,
            whole((8, LANES)),
            pl.BlockSpec((1, D, UNIT), lambda i: (i, 0, 0)),
            pl.BlockSpec((1, D // 2, UNIT), lambda i: (i, 2, 0)),
            pl.BlockSpec((CTX, ATTN_ROWS, UNIT), lambda i: (0, EXPERT_ROWS // ATTN_ROWS, 0)),
        ]
        + [in_spec] * 3
        + [out_spec] * 3
        + [attn_spec] * 3
        + [whole(gain_shape)] * 3
        + [whole(router_shape)] * 3,
        out_specs=[in_spec] * 5
        + [out_spec] * 5
        + [attn_spec] * 5
        + [whole(gain_shape)] * 5
        + [whole(router_shape)] * 5
        + [whole((8, LANES))],
        scratch_shapes=[pltpu.VMEM((in_rows, units), F32), pltpu.VMEM(attn_shape, F32)],
        compiler_params=pltpu.CompilerParams(vmem_limit_bytes=VMEM_LIMIT),
        name="update",
    )(
        fixes, squares, sums_all, sums_all, sums_all,
        *(array.reshape(in_shape) for array in in_old),
        *(array.reshape(out_shape) for array in out_old),
        *(array.reshape(attn_shape) for array in attn_old),
        *(array.reshape(gain_shape) for array in gain_old),
        *(array.reshape(router_shape) for array in router_old),
    )


def on_device(
    inputs, cotangent, lengths, routes, step_count,
    norm_gains, gains_mean, gains_square,
    attn_weight, attn_mean, attn_square,
    router_weight, router_mean, router_square,
    expert_in, in_mean, in_square,
    expert_out, out_mean, out_square,
):
    section = lax.axis_index("section")
    ctx_index = lax.axis_index("ctx")
    fsdp = lax.axis_size("fsdp")
    everyone = ("section", "fsdp")
    shard_rows = attn_weight.shape[1]
    units = expert_in.shape[4]
    first_core = section == 0

    def own_columns(matrix, part):
        return lax.dynamic_slice_in_dim(matrix, part * D + ctx_index * COLS, COLS, 1)

    def swap(block):
        return lax.ppermute(block, "section", [(0, 1), (1, 0)])

    attn_shard = jnp.concatenate(
        [attn_weight[0][:, 3 * D :]]
        + [own_columns(attn_weight[0], part) for part in range(3)]
        + [jnp.zeros((shard_rows, HEAD_DIM), F32), router_weight[0], norm_gains[0].T]
        + [jnp.zeros((shard_rows, LANES - EXPERTS - 2), F32)],
        axis=1,
    ).astype(BF16)
    attn_shard = attn_shard.reshape(shard_rows, 6, UNIT).transpose(1, 0, 2).reshape(-1, UNIT)
    left_out = (3 - routes[0, :, :, 0] - routes[0, :, :, 1]).astype(F32)
    packs, codes = gather_shards(attn_shard, jnp.pad(left_out, ((0, 8 - left_out.shape[0]), (0, 0))))
    packs = packs.reshape(2, fsdp, ATTN_ROWS, UNIT)
    in_shard = (
        lax.dynamic_index_in_dim(expert_in[0], ctx_index, 0, keepdims=False)
        .astype(BF16)
        .reshape(D, 2 * units)
    )
    out_shard = lax.dynamic_index_in_dim(expert_out[0], ctx_index, 0, keepdims=False).astype(BF16)
    halves = jnp.concatenate(
        [in_shard] + [out_shard[:, at : at + 2 * units] for at in range(0, D, 2 * units)], axis=0
    ).reshape(2, SPLIT, 2 * units)
    other = swap(jnp.where(first_core, halves[1], halves[0]))
    pieces = (jnp.where(first_core, halves[0], other), jnp.where(first_core, other, halves[1]))
    experts = [
        lax.all_gather(piece, everyone).reshape(2, fsdp, SPLIT, 2 * units) for piece in pieces
    ]
    length = lax.dynamic_slice_in_dim(lengths, section, 1, 0)
    tokens = lax.dynamic_index_in_dim(inputs, section, 0, keepdims=False)
    positions = ctx_index * ROWS + jnp.arange(ROWS, dtype=jnp.int32)
    seed = lax.dynamic_index_in_dim(cotangent, section, 0, keepdims=False)
    seed = jnp.where((positions < length[0])[:, None], seed, jnp.zeros_like(seed))
    table = rotary_table()

    lower_out, lower_saved = layer_forward(0, packs, experts[0], tokens, length, codes[0], table)
    upper_out, upper_saved = layer_forward(1, packs, experts[1], lower_out, length, codes[1], table)
    upper_experts, (upper_grad, upper_attn, lower_seed) = layer_backward(
        experts[1], upper_saved, seed, length, table
    )
    lower_experts, (lower_grad, lower_attn, _, upper_half) = layer_backward(
        experts[0], lower_saved, lower_seed, length, table, (upper_experts, upper_attn)
    )
    shard_sum, layer_outputs, input_grads = sum_shards(
        lower_experts, lower_attn, upper_half, lower_out, upper_out, lower_grad, upper_grad
    )
    sums_all, squares = spread_sums(shard_sum)
    step_value = step_count[0].astype(F32)
    fixes = jnp.stack([1.0 - BETA_ONE**step_value, 1.0 - BETA_TWO**step_value])
    changed = update(
        fixes,
        squares,
        sums_all,
        (expert_in, in_mean, in_square),
        (expert_out, out_mean, out_square),
        (attn_weight, attn_mean, attn_square),
        (norm_gains, gains_mean, gains_square),
        (router_weight, router_mean, router_square),
    )

    def shaped(first, like):
        return tuple(array.reshape(like.shape) for array in changed[first : first + 5])

    return (
        (layer_outputs[None], input_grads[None])
        + shaped(15, norm_gains)
        + shaped(10, attn_weight)
        + shaped(20, router_weight)
        + shaped(0, expert_in)
        + shaped(5, expert_out)
        + (changed[25][:1, :5],)
    )


def solution(mesh):
    gains = P("section", None, "fsdp")
    rows = P("section", "fsdp", None)
    wide = P("section", None, None, None, "fsdp")
    down = P("section", None, "fsdp", None)
    tokens = P("section", "fsdp", "ctx", None)
    return jax.shard_map(
        on_device,
        mesh=mesh,
        in_specs=(
            P("fsdp", "ctx", None),
            P("fsdp", "ctx", None),
            P("fsdp"),
            tokens,
            P(),
        )
        + (gains,) * 3
        + (rows,) * 6
        + (wide,) * 3
        + (down,) * 3,
        out_specs=(tokens, tokens)
        + (gains,) * 5
        + (rows,) * 10
        + (wide,) * 5
        + (down,) * 5
        + (P("section", None),),
        check_vma=False,
    )
```

```python
import functools

import jax
import jax.numpy as jnp
import numpy as np
from jax import lax
from jax.experimental import pallas as pl
from jax.experimental.pallas import tpu as pltpu
from jax.sharding import PartitionSpec as P

D = 768
HEADS = 12
HEAD_DIM = 64
FFN = 2048
EXPERTS = 3
ROWS = 256
CTX = 4
SEQ = ROWS * CTX
HEADS_DEV = HEADS // CTX
WIDE = 128
EXT = 3 * HEADS_DEV * WIDE
COLS = HEADS_DEV * HEAD_DIM

EPS_NORM = 1e-06
BETA_ONE = 0.9
BETA_TWO = 0.95
RATE_FACTOR = 3.0
GAIN_RATE = 0.3
DECAY_RATE = 0.1
ADAM_EPS = 1e-08
CLIP_LIMIT = 1.0
MASK_VALUE = -1e30
SCORE_SCALE = HEAD_DIM ** (-0.5) / 2.0
BF16 = jnp.bfloat16
F32 = jnp.float32
VMEM_LIMIT = 56 * 1024 * 1024
NT = (((1,), (1,)), ((), ()))
TN = (((0,), (0,)), ((), ()))
HALF = ROWS // 2
LANES = 128
MESH = pl.DeviceIdType.MESH
EXACT = lax.Precision.HIGHEST


def dot(left, right):
    return jnp.dot(left, right, preferred_element_type=F32)


def dot_nt(left, right):
    return lax.dot_general(left, right, NT, preferred_element_type=F32)


def dot_tn(left, right):
    return lax.dot_general(left, right, TN, preferred_element_type=F32)


def params(collective_id):
    return pltpu.CompilerParams(
        vmem_limit_bytes=VMEM_LIMIT, collective_id=collective_id, has_side_effects=True
    )


def whole(shape):
    return pl.BlockSpec(shape, lambda *_: (0,) * len(shape))


def allowed_keys(block, keys, length):
    key_pos = lax.broadcasted_iota(jnp.int32, (ROWS, keys), 1)
    query_pos = lax.broadcasted_iota(jnp.int32, (ROWS, keys), 0) + block * ROWS
    return (key_pos <= query_pos) & (key_pos < length)


VMEM = pl.BlockSpec(memory_space=pltpu.VMEM)
SMEM = pl.BlockSpec(memory_space=pltpu.SMEM)
ANY = pl.BlockSpec(memory_space=pl.ANY)


def ring():
    me = lax.axis_index("ctx")
    return me, lax.rem(me + 1, CTX), lax.rem(me + 3, CTX), lax.rem(me + 2, CTX)


def greet(peers):
    barrier = pltpu.get_barrier_semaphore()
    for peer in peers:
        pl.semaphore_signal(barrier, inc=1, device_id={"ctx": peer}, device_id_type=MESH)


def met(count):
    pl.semaphore_wait(pltpu.get_barrier_semaphore(), count)


def remote(source, target, send, recv, peer):
    return pltpu.make_async_remote_copy(
        src_ref=source,
        dst_ref=target,
        send_sem=send,
        recv_sem=recv,
        device_id={"ctx": peer},
        device_id_type=MESH,
    )


def rows_of(block, half=None):
    if half is None:
        return pl.ds(pl.multiple_of(block * ROWS, ROWS), ROWS)
    return pl.ds(pl.multiple_of(block * ROWS + half * HALF, HALF), HALF)


def gather_rows(all_ref, send, recv, beside=None):
    me, right, left, _ = ring()

    def piece(index, block, half, peer):
        spot = all_ref.at[rows_of(block, half)]
        return remote(spot, spot, send.at[index], recv.at[index], peer)

    copies = [
        piece(0, me, 0, right),
        piece(1, me, 1, left),
        piece(2, me, 1, right),
        piece(3, me, 0, left),
    ]
    for copy in copies:
        copy.start()
    if beside is not None:
        beside()
    copies[0].wait_recv()
    copies.append(piece(4, left, 0, right))
    copies[4].start()
    copies[1].wait_recv()
    copies.append(piece(5, right, 1, left))
    copies[5].start()
    for index in range(2, 6):
        copies[index].wait_recv()
    for copy in copies:
        copy.wait_send()


def reduce_rows(make, part, across_in, from_left, from_right, send, recv, beside=None):
    me, right, left, across = ring()
    top, bottom = pl.ds(0, HALF), pl.ds(HALF, HALF)

    def piece(index, block, half, target, peer):
        return remote(part.at[rows_of(block, half)], target, send.at[index], recv.at[index], peer)

    make(across)
    copies = [
        piece(0, across, 0, across_in.at[0], right),
        piece(1, across, 1, across_in.at[1], left),
    ]
    copies[0].start()
    copies[1].start()
    make(right)
    copies.append(piece(2, right, 1, from_left.at[bottom], right))
    copies[2].start()
    make(left)
    copies.append(piece(3, left, 0, from_right.at[top], left))
    copies[3].start()
    copies[0].wait_recv()
    spot = rows_of(right, 0)
    part[spot, :] = (part[spot, :].astype(F32) + across_in[0].astype(F32)).astype(BF16)
    copies.append(piece(4, right, 0, from_left.at[top], right))
    copies[4].start()
    copies[1].wait_recv()
    spot = rows_of(left, 1)
    part[spot, :] = (part[spot, :].astype(F32) + across_in[1].astype(F32)).astype(BF16)
    copies.append(piece(5, left, 1, from_right.at[bottom], left))
    copies[5].start()
    make(me)
    if beside is not None:
        beside()
    for index in range(2, 6):
        copies[index].wait_recv()
    for copy in copies:
        copy.wait_send()
    return (
        part[rows_of(me), :].astype(F32) + from_left[...].astype(F32) + from_right[...].astype(F32)
    )


REDUCE_SCRATCH = [
    pltpu.VMEM((SEQ, D), BF16),
    pltpu.VMEM((2, HALF, D), BF16),
    pltpu.VMEM((ROWS, D), BF16),
    pltpu.VMEM((ROWS, D), BF16),
    pltpu.SemaphoreType.DMA((6,)),
    pltpu.SemaphoreType.DMA((6,)),
]


def greet_ids(peers):
    barrier = pltpu.get_barrier_semaphore()
    for peer in peers:
        pl.semaphore_signal(barrier, inc=1, device_id=peer, device_id_type=MESH)


class Ring:
    def __init__(self, axis):
        if axis == "x":
            self.me = lax.axis_index("ctx")
            self.place = lambda index: {"ctx": index}
        else:
            shard = lax.axis_index("fsdp")
            inner, outer = lax.rem(shard, CTX), lax.div(shard, CTX)
            if axis == "y":
                self.me = inner
                self.place = lambda index: {"fsdp": outer * CTX + index}
            else:
                self.me = outer
                self.place = lambda index: {"fsdp": index * CTX + inner}
        self.right = lax.rem(self.me + 1, CTX)
        self.left = lax.rem(self.me + 3, CTX)
        self.across = lax.rem(self.me + 2, CTX)

    def order(self):
        return (self.across, self.right, self.left, self.me)

    def near(self):
        return [self.place(self.right), self.place(self.left)]

    def copy(self, source, target, send, recv, index):
        return pltpu.make_async_remote_copy(
            src_ref=source,
            dst_ref=target,
            send_sem=send,
            recv_sem=recv,
            device_id=self.place(index),
            device_id_type=MESH,
        )


class RingGather:
    def __init__(self, ring, at, send, recv):
        self.ring, self.at, self.send, self.recv = ring, at, send, recv
        self.sends = (
            (ring.me, 0, ring.right),
            (ring.me, 1, ring.left),
            (ring.me, 1, ring.right),
            (ring.me, 0, ring.left),
            (ring.left, 0, ring.right),
            (ring.right, 1, ring.left),
        )

    def piece(self, index, block, half, to):
        spot = self.at(block, half)
        return self.ring.copy(spot, spot, self.send.at[index], self.recv.at[index], to)

    def go(self, index):
        self.piece(index, *self.sends[index]).start()

    def landed(self, index, block, half):
        self.piece(index, block, half, self.ring.right).wait_recv()

    def start(self):
        for index in range(4):
            self.go(index)

    def forward(self):
        self.landed(0, self.ring.left, 0)
        self.go(4)
        self.landed(1, self.ring.right, 1)
        self.go(5)

    def near(self):
        self.landed(2, self.ring.left, 1)
        self.landed(3, self.ring.right, 0)

    def far(self):
        self.landed(4, self.ring.across, 0)
        self.landed(5, self.ring.across, 1)

    def sent(self):
        for index in range(6):
            self.piece(index, *self.sends[index]).wait_send()

    def finish(self):
        self.near()
        self.far()
        self.sent()


class RingSum:
    def __init__(self, ring, part, across_in, from_left, from_right, send, recv, cut, make):
        self.ring, self.part, self.across_in = ring, part, across_in
        self.from_left, self.from_right, self.send, self.recv = from_left, from_right, send, recv
        size = part.shape[1]
        self.halves = (pl.ds(0, cut), pl.ds(cut, size - cut))
        self.make = make
        self.copies = {}

    def go(self, index, block, half, target, to):
        self.copies[index] = self.ring.copy(
            self.part.at[block, self.halves[half]], target, self.send.at[index], self.recv.at[index], to
        )
        self.copies[index].start()

    def arrived(self, half, block):
        self.copies[half].wait_recv()
        incoming = self.across_in[half]
        if len(self.part.shape) == 3:
            spot = (block, self.halves[half])
            self.part[spot] = (self.part[spot].astype(F32) + incoming[...].astype(F32)).astype(BF16)
            return
        start = (0, self.part.shape[1] - incoming.shape[0])[half]
        for index in range(incoming.shape[0]):
            self.part[block, start + index] = (
                self.part[block, start + index].astype(F32) + incoming[index].astype(F32)
            ).astype(BF16)

    def stage(self, number):
        ring = self.ring
        if number == 0:
            self.make(0, ring.across)
            self.go(0, ring.across, 0, self.across_in[0], ring.right)
            self.go(1, ring.across, 1, self.across_in[1], ring.left)
        elif number == 1:
            self.make(1, ring.right)
            self.go(2, ring.right, 1, self.from_left.at[self.halves[1]], ring.right)
        elif number == 2:
            self.make(2, ring.left)
            self.go(3, ring.left, 0, self.from_right.at[self.halves[0]], ring.left)
        elif number == 3:
            self.arrived(0, ring.right)
            self.go(4, ring.right, 0, self.from_left.at[self.halves[0]], ring.right)
            self.arrived(1, ring.left)
            self.go(5, ring.left, 1, self.from_right.at[self.halves[1]], ring.left)
        elif number == 4:
            self.make(3, ring.me)
        else:
            for index in range(2, 6):
                self.copies[index].wait_recv()
            for index in range(6):
                self.copies[index].wait_send()

    def total(self, index=None):
        spot = (self.ring.me,) if index is None else (self.ring.me, index)
        tail = () if index is None else (index,)
        return (
            self.part[spot].astype(F32)
            + self.from_left[tail or ...].astype(F32)
            + self.from_right[tail or ...].astype(F32)
        )


UNIT = 256
EXPERT_ROWS = D + D // 2
ATTN_ROWS = 288
SHARD_ROWS = EXPERT_ROWS + ATTN_ROWS
FIRST = SHARD_ROWS // 2
KEPT = EXPERT_ROWS - FIRST
CUT = 352
SEMS = pltpu.SemaphoreType.DMA


def gather_shards_kernel(shard_ref, code_ref, out_ref, codes_ref, *sems):
    section = lax.axis_index("section")
    sibling = {"section": 1 - section}
    ring_y, ring_z = Ring("y"), Ring("z")
    y, z = ring_y.me, ring_z.me
    ring_x = Ring("x")
    x_peers = (ring_x.right, ring_x.left, ring_x.across)
    greet_ids(
        [sibling] + ring_y.near() + ring_z.near() + [ring_x.place(peer) for peer in x_peers]
    )
    out_ref[section, z, y] = shard_ref[...]
    codes_ref[section, ring_x.me] = code_ref[...]
    met(8)
    spot = codes_ref.at[section, ring_x.me]
    code_copies = [
        ring_x.copy(spot, spot, sems[10].at[index], sems[11].at[index], peer)
        for index, peer in enumerate(x_peers)
    ]
    for copy in code_copies:
        copy.start()
    half = ATTN_ROWS // 2
    low = (pl.ds(0, 64), pl.ds(64, half - 64))
    high = (pl.ds(half, 64), pl.ds(half + 64, half - 64))
    pair = (pl.ds(0, 2), pl.ds(2, 2))
    near_y = RingGather(ring_y, lambda b, h: out_ref.at[section, z, b, low[h]], sems[0], sems[1])
    near_z = RingGather(ring_z, lambda b, h: out_ref.at[section, b, y, high[h]], sems[2], sems[3])
    far_z = RingGather(
        ring_z, lambda b, h: out_ref.at[section, b, pair[h], pl.ds(0, half)], sems[4], sems[5]
    )
    far_y = RingGather(
        ring_y, lambda b, h: out_ref.at[section, pair[h], b, pl.ds(half, half)], sems[6], sems[7]
    )
    for rings in ((near_y, near_z), (far_z, far_y)):
        for one in rings:
            one.start()
        for one in rings:
            one.forward()
        for one in rings:
            one.finish()
    across = pltpu.make_async_remote_copy(
        src_ref=out_ref.at[section],
        dst_ref=out_ref.at[section],
        send_sem=sems[8],
        recv_sem=sems[9],
        device_id=sibling,
        device_id_type=MESH,
    )
    across.start()
    for copy in code_copies:
        copy.wait()
    codes_across = pltpu.make_async_remote_copy(
        src_ref=codes_ref.at[section],
        dst_ref=codes_ref.at[section],
        send_sem=sems[12],
        recv_sem=sems[13],
        device_id=sibling,
        device_id_type=MESH,
    )
    codes_across.start()
    codes_across.wait()
    across.wait()


def gather_shards(shard, codes):
    return pl.pallas_call(
        gather_shards_kernel,
        out_shape=(
            jax.ShapeDtypeStruct((2, CTX, CTX, ATTN_ROWS, UNIT), BF16),
            jax.ShapeDtypeStruct((2, CTX, 8, ROWS), F32),
        ),
        in_specs=[VMEM, VMEM],
        out_specs=[VMEM, VMEM],
        scratch_shapes=[SEMS((6,))] * 8 + [SEMS, SEMS, SEMS((3,)), SEMS((3,)), SEMS, SEMS],
        compiler_params=params(7),
        name="gather_shards",
    )(shard, codes)


HALF_SHARD = SHARD_ROWS // 2
Y_ROWS, Z_ROWS = 352, 368
Z_CUT = Z_ROWS - ATTN_ROWS


def half_sources(half, experts, attn):
    if half == 0:
        return (
            experts.at[:, :, pl.ds(0, Y_ROWS), :],
            experts.at[:, :, pl.ds(Y_ROWS, Z_CUT), :],
            experts.at[:, :, pl.ds(Y_ROWS + Z_CUT, ATTN_ROWS), :],
        )
    return (
        experts.at[:, :, pl.ds(HALF_SHARD, Y_ROWS), :],
        experts.at[:, :, pl.ds(HALF_SHARD + Y_ROWS, Z_CUT), :],
        attn,
    )


class HalfSums:
    def __init__(self, refs, sems, make_y, make_z):
        (
            self.part_y, self.part_z, top_y, bottom_y, left_y, right_y, top_z, bottom_z, left_z, right_z,
            more_z, more_y, top_zz, bottom_zz, left_zz, right_zz, top_yy, bottom_yy, left_yy, right_yy,
        ) = refs
        ring_y, ring_z = Ring("y"), Ring("z")
        self.ring_y, self.ring_z = ring_y, ring_z
        self.first_y = RingSum(
            ring_y, self.part_y, (top_y, bottom_y), left_y, right_y, sems[0], sems[1], 2, make_y
        )
        self.first_z = RingSum(
            ring_z, self.part_z, (top_z, bottom_z), left_z, right_z, sems[2], sems[3], 2, make_z
        )

        def make_zz(index, block):
            more_z[block] = self.first_y.total(block).astype(BF16)

        def make_yy(index, block):
            more_y[block] = self.first_z.total(block).astype(BF16)

        self.then_z = RingSum(
            ring_z, more_z, (top_zz, bottom_zz), left_zz, right_zz, sems[4], sems[5], Y_ROWS // 2, make_zz
        )
        self.then_y = RingSum(
            ring_y, more_y, (top_yy, bottom_yy), left_yy, right_yy, sems[6], sems[7], 176, make_yy
        )

    def first(self, number):
        self.first_y.stage(number)
        self.first_z.stage(number)

    def then(self, number):
        self.then_z.stage(number)
        self.then_y.stage(number)

    def result(self, out_ref):
        out_ref[pl.ds(0, Y_ROWS), :] = self.then_z.total().astype(BF16)
        out_ref[pl.ds(Y_ROWS, Z_ROWS), :] = self.then_y.total().astype(BF16)


def half_scratch():
    shapes = [(CTX, CTX, Y_ROWS, UNIT), (CTX, CTX, Z_ROWS, UNIT)]
    for rows in (Y_ROWS, Z_ROWS):
        shapes += [(2, rows, UNIT)] * 2 + [(CTX, rows, UNIT)] * 2
    shapes += [(CTX, Y_ROWS, UNIT), (CTX, Z_ROWS, UNIT)]
    for rows in (Y_ROWS, Z_ROWS):
        shapes += [(176, UNIT), (rows - 176, UNIT)] + [(rows, UNIT)] * 2
    return [pltpu.VMEM(shape, BF16) for shape in shapes]


HALF_REFS = 20


def add_block(part, incoming, block):
    for other in range(CTX):
        part[block, other] = (part[block, other].astype(F32) + incoming[block, other].astype(F32)).astype(
            BF16
        )


def shared_squares(all_ref, ring_y, ring_z, spread):
    from_y, from_z, *sems = spread

    def folded(values):
        squared = values * values
        return jnp.sum(squared, axis=0, keepdims=True)

    in_row = jnp.zeros((1, UNIT), F32)
    out_row = jnp.zeros((1, UNIT), F32)
    attn_row = jnp.zeros((1, UNIT), F32)
    back = jnp.zeros((ATTN_ROWS // 2, UNIT), F32)
    small = jnp.zeros((48, UNIT), F32)
    lanes = lax.broadcasted_iota(jnp.int32, (1, UNIT), 1)
    for block in range(CTX):
        in_row += folded(all_ref[block, :D, :].astype(F32))
        out_row += folded(all_ref[block, D:EXPERT_ROWS, :].astype(F32))
        middle = EXPERT_ROWS + ATTN_ROWS // 2
        back += all_ref[block, EXPERT_ROWS:middle, :].astype(F32)
        attn_row += folded(all_ref[block, middle : middle + 96, :].astype(F32))
        final = all_ref[block, middle + 96 :, :].astype(F32)
        attn_row += jnp.where(lanes < HEAD_DIM, folded(final), 0.0)
        small += final
    attn_row += folded(back)
    small_row = folded(small)
    is_router = (lanes >= LANES) & (lanes < LANES + EXPERTS)
    is_gain = (lanes >= LANES + EXPERTS) & (lanes < LANES + EXPERTS + 2)
    sums = [
        jnp.where(is_gain, small_row, 0.0),
        attn_row,
        jnp.where(is_router, small_row, 0.0),
        in_row,
        out_row,
    ]
    places = lax.broadcasted_iota(jnp.int32, (8, LANES), 1)
    tile = jnp.zeros((8, LANES), F32)
    for index, row in enumerate(sums):
        tile = jnp.where(places == index, jnp.sum(row, axis=1, keepdims=True), tile)

    def shared(one, slots, send, recv, tile):
        slots[one.me] = tile
        copies = []
        for index, peer in enumerate((one.right, one.left, one.across)):
            spot = slots.at[one.me]
            copies.append(one.copy(spot, spot, send.at[index], recv.at[index], peer))
            copies[-1].start()
        for copy in copies:
            copy.wait()
        return (slots[0] + slots[1]) + (slots[2] + slots[3])

    tile = shared(ring_y, from_y, sems[0], sems[1], tile)
    return shared(ring_z, from_z, sems[2], sems[3], tile)


def sum_shards_kernel(
    experts, attn, upper_half_ref, lower_out_ref, upper_out_ref, lower_grad_ref, upper_grad_ref,
    all_ref, squares_ref, outputs_ref, grads_ref, *rest,
):
    halves, rest = rest[:HALF_REFS], rest[HALF_REFS:]
    in_y, in_z, sent_out, sent_grad, sent_half, local, send_s, recv_s, send_w, recv_w, *rest = rest
    spread, rest = rest[:8], rest[8:]
    ring_x = Ring("x")
    section = lax.axis_index("section")
    sibling = {"section": 1 - section}
    first_core = section == 0
    part_y, part_z = halves[:2]

    def make_y(index, block):
        ready(index, 0)
        add_block(part_y, in_y, block)

    def make_z(index, block):
        ready(index, 1)
        ready(index, 2)
        add_block(part_z, in_z, block)

    sums = HalfSums(halves, rest, make_y, make_z)
    ring_y, ring_z = sums.ring_y, sums.ring_z
    far = [one.place(one.across) for one in (ring_y, ring_z)]
    greet_ids([sibling] + ring_x.near() + ring_y.near() + ring_z.near() + far)

    def pieces(index, half, target_y, target_z):
        b_y, b_z = ring_y.order()[index], ring_z.order()[index]
        sources = half_sources(half, experts, attn)
        return (
            (sources[0].at[:, b_y], target_y.at[b_y]),
            (sources[1].at[b_z], target_z.at[b_z, :, pl.ds(0, Z_CUT), :]),
            (sources[2].at[b_z], target_z.at[b_z, :, pl.ds(Z_CUT, ATTN_ROWS), :]),
        )

    def fetch(index, number, source, target):
        return pltpu.make_async_copy(source, target, local.at[index * 3 + number])

    def pass_on(source, target, send, recv):
        return pltpu.make_async_remote_copy(
            src_ref=source,
            dst_ref=target,
            send_sem=send,
            recv_sem=recv,
            device_id=sibling,
            device_id_type=MESH,
        )

    def lend(index, number, source, target):
        at = index * 3 + number
        return pass_on(source, target, send_s.at[at], recv_s.at[at])

    def ready(index, number):
        source, target = pieces(index, 0, part_y, part_z)[number]
        fetch(index, number, source, target).wait()
        source, target = pieces(index, 0, in_y, in_z)[number]
        lend(index, number, source, target).wait_recv()

    def start(kept):
        for index in range(CTX):
            for number, pair in enumerate(pieces(index, kept, part_y, part_z)):
                fetch(index, number, *pair).start()

    def hand(given):
        for index in range(CTX):
            for number, pair in enumerate(pieces(index, given, in_y, in_z)):
                lend(index, number, *pair).start()

    for core in range(2):

        @pl.when(section == core)
        def _():
            start(core)

    met(9)
    own_at = pl.ds(pl.multiple_of(section * HALF_SHARD, HALF_SHARD), HALF_SHARD)
    own = all_ref.at[ring_x.me, own_at]
    cuts = (pl.ds(0, HALF_SHARD), pl.ds(HALF_SHARD, HALF_SHARD))
    rows = RingGather(ring_x, lambda b, h: all_ref.at[b, cuts[h]], spread[0], spread[1])

    @pl.when(first_core)
    def _():
        pass_on(upper_half_ref, own, send_w.at[2], recv_w.at[2]).start()

    @pl.when(section == 1)
    def _():
        own[...] = upper_half_ref[...]

    for core in range(2):

        @pl.when(section == core)
        def _():
            hand(1 - core)

    lower_out, upper_out = lower_out_ref[...], upper_out_ref[...]
    outputs_ref[section] = jnp.where(first_core, lower_out, upper_out)
    sent_out[...] = jnp.where(first_core, upper_out, lower_out)
    lower_grad, upper_grad = lower_grad_ref[...], upper_grad_ref[...]
    grads_ref[section] = jnp.where(first_core, lower_grad, upper_grad)
    sent_grad[...] = jnp.where(first_core, upper_grad, lower_grad)
    swaps = [
        pass_on(sent_out, outputs_ref.at[section], send_w.at[0], recv_w.at[0]),
        pass_on(sent_grad, grads_ref.at[section], send_w.at[1], recv_w.at[1]),
    ]
    for number in range(3):
        sums.first(number)

    @pl.when(section == 1)
    def _():
        pass_on(sent_half, own, send_w.at[2], recv_w.at[2]).wait_recv()
        rows.start()

    for copy in swaps:
        copy.start()
    sums.first(3)
    sums.first(4)

    @pl.when(section == 1)
    def _():
        rows.forward()

    sums.first(5)
    for number in range(6):
        sums.then(number)

    @pl.when(first_core)
    def _():
        sums.result(own)
        pass_on(upper_half_ref, own, send_w.at[2], recv_w.at[2]).wait()
        rows.start()
        rows.forward()

    @pl.when(section == 1)
    def _():
        sums.result(sent_half)
        back = pass_on(sent_half, own, send_w.at[2], recv_w.at[2])
        back.start()
        back.wait_send()

    rows.near()
    rows.far()
    squares_ref[...] = shared_squares(all_ref, ring_y, ring_z, spread[2:])
    rows.sent()
    for copy in swaps:
        copy.wait()
    for index in range(CTX):
        for number, pair in enumerate(pieces(index, 0, in_y, in_z)):
            lend(index, number, *pair).wait_send()


def by_place(array):
    return array.reshape((CTX, CTX) + array.shape[1:])


def sum_shards(lower_e, lower_a, upper_half, lower_out, upper_out, lower_grad, upper_grad):
    return pl.pallas_call(
        sum_shards_kernel,
        out_shape=(
            jax.ShapeDtypeStruct((CTX, SHARD_ROWS, UNIT), BF16),
            jax.ShapeDtypeStruct((8, LANES), F32),
            jax.ShapeDtypeStruct((2, ROWS, D), BF16),
            jax.ShapeDtypeStruct((2, ROWS, D), F32),
        ),
        in_specs=[ANY] * 2 + [VMEM] * 5,
        out_specs=[VMEM] * 4,
        scratch_shapes=half_scratch()
        + [
            pltpu.VMEM((CTX, CTX, Y_ROWS, UNIT), BF16),
            pltpu.VMEM((CTX, CTX, Z_ROWS, UNIT), BF16),
            pltpu.VMEM((ROWS, D), BF16),
            pltpu.VMEM((ROWS, D), F32),
            pltpu.VMEM((HALF_SHARD, UNIT), BF16),
        ]
        + [SEMS((12,))] * 3
        + [SEMS((3,))] * 2
        + [SEMS((6,))] * 2
        + [pltpu.VMEM((CTX, 8, LANES), F32)] * 2
        + [SEMS((3,))] * 4
        + [SEMS((6,))] * 8,
        compiler_params=params(8),
        name="sum_shards",
    )(by_place(lower_e), by_place(lower_a), upper_half, lower_out, upper_out, lower_grad, upper_grad)


def inverse_size(values):
    return lax.rsqrt(jnp.mean(values * values, axis=1, keepdims=True) + EPS_NORM)


def unpack(pack_ref, back_ref, heads_ref):
    def body(index, _):
        rows = pl.ds(pl.multiple_of(index * 48, 16), 48)
        for piece in range(6):
            target = back_ref if piece < 3 else heads_ref
            at = (piece % 3) * UNIT
            target[rows, at : at + UNIT] = pack_ref[index, piece * 48 : (piece + 1) * 48, :]
        return 0

    lax.fori_loop(0, 16, body, 0)


def repack(back_ref, heads_ref, pack_ref):
    def body(index, _):
        rows = pl.ds(pl.multiple_of(index * 48, 16), 48)
        for piece in range(6):
            source = back_ref if piece < 3 else heads_ref
            at = (piece % 3) * UNIT
            pack_ref[index, piece * 48 : (piece + 1) * 48, :] = source[rows, at : at + UNIT]
        return 0

    lax.fori_loop(0, 16, body, 0)


def extend(heads_ref, w_ref):
    lanes = lax.broadcasted_iota(jnp.int32, (D, WIDE), 1)
    for head in range(3 * HEADS_DEV):
        at = head // 2 * WIDE
        values = heads_ref[:, at : at + WIDE].astype(F32)
        if head % 2:
            values = pltpu.roll(values, HEAD_DIM, 1)
        if head < 2 * HEADS_DEV:
            upper = jnp.where(
                lanes < 96, -pltpu.roll(values, 32, 1), pltpu.roll(values, 96, 1)
            )
        else:
            upper = jnp.zeros_like(values)
        w_ref[:, head * WIDE : (head + 1) * WIDE] = jnp.where(
            lanes < HEAD_DIM, values, upper
        ).astype(BF16)


def attn_forward_kernel(
    layer, length_ref, u_ref, packs_ref, table_ref,
    a_out, qkv_out, mass_out, attended_ref, residual_ref, b_ref,
    gains_ref, router_ref, w_out, back_out,
    a_ref, qkv_ref, mass_ref, w_ref, back_ref, out_sem,
    heads_out, heads_w, pack_ref, pack_sem, send_a, recv_a, send_o, recv_o,
):
    me, right, left, across = ring()
    load = pltpu.make_async_copy(packs_ref.at[layer], pack_ref, pack_sem)
    load.start()
    greet((right, left, across))
    length = length_ref[0]
    tokens = u_ref[...].astype(F32)
    load.wait()
    unpack(pack_ref, back_ref, heads_w)
    leaving = [
        pltpu.make_async_copy(source, target, out_sem.at[index])
        for index, (source, target) in enumerate(
            ((back_ref, back_out), (w_ref, w_out), (a_ref, a_out), (qkv_ref, qkv_out), (mass_ref, mass_out))
        )
    ]
    leaving[0].start()
    router_ref[...] = heads_w[:, D - LANES :]
    places = lax.broadcasted_iota(jnp.int32, (8, LANES), 0) + EXPERTS
    picker = jnp.where(places == lax.broadcasted_iota(jnp.int32, (8, LANES), 1), 1.0, 0.0)
    gains_ref[...] = dot_nt(picker.astype(BF16), router_ref[...])
    a_ref[rows_of(me), :] = (tokens * inverse_size(tokens) * gains_ref[0:1, :]).astype(BF16)
    met(3)
    gather_rows(a_ref, send_a, recv_a, lambda: extend(heads_w, w_ref))
    leaving[1].start()
    leaving[2].start()
    for block in range(CTX):
        rows = pl.ds(block * ROWS, ROWS)
        table = table_ref[rows, :]
        mixed = dot(a_ref[rows, :], w_ref[...])
        for part in range(3 * HEADS_DEV):
            lanes = slice(part * WIDE, (part + 1) * WIDE)
            piece = mixed[:, lanes]
            if part < 2 * HEADS_DEV:
                turned = piece * table
                piece = turned + pltpu.roll(turned, WIDE // 2, 1)
            qkv_ref[rows, lanes] = piece.astype(BF16)
    leaving[3].start()

    def handed(block):
        step = lax.rem(block - me + CTX, CTX)
        return remote(
            heads_out.at[block], attended_ref.at[me], send_o.at[step], recv_o.at[step], block
        )

    for block in reversed(range(CTX)):
        rows = pl.ds(block * ROWS, ROWS)
        keys = (block + 1) * ROWS
        allowed = allowed_keys(block, keys, length)
        outs = []
        for head in range(HEADS_DEV):
            queries = qkv_ref[rows, head * WIDE : (head + 1) * WIDE]
            key_lanes = slice((HEADS_DEV + head) * WIDE, (HEADS_DEV + head + 1) * WIDE)
            value_lanes = slice((2 * HEADS_DEV + head) * WIDE, (2 * HEADS_DEV + head + 1) * WIDE)
            scores = dot_nt(queries, qkv_ref[:keys, key_lanes]) * SCORE_SCALE
            scores = jnp.where(allowed, scores, MASK_VALUE)
            top = jnp.max(scores, axis=1, keepdims=True)
            raw = jnp.exp(scores - top)
            total = jnp.sum(raw, axis=1, keepdims=True)
            probs = (raw * (1.0 / total)).astype(BF16)
            outs.append(dot(probs, qkv_ref[:keys, value_lanes]))
            mass_ref[head, rows, :] = top + jnp.log(total)
        first = (outs[0] + pltpu.roll(outs[1], WIDE // 2, 1)).astype(BF16)
        second = outs[2][:, : WIDE // 2].astype(BF16)
        heads_out[block, :, :WIDE] = first
        heads_out[block, :, WIDE:] = second

        @pl.when(block != me)
        def _():
            handed(block).start()

    leaving[4].start()
    attended_ref[me] = heads_out[me]
    for step in range(1, CTX):
        pltpu.make_async_copy(heads_out.at[0], attended_ref.at[0], recv_o.at[step]).wait()
    residual = tokens
    for block in range(CTX):
        residual = residual + dot(attended_ref[block], back_ref[block * COLS : (block + 1) * COLS, :])
    residual_ref[...] = residual
    b_ref[...] = (residual * inverse_size(residual) * gains_ref[1:2, :]).astype(BF16)
    for step in range(1, CTX):
        pltpu.make_async_copy(heads_out.at[0], attended_ref.at[0], send_o.at[step]).wait()
    for copy in leaving:
        copy.wait()


def attn_forward(layer, length, u, packs, table):
    sems = pltpu.SemaphoreType.DMA
    return pl.pallas_call(
        functools.partial(attn_forward_kernel, layer),
        out_shape=(
            jax.ShapeDtypeStruct((SEQ, D), BF16),
            jax.ShapeDtypeStruct((SEQ, EXT), BF16),
            jax.ShapeDtypeStruct((HEADS_DEV, SEQ, 1), F32),
            jax.ShapeDtypeStruct((CTX, ROWS, COLS), BF16),
            jax.ShapeDtypeStruct((ROWS, D), F32),
            jax.ShapeDtypeStruct((ROWS, D), BF16),
            jax.ShapeDtypeStruct((8, D), F32),
            jax.ShapeDtypeStruct((D, LANES), BF16),
            jax.ShapeDtypeStruct((D, EXT), BF16),
            jax.ShapeDtypeStruct((D, D), BF16),
        ),
        in_specs=[
            SMEM,
            VMEM,
            ANY,
            VMEM,
        ],
        out_specs=[ANY] * 3 + [VMEM] * 5 + [ANY] * 2,
        scratch_shapes=[
            pltpu.VMEM((SEQ, D), BF16),
            pltpu.VMEM((SEQ, EXT), BF16),
            pltpu.VMEM((HEADS_DEV, SEQ, 1), F32),
            pltpu.VMEM((D, EXT), BF16),
            pltpu.VMEM((D, D), BF16),
            sems((5,)),
            pltpu.VMEM((CTX, ROWS, COLS), BF16),
            pltpu.VMEM((D, D), BF16),
            pltpu.VMEM((16, ATTN_ROWS, UNIT), BF16),
            sems,
        ]
        + [sems((6,)), sems((6,)), sems((CTX,)), sems((CTX,))],
        compiler_params=params(1 + 10 * layer),
        name="attn_forward",
    )(length, u, packs, table)


def attn_backward_kernel(
    hosting, length_ref, u_ref, gains_ref, router_ref, w_in, back_in, table_in,
    a_in, qkv_in, mass_in, attended_in, residual_ref, second_in, gates_ref,
    delta_ref, db_ref, gate_grad_ref, *rest,
):
    (
        w_ref, back_ref, table_ref, a_ref, qkv_ref, mass_ref, attended_ref, second_ref, in_sem, *rest,
    ) = rest[-9:] + rest[:-9]
    coming = [
        pltpu.make_async_copy(source, target, in_sem.at[index])
        for index, (source, target) in enumerate(
            (
                (back_in, back_ref), (attended_in, attended_ref), (second_in, second_ref),
                (qkv_in, qkv_ref), (mass_in, mass_ref), (table_in, table_ref), (w_in, w_ref), (a_in, a_ref),
            )
        )
    ]
    for copy in coming:
        copy.start()
    if hosting:
        upper_e, upper_a, lent, *rest = rest
    input_ref, pack_ref, lower_ref = rest[:3]
    rest = rest[3:]
    if hosting:
        half_ref, *rest = rest
        rest, hosted = rest[:15], rest[15:]
    dheads_ref, dback_ref = rest[:2]
    rest = rest[2:]
    key_acc, value_acc, dz, grads_out, grads_in, send_o, recv_o = rest[:7]
    part, across_in, from_left, from_right, send_r, recv_r = rest[7:13]
    me, right, left, across = ring()
    greet((right, left, across))
    if hosting:
        refs, (in_y, in_z, local, *sems) = hosted[:HALF_REFS], hosted[HALF_REFS:]
        part_y, part_z = refs[:2]
        section = lax.axis_index("section")
        sums = HalfSums(
            refs,
            sems,
            lambda index, block: add_block(part_y, in_y, block),
            lambda index, block: add_block(part_z, in_z, block),
        )
        greet_ids(sums.ring_y.near() + sums.ring_z.near())

        def loads(half):
            sources = half_sources(half, upper_e, upper_a)
            pairs = [
                (sources[1], part_z.at[:, :, pl.ds(0, Z_CUT), :]),
                (sources[2], part_z.at[:, :, pl.ds(Z_CUT, ATTN_ROWS), :]),
                (lent.at[:, :, pl.ds(Y_ROWS, Z_ROWS), :], in_z),
            ]
            for block in range(CTX):
                pairs.append((sources[0].at[:, block], part_y.at[block]))
                pairs.append((lent.at[:, block, pl.ds(0, Y_ROWS), :], in_y.at[block]))
            return [
                pltpu.make_async_copy(source, target, local.at[index])
                for index, (source, target) in enumerate(pairs)
            ]

        for core in range(2):

            @pl.when(section == core)
            def _():
                for copy in loads(core):
                    copy.start()

    length = length_ref[0]
    lanes = lax.broadcasted_iota(jnp.int32, (ROWS, LANES), 1)
    gates = gates_ref[...]
    gate_grads = jnp.where(lanes < EXPERTS, gate_grad_ref[...], 0.0)
    logit_grad = gates * (gate_grads - jnp.sum(gates * gate_grads, axis=1, keepdims=True))
    logit_grad = logit_grad.astype(BF16)
    second_grad = db_ref[...] + dot_nt(logit_grad, router_ref[...])
    residual = residual_ref[...]
    scale_two = inverse_size(residual)
    normal_two = residual * scale_two
    gain_two_terms = second_grad * normal_two
    scaled_two = second_grad * gains_ref[1:2, :]
    residual_grad = delta_ref[...].astype(F32) + scale_two * (
        scaled_two - normal_two * jnp.mean(scaled_two * normal_two, axis=1, keepdims=True)
    )
    input_ref[...] = residual_grad
    branch_grad = residual_grad.astype(BF16)
    met(7 if hosting else 3)
    coming[0].wait()

    for block in range(CTX):
        grads_out[block] = dot_nt(branch_grad, back_ref[block * COLS : (block + 1) * COLS, :]).astype(
            BF16
        )

        @pl.when(block != me)
        def _():
            step = lax.rem(block - me + CTX, CTX)
            remote(
                grads_out.at[block], grads_in.at[me], send_o.at[step], recv_o.at[step], block
            ).start()

    grads_in[me] = grads_out[me]
    if hosting:
        for copy in loads(0):
            copy.wait()
        for number in range(3):
            sums.first(number)
    coming[1].wait()
    coming[2].wait()
    for block in range(CTX):
        dback_ref[block * COLS : (block + 1) * COLS, :] = dot_tn(
            attended_ref[block], branch_grad
        ).astype(BF16)
    router_terms = dot_tn(second_ref[...], logit_grad)
    ones = jnp.ones((ROWS, LANES), F32)
    gain_two_column = lax.dot_general(
        gain_two_terms, ones, TN, precision=EXACT, preferred_element_type=F32
    )
    key_acc[...] = jnp.zeros_like(key_acc)
    value_acc[...] = jnp.zeros_like(value_acc)
    for copy in coming[3:]:
        copy.wait()
    for step in range(1, CTX):
        pltpu.make_async_copy(grads_out.at[0], grads_in.at[0], recv_o.at[step]).wait()
    for step in range(1, CTX):
        pltpu.make_async_copy(grads_out.at[0], grads_in.at[0], send_o.at[step]).wait()
    for block in range(CTX):
        rows = pl.ds(block * ROWS, ROWS)
        keys = (block + 1) * ROWS
        allowed = allowed_keys(block, keys, length)
        pair = grads_in[block, :, :WIDE]
        tail = grads_in[block, :, WIDE:]
        head_grads = (
            pair,
            pltpu.roll(pair.astype(F32), WIDE // 2, 1).astype(BF16),
            jnp.concatenate([tail, jnp.zeros_like(tail)], axis=1),
        )
        for head in range(HEADS_DEV):
            queries = qkv_ref[rows, head * WIDE : (head + 1) * WIDE]
            keys_all = qkv_ref[:keys, (HEADS_DEV + head) * WIDE : (HEADS_DEV + head + 1) * WIDE]
            values_all = qkv_ref[
                :keys, (2 * HEADS_DEV + head) * WIDE : (2 * HEADS_DEV + head + 1) * WIDE
            ]
            grads = head_grads[head]
            scores = dot_nt(queries, keys_all) * SCORE_SCALE
            probs = jnp.where(allowed, jnp.exp(scores - mass_ref[head, rows, :]), 0.0)
            prob_grad = dot_nt(grads, values_all)
            row_sum = jnp.sum(probs * prob_grad, axis=1, keepdims=True)
            score_grad = (probs * (prob_grad - row_sum)).astype(BF16)
            query_grad = dot(score_grad, keys_all) * (HEAD_DIM**-0.5)
            dz[rows, head * WIDE : (head + 1) * WIDE] = (query_grad * table_ref[rows, :]).astype(BF16)
            spot = slice(head * WIDE, (head + 1) * WIDE)
            key_acc[:keys, spot] += dot_tn(score_grad, queries)
            value_acc[:keys, spot] += dot_tn(probs.astype(BF16), grads)
        if hosting and block == 2:
            sums.first(3)
            sums.first(4)
    for block in range(CTX):
        rows = pl.ds(block * ROWS, ROWS)
        table = table_ref[rows, :] * (HEAD_DIM**-0.5)
        for head in range(HEADS_DEV):
            spot = slice(head * WIDE, (head + 1) * WIDE)
            at = (HEADS_DEV + head) * WIDE
            dz[rows, at : at + WIDE] = (key_acc[rows, spot] * table).astype(BF16)
            at = (2 * HEADS_DEV + head) * WIDE
            dz[rows, at : at + WIDE] = value_acc[rows, spot].astype(BF16)

    if hosting:
        sums.first(5)
        for number in range(3):
            sums.then(number)

    def make(block):
        part[rows_of(block), :] = dot_nt(dz[rows_of(block), :], w_ref[...]).astype(BF16)

    def beside():
        wide_lanes = lax.broadcasted_iota(jnp.int32, (D, WIDE), 1)
        pieces = []
        for piece in range(3):
            spot = slice(piece * HEADS_DEV * WIDE, (piece + 1) * HEADS_DEV * WIDE)
            terms = dot_tn(a_ref[...], dz[:, spot])
            for head in range(HEADS_DEV):
                term = terms[:, head * WIDE : (head + 1) * WIDE]
                if piece < 2:
                    term = term + jnp.where(
                        wide_lanes < HEAD_DIM // 2,
                        pltpu.roll(term, HEAD_DIM // 2, 1),
                        -pltpu.roll(term, WIDE - HEAD_DIM // 2, 1),
                    )
                pieces.append(term)
        for pair in range(4):
            joined = jnp.where(
                wide_lanes < HEAD_DIM,
                pieces[2 * pair],
                pltpu.roll(pieces[2 * pair + 1], HEAD_DIM, 1),
            )
            dheads_ref[:, pair * WIDE : (pair + 1) * WIDE] = joined.astype(BF16)
        dheads_ref[:, 4 * WIDE : 5 * WIDE] = jnp.where(
            wide_lanes < HEAD_DIM, pieces[8], 0.0
        ).astype(BF16)
        if hosting:
            sums.then(3)
            sums.then(4)

    normed_grad = reduce_rows(make, part, across_in, from_left, from_right, send_r, recv_r, beside)
    tokens = u_ref[...].astype(F32)
    scale_one = inverse_size(tokens)
    normal_one = tokens * scale_one
    gain_one_column = lax.dot_general(
        normed_grad * normal_one, ones, TN, precision=EXACT, preferred_element_type=F32
    )
    scaled_one = normed_grad * gains_ref[0:1, :]
    input_grad = input_ref[...] + scale_one * (
        scaled_one - normal_one * jnp.mean(scaled_one * normal_one, axis=1, keepdims=True)
    )
    input_ref[...] = input_grad
    small_lanes = lax.broadcasted_iota(jnp.int32, (D, LANES), 1)
    dheads_ref[:, D - LANES :] = jnp.where(
        small_lanes == EXPERTS,
        gain_one_column,
        jnp.where(small_lanes == EXPERTS + 1, gain_two_column, router_terms),
    ).astype(BF16)
    repack(dback_ref, dheads_ref, pack_ref)
    lower_ref[...] = input_grad.astype(BF16)
    if hosting:
        sums.then(5)
        sums.result(half_ref)


def attn_backward(length, arrays, upper=()):
    sems = pltpu.SemaphoreType.DMA
    out_shape = [
        jax.ShapeDtypeStruct((ROWS, D), F32),
        jax.ShapeDtypeStruct((16, ATTN_ROWS, UNIT), BF16),
        jax.ShapeDtypeStruct((ROWS, D), BF16),
    ]
    if upper:
        out_shape.append(jax.ShapeDtypeStruct((HALF_SHARD, UNIT), BF16))
    scratch = [
        pltpu.VMEM((D, D), BF16),
        pltpu.VMEM((D, D), BF16),
        pltpu.VMEM((SEQ, HEADS_DEV * WIDE), F32),
        pltpu.VMEM((SEQ, HEADS_DEV * WIDE), F32),
        pltpu.VMEM((SEQ, EXT), BF16),
        pltpu.VMEM((CTX, ROWS, COLS), BF16),
        pltpu.VMEM((CTX, ROWS, COLS), BF16),
        sems((CTX,)),
        sems((CTX,)),
    ] + REDUCE_SCRATCH
    if upper:
        scratch += half_scratch()
        scratch += [
            pltpu.VMEM((CTX, CTX, Y_ROWS, UNIT), BF16),
            pltpu.VMEM((CTX, CTX, Z_ROWS, UNIT), BF16),
            sems((11,)),
        ] + [sems((6,))] * 8
    late = (3, 4, 5, 6, 7, 8, 9, 11)
    specs = [ANY if index in late else VMEM for index in range(len(arrays))]
    for index in late:
        scratch.append(pltpu.VMEM(arrays[index].shape, arrays[index].dtype))
    scratch.append(sems((len(late),)))
    return pl.pallas_call(
        functools.partial(attn_backward_kernel, bool(upper)),
        out_shape=tuple(out_shape),
        in_specs=[SMEM] + specs + [ANY] * len(upper),
        out_specs=[VMEM] * len(out_shape),
        scratch_shapes=scratch,
        compiler_params=params(4 if upper else 3),
        name="attn_backward",
    )(length, *arrays, *(by_place(array) for array in upper))


GROUP = 4
GROUPS = 16 // GROUP
GROUP_UNITS = GROUP * LANES
SPLIT = EXPERT_ROWS // 2
SUM_SCRATCH = [
    pltpu.VMEM((CTX, ROWS, D), BF16),
    pltpu.VMEM((HALF, D), BF16),
    pltpu.VMEM((HALF, D), BF16),
    pltpu.VMEM((ROWS, D), BF16),
    pltpu.VMEM((ROWS, D), BF16),
    SEMS((6,)),
    SEMS((6,)),
]


def weight_copies(w_ref, win, wout, sem):
    groups = []
    for group in range(GROUPS):
        shards = pl.ds(group * GROUP, GROUP)
        pairs = [
            (w_ref.at[0, shards], win.at[shards, pl.ds(0, SPLIT), :]),
            (w_ref.at[1, shards, pl.ds(0, D - SPLIT), :], win.at[shards, pl.ds(SPLIT, D - SPLIT), :]),
        ]
        for piece in range(D // UNIT):
            pairs.append(
                (
                    w_ref.at[1, shards, pl.ds(D - SPLIT + piece * LANES, LANES), :],
                    wout.at[shards, :, pl.ds(piece * UNIT, UNIT)],
                )
            )
        groups.append(
            [
                pltpu.make_async_copy(source, target, sem.at[group * 5 + index])
                for index, (source, target) in enumerate(pairs)
            ]
        )
    return groups


def wout_group(wout, group):
    return wout[group * GROUP : (group + 1) * GROUP].reshape(GROUP_UNITS, D)


def ffn_forward_kernel(
    b_own_ref, residual_ref, codes_ref, router_ref, w_ref,
    y_ref, b_ref, gates_ref, gate_ref, kept_ref,
    win, wout, kept_out, acc, w_sem, kept_sem, send_b, recv_b,
    part, top_in, bottom_in, from_left, from_right, send, recv,
):
    ring = Ring("x")
    greet_ids(ring.near())
    loads = weight_copies(w_ref, win, wout, w_sem)
    for group in loads:
        for copy in group:
            copy.start()
    b_ref[ring.me] = b_own_ref[...]
    met(2)
    halves = (pl.ds(0, HALF), pl.ds(HALF, HALF))
    rows = RingGather(ring, lambda b, h: b_ref.at[b, halves[h]], send_b, recv_b)
    rows.start()
    section = lax.axis_index("section")
    lanes = lax.broadcasted_iota(jnp.int32, (ROWS, LANES), 1)
    picker = jnp.where(lax.broadcasted_iota(jnp.int32, (8, LANES), 0) == section, 1.0, 0.0)
    stores = []

    def make(index, block):
        b_rows = b_ref[block]
        slot = index % 2
        for shard in range(16):
            if index == 0 and shard % GROUP == 0:
                for copy in loads[shard // GROUP]:
                    copy.wait()
            if index >= 2 and shard == 0:
                stores[index - 2].wait()
            hidden = dot(b_rows, win[shard])
            kept_out[slot, shard] = hidden.astype(BF16)
            gate_part = hidden[:, :LANES]
            at = shard % GROUP * LANES
            acc_act = (gate_part / (1.0 + jnp.exp(-gate_part)) * hidden[:, LANES:]).astype(BF16)
            if shard % GROUP == 0:
                acted = []
            acted.append(acc_act)
            if shard % GROUP == GROUP - 1:
                terms = dot(jnp.concatenate(acted, axis=1), wout_group(wout, shard // GROUP))
                acc[...] = terms if shard < GROUP else acc[...] + terms
        stores.append(pltpu.make_async_copy(kept_out.at[slot], kept_ref.at[block], kept_sem.at[slot]))
        stores[-1].start()
        logits = dot(b_rows, router_ref[...])
        codes = lax.dot_general(
            codes_ref[block], picker, TN, precision=EXACT, preferred_element_type=F32
        )
        named = (lanes < EXPERTS) & (lanes != jnp.round(codes).astype(jnp.int32))
        chosen = jnp.where(named, logits, MASK_VALUE)
        raw = jnp.where(named, jnp.exp(chosen - jnp.max(chosen, axis=1, keepdims=True)), 0.0)
        gates = raw / jnp.sum(raw, axis=1, keepdims=True)
        if index == 0:
            gates_ref[...] = gates
        gates = jnp.where(lanes == EXPERTS, 1.0, gates)
        gate = jnp.sum(jnp.where(lanes == ring.me, gates, 0.0), axis=1, keepdims=True)
        gate_ref[block] = gate
        part[block] = (acc[...] * gate).astype(BF16)

    order = {ring_index: number for number, ring_index in enumerate(("me", "right", "left", "across"))}

    def from_sum(position, block):
        make({0: order["across"], 1: order["right"], 2: order["left"], 3: order["me"]}[position], block)

    sums = RingSum(
        ring, part, (top_in, bottom_in), from_left, from_right, send, recv, HALF, from_sum
    )
    sums.stage(4)
    rows.forward()
    rows.near()
    sums.stage(1)
    sums.stage(2)
    rows.far()
    sums.stage(0)
    sums.stage(3)
    sums.stage(5)
    y_ref[...] = (residual_ref[...] + sums.total()).astype(BF16)
    rows.sent()
    stores[2].wait()
    stores[3].wait()


def ffn_forward(b_own, residual, codes, router, weights):
    return pl.pallas_call(
        ffn_forward_kernel,
        out_shape=(
            jax.ShapeDtypeStruct((ROWS, D), BF16),
            jax.ShapeDtypeStruct((CTX, ROWS, D), BF16),
            jax.ShapeDtypeStruct((ROWS, LANES), F32),
            jax.ShapeDtypeStruct((CTX, ROWS, 1), F32),
            jax.ShapeDtypeStruct((CTX, 16, ROWS, UNIT), BF16),
        ),
        in_specs=[VMEM] * 4 + [ANY],
        out_specs=[VMEM] * 4 + [ANY],
        scratch_shapes=[
            pltpu.VMEM((16, D, UNIT), BF16),
            pltpu.VMEM((16, LANES, D), BF16),
            pltpu.VMEM((2, 16, ROWS, UNIT), BF16),
            pltpu.VMEM((ROWS, D), F32),
            SEMS((5 * GROUPS,)),
            SEMS((2,)),
            SEMS((6,)),
            SEMS((6,)),
        ]
        + SUM_SCRATCH,
        compiler_params=params(5),
        name="ffn_forward",
    )(b_own, residual, codes, router, weights)


def ffn_backward_kernel(
    lending, b_ref, gate_ref, delta_own_ref, kept_ref, w_ref, *rest,
):
    if lending:
        upper_e, upper_a, db_ref, gate_grad_ref, dw_ref, lent_ref, *rest = rest
        *rest, send_l, recv_l = rest
    else:
        db_ref, gate_grad_ref, dw_ref, *rest = rest
    (
    delta, acc, gate_acc, slot_grad, hidden, acted, win, wout, staged, rows_out, rows_in, b_turned,
    w_sem, kept_sem, dw_sem, send_d, recv_d, send_g, recv_g,
    part, top_in, bottom_in, from_left, from_right, send, recv,
    ) = rest
    ring = Ring("x")
    peers = (ring.right, ring.left, ring.across)
    section = lax.axis_index("section")
    sibling = {"section": 1 - section}
    greet_ids([ring.place(peer) for peer in peers] + ([sibling] if lending else []))
    blocks = (ring.me, ring.right, ring.left, ring.across)
    kept_loads = [
        pltpu.make_async_copy(
            kept_ref.at[block], hidden.at[:, rows_of(block), :], kept_sem.at[index]
        )
        for index, block in enumerate(blocks)
    ]
    loads = weight_copies(w_ref, win, wout, w_sem)
    kept_loads[0].start()
    for group in loads:
        for copy in group:
            copy.start()
    for copy in kept_loads[1:]:
        copy.start()
    delta[ring.me] = delta_own_ref[...]
    met(4 if lending else 3)
    if lending:
        first_rows = pl.ds(0, KEPT)
        last_rows = pl.ds(KEPT, ATTN_ROWS)

        def lends(given):
            sources = (
                (upper_e.at[:, first_rows, :], upper_e.at[:, last_rows, :])
                if given == 0
                else (upper_e.at[:, pl.ds(HALF_SHARD, KEPT), :], upper_a)
            )
            return [
                pltpu.make_async_remote_copy(
                    src_ref=source,
                    dst_ref=lent_ref.at[:, target, :],
                    send_sem=send_l.at[index],
                    recv_sem=recv_l.at[index],
                    device_id=sibling,
                    device_id_type=MESH,
                )
                for index, (source, target) in enumerate(zip(sources, (first_rows, last_rows)))
            ]

        for core in range(2):

            @pl.when(section == core)
            def _():
                for copy in lends(1 - core):
                    copy.start()

    halves = (pl.ds(0, HALF), pl.ds(HALF, HALF))
    rows = RingGather(ring, lambda b, h: delta.at[b, halves[h]], send_d, recv_d)
    rows.start()
    own_row = lax.broadcasted_iota(jnp.int32, (8, LANES), 0) == ring.me
    picker = jnp.where(own_row, 1.0, 0.0)
    handed = [
        ring.copy(rows_out.at[peer], rows_in.at[index], send_g.at[index], recv_g.at[index], peer)
        for index, peer in enumerate(peers)
    ]

    def make(index, block):
        kept_loads[index].wait()
        at = rows_of(block)
        gate = gate_ref[block]
        delta_rows = delta[block]
        slot_grad[at, :] = (delta_rows.astype(F32) * gate).astype(BF16)
        gate_sum = jnp.zeros((ROWS, LANES), F32)
        for group in range(GROUPS):
            if index == 0:
                for copy in loads[group]:
                    copy.wait()
            act_grad_all = dot_nt(delta_rows, wout_group(wout, group))
            second_grad = None
            for inner in range(GROUP):
                shard = group * GROUP + inner
                values = hidden[shard, at, :].astype(F32)
                gate_part = values[:, :LANES]
                up_part = values[:, LANES:]
                act_grad = act_grad_all[:, inner * LANES : (inner + 1) * LANES]
                sigmoid = 1.0 / (1.0 + jnp.exp(-gate_part))
                silu = gate_part * sigmoid
                act = (silu * up_part).astype(BF16)
                acted[at, shard * LANES : (shard + 1) * LANES] = act
                gate_sum += act.astype(F32) * act_grad
                act_grad = act_grad * gate
                gate_grad = act_grad * up_part * (sigmoid * (1.0 + gate_part * (1.0 - sigmoid)))
                pair = jnp.concatenate([gate_grad, act_grad * silu], axis=1).astype(BF16)
                hidden[shard, at, :] = pair
                term = dot_nt(pair, win[shard])
                second_grad = term if second_grad is None else second_grad + term
            acc[...] = second_grad if group == 0 else acc[...] + second_grad
        part[block] = acc[...].astype(BF16)
        rows_out[block] = lax.dot_general(
            picker, gate_sum, NT, precision=EXACT, preferred_element_type=F32
        )
        if index > 0:
            handed[index - 1].start()

    def from_sum(position, block):
        make((3, 1, 2, 0)[position], block)

    sums = RingSum(
        ring, part, (top_in, bottom_in), from_left, from_right, send, recv, HALF, from_sum
    )
    sums.stage(4)
    b_turned[...] = b_ref[...].reshape(SEQ, D).T
    rows.forward()
    rows.near()
    sums.stage(1)
    sums.stage(2)
    rows.far()
    sums.stage(0)
    stores = []
    for group in range(GROUPS):
        slot = group % 2
        if group == 1:
            sums.stage(3)
        if group >= 2:
            stores[group - 2].wait()
        for inner in range(GROUP):
            staged[slot, inner, :D, :] = dot(b_turned[...], hidden[group * GROUP + inner]).astype(BF16)
        whole_out = dot_tn(
            acted[:, group * GROUP_UNITS : (group + 1) * GROUP_UNITS], slot_grad[...]
        ).astype(BF16)
        for inner in range(GROUP):
            for piece in range(D // UNIT):
                at = D + piece * LANES
                staged[slot, inner, at : at + LANES, :] = whole_out[
                    inner * LANES : (inner + 1) * LANES, piece * UNIT : (piece + 1) * UNIT
                ]
        stores.append(
            pltpu.make_async_copy(
                staged.at[slot], dw_ref.at[pl.ds(group * GROUP, GROUP)], dw_sem.at[slot]
            )
        )
        stores[-1].start()
    sums.stage(5)
    db_ref[...] = sums.total()
    for copy in handed:
        copy.wait()
    rows_all = rows_out[ring.me] + rows_in[0] + rows_in[1] + rows_in[2]
    diagonal = jnp.where(
        lax.broadcasted_iota(jnp.int32, (8, LANES), 0)
        == lax.broadcasted_iota(jnp.int32, (8, LANES), 1),
        1.0,
        0.0,
    )
    gate_grad_ref[...] = lax.dot_general(
        rows_all, diagonal, TN, precision=EXACT, preferred_element_type=F32
    )
    rows.sent()
    stores[2].wait()
    stores[3].wait()
    if lending:
        for copy in lends(0):
            copy.wait()


def ffn_backward(b_all, gate_col, delta_own, kept, weights, upper=()):
    out_shape = [
        jax.ShapeDtypeStruct((ROWS, D), F32),
        jax.ShapeDtypeStruct((ROWS, LANES), F32),
        jax.ShapeDtypeStruct((16, EXPERT_ROWS, UNIT), BF16),
    ]
    if upper:
        out_shape.append(jax.ShapeDtypeStruct((16, HALF_SHARD, UNIT), BF16))
    return pl.pallas_call(
        functools.partial(ffn_backward_kernel, bool(upper)),
        out_shape=out_shape,
        in_specs=[VMEM] * 3 + [ANY] * (2 + len(upper)),
        out_specs=[VMEM] * 2 + [ANY] * (len(out_shape) - 2),
        scratch_shapes=[
            pltpu.VMEM((CTX, ROWS, D), BF16),
            pltpu.VMEM((ROWS, D), F32),
            pltpu.VMEM((8, LANES), F32),
            pltpu.VMEM((SEQ, D), BF16),
            pltpu.VMEM((16, SEQ, UNIT), BF16),
            pltpu.VMEM((SEQ, FFN), BF16),
            pltpu.VMEM((16, D, UNIT), BF16),
            pltpu.VMEM((16, LANES, D), BF16),
            pltpu.VMEM((2, GROUP, EXPERT_ROWS, UNIT), BF16),
            pltpu.VMEM((CTX, 8, ROWS), F32),
            pltpu.VMEM((3, 8, ROWS), F32),
            pltpu.VMEM((D, SEQ), BF16),
            SEMS((5 * GROUPS,)),
            SEMS((CTX,)),
            SEMS((2,)),
            SEMS((6,)),
            SEMS((6,)),
            SEMS((3,)),
            SEMS((3,)),
        ]
        + SUM_SCRATCH
        + ([SEMS((2,)), SEMS((2,))] if upper else []),
        compiler_params=params(10 if upper else 6),
        name="ffn_backward",
    )(b_all, gate_col, delta_own, kept, weights, *upper)


def rotary_table():
    half_dim = HEAD_DIM // 2
    steps = 2.0 * np.arange(half_dim, dtype=np.float32) / np.float32(HEAD_DIM)
    frequency = np.exp(-np.log(np.float32(10000.0)) * steps)
    angles = np.arange(SEQ, dtype=np.float32)[:, None] * frequency[None, :]
    cosine, sine = np.cos(angles), np.sin(angles)
    return jnp.asarray(np.concatenate([cosine, cosine, sine, sine], axis=1), F32)


def layer_forward(layer, packs, experts, tokens_in, length, codes, table):
    a_all, qkv, mass, attended, residual, second, *unpacked = attn_forward(
        layer, length, tokens_in, packs, table
    )
    output, b_all, gates, gate_col, kept = ffn_forward(
        second, residual, codes, unpacked[1], experts
    )
    return output, (
        tokens_in, a_all, qkv, mass, attended, residual, second, b_all, gates, gate_col, kept, unpacked,
    )


def layer_backward(experts, saved, delta_own, length, table, upper=()):
    (
        tokens_in, a_all, qkv, mass, attended, residual, second, b_all, gates, gate_col, kept, unpacked,
    ) = saved
    db, gate_grads, dexperts, *lent = ffn_backward(b_all, gate_col, delta_own, kept, experts, upper)
    results = attn_backward(
        length,
        (
            tokens_in, *unpacked, table, a_all, qkv, mass,
            attended, residual, second, gates, delta_own, db, gate_grads,
        ),
        tuple(upper) + tuple(lent),
    )
    return dexperts, results


def factor_of(squares_ref, index):
    return jnp.minimum(1.0, CLIP_LIMIT / jnp.sqrt(squares_ref[0:1, index : index + 1]))


def updated(fixes_ref, gradient, factor, old, new, learn_rate, at=...):
    master_ref, mean_ref, square_ref = old
    gradient_ref, mean_new_ref, square_new_ref, master_new_ref, copy_ref = new
    clipped = gradient * factor
    master = master_ref[at]
    mean_new = BETA_ONE * mean_ref[at] + (1.0 - BETA_ONE) * clipped
    square_new = BETA_TWO * square_ref[at] + (1.0 - BETA_TWO) * clipped * clipped
    master_new = master - learn_rate * (
        mean_new / fixes_ref[0] / (jnp.sqrt(square_new / fixes_ref[1]) + ADAM_EPS) + DECAY_RATE * master
    )
    gradient_ref[at] = gradient
    mean_new_ref[at] = mean_new
    square_new_ref[at] = square_new
    master_new_ref[at] = master_new
    copy_ref[at] = master_new.astype(BF16)


def update_kernel(
    fixes_ref, squares_ref, in_sum_ref, out_sum_ref, attn_sum_ref, *refs,
):
    in_old, out_old, attn_old, gain_old, router_old = (refs[at : at + 3] for at in range(0, 15, 3))
    in_new, out_new, attn_new, gain_new, router_new = (refs[at : at + 5] for at in range(15, 40, 5))
    norms_ref, turned, wide = refs[40:]
    turned[pl.ds(0, D, 2), :] = in_sum_ref[0, :, :LANES].astype(F32)
    turned[pl.ds(1, D, 2), :] = in_sum_ref[0, :, LANES:].astype(F32)
    updated(
        fixes_ref, turned[...], factor_of(squares_ref, 3), in_old, in_new, RATE_FACTOR / D**0.5
    )
    pieces = [
        out_sum_ref[0, piece * LANES : (piece + 1) * LANES, :].astype(F32)
        for piece in range(D // UNIT)
    ]
    updated(
        fixes_ref,
        jnp.concatenate(pieces, axis=1),
        factor_of(squares_ref, 4),
        out_old,
        out_new,
        RATE_FACTOR / FFN**0.5,
        0,
    )

    @pl.when(pl.program_id(0) == 0)
    def _():
        back = [jnp.zeros((48, UNIT), F32) for _ in range(3)]
        small = jnp.zeros((48, UNIT), F32)
        for block in range(CTX):
            rows = [
                attn_sum_ref[block, piece * 48 : (piece + 1) * 48, :].astype(F32) for piece in range(6)
            ]
            back = [left + right for left, right in zip(back, rows[:3])]
            small = small + rows[5]
            heads = jnp.concatenate(rows[3:], axis=1)
            for part in range(3):
                at = part * D + block * COLS
                wide[:, at : at + COLS] = heads[:, part * COLS : (part + 1) * COLS]
        wide[:, 3 * D :] = jnp.concatenate(back, axis=1)
        small = small[:, LANES:]
        places = lax.broadcasted_iota(jnp.int32, (8, LANES), 0)
        picker = jnp.where(places == lax.broadcasted_iota(jnp.int32, (8, LANES), 1), 1.0, 0.0)
        turned_rows = lax.dot_general(
            picker, small, NT, precision=EXACT, preferred_element_type=F32
        )
        gain_rows = turned_rows[EXPERTS : EXPERTS + 2]
        updated(fixes_ref, gain_rows, factor_of(squares_ref, 0), gain_old, gain_new, GAIN_RATE)
        for expert in range(EXPERTS):
            updated(
                fixes_ref,
                turned_rows[expert : expert + 1],
                factor_of(squares_ref, 2),
                router_old,
                router_new,
                RATE_FACTOR / (D // 4) ** 0.5,
                expert,
            )
        norms_ref[...] = jnp.sqrt(squares_ref[...])
        for part in range(4):
            lanes = (slice(None), slice(part * D, (part + 1) * D))
            updated(
                fixes_ref,
                wide[lanes],
                factor_of(squares_ref, 1),
                attn_old,
                attn_new,
                RATE_FACTOR / D**0.5,
                lanes,
            )


def update(fixes, squares, sums_all, in_old, out_old, attn_old, gain_old, router_old):
    in_rows, units = 2 * D, LANES
    in_shape, out_shape, attn_shape = (CTX * in_rows, units), (CTX, units, D), (48, 4 * D)
    in_spec = pl.BlockSpec((in_rows, units), lambda i: (i, 0))
    out_spec = pl.BlockSpec((1, units, D), lambda i: (i, 0, 0))
    attn_spec = whole(attn_shape)
    gain_shape, router_shape = (2, 48), (EXPERTS, 1, 48)

    def five(shape):
        return [jax.ShapeDtypeStruct(shape, F32)] * 4 + [jax.ShapeDtypeStruct(shape, BF16)]

    return pl.pallas_call(
        update_kernel,
        grid=(CTX,),
        out_shape=five(in_shape)
        + five(out_shape)
        + five(attn_shape)
        + five(gain_shape)
        + five(router_shape)
        + [jax.ShapeDtypeStruct((8, LANES), F32)],
        in_specs=[
            SMEM,
            whole((8, LANES)),
            pl.BlockSpec((1, D, UNIT), lambda i: (i, 0, 0)),
            pl.BlockSpec((1, D // 2, UNIT), lambda i: (i, 2, 0)),
            pl.BlockSpec((CTX, ATTN_ROWS, UNIT), lambda i: (0, EXPERT_ROWS // ATTN_ROWS, 0)),
        ]
        + [in_spec] * 3
        + [out_spec] * 3
        + [attn_spec] * 3
        + [whole(gain_shape)] * 3
        + [whole(router_shape)] * 3,
        out_specs=[in_spec] * 5
        + [out_spec] * 5
        + [attn_spec] * 5
        + [whole(gain_shape)] * 5
        + [whole(router_shape)] * 5
        + [whole((8, LANES))],
        scratch_shapes=[pltpu.VMEM((in_rows, units), F32), pltpu.VMEM(attn_shape, F32)],
        compiler_params=pltpu.CompilerParams(vmem_limit_bytes=VMEM_LIMIT),
        name="update",
    )(
        fixes, squares, sums_all, sums_all, sums_all,
        *(array.reshape(in_shape) for array in in_old),
        *(array.reshape(out_shape) for array in out_old),
        *(array.reshape(attn_shape) for array in attn_old),
        *(array.reshape(gain_shape) for array in gain_old),
        *(array.transpose(2, 0, 1) for array in router_old),
    )


def on_device(
    inputs, cotangent, lengths, routes, step_count,
    norm_gains, gains_mean, gains_square,
    attn_weight, attn_mean, attn_square,
    router_weight, router_mean, router_square,
    expert_in, in_mean, in_square,
    expert_out, out_mean, out_square,
):
    section = lax.axis_index("section")
    ctx_index = lax.axis_index("ctx")
    fsdp = lax.axis_size("fsdp")
    everyone = ("section", "fsdp")
    shard_rows = attn_weight.shape[1]
    units = expert_in.shape[4]
    first_core = section == 0

    def own_columns(matrix, part):
        return lax.dynamic_slice_in_dim(matrix, part * D + ctx_index * COLS, COLS, 1)

    def swap(block):
        return lax.ppermute(block, "section", [(0, 1), (1, 0)])

    attn_shard = jnp.concatenate(
        [attn_weight[0][:, 3 * D :]]
        + [own_columns(attn_weight[0], part) for part in range(3)]
        + [jnp.zeros((shard_rows, HEAD_DIM), F32), router_weight[0], norm_gains[0].T]
        + [jnp.zeros((shard_rows, LANES - EXPERTS - 2), F32)],
        axis=1,
    ).astype(BF16)
    attn_shard = attn_shard.reshape(shard_rows, 6, UNIT).transpose(1, 0, 2).reshape(-1, UNIT)
    left_out = (3 - routes[0, :, :, 0] - routes[0, :, :, 1]).astype(F32)
    packs, codes = gather_shards(attn_shard, jnp.pad(left_out, ((0, 8 - left_out.shape[0]), (0, 0))))
    packs = packs.reshape(2, fsdp, ATTN_ROWS, UNIT)
    in_shard = (
        lax.dynamic_index_in_dim(expert_in[0], ctx_index, 0, keepdims=False)
        .astype(BF16)
        .reshape(D, 2 * units)
    )
    out_shard = lax.dynamic_index_in_dim(expert_out[0], ctx_index, 0, keepdims=False).astype(BF16)
    halves = jnp.concatenate(
        [in_shard] + [out_shard[:, at : at + 2 * units] for at in range(0, D, 2 * units)], axis=0
    ).reshape(2, SPLIT, 2 * units)
    other = swap(jnp.where(first_core, halves[1], halves[0]))
    pieces = (jnp.where(first_core, halves[0], other), jnp.where(first_core, other, halves[1]))
    experts = [
        lax.all_gather(piece, everyone).reshape(2, fsdp, SPLIT, 2 * units) for piece in pieces
    ]
    length = lax.dynamic_slice_in_dim(lengths, section, 1, 0)
    tokens = lax.dynamic_index_in_dim(inputs, section, 0, keepdims=False)
    positions = ctx_index * ROWS + jnp.arange(ROWS, dtype=jnp.int32)
    seed = lax.dynamic_index_in_dim(cotangent, section, 0, keepdims=False)
    seed = jnp.where((positions < length[0])[:, None], seed, jnp.zeros_like(seed))
    table = rotary_table()

    lower_out, lower_saved = layer_forward(0, packs, experts[0], tokens, length, codes[0], table)
    upper_out, upper_saved = layer_forward(1, packs, experts[1], lower_out, length, codes[1], table)
    upper_experts, (upper_grad, upper_attn, lower_seed) = layer_backward(
        experts[1], upper_saved, seed, length, table
    )
    lower_experts, (lower_grad, lower_attn, _, upper_half) = layer_backward(
        experts[0], lower_saved, lower_seed, length, table, (upper_experts, upper_attn)
    )
    sums_all, squares, layer_outputs, input_grads = sum_shards(
        lower_experts, lower_attn, upper_half, lower_out, upper_out, lower_grad, upper_grad
    )
    step_value = step_count[0].astype(F32)
    fixes = jnp.stack([1.0 - BETA_ONE**step_value, 1.0 - BETA_TWO**step_value])
    changed = update(
        fixes,
        squares,
        sums_all,
        (expert_in, in_mean, in_square),
        (expert_out, out_mean, out_square),
        (attn_weight, attn_mean, attn_square),
        (norm_gains, gains_mean, gains_square),
        (router_weight, router_mean, router_square),
    )

    def shaped(first, like):
        return tuple(array.reshape(like.shape) for array in changed[first : first + 5])

    return (
        (layer_outputs[None], input_grads[None])
        + shaped(15, norm_gains)
        + shaped(10, attn_weight)
        + tuple(array.transpose(1, 2, 0) for array in changed[20:25])
        + shaped(0, expert_in)
        + shaped(5, expert_out)
        + (changed[25][:1, :5],)
    )


def solution(mesh):
    gains = P("section", None, "fsdp")
    rows = P("section", "fsdp", None)
    wide = P("section", None, None, None, "fsdp")
    down = P("section", None, "fsdp", None)
    tokens = P("section", "fsdp", "ctx", None)
    return jax.shard_map(
        on_device,
        mesh=mesh,
        in_specs=(
            P("fsdp", "ctx", None),
            P("fsdp", "ctx", None),
            P("fsdp"),
            tokens,
            P(),
        )
        + (gains,) * 3
        + (rows,) * 6
        + (wide,) * 3
        + (down,) * 3,
        out_specs=(tokens, tokens)
        + (gains,) * 5
        + (rows,) * 10
        + (wide,) * 5
        + (down,) * 5
        + (P("section", None),),
        check_vma=False,
    )
```

```python
import functools

import jax
import jax.numpy as jnp
import numpy as np
from jax import lax
from jax.experimental import pallas as pl
from jax.experimental.pallas import tpu as pltpu
from jax.sharding import PartitionSpec as P

D = 768
HEADS = 12
HEAD_DIM = 64
FFN = 2048
EXPERTS = 3
ROWS = 256
CTX = 4
SEQ = ROWS * CTX
HEADS_DEV = HEADS // CTX
WIDE = 128
EXT = 3 * HEADS_DEV * WIDE
COLS = HEADS_DEV * HEAD_DIM

EPS_NORM = 1e-06
BETA_ONE = 0.9
BETA_TWO = 0.95
RATE_FACTOR = 3.0
GAIN_RATE = 0.3
DECAY_RATE = 0.1
ADAM_EPS = 1e-08
CLIP_LIMIT = 1.0
MASK_VALUE = -1e30
SCORE_SCALE = HEAD_DIM ** (-0.5) / 2.0
BF16 = jnp.bfloat16
F32 = jnp.float32
VMEM_LIMIT = 56 * 1024 * 1024
NT = (((1,), (1,)), ((), ()))
TN = (((0,), (0,)), ((), ()))
HALF = ROWS // 2
LANES = 128
MESH = pl.DeviceIdType.MESH
EXACT = lax.Precision.HIGHEST


def dot(left, right):
    return jnp.dot(left, right, preferred_element_type=F32)


def dot_nt(left, right):
    return lax.dot_general(left, right, NT, preferred_element_type=F32)


def dot_tn(left, right):
    return lax.dot_general(left, right, TN, preferred_element_type=F32)


def params(collective_id):
    return pltpu.CompilerParams(
        vmem_limit_bytes=VMEM_LIMIT, collective_id=collective_id, has_side_effects=True
    )


def whole(shape):
    return pl.BlockSpec(shape, lambda *_: (0,) * len(shape))


def allowed_keys(block, keys, length):
    key_pos = lax.broadcasted_iota(jnp.int32, (ROWS, keys), 1)
    query_pos = lax.broadcasted_iota(jnp.int32, (ROWS, keys), 0) + block * ROWS
    return (key_pos <= query_pos) & (key_pos < length)


VMEM = pl.BlockSpec(memory_space=pltpu.VMEM)
SMEM = pl.BlockSpec(memory_space=pltpu.SMEM)
ANY = pl.BlockSpec(memory_space=pl.ANY)


def ring():
    me = lax.axis_index("ctx")
    return me, lax.rem(me + 1, CTX), lax.rem(me + 3, CTX), lax.rem(me + 2, CTX)


def greet(peers):
    barrier = pltpu.get_barrier_semaphore()
    for peer in peers:
        pl.semaphore_signal(barrier, inc=1, device_id={"ctx": peer}, device_id_type=MESH)


def met(count):
    pl.semaphore_wait(pltpu.get_barrier_semaphore(), count)


def remote(source, target, send, recv, peer):
    return pltpu.make_async_remote_copy(
        src_ref=source,
        dst_ref=target,
        send_sem=send,
        recv_sem=recv,
        device_id={"ctx": peer},
        device_id_type=MESH,
    )


def rows_of(block, half=None):
    if half is None:
        return pl.ds(pl.multiple_of(block * ROWS, ROWS), ROWS)
    return pl.ds(pl.multiple_of(block * ROWS + half * HALF, HALF), HALF)


def gather_rows(all_ref, send, recv, beside=None):
    me, right, left, _ = ring()

    def piece(index, block, half, peer):
        spot = all_ref.at[rows_of(block, half)]
        return remote(spot, spot, send.at[index], recv.at[index], peer)

    copies = [
        piece(0, me, 0, right),
        piece(1, me, 1, left),
        piece(2, me, 1, right),
        piece(3, me, 0, left),
    ]
    for copy in copies:
        copy.start()
    if beside is not None:
        beside()
    copies[0].wait_recv()
    copies.append(piece(4, left, 0, right))
    copies[4].start()
    copies[1].wait_recv()
    copies.append(piece(5, right, 1, left))
    copies[5].start()
    for index in range(2, 6):
        copies[index].wait_recv()
    for copy in copies:
        copy.wait_send()


def reduce_rows(make, part, across_in, from_left, from_right, send, recv, beside=None):
    me, right, left, across = ring()
    top, bottom = pl.ds(0, HALF), pl.ds(HALF, HALF)

    def piece(index, block, half, target, peer):
        return remote(part.at[rows_of(block, half)], target, send.at[index], recv.at[index], peer)

    make(across)
    copies = [
        piece(0, across, 0, across_in.at[0], right),
        piece(1, across, 1, across_in.at[1], left),
    ]
    copies[0].start()
    copies[1].start()
    make(right)
    copies.append(piece(2, right, 1, from_left.at[bottom], right))
    copies[2].start()
    make(left)
    copies.append(piece(3, left, 0, from_right.at[top], left))
    copies[3].start()
    copies[0].wait_recv()
    spot = rows_of(right, 0)
    part[spot, :] = (part[spot, :].astype(F32) + across_in[0].astype(F32)).astype(BF16)
    copies.append(piece(4, right, 0, from_left.at[top], right))
    copies[4].start()
    copies[1].wait_recv()
    spot = rows_of(left, 1)
    part[spot, :] = (part[spot, :].astype(F32) + across_in[1].astype(F32)).astype(BF16)
    copies.append(piece(5, left, 1, from_right.at[bottom], left))
    copies[5].start()
    make(me)
    if beside is not None:
        beside()
    for index in range(2, 6):
        copies[index].wait_recv()
    for copy in copies:
        copy.wait_send()
    return (
        part[rows_of(me), :].astype(F32) + from_left[...].astype(F32) + from_right[...].astype(F32)
    )


REDUCE_SCRATCH = [
    pltpu.VMEM((SEQ, D), BF16),
    pltpu.VMEM((2, HALF, D), BF16),
    pltpu.VMEM((ROWS, D), BF16),
    pltpu.VMEM((ROWS, D), BF16),
    pltpu.SemaphoreType.DMA((6,)),
    pltpu.SemaphoreType.DMA((6,)),
]


def greet_ids(peers):
    barrier = pltpu.get_barrier_semaphore()
    for peer in peers:
        pl.semaphore_signal(barrier, inc=1, device_id=peer, device_id_type=MESH)


class Ring:
    def __init__(self, axis):
        if axis == "x":
            self.me = lax.axis_index("ctx")
            self.place = lambda index: {"ctx": index}
        else:
            shard = lax.axis_index("fsdp")
            inner, outer = lax.rem(shard, CTX), lax.div(shard, CTX)
            if axis == "y":
                self.me = inner
                self.place = lambda index: {"fsdp": outer * CTX + index}
            else:
                self.me = outer
                self.place = lambda index: {"fsdp": index * CTX + inner}
        self.right = lax.rem(self.me + 1, CTX)
        self.left = lax.rem(self.me + 3, CTX)
        self.across = lax.rem(self.me + 2, CTX)

    def order(self):
        return (self.across, self.right, self.left, self.me)

    def near(self):
        return [self.place(self.right), self.place(self.left)]

    def copy(self, source, target, send, recv, index):
        return pltpu.make_async_remote_copy(
            src_ref=source,
            dst_ref=target,
            send_sem=send,
            recv_sem=recv,
            device_id=self.place(index),
            device_id_type=MESH,
        )


class RingGather:
    def __init__(self, ring, at, send, recv):
        self.ring, self.at, self.send, self.recv = ring, at, send, recv
        self.sends = (
            (ring.me, 0, ring.right),
            (ring.me, 1, ring.left),
            (ring.me, 1, ring.right),
            (ring.me, 0, ring.left),
            (ring.left, 0, ring.right),
            (ring.right, 1, ring.left),
        )

    def piece(self, index, block, half, to):
        spot = self.at(block, half)
        return self.ring.copy(spot, spot, self.send.at[index], self.recv.at[index], to)

    def go(self, index):
        self.piece(index, *self.sends[index]).start()

    def landed(self, index, block, half):
        self.piece(index, block, half, self.ring.right).wait_recv()

    def start(self):
        for index in range(4):
            self.go(index)

    def forward(self):
        self.landed(0, self.ring.left, 0)
        self.go(4)
        self.landed(1, self.ring.right, 1)
        self.go(5)

    def near(self):
        self.landed(2, self.ring.left, 1)
        self.landed(3, self.ring.right, 0)

    def far(self):
        self.landed(4, self.ring.across, 0)
        self.landed(5, self.ring.across, 1)

    def sent(self):
        for index in range(6):
            self.piece(index, *self.sends[index]).wait_send()

    def finish(self):
        self.near()
        self.far()
        self.sent()


class RingSum:
    def __init__(self, ring, part, across_in, from_left, from_right, send, recv, cut, make):
        self.ring, self.part, self.across_in = ring, part, across_in
        self.from_left, self.from_right, self.send, self.recv = from_left, from_right, send, recv
        size = part.shape[1]
        self.halves = (pl.ds(0, cut), pl.ds(cut, size - cut))
        self.make = make
        self.copies = {}

    def go(self, index, block, half, target, to):
        self.copies[index] = self.ring.copy(
            self.part.at[block, self.halves[half]], target, self.send.at[index], self.recv.at[index], to
        )
        self.copies[index].start()

    def arrived(self, half, block):
        self.copies[half].wait_recv()
        incoming = self.across_in[half]
        if len(self.part.shape) == 3:
            spot = (block, self.halves[half])
            self.part[spot] = (self.part[spot].astype(F32) + incoming[...].astype(F32)).astype(BF16)
            return
        start = (0, self.part.shape[1] - incoming.shape[0])[half]
        for index in range(incoming.shape[0]):
            self.part[block, start + index] = (
                self.part[block, start + index].astype(F32) + incoming[index].astype(F32)
            ).astype(BF16)

    def stage(self, number):
        ring = self.ring
        if number == 0:
            self.make(0, ring.across)
            self.go(0, ring.across, 0, self.across_in[0], ring.right)
            self.go(1, ring.across, 1, self.across_in[1], ring.left)
        elif number == 1:
            self.make(1, ring.right)
            self.go(2, ring.right, 1, self.from_left.at[self.halves[1]], ring.right)
        elif number == 2:
            self.make(2, ring.left)
            self.go(3, ring.left, 0, self.from_right.at[self.halves[0]], ring.left)
        elif number == 3:
            self.arrived(0, ring.right)
            self.go(4, ring.right, 0, self.from_left.at[self.halves[0]], ring.right)
            self.arrived(1, ring.left)
            self.go(5, ring.left, 1, self.from_right.at[self.halves[1]], ring.left)
        elif number == 4:
            self.make(3, ring.me)
        else:
            for index in range(2, 6):
                self.copies[index].wait_recv()
            for index in range(6):
                self.copies[index].wait_send()

    def total(self, index=None):
        spot = (self.ring.me,) if index is None else (self.ring.me, index)
        tail = () if index is None else (index,)
        return (
            self.part[spot].astype(F32)
            + self.from_left[tail or ...].astype(F32)
            + self.from_right[tail or ...].astype(F32)
        )


UNIT = 256
EXPERT_ROWS = D + D // 2
ATTN_ROWS = 288
SHARD_ROWS = EXPERT_ROWS + ATTN_ROWS
FIRST = SHARD_ROWS // 2
KEPT = EXPERT_ROWS - FIRST
CUT = 352
SEMS = pltpu.SemaphoreType.DMA


def gather_shards_kernel(shard_ref, code_ref, out_ref, codes_ref, *sems):
    section = lax.axis_index("section")
    sibling = {"section": 1 - section}
    ring_y, ring_z = Ring("y"), Ring("z")
    y, z = ring_y.me, ring_z.me
    ring_x = Ring("x")
    x_peers = (ring_x.right, ring_x.left, ring_x.across)
    greet_ids(
        [sibling] + ring_y.near() + ring_z.near() + [ring_x.place(peer) for peer in x_peers]
    )
    out_ref[section, z, y] = shard_ref[...]
    codes_ref[section, ring_x.me] = code_ref[...]
    met(8)
    spot = codes_ref.at[section, ring_x.me]
    code_copies = [
        ring_x.copy(spot, spot, sems[10].at[index], sems[11].at[index], peer)
        for index, peer in enumerate(x_peers)
    ]
    for copy in code_copies:
        copy.start()
    half = ATTN_ROWS // 2
    low = (pl.ds(0, 64), pl.ds(64, half - 64))
    high = (pl.ds(half, 64), pl.ds(half + 64, half - 64))
    pair = (pl.ds(0, 2), pl.ds(2, 2))
    near_y = RingGather(ring_y, lambda b, h: out_ref.at[section, z, b, low[h]], sems[0], sems[1])
    near_z = RingGather(ring_z, lambda b, h: out_ref.at[section, b, y, high[h]], sems[2], sems[3])
    far_z = RingGather(
        ring_z, lambda b, h: out_ref.at[section, b, pair[h], pl.ds(0, half)], sems[4], sems[5]
    )
    far_y = RingGather(
        ring_y, lambda b, h: out_ref.at[section, pair[h], b, pl.ds(half, half)], sems[6], sems[7]
    )
    for rings in ((near_y, near_z), (far_z, far_y)):
        for one in rings:
            one.start()
        for one in rings:
            one.forward()
        for one in rings:
            one.finish()
    across = pltpu.make_async_remote_copy(
        src_ref=out_ref.at[section],
        dst_ref=out_ref.at[section],
        send_sem=sems[8],
        recv_sem=sems[9],
        device_id=sibling,
        device_id_type=MESH,
    )
    across.start()
    for copy in code_copies:
        copy.wait()
    codes_across = pltpu.make_async_remote_copy(
        src_ref=codes_ref.at[section],
        dst_ref=codes_ref.at[section],
        send_sem=sems[12],
        recv_sem=sems[13],
        device_id=sibling,
        device_id_type=MESH,
    )
    codes_across.start()
    codes_across.wait()
    across.wait()


def gather_shards(shard, codes):
    return pl.pallas_call(
        gather_shards_kernel,
        out_shape=(
            jax.ShapeDtypeStruct((2, CTX, CTX, ATTN_ROWS, UNIT), BF16),
            jax.ShapeDtypeStruct((2, CTX, 8, ROWS), F32),
        ),
        in_specs=[VMEM, VMEM],
        out_specs=[VMEM, VMEM],
        scratch_shapes=[SEMS((6,))] * 8 + [SEMS, SEMS, SEMS((3,)), SEMS((3,)), SEMS, SEMS],
        compiler_params=params(7),
        name="gather_shards",
    )(shard, codes)


HALF_SHARD = SHARD_ROWS // 2
Y_ROWS, Z_ROWS = 352, 368
Z_CUT = Z_ROWS - ATTN_ROWS


def half_sources(half, experts, attn):
    if half == 0:
        return (
            experts.at[:, :, pl.ds(0, Y_ROWS), :],
            experts.at[:, :, pl.ds(Y_ROWS, Z_CUT), :],
            experts.at[:, :, pl.ds(Y_ROWS + Z_CUT, ATTN_ROWS), :],
        )
    return (
        experts.at[:, :, pl.ds(HALF_SHARD, Y_ROWS), :],
        experts.at[:, :, pl.ds(HALF_SHARD + Y_ROWS, Z_CUT), :],
        attn,
    )


class HalfSums:
    def __init__(self, refs, sems, make_y, make_z):
        (
            self.part_y, self.part_z, top_y, bottom_y, left_y, right_y, top_z, bottom_z, left_z, right_z,
            more_z, more_y, top_zz, bottom_zz, left_zz, right_zz, top_yy, bottom_yy, left_yy, right_yy,
        ) = refs
        ring_y, ring_z = Ring("y"), Ring("z")
        self.ring_y, self.ring_z = ring_y, ring_z
        self.first_y = RingSum(
            ring_y, self.part_y, (top_y, bottom_y), left_y, right_y, sems[0], sems[1], 2, make_y
        )
        self.first_z = RingSum(
            ring_z, self.part_z, (top_z, bottom_z), left_z, right_z, sems[2], sems[3], 2, make_z
        )

        def make_zz(index, block):
            more_z[block] = self.first_y.total(block).astype(BF16)

        def make_yy(index, block):
            more_y[block] = self.first_z.total(block).astype(BF16)

        self.then_z = RingSum(
            ring_z, more_z, (top_zz, bottom_zz), left_zz, right_zz, sems[4], sems[5], Y_ROWS // 2, make_zz
        )
        self.then_y = RingSum(
            ring_y, more_y, (top_yy, bottom_yy), left_yy, right_yy, sems[6], sems[7], 176, make_yy
        )

    def first(self, number):
        self.first_y.stage(number)
        self.first_z.stage(number)

    def then(self, number):
        self.then_z.stage(number)
        self.then_y.stage(number)

    def result(self, out_ref):
        out_ref[pl.ds(0, Y_ROWS), :] = self.then_z.total().astype(BF16)
        out_ref[pl.ds(Y_ROWS, Z_ROWS), :] = self.then_y.total().astype(BF16)


def half_scratch():
    shapes = [(CTX, CTX, Y_ROWS, UNIT), (CTX, CTX, Z_ROWS, UNIT)]
    for rows in (Y_ROWS, Z_ROWS):
        shapes += [(2, rows, UNIT)] * 2 + [(CTX, rows, UNIT)] * 2
    shapes += [(CTX, Y_ROWS, UNIT), (CTX, Z_ROWS, UNIT)]
    for rows in (Y_ROWS, Z_ROWS):
        shapes += [(176, UNIT), (rows - 176, UNIT)] + [(rows, UNIT)] * 2
    return [pltpu.VMEM(shape, BF16) for shape in shapes]


HALF_REFS = 20


def add_block(part, incoming, block):
    for other in range(CTX):
        part[block, other] = (part[block, other].astype(F32) + incoming[block, other].astype(F32)).astype(
            BF16
        )


def shared_squares(all_ref, ring_y, ring_z, spread):
    from_y, from_z, *sems = spread

    def folded(values):
        squared = values * values
        return jnp.sum(squared, axis=0, keepdims=True)

    in_row = jnp.zeros((1, UNIT), F32)
    out_row = jnp.zeros((1, UNIT), F32)
    attn_row = jnp.zeros((1, UNIT), F32)
    back = jnp.zeros((ATTN_ROWS // 2, UNIT), F32)
    small = jnp.zeros((48, UNIT), F32)
    lanes = lax.broadcasted_iota(jnp.int32, (1, UNIT), 1)
    for block in range(CTX):
        in_row += folded(all_ref[block, :D, :].astype(F32))
        out_row += folded(all_ref[block, D:EXPERT_ROWS, :].astype(F32))
        middle = EXPERT_ROWS + ATTN_ROWS // 2
        back += all_ref[block, EXPERT_ROWS:middle, :].astype(F32)
        attn_row += folded(all_ref[block, middle : middle + 96, :].astype(F32))
        final = all_ref[block, middle + 96 :, :].astype(F32)
        attn_row += jnp.where(lanes < HEAD_DIM, folded(final), 0.0)
        small += final
    attn_row += folded(back)
    small_row = folded(small)
    is_router = (lanes >= LANES) & (lanes < LANES + EXPERTS)
    is_gain = (lanes >= LANES + EXPERTS) & (lanes < LANES + EXPERTS + 2)
    sums = [
        jnp.where(is_gain, small_row, 0.0),
        attn_row,
        jnp.where(is_router, small_row, 0.0),
        in_row,
        out_row,
    ]
    places = lax.broadcasted_iota(jnp.int32, (8, LANES), 1)
    tile = jnp.zeros((8, LANES), F32)
    for index, row in enumerate(sums):
        tile = jnp.where(places == index, jnp.sum(row, axis=1, keepdims=True), tile)

    def shared(one, slots, send, recv, tile):
        slots[one.me] = tile
        copies = []
        for index, peer in enumerate((one.right, one.left, one.across)):
            spot = slots.at[one.me]
            copies.append(one.copy(spot, spot, send.at[index], recv.at[index], peer))
            copies[-1].start()
        for copy in copies:
            copy.wait()
        return (slots[0] + slots[1]) + (slots[2] + slots[3])

    tile = shared(ring_y, from_y, sems[0], sems[1], tile)
    return shared(ring_z, from_z, sems[2], sems[3], tile)


def sum_shards_kernel(
    experts, attn, upper_half_ref, lower_out_ref, upper_out_ref, lower_grad_ref, upper_grad_ref,
    all_ref, squares_ref, outputs_ref, grads_ref, *rest,
):
    halves, rest = rest[:HALF_REFS], rest[HALF_REFS:]
    in_y, in_z, sent_out, sent_grad, sent_half, local, send_s, recv_s, send_w, recv_w, *rest = rest
    spread, rest = rest[:8], rest[8:]
    ring_x = Ring("x")
    section = lax.axis_index("section")
    sibling = {"section": 1 - section}
    first_core = section == 0
    part_y, part_z = halves[:2]

    def make_y(index, block):
        ready(index, 0)
        add_block(part_y, in_y, block)

    def make_z(index, block):
        ready(index, 1)
        ready(index, 2)
        add_block(part_z, in_z, block)

    sums = HalfSums(halves, rest, make_y, make_z)
    ring_y, ring_z = sums.ring_y, sums.ring_z
    far = [one.place(one.across) for one in (ring_y, ring_z)]
    greet_ids([sibling] + ring_x.near() + ring_y.near() + ring_z.near() + far)

    def pieces(index, half, target_y, target_z):
        b_y, b_z = ring_y.order()[index], ring_z.order()[index]
        sources = half_sources(half, experts, attn)
        return (
            (sources[0].at[:, b_y], target_y.at[b_y]),
            (sources[1].at[b_z], target_z.at[b_z, :, pl.ds(0, Z_CUT), :]),
            (sources[2].at[b_z], target_z.at[b_z, :, pl.ds(Z_CUT, ATTN_ROWS), :]),
        )

    def fetch(index, number, source, target):
        return pltpu.make_async_copy(source, target, local.at[index * 3 + number])

    def pass_on(source, target, send, recv):
        return pltpu.make_async_remote_copy(
            src_ref=source,
            dst_ref=target,
            send_sem=send,
            recv_sem=recv,
            device_id=sibling,
            device_id_type=MESH,
        )

    def lend(index, number, source, target):
        at = index * 3 + number
        return pass_on(source, target, send_s.at[at], recv_s.at[at])

    def ready(index, number):
        source, target = pieces(index, 0, part_y, part_z)[number]
        fetch(index, number, source, target).wait()
        source, target = pieces(index, 0, in_y, in_z)[number]
        lend(index, number, source, target).wait_recv()

    def start(kept):
        for index in range(CTX):
            for number, pair in enumerate(pieces(index, kept, part_y, part_z)):
                fetch(index, number, *pair).start()

    def hand(given):
        for index in range(CTX):
            for number, pair in enumerate(pieces(index, given, in_y, in_z)):
                lend(index, number, *pair).start()

    for core in range(2):

        @pl.when(section == core)
        def _():
            start(core)

    met(9)
    own_at = pl.ds(pl.multiple_of(section * HALF_SHARD, HALF_SHARD), HALF_SHARD)
    own = all_ref.at[ring_x.me, own_at]
    cuts = (pl.ds(0, HALF_SHARD), pl.ds(HALF_SHARD, HALF_SHARD))
    rows = RingGather(ring_x, lambda b, h: all_ref.at[b, cuts[h]], spread[0], spread[1])

    @pl.when(first_core)
    def _():
        pass_on(upper_half_ref, own, send_w.at[2], recv_w.at[2]).start()

    @pl.when(section == 1)
    def _():
        own[...] = upper_half_ref[...]

    for core in range(2):

        @pl.when(section == core)
        def _():
            hand(1 - core)

    lower_out, upper_out = lower_out_ref[...], upper_out_ref[...]
    outputs_ref[section] = jnp.where(first_core, lower_out, upper_out)
    sent_out[...] = jnp.where(first_core, upper_out, lower_out)
    lower_grad, upper_grad = lower_grad_ref[...], upper_grad_ref[...]
    grads_ref[section] = jnp.where(first_core, lower_grad, upper_grad)
    sent_grad[...] = jnp.where(first_core, upper_grad, lower_grad)
    swaps = [
        pass_on(sent_out, outputs_ref.at[section], send_w.at[0], recv_w.at[0]),
        pass_on(sent_grad, grads_ref.at[section], send_w.at[1], recv_w.at[1]),
    ]
    for number in range(3):
        sums.first(number)

    @pl.when(section == 1)
    def _():
        pass_on(sent_half, own, send_w.at[2], recv_w.at[2]).wait_recv()
        rows.start()

    for copy in swaps:
        copy.start()
    sums.first(3)
    sums.first(4)

    @pl.when(section == 1)
    def _():
        rows.forward()

    sums.first(5)
    for number in range(6):
        sums.then(number)

    @pl.when(first_core)
    def _():
        sums.result(own)
        pass_on(upper_half_ref, own, send_w.at[2], recv_w.at[2]).wait()
        rows.start()
        rows.forward()

    @pl.when(section == 1)
    def _():
        sums.result(sent_half)
        back = pass_on(sent_half, own, send_w.at[2], recv_w.at[2])
        back.start()
        back.wait_send()

    rows.near()
    rows.far()
    squares_ref[...] = shared_squares(all_ref, ring_y, ring_z, spread[2:])
    rows.sent()
    for copy in swaps:
        copy.wait()
    for index in range(CTX):
        for number, pair in enumerate(pieces(index, 0, in_y, in_z)):
            lend(index, number, *pair).wait_send()


def by_place(array):
    return array.reshape((CTX, CTX) + array.shape[1:])


def sum_shards(lower_e, lower_a, upper_half, lower_out, upper_out, lower_grad, upper_grad):
    return pl.pallas_call(
        sum_shards_kernel,
        out_shape=(
            jax.ShapeDtypeStruct((CTX, SHARD_ROWS, UNIT), BF16),
            jax.ShapeDtypeStruct((8, LANES), F32),
            jax.ShapeDtypeStruct((2, ROWS, D), BF16),
            jax.ShapeDtypeStruct((2, ROWS, D), F32),
        ),
        in_specs=[ANY] * 2 + [VMEM] * 5,
        out_specs=[VMEM] * 4,
        scratch_shapes=half_scratch()
        + [
            pltpu.VMEM((CTX, CTX, Y_ROWS, UNIT), BF16),
            pltpu.VMEM((CTX, CTX, Z_ROWS, UNIT), BF16),
            pltpu.VMEM((ROWS, D), BF16),
            pltpu.VMEM((ROWS, D), F32),
            pltpu.VMEM((HALF_SHARD, UNIT), BF16),
        ]
        + [SEMS((12,))] * 3
        + [SEMS((3,))] * 2
        + [SEMS((6,))] * 2
        + [pltpu.VMEM((CTX, 8, LANES), F32)] * 2
        + [SEMS((3,))] * 4
        + [SEMS((6,))] * 8,
        compiler_params=params(8),
        name="sum_shards",
    )(by_place(lower_e), by_place(lower_a), upper_half, lower_out, upper_out, lower_grad, upper_grad)


def inverse_size(values):
    return lax.rsqrt(jnp.mean(values * values, axis=1, keepdims=True) + EPS_NORM)


def unpack(pack_ref, back_ref, heads_ref):
    def body(index, _):
        rows = pl.ds(pl.multiple_of(index * 48, 16), 48)
        for piece in range(6):
            target = back_ref if piece < 3 else heads_ref
            at = (piece % 3) * UNIT
            target[rows, at : at + UNIT] = pack_ref[index, piece * 48 : (piece + 1) * 48, :]
        return 0

    lax.fori_loop(0, 16, body, 0)


def repack(back_ref, heads_ref, pack_ref):
    def body(index, _):
        rows = pl.ds(pl.multiple_of(index * 48, 16), 48)
        for piece in range(6):
            source = back_ref if piece < 3 else heads_ref
            at = (piece % 3) * UNIT
            pack_ref[index, piece * 48 : (piece + 1) * 48, :] = source[rows, at : at + UNIT]
        return 0

    lax.fori_loop(0, 16, body, 0)


def extend(heads_ref, w_ref):
    lanes = lax.broadcasted_iota(jnp.int32, (D, WIDE), 1)
    for head in range(3 * HEADS_DEV):
        at = head // 2 * WIDE
        values = heads_ref[:, at : at + WIDE].astype(F32)
        if head % 2:
            values = pltpu.roll(values, HEAD_DIM, 1)
        if head < 2 * HEADS_DEV:
            upper = jnp.where(
                lanes < 96, -pltpu.roll(values, 32, 1), pltpu.roll(values, 96, 1)
            )
        else:
            upper = jnp.zeros_like(values)
        w_ref[:, head * WIDE : (head + 1) * WIDE] = jnp.where(
            lanes < HEAD_DIM, values, upper
        ).astype(BF16)


def attn_forward_kernel(
    layer, length_ref, u_ref, packs_ref, table_ref,
    a_out, qkv_out, mass_out, attended_ref, residual_ref, b_ref,
    gains_ref, router_ref, w_out, back_out,
    a_ref, qkv_ref, mass_ref, w_ref, back_ref, out_sem,
    heads_out, heads_w, pack_ref, pack_sem, send_a, recv_a, send_o, recv_o,
):
    me, right, left, across = ring()
    load = pltpu.make_async_copy(packs_ref.at[layer], pack_ref, pack_sem)
    load.start()
    greet((right, left, across))
    length = length_ref[0]
    tokens = u_ref[...].astype(F32)
    load.wait()
    unpack(pack_ref, back_ref, heads_w)
    leaving = [
        pltpu.make_async_copy(source, target, out_sem.at[index])
        for index, (source, target) in enumerate(
            ((back_ref, back_out), (w_ref, w_out), (a_ref, a_out), (qkv_ref, qkv_out), (mass_ref, mass_out))
        )
    ]
    leaving[0].start()
    router_ref[...] = heads_w[:, D - LANES :]
    places = lax.broadcasted_iota(jnp.int32, (8, LANES), 0) + EXPERTS
    picker = jnp.where(places == lax.broadcasted_iota(jnp.int32, (8, LANES), 1), 1.0, 0.0)
    gains_ref[...] = dot_nt(picker.astype(BF16), router_ref[...])
    a_ref[rows_of(me), :] = (tokens * inverse_size(tokens) * gains_ref[0:1, :]).astype(BF16)
    met(3)
    gather_rows(a_ref, send_a, recv_a, lambda: extend(heads_w, w_ref))
    leaving[1].start()
    leaving[2].start()
    for block in range(CTX):
        rows = pl.ds(block * ROWS, ROWS)
        table = table_ref[rows, :]
        mixed = dot(a_ref[rows, :], w_ref[...])
        for part in range(3 * HEADS_DEV):
            lanes = slice(part * WIDE, (part + 1) * WIDE)
            piece = mixed[:, lanes]
            if part < 2 * HEADS_DEV:
                turned = piece * table
                piece = turned + pltpu.roll(turned, WIDE // 2, 1)
            qkv_ref[rows, lanes] = piece.astype(BF16)
    leaving[3].start()

    def handed(block):
        step = lax.rem(block - me + CTX, CTX)
        return remote(
            heads_out.at[block], attended_ref.at[me], send_o.at[step], recv_o.at[step], block
        )

    for block in reversed(range(CTX)):
        rows = pl.ds(block * ROWS, ROWS)
        keys = (block + 1) * ROWS
        allowed = allowed_keys(block, keys, length)
        outs = []
        for head in range(HEADS_DEV):
            queries = qkv_ref[rows, head * WIDE : (head + 1) * WIDE]
            key_lanes = slice((HEADS_DEV + head) * WIDE, (HEADS_DEV + head + 1) * WIDE)
            value_lanes = slice((2 * HEADS_DEV + head) * WIDE, (2 * HEADS_DEV + head + 1) * WIDE)
            scores = dot_nt(queries, qkv_ref[:keys, key_lanes]) * SCORE_SCALE
            scores = jnp.where(allowed, scores, MASK_VALUE)
            top = jnp.max(scores, axis=1, keepdims=True)
            raw = jnp.exp(scores - top)
            total = jnp.sum(raw, axis=1, keepdims=True)
            probs = (raw * (1.0 / total)).astype(BF16)
            outs.append(dot(probs, qkv_ref[:keys, value_lanes]))
            mass_ref[head, rows, :] = top + jnp.log(total)
        first = (outs[0] + pltpu.roll(outs[1], WIDE // 2, 1)).astype(BF16)
        second = outs[2][:, : WIDE // 2].astype(BF16)
        heads_out[block, :, :WIDE] = first
        heads_out[block, :, WIDE:] = second

        @pl.when(block != me)
        def _():
            handed(block).start()

    leaving[4].start()
    attended_ref[me] = heads_out[me]
    for step in range(1, CTX):
        pltpu.make_async_copy(heads_out.at[0], attended_ref.at[0], recv_o.at[step]).wait()
    residual = tokens
    for block in range(CTX):
        residual = residual + dot(attended_ref[block], back_ref[block * COLS : (block + 1) * COLS, :])
    residual_ref[...] = residual
    b_ref[...] = (residual * inverse_size(residual) * gains_ref[1:2, :]).astype(BF16)
    for step in range(1, CTX):
        pltpu.make_async_copy(heads_out.at[0], attended_ref.at[0], send_o.at[step]).wait()
    for copy in leaving:
        copy.wait()


def attn_forward(layer, length, u, packs, table):
    sems = pltpu.SemaphoreType.DMA
    return pl.pallas_call(
        functools.partial(attn_forward_kernel, layer),
        out_shape=(
            jax.ShapeDtypeStruct((SEQ, D), BF16),
            jax.ShapeDtypeStruct((SEQ, EXT), BF16),
            jax.ShapeDtypeStruct((HEADS_DEV, SEQ, 1), F32),
            jax.ShapeDtypeStruct((CTX, ROWS, COLS), BF16),
            jax.ShapeDtypeStruct((ROWS, D), F32),
            jax.ShapeDtypeStruct((ROWS, D), BF16),
            jax.ShapeDtypeStruct((8, D), F32),
            jax.ShapeDtypeStruct((D, LANES), BF16),
            jax.ShapeDtypeStruct((D, EXT), BF16),
            jax.ShapeDtypeStruct((D, D), BF16),
        ),
        in_specs=[
            SMEM,
            VMEM,
            ANY,
            VMEM,
        ],
        out_specs=[ANY] * 3 + [VMEM] * 5 + [ANY] * 2,
        scratch_shapes=[
            pltpu.VMEM((SEQ, D), BF16),
            pltpu.VMEM((SEQ, EXT), BF16),
            pltpu.VMEM((HEADS_DEV, SEQ, 1), F32),
            pltpu.VMEM((D, EXT), BF16),
            pltpu.VMEM((D, D), BF16),
            sems((5,)),
            pltpu.VMEM((CTX, ROWS, COLS), BF16),
            pltpu.VMEM((D, D), BF16),
            pltpu.VMEM((16, ATTN_ROWS, UNIT), BF16),
            sems,
        ]
        + [sems((6,)), sems((6,)), sems((CTX,)), sems((CTX,))],
        compiler_params=params(1 + 10 * layer),
        name="attn_forward",
    )(length, u, packs, table)


def attn_backward_kernel(
    hosting, length_ref, u_ref, gains_ref, router_ref, w_in, back_in, table_in,
    a_in, qkv_in, mass_in, attended_in, residual_ref, second_in, gates_ref,
    delta_ref, db_ref, gate_grad_ref, *rest,
):
    (
        w_ref, back_ref, table_ref, a_ref, qkv_ref, mass_ref, attended_ref, second_ref, in_sem, *rest,
    ) = rest[-9:] + rest[:-9]
    coming = [
        pltpu.make_async_copy(source, target, in_sem.at[index])
        for index, (source, target) in enumerate(
            (
                (back_in, back_ref), (attended_in, attended_ref), (second_in, second_ref),
                (qkv_in, qkv_ref), (mass_in, mass_ref), (table_in, table_ref), (w_in, w_ref), (a_in, a_ref),
            )
        )
    ]
    for copy in coming:
        copy.start()
    if hosting:
        upper_e, upper_a, lent, *rest = rest
    input_ref, pack_ref, lower_ref = rest[:3]
    rest = rest[3:]
    if hosting:
        half_ref, *rest = rest
        rest, hosted = rest[:15], rest[15:]
    dheads_ref, dback_ref = rest[:2]
    rest = rest[2:]
    key_acc, value_acc, dz, grads_out, grads_in, send_o, recv_o = rest[:7]
    part, across_in, from_left, from_right, send_r, recv_r = rest[7:13]
    me, right, left, across = ring()
    greet((right, left, across))
    if hosting:
        refs, (in_y, in_z, local, *sems) = hosted[:HALF_REFS], hosted[HALF_REFS:]
        part_y, part_z = refs[:2]
        section = lax.axis_index("section")
        sums = HalfSums(
            refs,
            sems,
            lambda index, block: add_block(part_y, in_y, block),
            lambda index, block: add_block(part_z, in_z, block),
        )
        greet_ids(sums.ring_y.near() + sums.ring_z.near())

        def loads(half):
            sources = half_sources(half, upper_e, upper_a)
            pairs = [
                (sources[1], part_z.at[:, :, pl.ds(0, Z_CUT), :]),
                (sources[2], part_z.at[:, :, pl.ds(Z_CUT, ATTN_ROWS), :]),
                (lent.at[:, :, pl.ds(Y_ROWS, Z_ROWS), :], in_z),
            ]
            for block in range(CTX):
                pairs.append((sources[0].at[:, block], part_y.at[block]))
                pairs.append((lent.at[:, block, pl.ds(0, Y_ROWS), :], in_y.at[block]))
            return [
                pltpu.make_async_copy(source, target, local.at[index])
                for index, (source, target) in enumerate(pairs)
            ]

        for core in range(2):

            @pl.when(section == core)
            def _():
                for copy in loads(core):
                    copy.start()

    length = length_ref[0]
    lanes = lax.broadcasted_iota(jnp.int32, (ROWS, LANES), 1)
    gates = gates_ref[...]
    gate_grads = jnp.where(lanes < EXPERTS, gate_grad_ref[...], 0.0)
    logit_grad = gates * (gate_grads - jnp.sum(gates * gate_grads, axis=1, keepdims=True))
    logit_grad = logit_grad.astype(BF16)
    second_grad = db_ref[...] + dot_nt(logit_grad, router_ref[...])
    residual = residual_ref[...]
    scale_two = inverse_size(residual)
    normal_two = residual * scale_two
    gain_two_terms = second_grad * normal_two
    scaled_two = second_grad * gains_ref[1:2, :]
    residual_grad = delta_ref[...].astype(F32) + scale_two * (
        scaled_two - normal_two * jnp.mean(scaled_two * normal_two, axis=1, keepdims=True)
    )
    input_ref[...] = residual_grad
    branch_grad = residual_grad.astype(BF16)
    met(7 if hosting else 3)
    coming[0].wait()

    for block in range(CTX):
        grads_out[block] = dot_nt(branch_grad, back_ref[block * COLS : (block + 1) * COLS, :]).astype(
            BF16
        )

        @pl.when(block != me)
        def _():
            step = lax.rem(block - me + CTX, CTX)
            remote(
                grads_out.at[block], grads_in.at[me], send_o.at[step], recv_o.at[step], block
            ).start()

    grads_in[me] = grads_out[me]
    if hosting:
        for copy in loads(0):
            copy.wait()
        for number in range(3):
            sums.first(number)
    coming[1].wait()
    coming[2].wait()
    for block in range(CTX):
        dback_ref[block * COLS : (block + 1) * COLS, :] = dot_tn(
            attended_ref[block], branch_grad
        ).astype(BF16)
    router_terms = dot_tn(second_ref[...], logit_grad)
    ones = jnp.ones((ROWS, LANES), F32)
    gain_two_column = lax.dot_general(
        gain_two_terms, ones, TN, precision=EXACT, preferred_element_type=F32
    )
    key_acc[...] = jnp.zeros_like(key_acc)
    value_acc[...] = jnp.zeros_like(value_acc)
    for copy in coming[3:]:
        copy.wait()
    for step in range(1, CTX):
        pltpu.make_async_copy(grads_out.at[0], grads_in.at[0], recv_o.at[step]).wait()
    for step in range(1, CTX):
        pltpu.make_async_copy(grads_out.at[0], grads_in.at[0], send_o.at[step]).wait()
    for block in range(CTX):
        rows = pl.ds(block * ROWS, ROWS)
        keys = (block + 1) * ROWS
        allowed = allowed_keys(block, keys, length)
        pair = grads_in[block, :, :WIDE]
        tail = grads_in[block, :, WIDE:]
        head_grads = (
            pair,
            pltpu.roll(pair.astype(F32), WIDE // 2, 1).astype(BF16),
            jnp.concatenate([tail, jnp.zeros_like(tail)], axis=1),
        )
        for head in range(HEADS_DEV):
            queries = qkv_ref[rows, head * WIDE : (head + 1) * WIDE]
            keys_all = qkv_ref[:keys, (HEADS_DEV + head) * WIDE : (HEADS_DEV + head + 1) * WIDE]
            values_all = qkv_ref[
                :keys, (2 * HEADS_DEV + head) * WIDE : (2 * HEADS_DEV + head + 1) * WIDE
            ]
            grads = head_grads[head]
            scores = dot_nt(queries, keys_all) * SCORE_SCALE
            probs = jnp.where(allowed, jnp.exp(scores - mass_ref[head, rows, :]), 0.0)
            prob_grad = dot_nt(grads, values_all)
            row_sum = jnp.sum(probs * prob_grad, axis=1, keepdims=True)
            score_grad = (probs * (prob_grad - row_sum)).astype(BF16)
            query_grad = dot(score_grad, keys_all) * (HEAD_DIM**-0.5)
            dz[rows, head * WIDE : (head + 1) * WIDE] = (query_grad * table_ref[rows, :]).astype(BF16)
            spot = slice(head * WIDE, (head + 1) * WIDE)
            key_acc[:keys, spot] += dot_tn(score_grad, queries)
            value_acc[:keys, spot] += dot_tn(probs.astype(BF16), grads)
        if hosting and block == 2:
            sums.first(3)
            sums.first(4)
    for block in range(CTX):
        rows = pl.ds(block * ROWS, ROWS)
        table = table_ref[rows, :] * (HEAD_DIM**-0.5)
        for head in range(HEADS_DEV):
            spot = slice(head * WIDE, (head + 1) * WIDE)
            at = (HEADS_DEV + head) * WIDE
            dz[rows, at : at + WIDE] = (key_acc[rows, spot] * table).astype(BF16)
            at = (2 * HEADS_DEV + head) * WIDE
            dz[rows, at : at + WIDE] = value_acc[rows, spot].astype(BF16)

    if hosting:
        sums.first(5)
        for number in range(3):
            sums.then(number)

    def make(block):
        part[rows_of(block), :] = dot_nt(dz[rows_of(block), :], w_ref[...]).astype(BF16)

    def beside():
        wide_lanes = lax.broadcasted_iota(jnp.int32, (D, WIDE), 1)
        pieces = []
        for piece in range(3):
            spot = slice(piece * HEADS_DEV * WIDE, (piece + 1) * HEADS_DEV * WIDE)
            terms = dot_tn(a_ref[...], dz[:, spot])
            for head in range(HEADS_DEV):
                term = terms[:, head * WIDE : (head + 1) * WIDE]
                if piece < 2:
                    term = term + jnp.where(
                        wide_lanes < HEAD_DIM // 2,
                        pltpu.roll(term, HEAD_DIM // 2, 1),
                        -pltpu.roll(term, WIDE - HEAD_DIM // 2, 1),
                    )
                pieces.append(term)
        for pair in range(4):
            joined = jnp.where(
                wide_lanes < HEAD_DIM,
                pieces[2 * pair],
                pltpu.roll(pieces[2 * pair + 1], HEAD_DIM, 1),
            )
            dheads_ref[:, pair * WIDE : (pair + 1) * WIDE] = joined.astype(BF16)
        dheads_ref[:, 4 * WIDE : 5 * WIDE] = jnp.where(
            wide_lanes < HEAD_DIM, pieces[8], 0.0
        ).astype(BF16)
        if hosting:
            sums.then(3)
            sums.then(4)

    normed_grad = reduce_rows(make, part, across_in, from_left, from_right, send_r, recv_r, beside)
    tokens = u_ref[...].astype(F32)
    scale_one = inverse_size(tokens)
    normal_one = tokens * scale_one
    gain_one_column = lax.dot_general(
        normed_grad * normal_one, ones, TN, precision=EXACT, preferred_element_type=F32
    )
    scaled_one = normed_grad * gains_ref[0:1, :]
    input_grad = input_ref[...] + scale_one * (
        scaled_one - normal_one * jnp.mean(scaled_one * normal_one, axis=1, keepdims=True)
    )
    input_ref[...] = input_grad
    small_lanes = lax.broadcasted_iota(jnp.int32, (D, LANES), 1)
    dheads_ref[:, D - LANES :] = jnp.where(
        small_lanes == EXPERTS,
        gain_one_column,
        jnp.where(small_lanes == EXPERTS + 1, gain_two_column, router_terms),
    ).astype(BF16)
    repack(dback_ref, dheads_ref, pack_ref)
    lower_ref[...] = input_grad.astype(BF16)
    if hosting:
        sums.then(5)
        sums.result(half_ref)


def attn_backward(length, arrays, upper=()):
    sems = pltpu.SemaphoreType.DMA
    out_shape = [
        jax.ShapeDtypeStruct((ROWS, D), F32),
        jax.ShapeDtypeStruct((16, ATTN_ROWS, UNIT), BF16),
        jax.ShapeDtypeStruct((ROWS, D), BF16),
    ]
    if upper:
        out_shape.append(jax.ShapeDtypeStruct((HALF_SHARD, UNIT), BF16))
    scratch = [
        pltpu.VMEM((D, D), BF16),
        pltpu.VMEM((D, D), BF16),
        pltpu.VMEM((SEQ, HEADS_DEV * WIDE), F32),
        pltpu.VMEM((SEQ, HEADS_DEV * WIDE), F32),
        pltpu.VMEM((SEQ, EXT), BF16),
        pltpu.VMEM((CTX, ROWS, COLS), BF16),
        pltpu.VMEM((CTX, ROWS, COLS), BF16),
        sems((CTX,)),
        sems((CTX,)),
    ] + REDUCE_SCRATCH
    if upper:
        scratch += half_scratch()
        scratch += [
            pltpu.VMEM((CTX, CTX, Y_ROWS, UNIT), BF16),
            pltpu.VMEM((CTX, CTX, Z_ROWS, UNIT), BF16),
            sems((11,)),
        ] + [sems((6,))] * 8
    late = (3, 4, 5, 6, 7, 8, 9, 11)
    specs = [ANY if index in late else VMEM for index in range(len(arrays))]
    for index in late:
        scratch.append(pltpu.VMEM(arrays[index].shape, arrays[index].dtype))
    scratch.append(sems((len(late),)))
    return pl.pallas_call(
        functools.partial(attn_backward_kernel, bool(upper)),
        out_shape=tuple(out_shape),
        in_specs=[SMEM] + specs + [ANY] * len(upper),
        out_specs=[VMEM] * len(out_shape),
        scratch_shapes=scratch,
        compiler_params=params(4 if upper else 3),
        name="attn_backward",
    )(length, *arrays, *(by_place(array) for array in upper))


GROUP = 4
GROUPS = 16 // GROUP
GROUP_UNITS = GROUP * LANES
SPLIT = EXPERT_ROWS // 2
SUM_SCRATCH = [
    pltpu.VMEM((CTX, ROWS, D), BF16),
    pltpu.VMEM((HALF, D), BF16),
    pltpu.VMEM((HALF, D), BF16),
    pltpu.VMEM((ROWS, D), BF16),
    pltpu.VMEM((ROWS, D), BF16),
    SEMS((6,)),
    SEMS((6,)),
]


def weight_copies(w_ref, win, wout, sem):
    groups = []
    for group in range(GROUPS):
        shards = pl.ds(group * GROUP, GROUP)
        pairs = [
            (w_ref.at[0, shards], win.at[shards, pl.ds(0, SPLIT), :]),
            (w_ref.at[1, shards, pl.ds(0, D - SPLIT), :], win.at[shards, pl.ds(SPLIT, D - SPLIT), :]),
        ]
        for piece in range(D // UNIT):
            pairs.append(
                (
                    w_ref.at[1, shards, pl.ds(D - SPLIT + piece * LANES, LANES), :],
                    wout.at[shards, :, pl.ds(piece * UNIT, UNIT)],
                )
            )
        groups.append(
            [
                pltpu.make_async_copy(source, target, sem.at[group * 5 + index])
                for index, (source, target) in enumerate(pairs)
            ]
        )
    return groups


def wout_group(wout, group):
    return wout[group * GROUP : (group + 1) * GROUP].reshape(GROUP_UNITS, D)


def ffn_forward_kernel(
    b_own_ref, residual_ref, codes_ref, router_ref, w_ref,
    y_ref, b_ref, gates_ref, gate_ref, kept_ref,
    win, wout, kept_out, acc, w_sem, kept_sem, send_b, recv_b,
    part, top_in, bottom_in, from_left, from_right, send, recv,
):
    ring = Ring("x")
    greet_ids(ring.near())
    loads = weight_copies(w_ref, win, wout, w_sem)
    for group in loads:
        for copy in group:
            copy.start()
    b_ref[ring.me] = b_own_ref[...]
    met(2)
    halves = (pl.ds(0, HALF), pl.ds(HALF, HALF))
    rows = RingGather(ring, lambda b, h: b_ref.at[b, halves[h]], send_b, recv_b)
    rows.start()
    section = lax.axis_index("section")
    lanes = lax.broadcasted_iota(jnp.int32, (ROWS, LANES), 1)
    picker = jnp.where(lax.broadcasted_iota(jnp.int32, (8, LANES), 0) == section, 1.0, 0.0)
    stores = []

    def make(index, block):
        b_rows = b_ref[block]
        slot = index % 2
        for shard in range(16):
            if index == 0 and shard % GROUP == 0:
                for copy in loads[shard // GROUP]:
                    copy.wait()
            if index >= 2 and shard == 0:
                stores[index - 2].wait()
            hidden = dot(b_rows, win[shard])
            kept_out[slot, shard] = hidden.astype(BF16)
            gate_part = hidden[:, :LANES]
            at = shard % GROUP * LANES
            acc_act = (gate_part / (1.0 + jnp.exp(-gate_part)) * hidden[:, LANES:]).astype(BF16)
            if shard % GROUP == 0:
                acted = []
            acted.append(acc_act)
            if shard % GROUP == GROUP - 1:
                terms = dot(jnp.concatenate(acted, axis=1), wout_group(wout, shard // GROUP))
                acc[...] = terms if shard < GROUP else acc[...] + terms
        stores.append(pltpu.make_async_copy(kept_out.at[slot], kept_ref.at[block], kept_sem.at[slot]))
        stores[-1].start()
        logits = dot(b_rows, router_ref[...])
        codes = lax.dot_general(
            codes_ref[block], picker, TN, precision=EXACT, preferred_element_type=F32
        )
        named = (lanes < EXPERTS) & (lanes != jnp.round(codes).astype(jnp.int32))
        chosen = jnp.where(named, logits, MASK_VALUE)
        raw = jnp.where(named, jnp.exp(chosen - jnp.max(chosen, axis=1, keepdims=True)), 0.0)
        gates = raw / jnp.sum(raw, axis=1, keepdims=True)
        if index == 0:
            gates_ref[...] = gates
        gates = jnp.where(lanes == EXPERTS, 1.0, gates)
        gate = jnp.sum(jnp.where(lanes == ring.me, gates, 0.0), axis=1, keepdims=True)
        gate_ref[block] = gate
        part[block] = (acc[...] * gate).astype(BF16)

    order = {ring_index: number for number, ring_index in enumerate(("me", "right", "left", "across"))}

    def from_sum(position, block):
        make({0: order["across"], 1: order["right"], 2: order["left"], 3: order["me"]}[position], block)

    sums = RingSum(
        ring, part, (top_in, bottom_in), from_left, from_right, send, recv, HALF, from_sum
    )
    sums.stage(4)
    rows.forward()
    rows.near()
    sums.stage(1)
    sums.stage(2)
    rows.far()
    sums.stage(0)
    sums.stage(3)
    sums.stage(5)
    y_ref[...] = (residual_ref[...] + sums.total()).astype(BF16)
    rows.sent()
    stores[2].wait()
    stores[3].wait()


def ffn_forward(b_own, residual, codes, router, weights):
    return pl.pallas_call(
        ffn_forward_kernel,
        out_shape=(
            jax.ShapeDtypeStruct((ROWS, D), BF16),
            jax.ShapeDtypeStruct((CTX, ROWS, D), BF16),
            jax.ShapeDtypeStruct((ROWS, LANES), F32),
            jax.ShapeDtypeStruct((CTX, ROWS, 1), F32),
            jax.ShapeDtypeStruct((CTX, 16, ROWS, UNIT), BF16),
        ),
        in_specs=[VMEM] * 4 + [ANY],
        out_specs=[VMEM] * 4 + [ANY],
        scratch_shapes=[
            pltpu.VMEM((16, D, UNIT), BF16),
            pltpu.VMEM((16, LANES, D), BF16),
            pltpu.VMEM((2, 16, ROWS, UNIT), BF16),
            pltpu.VMEM((ROWS, D), F32),
            SEMS((5 * GROUPS,)),
            SEMS((2,)),
            SEMS((6,)),
            SEMS((6,)),
        ]
        + SUM_SCRATCH,
        compiler_params=params(5),
        name="ffn_forward",
    )(b_own, residual, codes, router, weights)


def ffn_backward_kernel(
    lending, b_ref, gate_ref, delta_own_ref, kept_ref, w_ref, *rest,
):
    if lending:
        upper_e, upper_a, db_ref, gate_grad_ref, dw_ref, lent_ref, *rest = rest
        *rest, send_l, recv_l = rest
    else:
        db_ref, gate_grad_ref, dw_ref, *rest = rest
    (
    delta, acc, gate_acc, slot_grad, hidden, acted, win, wout, staged, rows_out, rows_in, b_turned,
    w_sem, kept_sem, dw_sem, send_d, recv_d, send_g, recv_g,
    part, top_in, bottom_in, from_left, from_right, send, recv,
    ) = rest
    ring = Ring("x")
    peers = (ring.right, ring.left, ring.across)
    section = lax.axis_index("section")
    sibling = {"section": 1 - section}
    greet_ids([ring.place(peer) for peer in peers] + ([sibling] if lending else []))
    blocks = (ring.me, ring.right, ring.left, ring.across)
    kept_loads = [
        pltpu.make_async_copy(
            kept_ref.at[block], hidden.at[:, rows_of(block), :], kept_sem.at[index]
        )
        for index, block in enumerate(blocks)
    ]
    loads = weight_copies(w_ref, win, wout, w_sem)
    kept_loads[0].start()
    for group in loads:
        for copy in group:
            copy.start()
    for copy in kept_loads[1:]:
        copy.start()
    delta[ring.me] = delta_own_ref[...]
    met(4 if lending else 3)
    if lending:
        first_rows = pl.ds(0, KEPT)
        last_rows = pl.ds(KEPT, ATTN_ROWS)

        def lends(given):
            sources = (
                (upper_e.at[:, first_rows, :], upper_e.at[:, last_rows, :])
                if given == 0
                else (upper_e.at[:, pl.ds(HALF_SHARD, KEPT), :], upper_a)
            )
            return [
                pltpu.make_async_remote_copy(
                    src_ref=source,
                    dst_ref=lent_ref.at[:, target, :],
                    send_sem=send_l.at[index],
                    recv_sem=recv_l.at[index],
                    device_id=sibling,
                    device_id_type=MESH,
                )
                for index, (source, target) in enumerate(zip(sources, (first_rows, last_rows)))
            ]

        for core in range(2):

            @pl.when(section == core)
            def _():
                for copy in lends(1 - core):
                    copy.start()

    halves = (pl.ds(0, HALF), pl.ds(HALF, HALF))
    rows = RingGather(ring, lambda b, h: delta.at[b, halves[h]], send_d, recv_d)
    rows.start()
    own_row = lax.broadcasted_iota(jnp.int32, (8, LANES), 0) == ring.me
    picker = jnp.where(own_row, 1.0, 0.0)
    handed = [
        ring.copy(rows_out.at[peer], rows_in.at[index], send_g.at[index], recv_g.at[index], peer)
        for index, peer in enumerate(peers)
    ]

    def make(index, block):
        kept_loads[index].wait()
        at = rows_of(block)
        gate = gate_ref[block]
        delta_rows = delta[block]
        slot_grad[at, :] = (delta_rows.astype(F32) * gate).astype(BF16)
        gate_sum = jnp.zeros((ROWS, LANES), F32)
        for group in range(GROUPS):
            if index == 0:
                for copy in loads[group]:
                    copy.wait()
            act_grad_all = dot_nt(delta_rows, wout_group(wout, group))
            second_grad = None
            for inner in range(GROUP):
                shard = group * GROUP + inner
                values = hidden[shard, at, :].astype(F32)
                gate_part = values[:, :LANES]
                up_part = values[:, LANES:]
                act_grad = act_grad_all[:, inner * LANES : (inner + 1) * LANES]
                sigmoid = 1.0 / (1.0 + jnp.exp(-gate_part))
                silu = gate_part * sigmoid
                act = (silu * up_part).astype(BF16)
                acted[at, shard * LANES : (shard + 1) * LANES] = act
                gate_sum += act.astype(F32) * act_grad
                act_grad = act_grad * gate
                gate_grad = act_grad * up_part * (sigmoid * (1.0 + gate_part * (1.0 - sigmoid)))
                pair = jnp.concatenate([gate_grad, act_grad * silu], axis=1).astype(BF16)
                hidden[shard, at, :] = pair
                term = dot_nt(pair, win[shard])
                second_grad = term if second_grad is None else second_grad + term
            acc[...] = second_grad if group == 0 else acc[...] + second_grad
        part[block] = acc[...].astype(BF16)
        rows_out[block] = lax.dot_general(
            picker, gate_sum, NT, precision=EXACT, preferred_element_type=F32
        )
        if index > 0:
            handed[index - 1].start()

    def from_sum(position, block):
        make((3, 1, 2, 0)[position], block)

    sums = RingSum(
        ring, part, (top_in, bottom_in), from_left, from_right, send, recv, HALF, from_sum
    )
    sums.stage(4)
    b_turned[...] = b_ref[...].reshape(SEQ, D).T
    rows.forward()
    rows.near()
    sums.stage(1)
    sums.stage(2)
    rows.far()
    sums.stage(0)
    stores = []
    for group in range(GROUPS):
        slot = group % 2
        if group == 1:
            sums.stage(3)
        if group >= 2:
            stores[group - 2].wait()
        for inner in range(GROUP):
            staged[slot, inner, :D, :] = dot(b_turned[...], hidden[group * GROUP + inner]).astype(BF16)
        whole_out = dot_tn(
            acted[:, group * GROUP_UNITS : (group + 1) * GROUP_UNITS], slot_grad[...]
        ).astype(BF16)
        for inner in range(GROUP):
            for piece in range(D // UNIT):
                at = D + piece * LANES
                staged[slot, inner, at : at + LANES, :] = whole_out[
                    inner * LANES : (inner + 1) * LANES, piece * UNIT : (piece + 1) * UNIT
                ]
        stores.append(
            pltpu.make_async_copy(
                staged.at[slot], dw_ref.at[pl.ds(group * GROUP, GROUP)], dw_sem.at[slot]
            )
        )
        stores[-1].start()
    sums.stage(5)
    db_ref[...] = sums.total()
    for copy in handed:
        copy.wait()
    rows_all = rows_out[ring.me] + rows_in[0] + rows_in[1] + rows_in[2]
    diagonal = jnp.where(
        lax.broadcasted_iota(jnp.int32, (8, LANES), 0)
        == lax.broadcasted_iota(jnp.int32, (8, LANES), 1),
        1.0,
        0.0,
    )
    gate_grad_ref[...] = lax.dot_general(
        rows_all, diagonal, TN, precision=EXACT, preferred_element_type=F32
    )
    rows.sent()
    stores[2].wait()
    stores[3].wait()
    if lending:
        for copy in lends(0):
            copy.wait()


def ffn_backward(b_all, gate_col, delta_own, kept, weights, upper=()):
    out_shape = [
        jax.ShapeDtypeStruct((ROWS, D), F32),
        jax.ShapeDtypeStruct((ROWS, LANES), F32),
        jax.ShapeDtypeStruct((16, EXPERT_ROWS, UNIT), BF16),
    ]
    if upper:
        out_shape.append(jax.ShapeDtypeStruct((16, HALF_SHARD, UNIT), BF16))
    return pl.pallas_call(
        functools.partial(ffn_backward_kernel, bool(upper)),
        out_shape=out_shape,
        in_specs=[VMEM] * 3 + [ANY] * (2 + len(upper)),
        out_specs=[VMEM] * 2 + [ANY] * (len(out_shape) - 2),
        scratch_shapes=[
            pltpu.VMEM((CTX, ROWS, D), BF16),
            pltpu.VMEM((ROWS, D), F32),
            pltpu.VMEM((8, LANES), F32),
            pltpu.VMEM((SEQ, D), BF16),
            pltpu.VMEM((16, SEQ, UNIT), BF16),
            pltpu.VMEM((SEQ, FFN), BF16),
            pltpu.VMEM((16, D, UNIT), BF16),
            pltpu.VMEM((16, LANES, D), BF16),
            pltpu.VMEM((2, GROUP, EXPERT_ROWS, UNIT), BF16),
            pltpu.VMEM((CTX, 8, ROWS), F32),
            pltpu.VMEM((3, 8, ROWS), F32),
            pltpu.VMEM((D, SEQ), BF16),
            SEMS((5 * GROUPS,)),
            SEMS((CTX,)),
            SEMS((2,)),
            SEMS((6,)),
            SEMS((6,)),
            SEMS((3,)),
            SEMS((3,)),
        ]
        + SUM_SCRATCH
        + ([SEMS((2,)), SEMS((2,))] if upper else []),
        compiler_params=params(10 if upper else 6),
        name="ffn_backward",
    )(b_all, gate_col, delta_own, kept, weights, *upper)


def ffn_both_kernel(
    b_own_ref, residual_ref, codes_ref, router_ref, delta_own_ref, w_ref,
    y_ref, gates_ref, db_ref, gate_grad_ref, dw_ref,
    b_ref, gate_ref, delta, acc, slot_grad, hidden, acted, win, wout, staged, rows_out, rows_in, b_turned,
    w_sem, dw_sem, send_b, recv_b, send_d, recv_d, send_g, recv_g, *sum_refs,
):
    ring = Ring("x")
    peers = (ring.right, ring.left, ring.across)
    greet_ids([ring.place(peer) for peer in peers])
    loads = weight_copies(w_ref, win, wout, w_sem)
    for group in loads:
        for copy in group:
            copy.start()
    b_ref[ring.me] = b_own_ref[...]
    delta[ring.me] = delta_own_ref[...]
    met(3)
    halves = (pl.ds(0, HALF), pl.ds(HALF, HALF))
    rows = RingGather(ring, lambda b, h: b_ref.at[b, halves[h]], send_b, recv_b)
    seeds = RingGather(ring, lambda b, h: delta.at[b, halves[h]], send_d, recv_d)
    rows.start()
    section = lax.axis_index("section")
    lanes = lax.broadcasted_iota(jnp.int32, (ROWS, LANES), 1)
    code_picker = jnp.where(lax.broadcasted_iota(jnp.int32, (8, LANES), 0) == section, 1.0, 0.0)
    row_picker = jnp.where(lax.broadcasted_iota(jnp.int32, (8, LANES), 0) == ring.me, 1.0, 0.0)
    handed = [
        ring.copy(rows_out.at[peer], rows_in.at[index], send_g.at[index], recv_g.at[index], peer)
        for index, peer in enumerate(peers)
    ]
    part_y, part_b = sum_refs[0], sum_refs[7]

    def forward(index, block):
        at = rows_of(block)
        b_rows = b_ref[block]
        for group in range(GROUPS):
            if index == 0:
                for copy in loads[group]:
                    copy.wait()
            acts = []
            for inner in range(GROUP):
                shard = group * GROUP + inner
                values = dot(b_rows, win[shard])
                hidden[shard, at, :] = values.astype(BF16)
                gate_part = values[:, :LANES]
                acts.append(
                    (gate_part / (1.0 + jnp.exp(-gate_part)) * values[:, LANES:]).astype(BF16)
                )
            terms = dot(jnp.concatenate(acts, axis=1), wout_group(wout, group))
            acc[...] = terms if group == 0 else acc[...] + terms
        logits = dot(b_rows, router_ref[...])
        codes = lax.dot_general(
            codes_ref[block], code_picker, TN, precision=EXACT, preferred_element_type=F32
        )
        named = (lanes < EXPERTS) & (lanes != jnp.round(codes).astype(jnp.int32))
        chosen = jnp.where(named, logits, MASK_VALUE)
        raw = jnp.where(named, jnp.exp(chosen - jnp.max(chosen, axis=1, keepdims=True)), 0.0)
        gates = raw / jnp.sum(raw, axis=1, keepdims=True)
        if index == 0:
            gates_ref[...] = gates
        gates = jnp.where(lanes == EXPERTS, 1.0, gates)
        gate = jnp.sum(jnp.where(lanes == ring.me, gates, 0.0), axis=1, keepdims=True)
        gate_ref[block] = gate
        part_y[block] = (acc[...] * gate).astype(BF16)

    def backward(index, block):
        at = rows_of(block)
        gate = gate_ref[block]
        delta_rows = delta[block]
        slot_grad[at, :] = (delta_rows.astype(F32) * gate).astype(BF16)
        gate_sum = jnp.zeros((ROWS, LANES), F32)
        for group in range(GROUPS):
            act_grad_all = dot_nt(delta_rows, wout_group(wout, group))
            second_grad = None
            for inner in range(GROUP):
                shard = group * GROUP + inner
                values = hidden[shard, at, :].astype(F32)
                gate_part = values[:, :LANES]
                up_part = values[:, LANES:]
                act_grad = act_grad_all[:, inner * LANES : (inner + 1) * LANES]
                sigmoid = 1.0 / (1.0 + jnp.exp(-gate_part))
                silu = gate_part * sigmoid
                act = (silu * up_part).astype(BF16)
                acted[at, shard * LANES : (shard + 1) * LANES] = act
                gate_sum += act.astype(F32) * act_grad
                act_grad = act_grad * gate
                gate_grad = act_grad * up_part * (sigmoid * (1.0 + gate_part * (1.0 - sigmoid)))
                pair = jnp.concatenate([gate_grad, act_grad * silu], axis=1).astype(BF16)
                hidden[shard, at, :] = pair
                term = dot_nt(pair, win[shard])
                second_grad = term if second_grad is None else second_grad + term
            acc[...] = second_grad if group == 0 else acc[...] + second_grad
        part_b[block] = acc[...].astype(BF16)
        rows_out[block] = lax.dot_general(
            row_picker, gate_sum, NT, precision=EXACT, preferred_element_type=F32
        )
        if index > 0:
            handed[index - 1].start()

    def summing(refs, make):
        part, top_in, bottom_in, from_left, from_right, send, recv = refs
        return RingSum(
            ring, part, (top_in, bottom_in), from_left, from_right, send, recv, HALF,
            lambda position, block: make((3, 1, 2, 0)[position], block),
        )

    ahead = summing(sum_refs[:7], forward)
    behind = summing(sum_refs[7:], backward)
    ahead.stage(4)
    rows.forward()
    rows.near()
    seeds.start()
    ahead.stage(1)
    ahead.stage(2)
    rows.far()
    ahead.stage(0)
    seeds.forward()
    b_turned[...] = b_ref[...].reshape(SEQ, D).T
    behind.stage(4)
    ahead.stage(3)
    seeds.near()
    behind.stage(1)
    behind.stage(2)
    seeds.far()
    behind.stage(0)
    ahead.stage(5)
    y_ref[...] = (residual_ref[...] + ahead.total()).astype(BF16)
    stores = []
    for group in range(GROUPS):
        slot = group % 2
        if group == 1:
            behind.stage(3)
        if group >= 2:
            stores[group - 2].wait()
        for inner in range(GROUP):
            staged[slot, inner, :D, :] = dot(b_turned[...], hidden[group * GROUP + inner]).astype(BF16)
        whole_out = dot_tn(
            acted[:, group * GROUP_UNITS : (group + 1) * GROUP_UNITS], slot_grad[...]
        ).astype(BF16)
        for inner in range(GROUP):
            for piece in range(D // UNIT):
                at = D + piece * LANES
                staged[slot, inner, at : at + LANES, :] = whole_out[
                    inner * LANES : (inner + 1) * LANES, piece * UNIT : (piece + 1) * UNIT
                ]
        stores.append(
            pltpu.make_async_copy(
                staged.at[slot], dw_ref.at[pl.ds(group * GROUP, GROUP)], dw_sem.at[slot]
            )
        )
        stores[-1].start()
    behind.stage(5)
    db_ref[...] = behind.total()
    for copy in handed:
        copy.wait()
    rows_all = rows_out[ring.me] + rows_in[0] + rows_in[1] + rows_in[2]
    diagonal = jnp.where(
        lax.broadcasted_iota(jnp.int32, (8, LANES), 0)
        == lax.broadcasted_iota(jnp.int32, (8, LANES), 1),
        1.0,
        0.0,
    )
    gate_grad_ref[...] = lax.dot_general(
        rows_all, diagonal, TN, precision=EXACT, preferred_element_type=F32
    )
    rows.sent()
    seeds.sent()
    stores[2].wait()
    stores[3].wait()


def ffn_both(b_own, residual, codes, router, delta_own, weights):
    return pl.pallas_call(
        ffn_both_kernel,
        out_shape=(
            jax.ShapeDtypeStruct((ROWS, D), BF16),
            jax.ShapeDtypeStruct((ROWS, LANES), F32),
            jax.ShapeDtypeStruct((ROWS, D), F32),
            jax.ShapeDtypeStruct((ROWS, LANES), F32),
            jax.ShapeDtypeStruct((16, EXPERT_ROWS, UNIT), BF16),
        ),
        in_specs=[VMEM] * 5 + [ANY],
        out_specs=[VMEM] * 4 + [ANY],
        scratch_shapes=[
            pltpu.VMEM((CTX, ROWS, D), BF16),
            pltpu.VMEM((CTX, ROWS, 1), F32),
            pltpu.VMEM((CTX, ROWS, D), BF16),
            pltpu.VMEM((ROWS, D), F32),
            pltpu.VMEM((SEQ, D), BF16),
            pltpu.VMEM((16, SEQ, UNIT), BF16),
            pltpu.VMEM((SEQ, FFN), BF16),
            pltpu.VMEM((16, D, UNIT), BF16),
            pltpu.VMEM((16, LANES, D), BF16),
            pltpu.VMEM((2, GROUP, EXPERT_ROWS, UNIT), BF16),
            pltpu.VMEM((CTX, 8, ROWS), F32),
            pltpu.VMEM((3, 8, ROWS), F32),
            pltpu.VMEM((D, SEQ), BF16),
            SEMS((5 * GROUPS,)),
            SEMS((2,)),
            SEMS((6,)),
            SEMS((6,)),
            SEMS((6,)),
            SEMS((6,)),
            SEMS((3,)),
            SEMS((3,)),
        ]
        + SUM_SCRATCH * 2,
        compiler_params=params(6),
        name="ffn_both",
    )(b_own, residual, codes, router, delta_own, weights)


def rotary_table():
    half_dim = HEAD_DIM // 2
    steps = 2.0 * np.arange(half_dim, dtype=np.float32) / np.float32(HEAD_DIM)
    frequency = np.exp(-np.log(np.float32(10000.0)) * steps)
    angles = np.arange(SEQ, dtype=np.float32)[:, None] * frequency[None, :]
    cosine, sine = np.cos(angles), np.sin(angles)
    return jnp.asarray(np.concatenate([cosine, cosine, sine, sine], axis=1), F32)


def lower_forward(packs, experts, tokens_in, length, codes, table):
    a_all, qkv, mass, attended, residual, second, *unpacked = attn_forward(
        0, length, tokens_in, packs, table
    )
    output, b_all, gates, gate_col, kept = ffn_forward(
        second, residual, codes, unpacked[1], experts
    )
    late = (a_all, qkv, mass, attended, residual, second, gates)
    return output, (tokens_in, b_all, gate_col, kept, unpacked, late)


def upper_layer(packs, experts, tokens_in, length, codes, table, seed):
    a_all, qkv, mass, attended, residual, second, *unpacked = attn_forward(
        1, length, tokens_in, packs, table
    )
    output, gates, db, gate_grads, dexperts = ffn_both(
        second, residual, codes, unpacked[1], seed, experts
    )
    late = (a_all, qkv, mass, attended, residual, second, gates)
    results = attn_backward(length, (tokens_in, *unpacked, table, *late, seed, db, gate_grads))
    return output, dexperts, results


def lower_backward(experts, saved, delta_own, length, table, upper):
    tokens_in, b_all, gate_col, kept, unpacked, late = saved
    db, gate_grads, dexperts, lent = ffn_backward(b_all, gate_col, delta_own, kept, experts, upper)
    results = attn_backward(
        length, (tokens_in, *unpacked, table, *late, delta_own, db, gate_grads), (*upper, lent)
    )
    return dexperts, results


def factor_of(squares_ref, index):
    return jnp.minimum(1.0, CLIP_LIMIT / jnp.sqrt(squares_ref[0:1, index : index + 1]))


def updated(fixes_ref, gradient, factor, old, new, learn_rate, at=...):
    master_ref, mean_ref, square_ref = old
    gradient_ref, mean_new_ref, square_new_ref, master_new_ref, copy_ref = new
    clipped = gradient * factor
    master = master_ref[at]
    mean_new = BETA_ONE * mean_ref[at] + (1.0 - BETA_ONE) * clipped
    square_new = BETA_TWO * square_ref[at] + (1.0 - BETA_TWO) * clipped * clipped
    master_new = master - learn_rate * (
        mean_new * fixes_ref[0] / (jnp.sqrt(square_new * fixes_ref[1]) + ADAM_EPS) + DECAY_RATE * master
    )
    gradient_ref[at] = gradient
    mean_new_ref[at] = mean_new
    square_new_ref[at] = square_new
    master_new_ref[at] = master_new
    copy_ref[at] = master_new.astype(BF16)


def update_kernel(
    fixes_ref, squares_ref, in_sum_ref, out_sum_ref, attn_sum_ref, *refs,
):
    in_old, out_old, attn_old, gain_old, router_old = (refs[at : at + 3] for at in range(0, 15, 3))
    in_new, out_new, attn_new, gain_new, router_new = (refs[at : at + 5] for at in range(15, 40, 5))
    norms_ref, turned, wide = refs[40:]
    turned[pl.ds(0, D, 2), :] = in_sum_ref[0, :, :LANES].astype(F32)
    turned[pl.ds(1, D, 2), :] = in_sum_ref[0, :, LANES:].astype(F32)
    updated(
        fixes_ref, turned[...], factor_of(squares_ref, 3), in_old, in_new, RATE_FACTOR / D**0.5
    )
    pieces = [
        out_sum_ref[0, piece * LANES : (piece + 1) * LANES, :].astype(F32)
        for piece in range(D // UNIT)
    ]
    updated(
        fixes_ref,
        jnp.concatenate(pieces, axis=1),
        factor_of(squares_ref, 4),
        out_old,
        out_new,
        RATE_FACTOR / FFN**0.5,
        0,
    )

    @pl.when(pl.program_id(0) == 0)
    def _():
        back = [jnp.zeros((48, UNIT), F32) for _ in range(3)]
        small = jnp.zeros((48, UNIT), F32)
        for block in range(CTX):
            rows = [
                attn_sum_ref[block, piece * 48 : (piece + 1) * 48, :].astype(F32) for piece in range(6)
            ]
            back = [left + right for left, right in zip(back, rows[:3])]
            small = small + rows[5]
            heads = jnp.concatenate(rows[3:], axis=1)
            for part in range(3):
                at = part * D + block * COLS
                wide[:, at : at + COLS] = heads[:, part * COLS : (part + 1) * COLS]
        wide[:, 3 * D :] = jnp.concatenate(back, axis=1)
        small = small[:, LANES:]
        places = lax.broadcasted_iota(jnp.int32, (8, LANES), 0)
        picker = jnp.where(places == lax.broadcasted_iota(jnp.int32, (8, LANES), 1), 1.0, 0.0)
        turned_rows = lax.dot_general(
            picker, small, NT, precision=EXACT, preferred_element_type=F32
        )
        gain_rows = turned_rows[EXPERTS : EXPERTS + 2]
        updated(fixes_ref, gain_rows, factor_of(squares_ref, 0), gain_old, gain_new, GAIN_RATE)
        for expert in range(EXPERTS):
            updated(
                fixes_ref,
                turned_rows[expert : expert + 1],
                factor_of(squares_ref, 2),
                router_old,
                router_new,
                RATE_FACTOR / (D // 4) ** 0.5,
                expert,
            )
        norms_ref[...] = jnp.sqrt(squares_ref[...])
        for part in range(4):
            lanes = (slice(None), slice(part * D, (part + 1) * D))
            updated(
                fixes_ref,
                wide[lanes],
                factor_of(squares_ref, 1),
                attn_old,
                attn_new,
                RATE_FACTOR / D**0.5,
                lanes,
            )


def update(fixes, squares, sums_all, in_old, out_old, attn_old, gain_old, router_old):
    in_rows, units = 2 * D, LANES
    in_shape, out_shape, attn_shape = (CTX * in_rows, units), (CTX, units, D), (48, 4 * D)
    in_spec = pl.BlockSpec((in_rows, units), lambda i: (i, 0))
    out_spec = pl.BlockSpec((1, units, D), lambda i: (i, 0, 0))
    attn_spec = whole(attn_shape)
    gain_shape, router_shape = (2, 48), (EXPERTS, 1, 48)

    def five(shape):
        return [jax.ShapeDtypeStruct(shape, F32)] * 4 + [jax.ShapeDtypeStruct(shape, BF16)]

    return pl.pallas_call(
        update_kernel,
        grid=(CTX,),
        out_shape=five(in_shape)
        + five(out_shape)
        + five(attn_shape)
        + five(gain_shape)
        + five(router_shape)
        + [jax.ShapeDtypeStruct((8, LANES), F32)],
        in_specs=[
            SMEM,
            whole((8, LANES)),
            pl.BlockSpec((1, D, UNIT), lambda i: (i, 0, 0)),
            pl.BlockSpec((1, D // 2, UNIT), lambda i: (i, 2, 0)),
            pl.BlockSpec((CTX, ATTN_ROWS, UNIT), lambda i: (0, EXPERT_ROWS // ATTN_ROWS, 0)),
        ]
        + [in_spec] * 3
        + [out_spec] * 3
        + [attn_spec] * 3
        + [whole(gain_shape)] * 3
        + [whole(router_shape)] * 3,
        out_specs=[in_spec] * 5
        + [out_spec] * 5
        + [attn_spec] * 5
        + [whole(gain_shape)] * 5
        + [whole(router_shape)] * 5
        + [whole((8, LANES))],
        scratch_shapes=[pltpu.VMEM((in_rows, units), F32), pltpu.VMEM(attn_shape, F32)],
        compiler_params=pltpu.CompilerParams(vmem_limit_bytes=VMEM_LIMIT),
        name="update",
    )(
        fixes, squares, sums_all, sums_all, sums_all,
        *(array.reshape(in_shape) for array in in_old),
        *(array.reshape(out_shape) for array in out_old),
        *(array.reshape(attn_shape) for array in attn_old),
        *(array.reshape(gain_shape) for array in gain_old),
        *(array.transpose(2, 0, 1) for array in router_old),
    )


def on_device(
    inputs, cotangent, lengths, routes, step_count,
    norm_gains, gains_mean, gains_square,
    attn_weight, attn_mean, attn_square,
    router_weight, router_mean, router_square,
    expert_in, in_mean, in_square,
    expert_out, out_mean, out_square,
):
    section = lax.axis_index("section")
    ctx_index = lax.axis_index("ctx")
    fsdp = lax.axis_size("fsdp")
    everyone = ("section", "fsdp")
    shard_rows = attn_weight.shape[1]
    units = expert_in.shape[4]
    first_core = section == 0

    def own_columns(matrix, part):
        return lax.dynamic_slice_in_dim(matrix, part * D + ctx_index * COLS, COLS, 1)

    def swap(block):
        return lax.ppermute(block, "section", [(0, 1), (1, 0)])

    attn_shard = jnp.concatenate(
        [attn_weight[0][:, 3 * D :]]
        + [own_columns(attn_weight[0], part) for part in range(3)]
        + [jnp.zeros((shard_rows, HEAD_DIM), F32), router_weight[0], norm_gains[0].T]
        + [jnp.zeros((shard_rows, LANES - EXPERTS - 2), F32)],
        axis=1,
    ).astype(BF16)
    attn_shard = attn_shard.reshape(shard_rows, 6, UNIT).transpose(1, 0, 2).reshape(-1, UNIT)
    left_out = (3 - routes[0, :, :, 0] - routes[0, :, :, 1]).astype(F32)
    packs, codes = gather_shards(attn_shard, jnp.pad(left_out, ((0, 8 - left_out.shape[0]), (0, 0))))
    packs = packs.reshape(2, fsdp, ATTN_ROWS, UNIT)
    in_shard = (
        lax.dynamic_index_in_dim(expert_in[0], ctx_index, 0, keepdims=False)
        .astype(BF16)
        .reshape(D, 2 * units)
    )
    out_shard = lax.dynamic_index_in_dim(expert_out[0], ctx_index, 0, keepdims=False).astype(BF16)
    halves = jnp.concatenate(
        [in_shard] + [out_shard[:, at : at + 2 * units] for at in range(0, D, 2 * units)], axis=0
    ).reshape(2, SPLIT, 2 * units)
    other = swap(jnp.where(first_core, halves[1], halves[0]))
    pieces = (jnp.where(first_core, halves[0], other), jnp.where(first_core, other, halves[1]))
    experts = [
        lax.all_gather(piece, everyone).reshape(2, fsdp, SPLIT, 2 * units) for piece in pieces
    ]
    length = lax.dynamic_slice_in_dim(lengths, section, 1, 0)
    tokens = lax.dynamic_index_in_dim(inputs, section, 0, keepdims=False)
    positions = ctx_index * ROWS + jnp.arange(ROWS, dtype=jnp.int32)
    seed = lax.dynamic_index_in_dim(cotangent, section, 0, keepdims=False)
    seed = jnp.where((positions < length[0])[:, None], seed, jnp.zeros_like(seed))
    table = rotary_table()

    lower_out, lower_saved = lower_forward(packs, experts[0], tokens, length, codes[0], table)
    upper_out, upper_experts, (upper_grad, upper_attn, lower_seed) = upper_layer(
        packs, experts[1], lower_out, length, codes[1], table, seed
    )
    lower_experts, (lower_grad, lower_attn, _, upper_half) = lower_backward(
        experts[0], lower_saved, lower_seed, length, table, (upper_experts, upper_attn)
    )
    sums_all, squares, layer_outputs, input_grads = sum_shards(
        lower_experts, lower_attn, upper_half, lower_out, upper_out, lower_grad, upper_grad
    )
    step_value = step_count[0].astype(F32)
    fixes = 1.0 / jnp.stack([1.0 - BETA_ONE**step_value, 1.0 - BETA_TWO**step_value])
    changed = update(
        fixes,
        squares,
        sums_all,
        (expert_in, in_mean, in_square),
        (expert_out, out_mean, out_square),
        (attn_weight, attn_mean, attn_square),
        (norm_gains, gains_mean, gains_square),
        (router_weight, router_mean, router_square),
    )

    def shaped(first, like):
        return tuple(array.reshape(like.shape) for array in changed[first : first + 5])

    return (
        (layer_outputs[None], input_grads[None])
        + shaped(15, norm_gains)
        + shaped(10, attn_weight)
        + tuple(array.transpose(1, 2, 0) for array in changed[20:25])
        + shaped(0, expert_in)
        + shaped(5, expert_out)
        + (changed[25][:1, :5],)
    )


def solution(mesh):
    gains = P("section", None, "fsdp")
    rows = P("section", "fsdp", None)
    wide = P("section", None, None, None, "fsdp")
    down = P("section", None, "fsdp", None)
    tokens = P("section", "fsdp", "ctx", None)
    return jax.shard_map(
        on_device,
        mesh=mesh,
        in_specs=(
            P("fsdp", "ctx", None),
            P("fsdp", "ctx", None),
            P("fsdp"),
            tokens,
            P(),
        )
        + (gains,) * 3
        + (rows,) * 6
        + (wide,) * 3
        + (down,) * 3,
        out_specs=(tokens, tokens)
        + (gains,) * 5
        + (rows,) * 10
        + (wide,) * 5
        + (down,) * 5
        + (P("section", None),),
        check_vma=False,
    )
```

```python
import functools

import jax
import jax.numpy as jnp
import numpy as np
from jax import lax
from jax.experimental import pallas as pl
from jax.experimental.pallas import tpu as pltpu
from jax.sharding import PartitionSpec as P

D = 768
HEADS = 12
HEAD_DIM = 64
FFN = 2048
EXPERTS = 3
ROWS = 256
CTX = 4
SEQ = ROWS * CTX
HEADS_DEV = HEADS // CTX
WIDE = 128
EXT = 3 * HEADS_DEV * WIDE
COLS = HEADS_DEV * HEAD_DIM

EPS_NORM = 1e-06
BETA_ONE = 0.9
BETA_TWO = 0.95
RATE_FACTOR = 3.0
GAIN_RATE = 0.3
DECAY_RATE = 0.1
ADAM_EPS = 1e-08
CLIP_LIMIT = 1.0
MASK_VALUE = -1e30
SCORE_SCALE = HEAD_DIM ** (-0.5) / 2.0
BF16 = jnp.bfloat16
F32 = jnp.float32
VMEM_LIMIT = 56 * 1024 * 1024
NT = (((1,), (1,)), ((), ()))
TN = (((0,), (0,)), ((), ()))
HALF = ROWS // 2
LANES = 128
MESH = pl.DeviceIdType.MESH
EXACT = lax.Precision.HIGHEST


def dot(left, right):
    return jnp.dot(left, right, preferred_element_type=F32)


def dot_nt(left, right):
    return lax.dot_general(left, right, NT, preferred_element_type=F32)


def dot_tn(left, right):
    return lax.dot_general(left, right, TN, preferred_element_type=F32)


def params(collective_id):
    return pltpu.CompilerParams(
        vmem_limit_bytes=VMEM_LIMIT, collective_id=collective_id, has_side_effects=True
    )


def whole(shape):
    return pl.BlockSpec(shape, lambda *_: (0,) * len(shape))


def allowed_keys(block, keys, length):
    key_pos = lax.broadcasted_iota(jnp.int32, (ROWS, keys), 1)
    query_pos = lax.broadcasted_iota(jnp.int32, (ROWS, keys), 0) + block * ROWS
    return (key_pos <= query_pos) & (key_pos < length)


VMEM = pl.BlockSpec(memory_space=pltpu.VMEM)
SMEM = pl.BlockSpec(memory_space=pltpu.SMEM)
ANY = pl.BlockSpec(memory_space=pl.ANY)


def ring():
    me = lax.axis_index("ctx")
    return me, lax.rem(me + 1, CTX), lax.rem(me + 3, CTX), lax.rem(me + 2, CTX)


def greet(peers):
    barrier = pltpu.get_barrier_semaphore()
    for peer in peers:
        pl.semaphore_signal(barrier, inc=1, device_id={"ctx": peer}, device_id_type=MESH)


def met(count):
    pl.semaphore_wait(pltpu.get_barrier_semaphore(), count)


def remote(source, target, send, recv, peer):
    return pltpu.make_async_remote_copy(
        src_ref=source,
        dst_ref=target,
        send_sem=send,
        recv_sem=recv,
        device_id={"ctx": peer},
        device_id_type=MESH,
    )


def rows_of(block, half=None):
    if half is None:
        return pl.ds(pl.multiple_of(block * ROWS, ROWS), ROWS)
    return pl.ds(pl.multiple_of(block * ROWS + half * HALF, HALF), HALF)


def gather_rows(all_ref, send, recv, beside=None):
    me, right, left, _ = ring()

    def piece(index, block, half, peer):
        spot = all_ref.at[rows_of(block, half)]
        return remote(spot, spot, send.at[index], recv.at[index], peer)

    copies = [
        piece(0, me, 0, right),
        piece(1, me, 1, left),
        piece(2, me, 1, right),
        piece(3, me, 0, left),
    ]
    for copy in copies:
        copy.start()
    if beside is not None:
        beside()
    copies[0].wait_recv()
    copies.append(piece(4, left, 0, right))
    copies[4].start()
    copies[1].wait_recv()
    copies.append(piece(5, right, 1, left))
    copies[5].start()
    for index in range(2, 6):
        copies[index].wait_recv()
    for copy in copies:
        copy.wait_send()


def reduce_rows(make, part, across_in, from_left, from_right, send, recv, beside=None):
    me, right, left, across = ring()
    top, bottom = pl.ds(0, HALF), pl.ds(HALF, HALF)

    def piece(index, block, half, target, peer):
        return remote(part.at[rows_of(block, half)], target, send.at[index], recv.at[index], peer)

    make(across)
    copies = [
        piece(0, across, 0, across_in.at[0], right),
        piece(1, across, 1, across_in.at[1], left),
    ]
    copies[0].start()
    copies[1].start()
    make(right)
    copies.append(piece(2, right, 1, from_left.at[bottom], right))
    copies[2].start()
    make(left)
    copies.append(piece(3, left, 0, from_right.at[top], left))
    copies[3].start()
    copies[0].wait_recv()
    spot = rows_of(right, 0)
    part[spot, :] = (part[spot, :].astype(F32) + across_in[0].astype(F32)).astype(BF16)
    copies.append(piece(4, right, 0, from_left.at[top], right))
    copies[4].start()
    copies[1].wait_recv()
    spot = rows_of(left, 1)
    part[spot, :] = (part[spot, :].astype(F32) + across_in[1].astype(F32)).astype(BF16)
    copies.append(piece(5, left, 1, from_right.at[bottom], left))
    copies[5].start()
    make(me)
    if beside is not None:
        beside()
    for index in range(2, 6):
        copies[index].wait_recv()
    for copy in copies:
        copy.wait_send()
    return (
        part[rows_of(me), :].astype(F32) + from_left[...].astype(F32) + from_right[...].astype(F32)
    )


REDUCE_SCRATCH = [
    pltpu.VMEM((SEQ, D), BF16),
    pltpu.VMEM((2, HALF, D), BF16),
    pltpu.VMEM((ROWS, D), BF16),
    pltpu.VMEM((ROWS, D), BF16),
    pltpu.SemaphoreType.DMA((6,)),
    pltpu.SemaphoreType.DMA((6,)),
]


def greet_ids(peers):
    barrier = pltpu.get_barrier_semaphore()
    for peer in peers:
        pl.semaphore_signal(barrier, inc=1, device_id=peer, device_id_type=MESH)


class Ring:
    def __init__(self, axis):
        if axis == "x":
            self.me = lax.axis_index("ctx")
            self.place = lambda index: {"ctx": index}
        else:
            shard = lax.axis_index("fsdp")
            inner, outer = lax.rem(shard, CTX), lax.div(shard, CTX)
            if axis == "y":
                self.me = inner
                self.place = lambda index: {"fsdp": outer * CTX + index}
            else:
                self.me = outer
                self.place = lambda index: {"fsdp": index * CTX + inner}
        self.right = lax.rem(self.me + 1, CTX)
        self.left = lax.rem(self.me + 3, CTX)
        self.across = lax.rem(self.me + 2, CTX)

    def order(self):
        return (self.across, self.right, self.left, self.me)

    def near(self):
        return [self.place(self.right), self.place(self.left)]

    def copy(self, source, target, send, recv, index):
        return pltpu.make_async_remote_copy(
            src_ref=source,
            dst_ref=target,
            send_sem=send,
            recv_sem=recv,
            device_id=self.place(index),
            device_id_type=MESH,
        )


class RingGather:
    def __init__(self, ring, at, send, recv):
        self.ring, self.at, self.send, self.recv = ring, at, send, recv
        self.sends = (
            (ring.me, 0, ring.right),
            (ring.me, 1, ring.left),
            (ring.me, 1, ring.right),
            (ring.me, 0, ring.left),
            (ring.left, 0, ring.right),
            (ring.right, 1, ring.left),
        )

    def piece(self, index, block, half, to):
        spot = self.at(block, half)
        return self.ring.copy(spot, spot, self.send.at[index], self.recv.at[index], to)

    def go(self, index):
        self.piece(index, *self.sends[index]).start()

    def landed(self, index, block, half):
        self.piece(index, block, half, self.ring.right).wait_recv()

    def start(self):
        for index in range(4):
            self.go(index)

    def forward(self):
        self.landed(0, self.ring.left, 0)
        self.go(4)
        self.landed(1, self.ring.right, 1)
        self.go(5)

    def near(self):
        self.landed(2, self.ring.left, 1)
        self.landed(3, self.ring.right, 0)

    def far(self):
        self.landed(4, self.ring.across, 0)
        self.landed(5, self.ring.across, 1)

    def sent(self):
        for index in range(6):
            self.piece(index, *self.sends[index]).wait_send()

    def finish(self):
        self.near()
        self.far()
        self.sent()


class RingSum:
    def __init__(self, ring, part, across_in, from_left, from_right, send, recv, cut, make):
        self.ring, self.part, self.across_in = ring, part, across_in
        self.from_left, self.from_right, self.send, self.recv = from_left, from_right, send, recv
        size = part.shape[1]
        self.halves = (pl.ds(0, cut), pl.ds(cut, size - cut))
        self.make = make
        self.copies = {}

    def go(self, index, block, half, target, to):
        self.copies[index] = self.ring.copy(
            self.part.at[block, self.halves[half]], target, self.send.at[index], self.recv.at[index], to
        )
        self.copies[index].start()

    def arrived(self, half, block):
        self.copies[half].wait_recv()
        incoming = self.across_in[half]
        if len(self.part.shape) == 3:
            spot = (block, self.halves[half])
            self.part[spot] = self.part[spot] + incoming[...]
            return
        start = (0, self.part.shape[1] - incoming.shape[0])[half]
        for index in range(incoming.shape[0]):
            self.part[block, start + index] = self.part[block, start + index] + incoming[index]

    def stage(self, number):
        ring = self.ring
        if number == 0:
            self.make(0, ring.across)
            self.go(0, ring.across, 0, self.across_in[0], ring.right)
            self.go(1, ring.across, 1, self.across_in[1], ring.left)
        elif number == 1:
            self.make(1, ring.right)
            self.go(2, ring.right, 1, self.from_left.at[self.halves[1]], ring.right)
        elif number == 2:
            self.make(2, ring.left)
            self.go(3, ring.left, 0, self.from_right.at[self.halves[0]], ring.left)
        elif number == 3:
            self.arrived(0, ring.right)
            self.go(4, ring.right, 0, self.from_left.at[self.halves[0]], ring.right)
            self.arrived(1, ring.left)
            self.go(5, ring.left, 1, self.from_right.at[self.halves[1]], ring.left)
        elif number == 4:
            self.make(3, ring.me)
        else:
            for index in range(2, 6):
                self.copies[index].wait_recv()
            for index in range(6):
                self.copies[index].wait_send()

    def total(self, index=None):
        spot = (self.ring.me,) if index is None else (self.ring.me, index)
        tail = () if index is None else (index,)
        return (
            self.part[spot].astype(F32)
            + self.from_left[tail or ...].astype(F32)
            + self.from_right[tail or ...].astype(F32)
        )


UNIT = 256
EXPERT_ROWS = D + D // 2
ATTN_ROWS = 288
SHARD_ROWS = EXPERT_ROWS + ATTN_ROWS
FIRST = SHARD_ROWS // 2
KEPT = EXPERT_ROWS - FIRST
CUT = 352
SEMS = pltpu.SemaphoreType.DMA


def gather_shards_kernel(shard_ref, code_ref, seed_ref, out_ref, codes_ref, seeds_ref, *sems):
    section = lax.axis_index("section")
    sibling = {"section": 1 - section}
    ring_y, ring_z = Ring("y"), Ring("z")
    y, z = ring_y.me, ring_z.me
    ring_x = Ring("x")
    x_peers = (ring_x.right, ring_x.left, ring_x.across)
    greet_ids(
        [sibling] + ring_y.near() + ring_z.near() + [ring_x.place(peer) for peer in x_peers]
    )
    out_ref[section, z, y] = shard_ref[...]
    codes_ref[section, ring_x.me] = code_ref[...]
    seeds_ref[ring_x.me] = seed_ref[...]
    halves = (pl.ds(0, HALF), pl.ds(HALF, HALF))
    seeds = RingGather(ring_x, lambda b, h: seeds_ref.at[b, halves[h]], sems[14], sems[15])
    met(8)
    spot = codes_ref.at[section, ring_x.me]
    code_copies = [
        ring_x.copy(spot, spot, sems[10].at[index], sems[11].at[index], peer)
        for index, peer in enumerate(x_peers)
    ]
    for copy in code_copies:
        copy.start()
    half = ATTN_ROWS // 2
    low = (pl.ds(0, 64), pl.ds(64, half - 64))
    high = (pl.ds(half, 64), pl.ds(half + 64, half - 64))
    pair = (pl.ds(0, 2), pl.ds(2, 2))
    near_y = RingGather(ring_y, lambda b, h: out_ref.at[section, z, b, low[h]], sems[0], sems[1])
    near_z = RingGather(ring_z, lambda b, h: out_ref.at[section, b, y, high[h]], sems[2], sems[3])
    far_z = RingGather(
        ring_z, lambda b, h: out_ref.at[section, b, pair[h], pl.ds(0, half)], sems[4], sems[5]
    )
    far_y = RingGather(
        ring_y, lambda b, h: out_ref.at[section, pair[h], b, pl.ds(half, half)], sems[6], sems[7]
    )
    for first, rings in ((True, (near_y, near_z)), (False, (far_z, far_y))):
        for one in rings:
            one.start()
        if first:
            seeds.start()
        for one in rings:
            one.forward()
        if not first:
            seeds.forward()
        for one in rings:
            one.finish()
    across = pltpu.make_async_remote_copy(
        src_ref=out_ref.at[section],
        dst_ref=out_ref.at[section],
        send_sem=sems[8],
        recv_sem=sems[9],
        device_id=sibling,
        device_id_type=MESH,
    )
    across.start()
    for copy in code_copies:
        copy.wait()
    codes_across = pltpu.make_async_remote_copy(
        src_ref=codes_ref.at[section],
        dst_ref=codes_ref.at[section],
        send_sem=sems[12],
        recv_sem=sems[13],
        device_id=sibling,
        device_id_type=MESH,
    )
    codes_across.start()
    codes_across.wait()
    seeds.finish()
    across.wait()


def gather_shards(shard, codes, seed):
    return pl.pallas_call(
        gather_shards_kernel,
        out_shape=(
            jax.ShapeDtypeStruct((2, CTX, CTX, ATTN_ROWS, UNIT), BF16),
            jax.ShapeDtypeStruct((2, CTX, 8, ROWS), F32),
            jax.ShapeDtypeStruct((CTX, ROWS, D), BF16),
        ),
        in_specs=[VMEM] * 3,
        out_specs=[VMEM] * 3,
        scratch_shapes=[SEMS((6,))] * 8
        + [SEMS, SEMS, SEMS((3,)), SEMS((3,)), SEMS, SEMS, SEMS((6,)), SEMS((6,))],
        compiler_params=params(7),
        name="gather_shards",
    )(shard, codes, seed)


HALF_SHARD = SHARD_ROWS // 2
Y_ROWS, Z_ROWS = 352, 368
Z_CUT = Z_ROWS - ATTN_ROWS


def half_sources(half, experts, attn):
    if half == 0:
        return (
            experts.at[:, :, pl.ds(0, Y_ROWS), :],
            experts.at[:, :, pl.ds(Y_ROWS, Z_CUT), :],
            experts.at[:, :, pl.ds(Y_ROWS + Z_CUT, ATTN_ROWS), :],
        )
    return (
        experts.at[:, :, pl.ds(HALF_SHARD, Y_ROWS), :],
        experts.at[:, :, pl.ds(HALF_SHARD + Y_ROWS, Z_CUT), :],
        attn,
    )


class HalfSums:
    def __init__(self, refs, sems, make_y, make_z):
        (
            self.part_y, self.part_z, top_y, bottom_y, left_y, right_y, top_z, bottom_z, left_z, right_z,
            more_z, more_y, top_zz, bottom_zz, left_zz, right_zz, top_yy, bottom_yy, left_yy, right_yy,
        ) = refs
        ring_y, ring_z = Ring("y"), Ring("z")
        self.ring_y, self.ring_z = ring_y, ring_z
        self.first_y = RingSum(
            ring_y, self.part_y, (top_y, bottom_y), left_y, right_y, sems[0], sems[1], 2, make_y
        )
        self.first_z = RingSum(
            ring_z, self.part_z, (top_z, bottom_z), left_z, right_z, sems[2], sems[3], 2, make_z
        )

        def make_zz(index, block):
            more_z[block] = self.first_y.total(block).astype(BF16)

        def make_yy(index, block):
            more_y[block] = self.first_z.total(block).astype(BF16)

        self.then_z = RingSum(
            ring_z, more_z, (top_zz, bottom_zz), left_zz, right_zz, sems[4], sems[5], Y_ROWS // 2, make_zz
        )
        self.then_y = RingSum(
            ring_y, more_y, (top_yy, bottom_yy), left_yy, right_yy, sems[6], sems[7], 176, make_yy
        )

    def first(self, number):
        self.first_y.stage(number)
        self.first_z.stage(number)

    def then(self, number):
        self.then_z.stage(number)
        self.then_y.stage(number)

    def result(self, out_ref):
        out_ref[pl.ds(0, Y_ROWS), :] = self.then_z.total().astype(BF16)
        out_ref[pl.ds(Y_ROWS, Z_ROWS), :] = self.then_y.total().astype(BF16)


def half_scratch():
    shapes = [(CTX, CTX, Y_ROWS, UNIT), (CTX, CTX, Z_ROWS, UNIT)]
    for rows in (Y_ROWS, Z_ROWS):
        shapes += [(2, rows, UNIT)] * 2 + [(CTX, rows, UNIT)] * 2
    shapes += [(CTX, Y_ROWS, UNIT), (CTX, Z_ROWS, UNIT)]
    for rows in (Y_ROWS, Z_ROWS):
        shapes += [(176, UNIT), (rows - 176, UNIT)] + [(rows, UNIT)] * 2
    return [pltpu.VMEM(shape, BF16) for shape in shapes]


HALF_REFS = 20


def add_block(part, incoming, block):
    for other in range(CTX):
        part[block, other] = part[block, other] + incoming[block, other]


def shared_squares(all_ref, ring_y, ring_z, spread):
    from_y, from_z, *sems = spread

    def folded(values):
        squared = values * values
        return jnp.sum(squared, axis=0, keepdims=True)

    in_row = jnp.zeros((1, UNIT), F32)
    out_row = jnp.zeros((1, UNIT), F32)
    attn_row = jnp.zeros((1, UNIT), F32)
    back = jnp.zeros((ATTN_ROWS // 2, UNIT), F32)
    small = jnp.zeros((48, UNIT), F32)
    lanes = lax.broadcasted_iota(jnp.int32, (1, UNIT), 1)
    for block in range(CTX):
        in_row += folded(all_ref[block, :D, :].astype(F32))
        out_row += folded(all_ref[block, D:EXPERT_ROWS, :].astype(F32))
        middle = EXPERT_ROWS + ATTN_ROWS // 2
        back += all_ref[block, EXPERT_ROWS:middle, :].astype(F32)
        attn_row += folded(all_ref[block, middle : middle + 96, :].astype(F32))
        final = all_ref[block, middle + 96 :, :].astype(F32)
        attn_row += jnp.where(lanes < HEAD_DIM, folded(final), 0.0)
        small += final
    attn_row += folded(back)
    small_row = folded(small)
    is_router = (lanes >= LANES) & (lanes < LANES + EXPERTS)
    is_gain = (lanes >= LANES + EXPERTS) & (lanes < LANES + EXPERTS + 2)
    sums = [
        jnp.where(is_gain, small_row, 0.0),
        attn_row,
        jnp.where(is_router, small_row, 0.0),
        in_row,
        out_row,
    ]
    places = lax.broadcasted_iota(jnp.int32, (8, LANES), 1)
    tile = jnp.zeros((8, LANES), F32)
    for index, row in enumerate(sums):
        tile = jnp.where(places == index, jnp.sum(row, axis=1, keepdims=True), tile)

    def shared(one, slots, send, recv, tile):
        slots[one.me] = tile
        copies = []
        for index, peer in enumerate((one.right, one.left, one.across)):
            spot = slots.at[one.me]
            copies.append(one.copy(spot, spot, send.at[index], recv.at[index], peer))
            copies[-1].start()
        for copy in copies:
            copy.wait()
        return (slots[0] + slots[1]) + (slots[2] + slots[3])

    tile = shared(ring_y, from_y, sems[0], sems[1], tile)
    return shared(ring_z, from_z, sems[2], sems[3], tile)


def sum_shards_kernel(
    experts, attn, upper_half_ref, lower_out_ref, upper_out_ref, lower_grad_ref, upper_grad_ref,
    all_ref, squares_ref, outputs_ref, grads_ref, *rest,
):
    halves, rest = rest[:HALF_REFS], rest[HALF_REFS:]
    in_y, in_z, sent_out, sent_grad, sent_half, local, send_s, recv_s, send_w, recv_w, *rest = rest
    spread, rest = rest[:8], rest[8:]
    ring_x = Ring("x")
    section = lax.axis_index("section")
    sibling = {"section": 1 - section}
    first_core = section == 0
    part_y, part_z = halves[:2]

    def make_y(index, block):
        ready(index, 0)
        add_block(part_y, in_y, block)

    def make_z(index, block):
        ready(index, 1)
        ready(index, 2)
        add_block(part_z, in_z, block)

    sums = HalfSums(halves, rest, make_y, make_z)
    ring_y, ring_z = sums.ring_y, sums.ring_z
    far = [one.place(one.across) for one in (ring_y, ring_z)]
    greet_ids([sibling] + ring_x.near() + ring_y.near() + ring_z.near() + far)

    def pieces(index, half, target_y, target_z):
        b_y, b_z = ring_y.order()[index], ring_z.order()[index]
        sources = half_sources(half, experts, attn)
        return (
            (sources[0].at[:, b_y], target_y.at[b_y]),
            (sources[1].at[b_z], target_z.at[b_z, :, pl.ds(0, Z_CUT), :]),
            (sources[2].at[b_z], target_z.at[b_z, :, pl.ds(Z_CUT, ATTN_ROWS), :]),
        )

    def fetch(index, number, source, target):
        return pltpu.make_async_copy(source, target, local.at[index * 3 + number])

    def pass_on(source, target, send, recv):
        return pltpu.make_async_remote_copy(
            src_ref=source,
            dst_ref=target,
            send_sem=send,
            recv_sem=recv,
            device_id=sibling,
            device_id_type=MESH,
        )

    def lend(index, number, source, target):
        at = index * 3 + number
        return pass_on(source, target, send_s.at[at], recv_s.at[at])

    def ready(index, number):
        source, target = pieces(index, 0, part_y, part_z)[number]
        fetch(index, number, source, target).wait()
        source, target = pieces(index, 0, in_y, in_z)[number]
        lend(index, number, source, target).wait_recv()

    def start(kept):
        for index in range(CTX):
            for number, pair in enumerate(pieces(index, kept, part_y, part_z)):
                fetch(index, number, *pair).start()

    def hand(given):
        for index in range(CTX):
            for number, pair in enumerate(pieces(index, given, in_y, in_z)):
                lend(index, number, *pair).start()

    for core in range(2):

        @pl.when(section == core)
        def _():
            start(core)

    met(9)
    own_at = pl.ds(pl.multiple_of(section * HALF_SHARD, HALF_SHARD), HALF_SHARD)
    own = all_ref.at[ring_x.me, own_at]
    cuts = (pl.ds(0, HALF_SHARD), pl.ds(HALF_SHARD, HALF_SHARD))
    rows = RingGather(ring_x, lambda b, h: all_ref.at[b, cuts[h]], spread[0], spread[1])

    @pl.when(first_core)
    def _():
        pass_on(upper_half_ref, own, send_w.at[2], recv_w.at[2]).start()

    @pl.when(section == 1)
    def _():
        own[...] = upper_half_ref[...]

    for core in range(2):

        @pl.when(section == core)
        def _():
            hand(1 - core)

    lower_out, upper_out = lower_out_ref[...], upper_out_ref[...]
    outputs_ref[section] = jnp.where(first_core, lower_out, upper_out)
    sent_out[...] = jnp.where(first_core, upper_out, lower_out)
    lower_grad, upper_grad = lower_grad_ref[...], upper_grad_ref[...]
    grads_ref[section] = jnp.where(first_core, lower_grad, upper_grad)
    sent_grad[...] = jnp.where(first_core, upper_grad, lower_grad)
    swaps = [
        pass_on(sent_out, outputs_ref.at[section], send_w.at[0], recv_w.at[0]),
        pass_on(sent_grad, grads_ref.at[section], send_w.at[1], recv_w.at[1]),
    ]
    for number in range(3):
        sums.first(number)

    @pl.when(section == 1)
    def _():
        pass_on(sent_half, own, send_w.at[2], recv_w.at[2]).wait_recv()
        rows.start()

    for copy in swaps:
        copy.start()
    sums.first(3)
    sums.first(4)

    @pl.when(section == 1)
    def _():
        rows.forward()

    sums.first(5)
    for number in range(6):
        sums.then(number)

    @pl.when(first_core)
    def _():
        sums.result(own)
        pass_on(upper_half_ref, own, send_w.at[2], recv_w.at[2]).wait()
        rows.start()
        rows.forward()

    @pl.when(section == 1)
    def _():
        sums.result(sent_half)
        back = pass_on(sent_half, own, send_w.at[2], recv_w.at[2])
        back.start()
        back.wait_send()

    rows.near()
    rows.far()
    squares_ref[...] = shared_squares(all_ref, ring_y, ring_z, spread[2:])
    rows.sent()
    for copy in swaps:
        copy.wait()
    for index in range(CTX):
        for number, pair in enumerate(pieces(index, 0, in_y, in_z)):
            lend(index, number, *pair).wait_send()


def by_place(array):
    return array.reshape((CTX, CTX) + array.shape[1:])


def sum_shards(lower_e, lower_a, upper_half, lower_out, upper_out, lower_grad, upper_grad):
    return pl.pallas_call(
        sum_shards_kernel,
        out_shape=(
            jax.ShapeDtypeStruct((CTX, SHARD_ROWS, UNIT), BF16),
            jax.ShapeDtypeStruct((8, LANES), F32),
            jax.ShapeDtypeStruct((2, ROWS, D), BF16),
            jax.ShapeDtypeStruct((2, ROWS, D), F32),
        ),
        in_specs=[ANY] * 2 + [VMEM] * 5,
        out_specs=[VMEM] * 4,
        scratch_shapes=half_scratch()
        + [
            pltpu.VMEM((CTX, CTX, Y_ROWS, UNIT), BF16),
            pltpu.VMEM((CTX, CTX, Z_ROWS, UNIT), BF16),
            pltpu.VMEM((ROWS, D), BF16),
            pltpu.VMEM((ROWS, D), F32),
            pltpu.VMEM((HALF_SHARD, UNIT), BF16),
        ]
        + [SEMS((12,))] * 3
        + [SEMS((3,))] * 2
        + [SEMS((6,))] * 2
        + [pltpu.VMEM((CTX, 8, LANES), F32)] * 2
        + [SEMS((3,))] * 4
        + [SEMS((6,))] * 8,
        compiler_params=params(8),
        name="sum_shards",
    )(by_place(lower_e), by_place(lower_a), upper_half, lower_out, upper_out, lower_grad, upper_grad)


def inverse_size(values):
    return lax.rsqrt(jnp.mean(values * values, axis=1, keepdims=True) + EPS_NORM)


def unpack(pack_ref, back_ref, heads_ref):
    def body(index, _):
        rows = pl.ds(pl.multiple_of(index * 48, 16), 48)
        for piece in range(6):
            target = back_ref if piece < 3 else heads_ref
            at = (piece % 3) * UNIT
            target[rows, at : at + UNIT] = pack_ref[index, piece * 48 : (piece + 1) * 48, :]
        return 0

    lax.fori_loop(0, 16, body, 0)


def repack(back_ref, heads_ref, pack_ref):
    def body(index, _):
        rows = pl.ds(pl.multiple_of(index * 48, 16), 48)
        for piece in range(6):
            source = back_ref if piece < 3 else heads_ref
            at = (piece % 3) * UNIT
            pack_ref[index, piece * 48 : (piece + 1) * 48, :] = source[rows, at : at + UNIT]
        return 0

    lax.fori_loop(0, 16, body, 0)


def extend(heads_ref, w_ref):
    lanes = lax.broadcasted_iota(jnp.int32, (D, WIDE), 1)
    for head in range(3 * HEADS_DEV):
        at = head // 2 * WIDE
        values = heads_ref[:, at : at + WIDE].astype(F32)
        if head % 2:
            values = pltpu.roll(values, HEAD_DIM, 1)
        if head < 2 * HEADS_DEV:
            upper = jnp.where(
                lanes < 96, -pltpu.roll(values, 32, 1), pltpu.roll(values, 96, 1)
            )
        else:
            upper = jnp.zeros_like(values)
        w_ref[:, head * WIDE : (head + 1) * WIDE] = jnp.where(
            lanes < HEAD_DIM, values, upper
        ).astype(BF16)


def attn_forward_kernel(
    layer, length_ref, u_ref, packs_ref, table_ref,
    a_out, qkv_out, mass_out, attended_ref, residual_ref, b_ref,
    gains_ref, router_ref, w_out, back_out,
    a_ref, qkv_ref, mass_ref, w_ref, back_ref, out_sem,
    heads_out, heads_w, pack_ref, pack_sem, send_a, recv_a, send_o, recv_o,
):
    me, right, left, across = ring()
    load = pltpu.make_async_copy(packs_ref.at[layer], pack_ref, pack_sem)
    load.start()
    greet((right, left, across))
    length = length_ref[0]
    tokens = u_ref[...].astype(F32)
    load.wait()
    unpack(pack_ref, back_ref, heads_w)
    leaving = [
        pltpu.make_async_copy(source, target, out_sem.at[index])
        for index, (source, target) in enumerate(
            ((back_ref, back_out), (w_ref, w_out), (a_ref, a_out), (qkv_ref, qkv_out), (mass_ref, mass_out))
        )
    ]
    leaving[0].start()
    router_ref[...] = heads_w[:, D - LANES :]
    places = lax.broadcasted_iota(jnp.int32, (8, LANES), 0) + EXPERTS
    picker = jnp.where(places == lax.broadcasted_iota(jnp.int32, (8, LANES), 1), 1.0, 0.0)
    gains_ref[...] = dot_nt(picker.astype(BF16), router_ref[...])
    a_ref[rows_of(me), :] = (tokens * inverse_size(tokens) * gains_ref[0:1, :]).astype(BF16)
    met(3)
    gather_rows(a_ref, send_a, recv_a, lambda: extend(heads_w, w_ref))
    leaving[1].start()
    leaving[2].start()
    for block in range(CTX):
        rows = pl.ds(block * ROWS, ROWS)
        table = table_ref[rows, :]
        mixed = dot(a_ref[rows, :], w_ref[...])
        for part in range(3 * HEADS_DEV):
            lanes = slice(part * WIDE, (part + 1) * WIDE)
            piece = mixed[:, lanes]
            if part < 2 * HEADS_DEV:
                turned = piece * table
                piece = turned + pltpu.roll(turned, WIDE // 2, 1)
            qkv_ref[rows, lanes] = piece.astype(BF16)
    leaving[3].start()

    def handed(block):
        step = lax.rem(block - me + CTX, CTX)
        return remote(
            heads_out.at[block], attended_ref.at[me], send_o.at[step], recv_o.at[step], block
        )

    for block in reversed(range(CTX)):
        rows = pl.ds(block * ROWS, ROWS)
        keys = (block + 1) * ROWS
        allowed = allowed_keys(block, keys, length)
        outs = []
        for head in range(HEADS_DEV):
            queries = qkv_ref[rows, head * WIDE : (head + 1) * WIDE]
            key_lanes = slice((HEADS_DEV + head) * WIDE, (HEADS_DEV + head + 1) * WIDE)
            value_lanes = slice((2 * HEADS_DEV + head) * WIDE, (2 * HEADS_DEV + head + 1) * WIDE)
            scores = dot_nt(queries, qkv_ref[:keys, key_lanes]) * SCORE_SCALE
            scores = jnp.where(allowed, scores, MASK_VALUE)
            top = jnp.max(scores, axis=1, keepdims=True)
            raw = jnp.exp(scores - top)
            total = jnp.sum(raw, axis=1, keepdims=True)
            probs = (raw * (1.0 / total)).astype(BF16)
            outs.append(dot(probs, qkv_ref[:keys, value_lanes]))
            mass_ref[head, rows, :] = top + jnp.log(total)
        first = (outs[0] + pltpu.roll(outs[1], WIDE // 2, 1)).astype(BF16)
        second = outs[2][:, : WIDE // 2].astype(BF16)
        heads_out[block, :, :WIDE] = first
        heads_out[block, :, WIDE:] = second

        @pl.when(block != me)
        def _():
            handed(block).start()

    leaving[4].start()
    attended_ref[me] = heads_out[me]
    for step in range(1, CTX):
        pltpu.make_async_copy(heads_out.at[0], attended_ref.at[0], recv_o.at[step]).wait()
    residual = tokens
    for block in range(CTX):
        residual = residual + dot(attended_ref[block], back_ref[block * COLS : (block + 1) * COLS, :])
    residual_ref[...] = residual
    b_ref[...] = (residual * inverse_size(residual) * gains_ref[1:2, :]).astype(BF16)
    for step in range(1, CTX):
        pltpu.make_async_copy(heads_out.at[0], attended_ref.at[0], send_o.at[step]).wait()
    for copy in leaving:
        copy.wait()


def attn_forward(layer, length, u, packs, table):
    sems = pltpu.SemaphoreType.DMA
    return pl.pallas_call(
        functools.partial(attn_forward_kernel, layer),
        out_shape=(
            jax.ShapeDtypeStruct((SEQ, D), BF16),
            jax.ShapeDtypeStruct((SEQ, EXT), BF16),
            jax.ShapeDtypeStruct((HEADS_DEV, SEQ, 1), F32),
            jax.ShapeDtypeStruct((CTX, ROWS, COLS), BF16),
            jax.ShapeDtypeStruct((ROWS, D), F32),
            jax.ShapeDtypeStruct((ROWS, D), BF16),
            jax.ShapeDtypeStruct((8, D), F32),
            jax.ShapeDtypeStruct((D, LANES), BF16),
            jax.ShapeDtypeStruct((D, EXT), BF16),
            jax.ShapeDtypeStruct((D, D), BF16),
        ),
        in_specs=[
            SMEM,
            VMEM,
            ANY,
            VMEM,
        ],
        out_specs=[ANY] * 3 + [VMEM] * 5 + [ANY] * 2,
        scratch_shapes=[
            pltpu.VMEM((SEQ, D), BF16),
            pltpu.VMEM((SEQ, EXT), BF16),
            pltpu.VMEM((HEADS_DEV, SEQ, 1), F32),
            pltpu.VMEM((D, EXT), BF16),
            pltpu.VMEM((D, D), BF16),
            sems((5,)),
            pltpu.VMEM((CTX, ROWS, COLS), BF16),
            pltpu.VMEM((D, D), BF16),
            pltpu.VMEM((16, ATTN_ROWS, UNIT), BF16),
            sems,
        ]
        + [sems((6,)), sems((6,)), sems((CTX,)), sems((CTX,))],
        compiler_params=params(1 + 10 * layer),
        name="attn_forward",
    )(length, u, packs, table)


def attn_backward_kernel(
    hosting, length_ref, u_ref, gains_ref, router_ref, w_in, back_in, table_in,
    a_in, qkv_in, mass_in, attended_in, residual_ref, second_in, gates_ref,
    delta_ref, db_ref, gate_grad_ref, *rest,
):
    (
        w_ref, back_ref, table_ref, a_ref, qkv_ref, mass_ref, attended_ref, second_ref, in_sem, *rest,
    ) = rest[-9:] + rest[:-9]
    coming = [
        pltpu.make_async_copy(source, target, in_sem.at[index])
        for index, (source, target) in enumerate(
            (
                (back_in, back_ref), (attended_in, attended_ref), (second_in, second_ref),
                (qkv_in, qkv_ref), (mass_in, mass_ref), (table_in, table_ref), (w_in, w_ref), (a_in, a_ref),
            )
        )
    ]
    for copy in coming:
        copy.start()
    if hosting:
        upper_e, upper_a, lent, *rest = rest
    input_ref, pack_ref, lower_ref = rest[:3]
    rest = rest[3:]
    if hosting:
        half_ref, *rest = rest
        rest, hosted = rest[:15], rest[15:]
    dheads_ref, dback_ref = rest[:2]
    rest = rest[2:]
    key_acc, value_acc, dz, grads_out, grads_in, send_o, recv_o = rest[:7]
    part, across_in, from_left, from_right, send_r, recv_r = rest[7:13]
    me, right, left, across = ring()
    greet((right, left, across))
    if hosting:
        refs, (in_y, in_z, local, *sems) = hosted[:HALF_REFS], hosted[HALF_REFS:]
        part_y, part_z = refs[:2]
        section = lax.axis_index("section")
        sums = HalfSums(
            refs,
            sems,
            lambda index, block: add_block(part_y, in_y, block),
            lambda index, block: add_block(part_z, in_z, block),
        )
        greet_ids(sums.ring_y.near() + sums.ring_z.near())

        def loads(half):
            sources = half_sources(half, upper_e, upper_a)
            pairs = [
                (sources[1], part_z.at[:, :, pl.ds(0, Z_CUT), :]),
                (sources[2], part_z.at[:, :, pl.ds(Z_CUT, ATTN_ROWS), :]),
                (lent.at[:, :, pl.ds(Y_ROWS, Z_ROWS), :], in_z),
            ]
            for block in range(CTX):
                pairs.append((sources[0].at[:, block], part_y.at[block]))
                pairs.append((lent.at[:, block, pl.ds(0, Y_ROWS), :], in_y.at[block]))
            return [
                pltpu.make_async_copy(source, target, local.at[index])
                for index, (source, target) in enumerate(pairs)
            ]

        for core in range(2):

            @pl.when(section == core)
            def _():
                for copy in loads(core):
                    copy.start()

    length = length_ref[0]
    lanes = lax.broadcasted_iota(jnp.int32, (ROWS, LANES), 1)
    gates = gates_ref[...]
    gate_grads = jnp.where(lanes < EXPERTS, gate_grad_ref[...], 0.0)
    logit_grad = gates * (gate_grads - jnp.sum(gates * gate_grads, axis=1, keepdims=True))
    logit_grad = logit_grad.astype(BF16)
    second_grad = db_ref[...] + dot_nt(logit_grad, router_ref[...])
    residual = residual_ref[...]
    scale_two = inverse_size(residual)
    normal_two = residual * scale_two
    gain_two_terms = second_grad * normal_two
    scaled_two = second_grad * gains_ref[1:2, :]
    residual_grad = delta_ref[...].astype(F32) + scale_two * (
        scaled_two - normal_two * jnp.mean(scaled_two * normal_two, axis=1, keepdims=True)
    )
    input_ref[...] = residual_grad
    branch_grad = residual_grad.astype(BF16)
    met(7 if hosting else 3)
    coming[0].wait()

    for block in range(CTX):
        grads_out[block] = dot_nt(branch_grad, back_ref[block * COLS : (block + 1) * COLS, :]).astype(
            BF16
        )

        @pl.when(block != me)
        def _():
            step = lax.rem(block - me + CTX, CTX)
            remote(
                grads_out.at[block], grads_in.at[me], send_o.at[step], recv_o.at[step], block
            ).start()

    grads_in[me] = grads_out[me]
    if hosting:
        for copy in loads(0):
            copy.wait()
        for number in range(3):
            sums.first(number)
    coming[1].wait()
    coming[2].wait()
    for block in range(CTX):
        dback_ref[block * COLS : (block + 1) * COLS, :] = dot_tn(
            attended_ref[block], branch_grad
        ).astype(BF16)
    router_terms = dot_tn(second_ref[...], logit_grad)
    ones = jnp.ones((ROWS, LANES), F32)
    gain_two_column = lax.dot_general(
        gain_two_terms, ones, TN, precision=EXACT, preferred_element_type=F32
    )
    key_acc[...] = jnp.zeros_like(key_acc)
    value_acc[...] = jnp.zeros_like(value_acc)
    for copy in coming[3:]:
        copy.wait()
    for step in range(1, CTX):
        pltpu.make_async_copy(grads_out.at[0], grads_in.at[0], recv_o.at[step]).wait()
    for step in range(1, CTX):
        pltpu.make_async_copy(grads_out.at[0], grads_in.at[0], send_o.at[step]).wait()
    for block in range(CTX):
        rows = pl.ds(block * ROWS, ROWS)
        keys = (block + 1) * ROWS
        allowed = allowed_keys(block, keys, length)
        pair = grads_in[block, :, :WIDE]
        tail = grads_in[block, :, WIDE:]
        head_grads = (
            pair,
            pltpu.roll(pair.astype(F32), WIDE // 2, 1).astype(BF16),
            jnp.concatenate([tail, jnp.zeros_like(tail)], axis=1),
        )
        for head in range(HEADS_DEV):
            queries = qkv_ref[rows, head * WIDE : (head + 1) * WIDE]
            keys_all = qkv_ref[:keys, (HEADS_DEV + head) * WIDE : (HEADS_DEV + head + 1) * WIDE]
            values_all = qkv_ref[
                :keys, (2 * HEADS_DEV + head) * WIDE : (2 * HEADS_DEV + head + 1) * WIDE
            ]
            grads = head_grads[head]
            scores = dot_nt(queries, keys_all) * SCORE_SCALE
            probs = jnp.where(allowed, jnp.exp(scores - mass_ref[head, rows, :]), 0.0)
            prob_grad = dot_nt(grads, values_all)
            row_sum = jnp.sum(probs * prob_grad, axis=1, keepdims=True)
            score_grad = (probs * (prob_grad - row_sum)).astype(BF16)
            query_grad = dot(score_grad, keys_all) * (HEAD_DIM**-0.5)
            dz[rows, head * WIDE : (head + 1) * WIDE] = (query_grad * table_ref[rows, :]).astype(BF16)
            spot = slice(head * WIDE, (head + 1) * WIDE)
            key_acc[:keys, spot] += dot_tn(score_grad, queries)
            value_acc[:keys, spot] += dot_tn(probs.astype(BF16), grads)
        if hosting and block == 2:
            sums.first(3)
            sums.first(4)
    for block in range(CTX):
        rows = pl.ds(block * ROWS, ROWS)
        table = table_ref[rows, :] * (HEAD_DIM**-0.5)
        for head in range(HEADS_DEV):
            spot = slice(head * WIDE, (head + 1) * WIDE)
            at = (HEADS_DEV + head) * WIDE
            dz[rows, at : at + WIDE] = (key_acc[rows, spot] * table).astype(BF16)
            at = (2 * HEADS_DEV + head) * WIDE
            dz[rows, at : at + WIDE] = value_acc[rows, spot].astype(BF16)

    if hosting:
        sums.first(5)
        for number in range(3):
            sums.then(number)

    def make(block):
        part[rows_of(block), :] = dot_nt(dz[rows_of(block), :], w_ref[...]).astype(BF16)

    def beside():
        wide_lanes = lax.broadcasted_iota(jnp.int32, (D, WIDE), 1)
        pieces = []
        for piece in range(3):
            spot = slice(piece * HEADS_DEV * WIDE, (piece + 1) * HEADS_DEV * WIDE)
            terms = dot_tn(a_ref[...], dz[:, spot])
            for head in range(HEADS_DEV):
                term = terms[:, head * WIDE : (head + 1) * WIDE]
                if piece < 2:
                    term = term + jnp.where(
                        wide_lanes < HEAD_DIM // 2,
                        pltpu.roll(term, HEAD_DIM // 2, 1),
                        -pltpu.roll(term, WIDE - HEAD_DIM // 2, 1),
                    )
                pieces.append(term)
        for pair in range(4):
            joined = jnp.where(
                wide_lanes < HEAD_DIM,
                pieces[2 * pair],
                pltpu.roll(pieces[2 * pair + 1], HEAD_DIM, 1),
            )
            dheads_ref[:, pair * WIDE : (pair + 1) * WIDE] = joined.astype(BF16)
        dheads_ref[:, 4 * WIDE : 5 * WIDE] = jnp.where(
            wide_lanes < HEAD_DIM, pieces[8], 0.0
        ).astype(BF16)
        if hosting:
            sums.then(3)
            sums.then(4)

    normed_grad = reduce_rows(make, part, across_in, from_left, from_right, send_r, recv_r, beside)
    tokens = u_ref[...].astype(F32)
    scale_one = inverse_size(tokens)
    normal_one = tokens * scale_one
    gain_one_column = lax.dot_general(
        normed_grad * normal_one, ones, TN, precision=EXACT, preferred_element_type=F32
    )
    scaled_one = normed_grad * gains_ref[0:1, :]
    input_grad = input_ref[...] + scale_one * (
        scaled_one - normal_one * jnp.mean(scaled_one * normal_one, axis=1, keepdims=True)
    )
    input_ref[...] = input_grad
    small_lanes = lax.broadcasted_iota(jnp.int32, (D, LANES), 1)
    dheads_ref[:, D - LANES :] = jnp.where(
        small_lanes == EXPERTS,
        gain_one_column,
        jnp.where(small_lanes == EXPERTS + 1, gain_two_column, router_terms),
    ).astype(BF16)
    repack(dback_ref, dheads_ref, pack_ref)
    lower_ref[...] = input_grad.astype(BF16)
    if hosting:
        sums.then(5)
        sums.result(half_ref)


def attn_backward(length, arrays, upper=()):
    sems = pltpu.SemaphoreType.DMA
    out_shape = [
        jax.ShapeDtypeStruct((ROWS, D), F32),
        jax.ShapeDtypeStruct((16, ATTN_ROWS, UNIT), BF16),
        jax.ShapeDtypeStruct((ROWS, D), BF16),
    ]
    if upper:
        out_shape.append(jax.ShapeDtypeStruct((HALF_SHARD, UNIT), BF16))
    scratch = [
        pltpu.VMEM((D, D), BF16),
        pltpu.VMEM((D, D), BF16),
        pltpu.VMEM((SEQ, HEADS_DEV * WIDE), F32),
        pltpu.VMEM((SEQ, HEADS_DEV * WIDE), F32),
        pltpu.VMEM((SEQ, EXT), BF16),
        pltpu.VMEM((CTX, ROWS, COLS), BF16),
        pltpu.VMEM((CTX, ROWS, COLS), BF16),
        sems((CTX,)),
        sems((CTX,)),
    ] + REDUCE_SCRATCH
    if upper:
        scratch += half_scratch()
        scratch += [
            pltpu.VMEM((CTX, CTX, Y_ROWS, UNIT), BF16),
            pltpu.VMEM((CTX, CTX, Z_ROWS, UNIT), BF16),
            sems((11,)),
        ] + [sems((6,))] * 8
    late = (3, 4, 5, 6, 7, 8, 9, 11)
    specs = [ANY if index in late else VMEM for index in range(len(arrays))]
    for index in late:
        scratch.append(pltpu.VMEM(arrays[index].shape, arrays[index].dtype))
    scratch.append(sems((len(late),)))
    return pl.pallas_call(
        functools.partial(attn_backward_kernel, bool(upper)),
        out_shape=tuple(out_shape),
        in_specs=[SMEM] + specs + [ANY] * len(upper),
        out_specs=[VMEM] * len(out_shape),
        scratch_shapes=scratch,
        compiler_params=params(4 if upper else 3),
        name="attn_backward",
    )(length, *arrays, *(by_place(array) for array in upper))


GROUP = 4
GROUPS = 16 // GROUP
GROUP_UNITS = GROUP * LANES
SPLIT = EXPERT_ROWS // 2
SUM_SCRATCH = [
    pltpu.VMEM((CTX, ROWS, D), BF16),
    pltpu.VMEM((HALF, D), BF16),
    pltpu.VMEM((HALF, D), BF16),
    pltpu.VMEM((ROWS, D), BF16),
    pltpu.VMEM((ROWS, D), BF16),
    SEMS((6,)),
    SEMS((6,)),
]


def weight_copies(w_ref, win, wout, sem):
    groups = []
    for group in range(GROUPS):
        shards = pl.ds(group * GROUP, GROUP)
        pairs = [
            (w_ref.at[0, shards], win.at[shards, pl.ds(0, SPLIT), :]),
            (w_ref.at[1, shards, pl.ds(0, D - SPLIT), :], win.at[shards, pl.ds(SPLIT, D - SPLIT), :]),
        ]
        for piece in range(D // UNIT):
            pairs.append(
                (
                    w_ref.at[1, shards, pl.ds(D - SPLIT + piece * LANES, LANES), :],
                    wout.at[shards, :, pl.ds(piece * UNIT, UNIT)],
                )
            )
        groups.append(
            [
                pltpu.make_async_copy(source, target, sem.at[group * 5 + index])
                for index, (source, target) in enumerate(pairs)
            ]
        )
    return groups


def wout_group(wout, group):
    return wout[group * GROUP : (group + 1) * GROUP].reshape(GROUP_UNITS, D)


def ffn_forward_kernel(
    b_own_ref, residual_ref, codes_ref, router_ref, w_ref,
    y_ref, b_ref, gates_ref, gate_ref, kept_ref,
    win, wout, kept_out, acc, w_sem, kept_sem, send_b, recv_b,
    part, top_in, bottom_in, from_left, from_right, send, recv,
):
    ring = Ring("x")
    greet_ids(ring.near())
    loads = weight_copies(w_ref, win, wout, w_sem)
    for group in loads:
        for copy in group:
            copy.start()
    b_ref[ring.me] = b_own_ref[...]
    met(2)
    halves = (pl.ds(0, HALF), pl.ds(HALF, HALF))
    rows = RingGather(ring, lambda b, h: b_ref.at[b, halves[h]], send_b, recv_b)
    rows.start()
    section = lax.axis_index("section")
    lanes = lax.broadcasted_iota(jnp.int32, (ROWS, LANES), 1)
    picker = jnp.where(lax.broadcasted_iota(jnp.int32, (8, LANES), 0) == section, 1.0, 0.0)
    stores = []

    def make(index, block):
        b_rows = b_ref[block]
        slot = index % 2
        for shard in range(16):
            if index == 0 and shard % GROUP == 0:
                for copy in loads[shard // GROUP]:
                    copy.wait()
            if index >= 2 and shard == 0:
                stores[index - 2].wait()
            hidden = dot(b_rows, win[shard])
            kept_out[slot, shard] = hidden.astype(BF16)
            gate_part = hidden[:, :LANES]
            at = shard % GROUP * LANES
            acc_act = (gate_part / (1.0 + jnp.exp(-gate_part)) * hidden[:, LANES:]).astype(BF16)
            if shard % GROUP == 0:
                acted = []
            acted.append(acc_act)
            if shard % GROUP == GROUP - 1:
                terms = dot(jnp.concatenate(acted, axis=1), wout_group(wout, shard // GROUP))
                acc[...] = terms if shard < GROUP else acc[...] + terms
        stores.append(pltpu.make_async_copy(kept_out.at[slot], kept_ref.at[block], kept_sem.at[slot]))
        stores[-1].start()
        logits = dot(b_rows, router_ref[...])
        codes = lax.dot_general(
            codes_ref[block], picker, TN, precision=EXACT, preferred_element_type=F32
        )
        named = (lanes < EXPERTS) & (lanes != jnp.round(codes).astype(jnp.int32))
        chosen = jnp.where(named, logits, MASK_VALUE)
        raw = jnp.where(named, jnp.exp(chosen - jnp.max(chosen, axis=1, keepdims=True)), 0.0)
        gates = raw / jnp.sum(raw, axis=1, keepdims=True)
        if index == 0:
            gates_ref[...] = gates
        gates = jnp.where(lanes == EXPERTS, 1.0, gates)
        gate = jnp.sum(jnp.where(lanes == ring.me, gates, 0.0), axis=1, keepdims=True)
        gate_ref[block] = gate
        part[block] = (acc[...] * gate).astype(BF16)

    order = {ring_index: number for number, ring_index in enumerate(("me", "right", "left", "across"))}

    def from_sum(position, block):
        make({0: order["across"], 1: order["right"], 2: order["left"], 3: order["me"]}[position], block)

    sums = RingSum(
        ring, part, (top_in, bottom_in), from_left, from_right, send, recv, HALF, from_sum
    )
    sums.stage(4)
    rows.forward()
    rows.near()
    sums.stage(1)
    sums.stage(2)
    rows.far()
    sums.stage(0)
    sums.stage(3)
    sums.stage(5)
    y_ref[...] = (residual_ref[...] + sums.total()).astype(BF16)
    rows.sent()
    stores[2].wait()
    stores[3].wait()


def ffn_forward(b_own, residual, codes, router, weights):
    return pl.pallas_call(
        ffn_forward_kernel,
        out_shape=(
            jax.ShapeDtypeStruct((ROWS, D), BF16),
            jax.ShapeDtypeStruct((CTX, ROWS, D), BF16),
            jax.ShapeDtypeStruct((ROWS, LANES), F32),
            jax.ShapeDtypeStruct((CTX, ROWS, 1), F32),
            jax.ShapeDtypeStruct((CTX, 16, ROWS, UNIT), BF16),
        ),
        in_specs=[VMEM] * 4 + [ANY],
        out_specs=[VMEM] * 4 + [ANY],
        scratch_shapes=[
            pltpu.VMEM((16, D, UNIT), BF16),
            pltpu.VMEM((16, LANES, D), BF16),
            pltpu.VMEM((2, 16, ROWS, UNIT), BF16),
            pltpu.VMEM((ROWS, D), F32),
            SEMS((5 * GROUPS,)),
            SEMS((2,)),
            SEMS((6,)),
            SEMS((6,)),
        ]
        + SUM_SCRATCH,
        compiler_params=params(5),
        name="ffn_forward",
    )(b_own, residual, codes, router, weights)


def ffn_backward_kernel(
    lending, b_ref, gate_ref, delta_own_ref, kept_ref, w_ref, *rest,
):
    if lending:
        upper_e, upper_a, db_ref, gate_grad_ref, dw_ref, lent_ref, *rest = rest
        *rest, send_l, recv_l = rest
    else:
        db_ref, gate_grad_ref, dw_ref, *rest = rest
    (
    delta, acc, gate_acc, slot_grad, hidden, acted, win, wout, staged, rows_out, rows_in, b_turned,
    w_sem, kept_sem, dw_sem, send_d, recv_d, send_g, recv_g,
    part, top_in, bottom_in, from_left, from_right, send, recv,
    ) = rest
    ring = Ring("x")
    peers = (ring.right, ring.left, ring.across)
    section = lax.axis_index("section")
    sibling = {"section": 1 - section}
    greet_ids([ring.place(peer) for peer in peers] + ([sibling] if lending else []))
    blocks = (ring.me, ring.right, ring.left, ring.across)
    kept_loads = [
        pltpu.make_async_copy(
            kept_ref.at[block], hidden.at[:, rows_of(block), :], kept_sem.at[index]
        )
        for index, block in enumerate(blocks)
    ]
    loads = weight_copies(w_ref, win, wout, w_sem)
    kept_loads[0].start()
    for group in loads:
        for copy in group:
            copy.start()
    for copy in kept_loads[1:]:
        copy.start()
    delta[ring.me] = delta_own_ref[...]
    met(4 if lending else 3)
    if lending:
        first_rows = pl.ds(0, KEPT)
        last_rows = pl.ds(KEPT, ATTN_ROWS)

        def lends(given):
            sources = (
                (upper_e.at[:, first_rows, :], upper_e.at[:, last_rows, :])
                if given == 0
                else (upper_e.at[:, pl.ds(HALF_SHARD, KEPT), :], upper_a)
            )
            return [
                pltpu.make_async_remote_copy(
                    src_ref=source,
                    dst_ref=lent_ref.at[:, target, :],
                    send_sem=send_l.at[index],
                    recv_sem=recv_l.at[index],
                    device_id=sibling,
                    device_id_type=MESH,
                )
                for index, (source, target) in enumerate(zip(sources, (first_rows, last_rows)))
            ]

        for core in range(2):

            @pl.when(section == core)
            def _():
                for copy in lends(1 - core):
                    copy.start()

    halves = (pl.ds(0, HALF), pl.ds(HALF, HALF))
    rows = RingGather(ring, lambda b, h: delta.at[b, halves[h]], send_d, recv_d)
    rows.start()
    own_row = lax.broadcasted_iota(jnp.int32, (8, LANES), 0) == ring.me
    picker = jnp.where(own_row, 1.0, 0.0)
    handed = [
        ring.copy(rows_out.at[peer], rows_in.at[index], send_g.at[index], recv_g.at[index], peer)
        for index, peer in enumerate(peers)
    ]

    def make(index, block):
        kept_loads[index].wait()
        at = rows_of(block)
        gate = gate_ref[block]
        delta_rows = delta[block]
        slot_grad[at, :] = (delta_rows.astype(F32) * gate).astype(BF16)
        gate_sum = jnp.zeros((ROWS, LANES), F32)
        for group in range(GROUPS):
            if index == 0:
                for copy in loads[group]:
                    copy.wait()
            act_grad_all = dot_nt(delta_rows, wout_group(wout, group))
            second_grad = None
            for inner in range(GROUP):
                shard = group * GROUP + inner
                values = hidden[shard, at, :].astype(F32)
                gate_part = values[:, :LANES]
                up_part = values[:, LANES:]
                act_grad = act_grad_all[:, inner * LANES : (inner + 1) * LANES]
                sigmoid = 1.0 / (1.0 + jnp.exp(-gate_part))
                silu = gate_part * sigmoid
                act = (silu * up_part).astype(BF16)
                acted[at, shard * LANES : (shard + 1) * LANES] = act
                gate_sum += act.astype(F32) * act_grad
                act_grad = act_grad * gate
                gate_grad = act_grad * up_part * (sigmoid * (1.0 + gate_part * (1.0 - sigmoid)))
                pair = jnp.concatenate([gate_grad, act_grad * silu], axis=1).astype(BF16)
                hidden[shard, at, :] = pair
                term = dot_nt(pair, win[shard])
                second_grad = term if second_grad is None else second_grad + term
            acc[...] = second_grad if group == 0 else acc[...] + second_grad
        part[block] = acc[...].astype(BF16)
        rows_out[block] = lax.dot_general(
            picker, gate_sum, NT, precision=EXACT, preferred_element_type=F32
        )
        if index > 0:
            handed[index - 1].start()

    def from_sum(position, block):
        make((3, 1, 2, 0)[position], block)

    sums = RingSum(
        ring, part, (top_in, bottom_in), from_left, from_right, send, recv, HALF, from_sum
    )
    sums.stage(4)
    b_turned[...] = b_ref[...].reshape(SEQ, D).T
    rows.forward()
    rows.near()
    sums.stage(1)
    sums.stage(2)
    rows.far()
    sums.stage(0)
    stores = []
    for group in range(GROUPS):
        slot = group % 2
        if group == 1:
            sums.stage(3)
        if group >= 2:
            stores[group - 2].wait()
        for inner in range(GROUP):
            staged[slot, inner, :D, :] = dot(b_turned[...], hidden[group * GROUP + inner]).astype(BF16)
        whole_out = dot_tn(
            acted[:, group * GROUP_UNITS : (group + 1) * GROUP_UNITS], slot_grad[...]
        ).astype(BF16)
        for inner in range(GROUP):
            for piece in range(D // UNIT):
                at = D + piece * LANES
                staged[slot, inner, at : at + LANES, :] = whole_out[
                    inner * LANES : (inner + 1) * LANES, piece * UNIT : (piece + 1) * UNIT
                ]
        stores.append(
            pltpu.make_async_copy(
                staged.at[slot], dw_ref.at[pl.ds(group * GROUP, GROUP)], dw_sem.at[slot]
            )
        )
        stores[-1].start()
    sums.stage(5)
    db_ref[...] = sums.total()
    for copy in handed:
        copy.wait()
    rows_all = rows_out[ring.me] + rows_in[0] + rows_in[1] + rows_in[2]
    diagonal = jnp.where(
        lax.broadcasted_iota(jnp.int32, (8, LANES), 0)
        == lax.broadcasted_iota(jnp.int32, (8, LANES), 1),
        1.0,
        0.0,
    )
    gate_grad_ref[...] = lax.dot_general(
        rows_all, diagonal, TN, precision=EXACT, preferred_element_type=F32
    )
    rows.sent()
    stores[2].wait()
    stores[3].wait()
    if lending:
        for copy in lends(0):
            copy.wait()


def ffn_backward(b_all, gate_col, delta_own, kept, weights, upper=()):
    out_shape = [
        jax.ShapeDtypeStruct((ROWS, D), F32),
        jax.ShapeDtypeStruct((ROWS, LANES), F32),
        jax.ShapeDtypeStruct((16, EXPERT_ROWS, UNIT), BF16),
    ]
    if upper:
        out_shape.append(jax.ShapeDtypeStruct((16, HALF_SHARD, UNIT), BF16))
    return pl.pallas_call(
        functools.partial(ffn_backward_kernel, bool(upper)),
        out_shape=out_shape,
        in_specs=[VMEM] * 3 + [ANY] * (2 + len(upper)),
        out_specs=[VMEM] * 2 + [ANY] * (len(out_shape) - 2),
        scratch_shapes=[
            pltpu.VMEM((CTX, ROWS, D), BF16),
            pltpu.VMEM((ROWS, D), F32),
            pltpu.VMEM((8, LANES), F32),
            pltpu.VMEM((SEQ, D), BF16),
            pltpu.VMEM((16, SEQ, UNIT), BF16),
            pltpu.VMEM((SEQ, FFN), BF16),
            pltpu.VMEM((16, D, UNIT), BF16),
            pltpu.VMEM((16, LANES, D), BF16),
            pltpu.VMEM((2, GROUP, EXPERT_ROWS, UNIT), BF16),
            pltpu.VMEM((CTX, 8, ROWS), F32),
            pltpu.VMEM((3, 8, ROWS), F32),
            pltpu.VMEM((D, SEQ), BF16),
            SEMS((5 * GROUPS,)),
            SEMS((CTX,)),
            SEMS((2,)),
            SEMS((6,)),
            SEMS((6,)),
            SEMS((3,)),
            SEMS((3,)),
        ]
        + SUM_SCRATCH
        + ([SEMS((2,)), SEMS((2,))] if upper else []),
        compiler_params=params(10 if upper else 6),
        name="ffn_backward",
    )(b_all, gate_col, delta_own, kept, weights, *upper)


def ffn_both_kernel(
    b_own_ref, residual_ref, codes_ref, router_ref, delta_in, w_ref,
    y_ref, gates_ref, db_ref, gate_grad_ref, dw_ref,
    b_ref, gate_ref, delta, acc, slot_grad, hidden, acted, win, wout, staged, rows_out, rows_in, b_turned,
    w_sem, dw_sem, send_b, recv_b, delta_sem, send_g, recv_g, *sum_refs,
):
    ring = Ring("x")
    peers = (ring.right, ring.left, ring.across)
    greet_ids([ring.place(peer) for peer in peers])
    loads = weight_copies(w_ref, win, wout, w_sem)
    for group in loads:
        for copy in group:
            copy.start()
    b_ref[ring.me] = b_own_ref[...]
    seeds = pltpu.make_async_copy(delta_in, delta, delta_sem)
    seeds.start()
    met(3)
    halves = (pl.ds(0, HALF), pl.ds(HALF, HALF))
    rows = RingGather(ring, lambda b, h: b_ref.at[b, halves[h]], send_b, recv_b)
    rows.start()
    section = lax.axis_index("section")
    lanes = lax.broadcasted_iota(jnp.int32, (ROWS, LANES), 1)
    code_picker = jnp.where(lax.broadcasted_iota(jnp.int32, (8, LANES), 0) == section, 1.0, 0.0)
    row_picker = jnp.where(lax.broadcasted_iota(jnp.int32, (8, LANES), 0) == ring.me, 1.0, 0.0)
    handed = [
        ring.copy(rows_out.at[peer], rows_in.at[index], send_g.at[index], recv_g.at[index], peer)
        for index, peer in enumerate(peers)
    ]
    part_y, part_b = sum_refs[0], sum_refs[7]

    def forward(index, block):
        at = rows_of(block)
        b_rows = b_ref[block]
        for group in range(GROUPS):
            if index == 0:
                for copy in loads[group]:
                    copy.wait()
            acts = []
            for inner in range(GROUP):
                shard = group * GROUP + inner
                values = dot(b_rows, win[shard])
                hidden[shard, at, :] = values.astype(BF16)
                gate_part = values[:, :LANES]
                acts.append(
                    (gate_part / (1.0 + jnp.exp(-gate_part)) * values[:, LANES:]).astype(BF16)
                )
            terms = dot(jnp.concatenate(acts, axis=1), wout_group(wout, group))
            acc[...] = terms if group == 0 else acc[...] + terms
        logits = dot(b_rows, router_ref[...])
        codes = lax.dot_general(
            codes_ref[block], code_picker, TN, precision=EXACT, preferred_element_type=F32
        )
        named = (lanes < EXPERTS) & (lanes != jnp.round(codes).astype(jnp.int32))
        chosen = jnp.where(named, logits, MASK_VALUE)
        raw = jnp.where(named, jnp.exp(chosen - jnp.max(chosen, axis=1, keepdims=True)), 0.0)
        gates = raw / jnp.sum(raw, axis=1, keepdims=True)
        if index == 0:
            gates_ref[...] = gates
        gates = jnp.where(lanes == EXPERTS, 1.0, gates)
        gate = jnp.sum(jnp.where(lanes == ring.me, gates, 0.0), axis=1, keepdims=True)
        gate_ref[block] = gate
        part_y[block] = (acc[...] * gate).astype(BF16)

    def backward(index, block):
        at = rows_of(block)
        gate = gate_ref[block]
        delta_rows = delta[block]
        slot_grad[at, :] = (delta_rows.astype(F32) * gate).astype(BF16)
        gate_sum = jnp.zeros((ROWS, LANES), F32)
        for group in range(GROUPS):
            act_grad_all = dot_nt(delta_rows, wout_group(wout, group))
            second_grad = None
            for inner in range(GROUP):
                shard = group * GROUP + inner
                values = hidden[shard, at, :].astype(F32)
                gate_part = values[:, :LANES]
                up_part = values[:, LANES:]
                act_grad = act_grad_all[:, inner * LANES : (inner + 1) * LANES]
                sigmoid = 1.0 / (1.0 + jnp.exp(-gate_part))
                silu = gate_part * sigmoid
                act = (silu * up_part).astype(BF16)
                acted[at, shard * LANES : (shard + 1) * LANES] = act
                gate_sum += act.astype(F32) * act_grad
                act_grad = act_grad * gate
                gate_grad = act_grad * up_part * (sigmoid * (1.0 + gate_part * (1.0 - sigmoid)))
                pair = jnp.concatenate([gate_grad, act_grad * silu], axis=1).astype(BF16)
                hidden[shard, at, :] = pair
                term = dot_nt(pair, win[shard])
                second_grad = term if second_grad is None else second_grad + term
            acc[...] = second_grad if group == 0 else acc[...] + second_grad
        part_b[block] = acc[...].astype(BF16)
        rows_out[block] = lax.dot_general(
            row_picker, gate_sum, NT, precision=EXACT, preferred_element_type=F32
        )
        if index > 0:
            handed[index - 1].start()

    def summing(refs, make):
        part, top_in, bottom_in, from_left, from_right, send, recv = refs
        return RingSum(
            ring, part, (top_in, bottom_in), from_left, from_right, send, recv, HALF,
            lambda position, block: make((3, 1, 2, 0)[position], block),
        )

    ahead = summing(sum_refs[:7], forward)
    behind = summing(sum_refs[7:], backward)
    ahead.stage(4)
    rows.forward()
    rows.near()
    ahead.stage(1)
    ahead.stage(2)
    rows.far()
    ahead.stage(0)
    b_turned[...] = b_ref[...].reshape(SEQ, D).T
    seeds.wait()
    behind.stage(4)
    ahead.stage(3)
    behind.stage(1)
    behind.stage(2)
    behind.stage(0)
    ahead.stage(5)
    y_ref[...] = (residual_ref[...] + ahead.total()).astype(BF16)
    stores = []
    for group in range(GROUPS):
        slot = group % 2
        if group == 1:
            behind.stage(3)
        if group >= 2:
            stores[group - 2].wait()
        for inner in range(GROUP):
            staged[slot, inner, :D, :] = dot(b_turned[...], hidden[group * GROUP + inner]).astype(BF16)
        whole_out = dot_tn(
            acted[:, group * GROUP_UNITS : (group + 1) * GROUP_UNITS], slot_grad[...]
        ).astype(BF16)
        for inner in range(GROUP):
            for piece in range(D // UNIT):
                at = D + piece * LANES
                staged[slot, inner, at : at + LANES, :] = whole_out[
                    inner * LANES : (inner + 1) * LANES, piece * UNIT : (piece + 1) * UNIT
                ]
        stores.append(
            pltpu.make_async_copy(
                staged.at[slot], dw_ref.at[pl.ds(group * GROUP, GROUP)], dw_sem.at[slot]
            )
        )
        stores[-1].start()
    behind.stage(5)
    db_ref[...] = behind.total()
    for copy in handed:
        copy.wait()
    rows_all = rows_out[ring.me] + rows_in[0] + rows_in[1] + rows_in[2]
    diagonal = jnp.where(
        lax.broadcasted_iota(jnp.int32, (8, LANES), 0)
        == lax.broadcasted_iota(jnp.int32, (8, LANES), 1),
        1.0,
        0.0,
    )
    gate_grad_ref[...] = lax.dot_general(
        rows_all, diagonal, TN, precision=EXACT, preferred_element_type=F32
    )
    rows.sent()
    stores[2].wait()
    stores[3].wait()


def ffn_both(b_own, residual, codes, router, delta_all, weights):
    return pl.pallas_call(
        ffn_both_kernel,
        out_shape=(
            jax.ShapeDtypeStruct((ROWS, D), BF16),
            jax.ShapeDtypeStruct((ROWS, LANES), F32),
            jax.ShapeDtypeStruct((ROWS, D), F32),
            jax.ShapeDtypeStruct((ROWS, LANES), F32),
            jax.ShapeDtypeStruct((16, EXPERT_ROWS, UNIT), BF16),
        ),
        in_specs=[VMEM] * 4 + [ANY] * 2,
        out_specs=[VMEM] * 4 + [ANY],
        scratch_shapes=[
            pltpu.VMEM((CTX, ROWS, D), BF16),
            pltpu.VMEM((CTX, ROWS, 1), F32),
            pltpu.VMEM((CTX, ROWS, D), BF16),
            pltpu.VMEM((ROWS, D), F32),
            pltpu.VMEM((SEQ, D), BF16),
            pltpu.VMEM((16, SEQ, UNIT), BF16),
            pltpu.VMEM((SEQ, FFN), BF16),
            pltpu.VMEM((16, D, UNIT), BF16),
            pltpu.VMEM((16, LANES, D), BF16),
            pltpu.VMEM((2, GROUP, EXPERT_ROWS, UNIT), BF16),
            pltpu.VMEM((CTX, 8, ROWS), F32),
            pltpu.VMEM((3, 8, ROWS), F32),
            pltpu.VMEM((D, SEQ), BF16),
            SEMS((5 * GROUPS,)),
            SEMS((2,)),
            SEMS((6,)),
            SEMS((6,)),
            SEMS,
            SEMS((3,)),
            SEMS((3,)),
        ]
        + SUM_SCRATCH * 2,
        compiler_params=params(6),
        name="ffn_both",
    )(b_own, residual, codes, router, delta_all, weights)


def rotary_table():
    half_dim = HEAD_DIM // 2
    steps = 2.0 * np.arange(half_dim, dtype=np.float32) / np.float32(HEAD_DIM)
    frequency = np.exp(-np.log(np.float32(10000.0)) * steps)
    angles = np.arange(SEQ, dtype=np.float32)[:, None] * frequency[None, :]
    cosine, sine = np.cos(angles), np.sin(angles)
    return jnp.asarray(np.concatenate([cosine, cosine, sine, sine], axis=1), F32)


def lower_forward(packs, experts, tokens_in, length, codes, table):
    a_all, qkv, mass, attended, residual, second, *unpacked = attn_forward(
        0, length, tokens_in, packs, table
    )
    output, b_all, gates, gate_col, kept = ffn_forward(
        second, residual, codes, unpacked[1], experts
    )
    late = (a_all, qkv, mass, attended, residual, second, gates)
    return output, (tokens_in, b_all, gate_col, kept, unpacked, late)


def upper_layer(packs, experts, tokens_in, length, codes, table, seed, seed_all):
    a_all, qkv, mass, attended, residual, second, *unpacked = attn_forward(
        1, length, tokens_in, packs, table
    )
    output, gates, db, gate_grads, dexperts = ffn_both(
        second, residual, codes, unpacked[1], seed_all, experts
    )
    late = (a_all, qkv, mass, attended, residual, second, gates)
    results = attn_backward(length, (tokens_in, *unpacked, table, *late, seed, db, gate_grads))
    return output, dexperts, results


def lower_backward(experts, saved, delta_own, length, table, upper):
    tokens_in, b_all, gate_col, kept, unpacked, late = saved
    db, gate_grads, dexperts, lent = ffn_backward(b_all, gate_col, delta_own, kept, experts, upper)
    results = attn_backward(
        length, (tokens_in, *unpacked, table, *late, delta_own, db, gate_grads), (*upper, lent)
    )
    return dexperts, results


def factor_of(squares_ref, index):
    return jnp.minimum(1.0, CLIP_LIMIT / jnp.sqrt(squares_ref[0:1, index : index + 1]))


def updated(fixes_ref, gradient, factor, old, new, learn_rate, at=...):
    master_ref, mean_ref, square_ref = old
    gradient_ref, mean_new_ref, square_new_ref, master_new_ref, copy_ref = new
    clipped = gradient * factor
    master = master_ref[at]
    mean_new = BETA_ONE * mean_ref[at] + (1.0 - BETA_ONE) * clipped
    square_new = BETA_TWO * square_ref[at] + (1.0 - BETA_TWO) * clipped * clipped
    master_new = master - learn_rate * (
        mean_new * fixes_ref[0] / (jnp.sqrt(square_new * fixes_ref[1]) + ADAM_EPS) + DECAY_RATE * master
    )
    gradient_ref[at] = gradient
    mean_new_ref[at] = mean_new
    square_new_ref[at] = square_new
    master_new_ref[at] = master_new
    copy_ref[at] = master_new.astype(BF16)


def update_kernel(
    fixes_ref, squares_ref, in_sum_ref, out_sum_ref, attn_sum_ref, *refs,
):
    in_old, out_old, attn_old, gain_old, router_old = (refs[at : at + 3] for at in range(0, 15, 3))
    in_new, out_new, attn_new, gain_new, router_new = (refs[at : at + 5] for at in range(15, 40, 5))
    norms_ref, turned, wide = refs[40:]
    turned[pl.ds(0, D, 2), :] = in_sum_ref[0, :, :LANES].astype(F32)
    turned[pl.ds(1, D, 2), :] = in_sum_ref[0, :, LANES:].astype(F32)
    updated(
        fixes_ref, turned[...], factor_of(squares_ref, 3), in_old, in_new, RATE_FACTOR / D**0.5
    )
    pieces = [
        out_sum_ref[0, piece * LANES : (piece + 1) * LANES, :].astype(F32)
        for piece in range(D // UNIT)
    ]
    updated(
        fixes_ref,
        jnp.concatenate(pieces, axis=1),
        factor_of(squares_ref, 4),
        out_old,
        out_new,
        RATE_FACTOR / FFN**0.5,
        0,
    )

    @pl.when(pl.program_id(0) == 0)
    def _():
        back = [jnp.zeros((48, UNIT), F32) for _ in range(3)]
        small = jnp.zeros((48, UNIT), F32)
        for block in range(CTX):
            rows = [
                attn_sum_ref[block, piece * 48 : (piece + 1) * 48, :].astype(F32) for piece in range(6)
            ]
            back = [left + right for left, right in zip(back, rows[:3])]
            small = small + rows[5]
            heads = jnp.concatenate(rows[3:], axis=1)
            for part in range(3):
                at = part * D + block * COLS
                wide[:, at : at + COLS] = heads[:, part * COLS : (part + 1) * COLS]
        wide[:, 3 * D :] = jnp.concatenate(back, axis=1)
        small = small[:, LANES:]
        places = lax.broadcasted_iota(jnp.int32, (8, LANES), 0)
        picker = jnp.where(places == lax.broadcasted_iota(jnp.int32, (8, LANES), 1), 1.0, 0.0)
        turned_rows = lax.dot_general(
            picker, small, NT, precision=EXACT, preferred_element_type=F32
        )
        gain_rows = turned_rows[EXPERTS : EXPERTS + 2]
        updated(fixes_ref, gain_rows, factor_of(squares_ref, 0), gain_old, gain_new, GAIN_RATE)
        for expert in range(EXPERTS):
            updated(
                fixes_ref,
                turned_rows[expert : expert + 1],
                factor_of(squares_ref, 2),
                router_old,
                router_new,
                RATE_FACTOR / (D // 4) ** 0.5,
                expert,
            )
        norms_ref[...] = jnp.sqrt(squares_ref[...])
        for part in range(4):
            lanes = (slice(None), slice(part * D, (part + 1) * D))
            updated(
                fixes_ref,
                wide[lanes],
                factor_of(squares_ref, 1),
                attn_old,
                attn_new,
                RATE_FACTOR / D**0.5,
                lanes,
            )


def update(fixes, squares, sums_all, in_old, out_old, attn_old, gain_old, router_old):
    in_rows, units = 2 * D, LANES
    in_shape, out_shape, attn_shape = (CTX * in_rows, units), (CTX, units, D), (48, 4 * D)
    in_spec = pl.BlockSpec((in_rows, units), lambda i: (i, 0))
    out_spec = pl.BlockSpec((1, units, D), lambda i: (i, 0, 0))
    attn_spec = whole(attn_shape)
    gain_shape, router_shape = (2, 48), (EXPERTS, 1, 48)

    def five(shape):
        return [jax.ShapeDtypeStruct(shape, F32)] * 4 + [jax.ShapeDtypeStruct(shape, BF16)]

    return pl.pallas_call(
        update_kernel,
        grid=(CTX,),
        out_shape=five(in_shape)
        + five(out_shape)
        + five(attn_shape)
        + five(gain_shape)
        + five(router_shape)
        + [jax.ShapeDtypeStruct((8, LANES), F32)],
        in_specs=[
            SMEM,
            whole((8, LANES)),
            pl.BlockSpec((1, D, UNIT), lambda i: (i, 0, 0)),
            pl.BlockSpec((1, D // 2, UNIT), lambda i: (i, 2, 0)),
            pl.BlockSpec((CTX, ATTN_ROWS, UNIT), lambda i: (0, EXPERT_ROWS // ATTN_ROWS, 0)),
        ]
        + [in_spec] * 3
        + [out_spec] * 3
        + [attn_spec] * 3
        + [whole(gain_shape)] * 3
        + [whole(router_shape)] * 3,
        out_specs=[in_spec] * 5
        + [out_spec] * 5
        + [attn_spec] * 5
        + [whole(gain_shape)] * 5
        + [whole(router_shape)] * 5
        + [whole((8, LANES))],
        scratch_shapes=[pltpu.VMEM((in_rows, units), F32), pltpu.VMEM(attn_shape, F32)],
        compiler_params=pltpu.CompilerParams(vmem_limit_bytes=VMEM_LIMIT),
        name="update",
    )(
        fixes, squares, sums_all, sums_all, sums_all,
        *(array.reshape(in_shape) for array in in_old),
        *(array.reshape(out_shape) for array in out_old),
        *(array.reshape(attn_shape) for array in attn_old),
        *(array.reshape(gain_shape) for array in gain_old),
        *(array.transpose(2, 0, 1) for array in router_old),
    )


def on_device(
    inputs, cotangent, lengths, routes, step_count,
    norm_gains, gains_mean, gains_square,
    attn_weight, attn_mean, attn_square,
    router_weight, router_mean, router_square,
    expert_in, in_mean, in_square,
    expert_out, out_mean, out_square,
):
    section = lax.axis_index("section")
    ctx_index = lax.axis_index("ctx")
    fsdp = lax.axis_size("fsdp")
    everyone = ("section", "fsdp")
    shard_rows = attn_weight.shape[1]
    units = expert_in.shape[4]
    first_core = section == 0

    def own_columns(matrix, part):
        return lax.dynamic_slice_in_dim(matrix, part * D + ctx_index * COLS, COLS, 1)

    def swap(block):
        return lax.ppermute(block, "section", [(0, 1), (1, 0)])

    attn_shard = jnp.concatenate(
        [attn_weight[0][:, 3 * D :]]
        + [own_columns(attn_weight[0], part) for part in range(3)]
        + [jnp.zeros((shard_rows, HEAD_DIM), F32), router_weight[0], norm_gains[0].T]
        + [jnp.zeros((shard_rows, LANES - EXPERTS - 2), F32)],
        axis=1,
    ).astype(BF16)
    attn_shard = attn_shard.reshape(shard_rows, 6, UNIT).transpose(1, 0, 2).reshape(-1, UNIT)
    length = lax.dynamic_slice_in_dim(lengths, section, 1, 0)
    tokens = lax.dynamic_index_in_dim(inputs, section, 0, keepdims=False)
    positions = ctx_index * ROWS + jnp.arange(ROWS, dtype=jnp.int32)
    seed = lax.dynamic_index_in_dim(cotangent, section, 0, keepdims=False)
    seed = jnp.where((positions < length[0])[:, None], seed, jnp.zeros_like(seed))
    left_out = (3 - routes[0, :, :, 0] - routes[0, :, :, 1]).astype(F32)
    packs, codes, seed_all = gather_shards(
        attn_shard, jnp.pad(left_out, ((0, 8 - left_out.shape[0]), (0, 0))), seed
    )
    packs = packs.reshape(2, fsdp, ATTN_ROWS, UNIT)
    in_shard = (
        lax.dynamic_index_in_dim(expert_in[0], ctx_index, 0, keepdims=False)
        .astype(BF16)
        .reshape(D, 2 * units)
    )
    out_shard = lax.dynamic_index_in_dim(expert_out[0], ctx_index, 0, keepdims=False).astype(BF16)
    halves = jnp.concatenate(
        [in_shard] + [out_shard[:, at : at + 2 * units] for at in range(0, D, 2 * units)], axis=0
    ).reshape(2, SPLIT, 2 * units)
    other = swap(jnp.where(first_core, halves[1], halves[0]))
    pieces = (jnp.where(first_core, halves[0], other), jnp.where(first_core, other, halves[1]))
    experts = [
        lax.all_gather(piece, everyone).reshape(2, fsdp, SPLIT, 2 * units) for piece in pieces
    ]
    table = rotary_table()

    lower_out, lower_saved = lower_forward(packs, experts[0], tokens, length, codes[0], table)
    upper_out, upper_experts, (upper_grad, upper_attn, lower_seed) = upper_layer(
        packs, experts[1], lower_out, length, codes[1], table, seed, seed_all
    )
    lower_experts, (lower_grad, lower_attn, _, upper_half) = lower_backward(
        experts[0], lower_saved, lower_seed, length, table, (upper_experts, upper_attn)
    )
    sums_all, squares, layer_outputs, input_grads = sum_shards(
        lower_experts, lower_attn, upper_half, lower_out, upper_out, lower_grad, upper_grad
    )
    step_value = step_count[0].astype(F32)
    fixes = 1.0 / jnp.stack([1.0 - BETA_ONE**step_value, 1.0 - BETA_TWO**step_value])
    changed = update(
        fixes,
        squares,
        sums_all,
        (expert_in, in_mean, in_square),
        (expert_out, out_mean, out_square),
        (attn_weight, attn_mean, attn_square),
        (norm_gains, gains_mean, gains_square),
        (router_weight, router_mean, router_square),
    )

    def shaped(first, like):
        return tuple(array.reshape(like.shape) for array in changed[first : first + 5])

    return (
        (layer_outputs[None], input_grads[None])
        + shaped(15, norm_gains)
        + shaped(10, attn_weight)
        + tuple(array.transpose(1, 2, 0) for array in changed[20:25])
        + shaped(0, expert_in)
        + shaped(5, expert_out)
        + (changed[25][:1, :5],)
    )


def solution(mesh):
    gains = P("section", None, "fsdp")
    rows = P("section", "fsdp", None)
    wide = P("section", None, None, None, "fsdp")
    down = P("section", None, "fsdp", None)
    tokens = P("section", "fsdp", "ctx", None)
    return jax.shard_map(
        on_device,
        mesh=mesh,
        in_specs=(
            P("fsdp", "ctx", None),
            P("fsdp", "ctx", None),
            P("fsdp"),
            tokens,
            P(),
        )
        + (gains,) * 3
        + (rows,) * 6
        + (wide,) * 3
        + (down,) * 3,
        out_specs=(tokens, tokens)
        + (gains,) * 5
        + (rows,) * 10
        + (wide,) * 5
        + (down,) * 5
        + (P("section", None),),
        check_vma=False,
    )
```

```python
import functools

import jax
import jax.numpy as jnp
import numpy as np
from jax import lax
from jax.experimental import pallas as pl
from jax.experimental.pallas import tpu as pltpu
from jax.sharding import PartitionSpec as P

D = 768
HEADS = 12
HEAD_DIM = 64
FFN = 2048
EXPERTS = 3
ROWS = 256
CTX = 4
SEQ = ROWS * CTX
HEADS_DEV = HEADS // CTX
WIDE = 128
EXT = 3 * HEADS_DEV * WIDE
COLS = HEADS_DEV * HEAD_DIM

EPS_NORM = 1e-06
BETA_ONE = 0.9
BETA_TWO = 0.95
RATE_FACTOR = 3.0
GAIN_RATE = 0.3
DECAY_RATE = 0.1
ADAM_EPS = 1e-08
CLIP_LIMIT = 1.0
MASK_VALUE = -1e30
SCORE_SCALE = HEAD_DIM ** (-0.5) / 2.0
BF16 = jnp.bfloat16
F32 = jnp.float32
VMEM_LIMIT = 56 * 1024 * 1024
NT = (((1,), (1,)), ((), ()))
TN = (((0,), (0,)), ((), ()))
HALF = ROWS // 2
LANES = 128
MESH = pl.DeviceIdType.MESH
EXACT = lax.Precision.HIGHEST


def dot(left, right):
    return jnp.dot(left, right, preferred_element_type=F32)


def dot_nt(left, right):
    return lax.dot_general(left, right, NT, preferred_element_type=F32)


def dot_tn(left, right):
    return lax.dot_general(left, right, TN, preferred_element_type=F32)


def params(collective_id, limit=VMEM_LIMIT):
    return pltpu.CompilerParams(
        vmem_limit_bytes=limit, collective_id=collective_id, has_side_effects=True
    )


def whole(shape):
    return pl.BlockSpec(shape, lambda *_: (0,) * len(shape))


def allowed_keys(block, keys, length):
    key_pos = lax.broadcasted_iota(jnp.int32, (ROWS, keys), 1)
    query_pos = lax.broadcasted_iota(jnp.int32, (ROWS, keys), 0) + block * ROWS
    return (key_pos <= query_pos) & (key_pos < length)


VMEM = pl.BlockSpec(memory_space=pltpu.VMEM)
SMEM = pl.BlockSpec(memory_space=pltpu.SMEM)
ANY = pl.BlockSpec(memory_space=pl.ANY)


def ring():
    me = lax.axis_index("ctx")
    return me, lax.rem(me + 1, CTX), lax.rem(me + 3, CTX), lax.rem(me + 2, CTX)


def greet(peers):
    barrier = pltpu.get_barrier_semaphore()
    for peer in peers:
        pl.semaphore_signal(barrier, inc=1, device_id={"ctx": peer}, device_id_type=MESH)


def met(count):
    pl.semaphore_wait(pltpu.get_barrier_semaphore(), count)


def remote(source, target, send, recv, peer):
    return pltpu.make_async_remote_copy(
        src_ref=source,
        dst_ref=target,
        send_sem=send,
        recv_sem=recv,
        device_id={"ctx": peer},
        device_id_type=MESH,
    )


def rows_of(block, half=None):
    if half is None:
        return pl.ds(pl.multiple_of(block * ROWS, ROWS), ROWS)
    return pl.ds(pl.multiple_of(block * ROWS + half * HALF, HALF), HALF)


def gather_rows(all_ref, send, recv, beside=None):
    me, right, left, _ = ring()

    def piece(index, block, half, peer):
        spot = all_ref.at[rows_of(block, half)]
        return remote(spot, spot, send.at[index], recv.at[index], peer)

    copies = [
        piece(0, me, 0, right),
        piece(1, me, 1, left),
        piece(2, me, 1, right),
        piece(3, me, 0, left),
    ]
    for copy in copies:
        copy.start()
    if beside is not None:
        beside()
    copies[0].wait_recv()
    copies.append(piece(4, left, 0, right))
    copies[4].start()
    copies[1].wait_recv()
    copies.append(piece(5, right, 1, left))
    copies[5].start()
    for index in range(2, 6):
        copies[index].wait_recv()
    for copy in copies:
        copy.wait_send()


def reduce_rows(make, part, across_in, from_left, from_right, send, recv, beside=None):
    me, right, left, across = ring()
    top, bottom = pl.ds(0, HALF), pl.ds(HALF, HALF)

    def piece(index, block, half, target, peer):
        return remote(part.at[rows_of(block, half)], target, send.at[index], recv.at[index], peer)

    make(across)
    copies = [
        piece(0, across, 0, across_in.at[0], right),
        piece(1, across, 1, across_in.at[1], left),
    ]
    copies[0].start()
    copies[1].start()
    make(right)
    copies.append(piece(2, right, 1, from_left.at[bottom], right))
    copies[2].start()
    make(left)
    copies.append(piece(3, left, 0, from_right.at[top], left))
    copies[3].start()
    copies[0].wait_recv()
    spot = rows_of(right, 0)
    part[spot, :] = (part[spot, :].astype(F32) + across_in[0].astype(F32)).astype(BF16)
    copies.append(piece(4, right, 0, from_left.at[top], right))
    copies[4].start()
    copies[1].wait_recv()
    spot = rows_of(left, 1)
    part[spot, :] = (part[spot, :].astype(F32) + across_in[1].astype(F32)).astype(BF16)
    copies.append(piece(5, left, 1, from_right.at[bottom], left))
    copies[5].start()
    make(me)
    if beside is not None:
        beside()
    for index in range(2, 6):
        copies[index].wait_recv()
    for copy in copies:
        copy.wait_send()
    return (
        part[rows_of(me), :].astype(F32) + from_left[...].astype(F32) + from_right[...].astype(F32)
    )


REDUCE_SCRATCH = [
    pltpu.VMEM((SEQ, D), BF16),
    pltpu.VMEM((2, HALF, D), BF16),
    pltpu.VMEM((ROWS, D), BF16),
    pltpu.VMEM((ROWS, D), BF16),
    pltpu.SemaphoreType.DMA((6,)),
    pltpu.SemaphoreType.DMA((6,)),
]


def greet_ids(peers):
    barrier = pltpu.get_barrier_semaphore()
    for peer in peers:
        pl.semaphore_signal(barrier, inc=1, device_id=peer, device_id_type=MESH)


class Ring:
    def __init__(self, axis):
        if axis == "x":
            self.me = lax.axis_index("ctx")
            self.place = lambda index: {"ctx": index}
        else:
            shard = lax.axis_index("fsdp")
            inner, outer = lax.rem(shard, CTX), lax.div(shard, CTX)
            if axis == "y":
                self.me = inner
                self.place = lambda index: {"fsdp": outer * CTX + index}
            else:
                self.me = outer
                self.place = lambda index: {"fsdp": index * CTX + inner}
        self.right = lax.rem(self.me + 1, CTX)
        self.left = lax.rem(self.me + 3, CTX)
        self.across = lax.rem(self.me + 2, CTX)

    def order(self):
        return (self.across, self.right, self.left, self.me)

    def near(self):
        return [self.place(self.right), self.place(self.left)]

    def copy(self, source, target, send, recv, index):
        return pltpu.make_async_remote_copy(
            src_ref=source,
            dst_ref=target,
            send_sem=send,
            recv_sem=recv,
            device_id=self.place(index),
            device_id_type=MESH,
        )


class RingGather:
    def __init__(self, ring, at, send, recv):
        self.ring, self.at, self.send, self.recv = ring, at, send, recv
        self.sends = (
            (ring.me, 0, ring.right),
            (ring.me, 1, ring.left),
            (ring.me, 1, ring.right),
            (ring.me, 0, ring.left),
            (ring.left, 0, ring.right),
            (ring.right, 1, ring.left),
        )

    def piece(self, index, block, half, to):
        spot = self.at(block, half)
        return self.ring.copy(spot, spot, self.send.at[index], self.recv.at[index], to)

    def go(self, index):
        self.piece(index, *self.sends[index]).start()

    def landed(self, index, block, half):
        self.piece(index, block, half, self.ring.right).wait_recv()

    def start(self):
        for index in range(4):
            self.go(index)

    def forward(self):
        self.landed(0, self.ring.left, 0)
        self.go(4)
        self.landed(1, self.ring.right, 1)
        self.go(5)

    def near(self):
        self.landed(2, self.ring.left, 1)
        self.landed(3, self.ring.right, 0)

    def far(self):
        self.landed(4, self.ring.across, 0)
        self.landed(5, self.ring.across, 1)

    def sent(self):
        for index in range(6):
            self.piece(index, *self.sends[index]).wait_send()

    def finish(self):
        self.near()
        self.far()
        self.sent()


class RingSum:
    def __init__(self, ring, part, across_in, from_left, from_right, send, recv, cut, make):
        self.ring, self.part, self.across_in = ring, part, across_in
        self.from_left, self.from_right, self.send, self.recv = from_left, from_right, send, recv
        size = part.shape[1]
        self.halves = (pl.ds(0, cut), pl.ds(cut, size - cut))
        self.make = make
        self.copies = {}

    def go(self, index, block, half, target, to):
        self.copies[index] = self.ring.copy(
            self.part.at[block, self.halves[half]], target, self.send.at[index], self.recv.at[index], to
        )
        self.copies[index].start()

    def arrived(self, half, block):
        self.copies[half].wait_recv()
        incoming = self.across_in[half]
        if len(self.part.shape) == 3:
            spot = (block, self.halves[half])
            self.part[spot] = self.part[spot] + incoming[...]
            return
        start = (0, self.part.shape[1] - incoming.shape[0])[half]
        for index in range(incoming.shape[0]):
            self.part[block, start + index] = self.part[block, start + index] + incoming[index]

    def stage(self, number):
        ring = self.ring
        if number == 0:
            self.make(0, ring.across)
            self.go(0, ring.across, 0, self.across_in[0], ring.right)
            self.go(1, ring.across, 1, self.across_in[1], ring.left)
        elif number == 1:
            self.make(1, ring.right)
            self.go(2, ring.right, 1, self.from_left.at[self.halves[1]], ring.right)
        elif number == 2:
            self.make(2, ring.left)
            self.go(3, ring.left, 0, self.from_right.at[self.halves[0]], ring.left)
        elif number == 3:
            self.arrived(0, ring.right)
            self.go(4, ring.right, 0, self.from_left.at[self.halves[0]], ring.right)
            self.arrived(1, ring.left)
            self.go(5, ring.left, 1, self.from_right.at[self.halves[1]], ring.left)
        elif number == 4:
            self.make(3, ring.me)
        else:
            for index in range(2, 6):
                self.copies[index].wait_recv()
            for index in range(6):
                self.copies[index].wait_send()

    def total(self, index=None):
        spot = (self.ring.me,) if index is None else (self.ring.me, index)
        tail = () if index is None else (index,)
        return (
            self.part[spot].astype(F32)
            + self.from_left[tail or ...].astype(F32)
            + self.from_right[tail or ...].astype(F32)
        )


UNIT = 256
EXPERT_ROWS = D + D // 2
ATTN_ROWS = 288
SHARD_ROWS = EXPERT_ROWS + ATTN_ROWS
FIRST = SHARD_ROWS // 2
KEPT = EXPERT_ROWS - FIRST
CUT = 352
SEMS = pltpu.SemaphoreType.DMA


def gather_shards_kernel(shard_ref, code_ref, seed_ref, out_ref, codes_ref, seeds_ref, *sems):
    section = lax.axis_index("section")
    sibling = {"section": 1 - section}
    ring_y, ring_z = Ring("y"), Ring("z")
    y, z = ring_y.me, ring_z.me
    ring_x = Ring("x")
    x_peers = (ring_x.right, ring_x.left, ring_x.across)
    greet_ids(
        [sibling] + ring_y.near() + ring_z.near() + [ring_x.place(peer) for peer in x_peers]
    )
    out_ref[section, z, y] = shard_ref[...]
    codes_ref[section, ring_x.me] = code_ref[...]
    seeds_ref[ring_x.me] = seed_ref[...]
    halves = (pl.ds(0, HALF), pl.ds(HALF, HALF))
    seeds = RingGather(ring_x, lambda b, h: seeds_ref.at[b, halves[h]], sems[14], sems[15])
    met(8)
    spot = codes_ref.at[section, ring_x.me]
    code_copies = [
        ring_x.copy(spot, spot, sems[10].at[index], sems[11].at[index], peer)
        for index, peer in enumerate(x_peers)
    ]
    for copy in code_copies:
        copy.start()
    half = ATTN_ROWS // 2
    low = (pl.ds(0, 64), pl.ds(64, half - 64))
    high = (pl.ds(half, 64), pl.ds(half + 64, half - 64))
    pair = (pl.ds(0, 2), pl.ds(2, 2))
    near_y = RingGather(ring_y, lambda b, h: out_ref.at[section, z, b, low[h]], sems[0], sems[1])
    near_z = RingGather(ring_z, lambda b, h: out_ref.at[section, b, y, high[h]], sems[2], sems[3])
    far_z = RingGather(
        ring_z, lambda b, h: out_ref.at[section, b, pair[h], pl.ds(0, half)], sems[4], sems[5]
    )
    far_y = RingGather(
        ring_y, lambda b, h: out_ref.at[section, pair[h], b, pl.ds(half, half)], sems[6], sems[7]
    )
    for first, rings in ((True, (near_y, near_z)), (False, (far_z, far_y))):
        for one in rings:
            one.start()
        if first:
            seeds.start()
        for one in rings:
            one.forward()
        if not first:
            seeds.forward()
        for one in rings:
            one.finish()
    across = pltpu.make_async_remote_copy(
        src_ref=out_ref.at[section],
        dst_ref=out_ref.at[section],
        send_sem=sems[8],
        recv_sem=sems[9],
        device_id=sibling,
        device_id_type=MESH,
    )
    across.start()
    for copy in code_copies:
        copy.wait()
    codes_across = pltpu.make_async_remote_copy(
        src_ref=codes_ref.at[section],
        dst_ref=codes_ref.at[section],
        send_sem=sems[12],
        recv_sem=sems[13],
        device_id=sibling,
        device_id_type=MESH,
    )
    codes_across.start()
    codes_across.wait()
    seeds.finish()
    across.wait()


def gather_shards(shard, codes, seed):
    return pl.pallas_call(
        gather_shards_kernel,
        out_shape=(
            jax.ShapeDtypeStruct((2, CTX, CTX, ATTN_ROWS, UNIT), BF16),
            jax.ShapeDtypeStruct((2, CTX, 8, ROWS), F32),
            jax.ShapeDtypeStruct((CTX, ROWS, D), BF16),
        ),
        in_specs=[VMEM] * 3,
        out_specs=[VMEM] * 3,
        scratch_shapes=[SEMS((6,))] * 8
        + [SEMS, SEMS, SEMS((3,)), SEMS((3,)), SEMS, SEMS, SEMS((6,)), SEMS((6,))],
        compiler_params=params(7),
        name="gather_shards",
    )(shard, codes, seed)


HALF_SHARD = SHARD_ROWS // 2
Y_ROWS, Z_ROWS = 352, 368
Z_CUT = Z_ROWS - ATTN_ROWS


def half_sources(half, experts, attn):
    if half == 0:
        return (
            experts.at[:, :, pl.ds(0, Y_ROWS), :],
            experts.at[:, :, pl.ds(Y_ROWS, Z_CUT), :],
            experts.at[:, :, pl.ds(Y_ROWS + Z_CUT, ATTN_ROWS), :],
        )
    return (
        experts.at[:, :, pl.ds(HALF_SHARD, Y_ROWS), :],
        experts.at[:, :, pl.ds(HALF_SHARD + Y_ROWS, Z_CUT), :],
        attn,
    )


class HalfSums:
    def __init__(self, refs, sems, make_y, make_z):
        (
            self.part_y, self.part_z, top_y, bottom_y, left_y, right_y, top_z, bottom_z, left_z, right_z,
            more_z, more_y, top_zz, bottom_zz, left_zz, right_zz, top_yy, bottom_yy, left_yy, right_yy,
        ) = refs
        ring_y, ring_z = Ring("y"), Ring("z")
        self.ring_y, self.ring_z = ring_y, ring_z
        self.first_y = RingSum(
            ring_y, self.part_y, (top_y, bottom_y), left_y, right_y, sems[0], sems[1], 2, make_y
        )
        self.first_z = RingSum(
            ring_z, self.part_z, (top_z, bottom_z), left_z, right_z, sems[2], sems[3], 2, make_z
        )

        def make_zz(index, block):
            more_z[block] = self.first_y.total(block).astype(BF16)

        def make_yy(index, block):
            more_y[block] = self.first_z.total(block).astype(BF16)

        self.then_z = RingSum(
            ring_z, more_z, (top_zz, bottom_zz), left_zz, right_zz, sems[4], sems[5], Y_ROWS // 2, make_zz
        )
        self.then_y = RingSum(
            ring_y, more_y, (top_yy, bottom_yy), left_yy, right_yy, sems[6], sems[7], 176, make_yy
        )

    def first(self, number):
        self.first_y.stage(number)
        self.first_z.stage(number)

    def then(self, number):
        self.then_z.stage(number)
        self.then_y.stage(number)

    def result(self, out_ref):
        out_ref[pl.ds(0, Y_ROWS), :] = self.then_z.total().astype(BF16)
        out_ref[pl.ds(Y_ROWS, Z_ROWS), :] = self.then_y.total().astype(BF16)


def half_scratch():
    shapes = [(CTX, CTX, Y_ROWS, UNIT), (CTX, CTX, Z_ROWS, UNIT)]
    for rows in (Y_ROWS, Z_ROWS):
        shapes += [(2, rows, UNIT)] * 2 + [(CTX, rows, UNIT)] * 2
    shapes += [(CTX, Y_ROWS, UNIT), (CTX, Z_ROWS, UNIT)]
    for rows in (Y_ROWS, Z_ROWS):
        shapes += [(176, UNIT), (rows - 176, UNIT)] + [(rows, UNIT)] * 2
    return [pltpu.VMEM(shape, BF16) for shape in shapes]


HALF_REFS = 20


def add_block(part, incoming, block):
    for other in range(CTX):
        part[block, other] = part[block, other] + incoming[block, other]


def shared_squares(all_ref, ring_y, ring_z, spread):
    from_y, from_z, *sems = spread

    def folded(values):
        squared = values * values
        return jnp.sum(squared, axis=0, keepdims=True)

    in_row = jnp.zeros((1, UNIT), F32)
    out_row = jnp.zeros((1, UNIT), F32)
    attn_row = jnp.zeros((1, UNIT), F32)
    back = jnp.zeros((ATTN_ROWS // 2, UNIT), F32)
    small = jnp.zeros((48, UNIT), F32)
    lanes = lax.broadcasted_iota(jnp.int32, (1, UNIT), 1)
    for block in range(CTX):
        in_row += folded(all_ref[block, :D, :].astype(F32))
        out_row += folded(all_ref[block, D:EXPERT_ROWS, :].astype(F32))
        middle = EXPERT_ROWS + ATTN_ROWS // 2
        back += all_ref[block, EXPERT_ROWS:middle, :].astype(F32)
        attn_row += folded(all_ref[block, middle : middle + 96, :].astype(F32))
        final = all_ref[block, middle + 96 :, :].astype(F32)
        attn_row += jnp.where(lanes < HEAD_DIM, folded(final), 0.0)
        small += final
    attn_row += folded(back)
    small_row = folded(small)
    is_router = (lanes >= LANES) & (lanes < LANES + EXPERTS)
    is_gain = (lanes >= LANES + EXPERTS) & (lanes < LANES + EXPERTS + 2)
    sums = [
        jnp.where(is_gain, small_row, 0.0),
        attn_row,
        jnp.where(is_router, small_row, 0.0),
        in_row,
        out_row,
    ]
    places = lax.broadcasted_iota(jnp.int32, (8, LANES), 1)
    tile = jnp.zeros((8, LANES), F32)
    for index, row in enumerate(sums):
        tile = jnp.where(places == index, jnp.sum(row, axis=1, keepdims=True), tile)

    def shared(one, slots, send, recv, tile):
        slots[one.me] = tile
        copies = []
        for index, peer in enumerate((one.right, one.left, one.across)):
            spot = slots.at[one.me]
            copies.append(one.copy(spot, spot, send.at[index], recv.at[index], peer))
            copies[-1].start()
        for copy in copies:
            copy.wait()
        return (slots[0] + slots[1]) + (slots[2] + slots[3])

    tile = shared(ring_y, from_y, sems[0], sems[1], tile)
    return shared(ring_z, from_z, sems[2], sems[3], tile)


def sum_shards_kernel(
    experts, attn, upper_half_ref, lower_out_ref, upper_out_ref, lower_grad_ref, upper_grad_ref,
    all_ref, squares_ref, outputs_ref, grads_ref, *rest,
):
    halves, rest = rest[:HALF_REFS], rest[HALF_REFS:]
    in_y, in_z, sent_out, sent_grad, sent_half, local, send_s, recv_s, send_w, recv_w, *rest = rest
    spread, rest = rest[:8], rest[8:]
    ring_x = Ring("x")
    section = lax.axis_index("section")
    sibling = {"section": 1 - section}
    first_core = section == 0
    part_y, part_z = halves[:2]

    def make_y(index, block):
        ready(index, 0)
        add_block(part_y, in_y, block)

    def make_z(index, block):
        ready(index, 1)
        ready(index, 2)
        add_block(part_z, in_z, block)

    sums = HalfSums(halves, rest, make_y, make_z)
    ring_y, ring_z = sums.ring_y, sums.ring_z
    far = [one.place(one.across) for one in (ring_y, ring_z)]
    greet_ids([sibling] + ring_x.near() + ring_y.near() + ring_z.near() + far)

    def pieces(index, half, target_y, target_z):
        b_y, b_z = ring_y.order()[index], ring_z.order()[index]
        sources = half_sources(half, experts, attn)
        return (
            (sources[0].at[:, b_y], target_y.at[b_y]),
            (sources[1].at[b_z], target_z.at[b_z, :, pl.ds(0, Z_CUT), :]),
            (sources[2].at[b_z], target_z.at[b_z, :, pl.ds(Z_CUT, ATTN_ROWS), :]),
        )

    def fetch(index, number, source, target):
        return pltpu.make_async_copy(source, target, local.at[index * 3 + number])

    def pass_on(source, target, send, recv):
        return pltpu.make_async_remote_copy(
            src_ref=source,
            dst_ref=target,
            send_sem=send,
            recv_sem=recv,
            device_id=sibling,
            device_id_type=MESH,
        )

    def lend(index, number, source, target):
        at = index * 3 + number
        return pass_on(source, target, send_s.at[at], recv_s.at[at])

    def ready(index, number):
        source, target = pieces(index, 0, part_y, part_z)[number]
        fetch(index, number, source, target).wait()
        source, target = pieces(index, 0, in_y, in_z)[number]
        lend(index, number, source, target).wait_recv()

    def start(kept):
        for index in range(CTX):
            for number, pair in enumerate(pieces(index, kept, part_y, part_z)):
                fetch(index, number, *pair).start()

    def hand(given):
        for index in range(CTX):
            for number, pair in enumerate(pieces(index, given, in_y, in_z)):
                lend(index, number, *pair).start()

    for core in range(2):

        @pl.when(section == core)
        def _():
            start(core)

    met(9)
    own_at = pl.ds(pl.multiple_of(section * HALF_SHARD, HALF_SHARD), HALF_SHARD)
    own = all_ref.at[ring_x.me, own_at]
    cuts = (pl.ds(0, HALF_SHARD), pl.ds(HALF_SHARD, HALF_SHARD))
    rows = RingGather(ring_x, lambda b, h: all_ref.at[b, cuts[h]], spread[0], spread[1])

    @pl.when(first_core)
    def _():
        pass_on(upper_half_ref, own, send_w.at[2], recv_w.at[2]).start()

    @pl.when(section == 1)
    def _():
        own[...] = upper_half_ref[...]

    for core in range(2):

        @pl.when(section == core)
        def _():
            hand(1 - core)

    lower_out, upper_out = lower_out_ref[...], upper_out_ref[...]
    outputs_ref[section] = jnp.where(first_core, lower_out, upper_out)
    sent_out[...] = jnp.where(first_core, upper_out, lower_out)
    lower_grad, upper_grad = lower_grad_ref[...], upper_grad_ref[...]
    grads_ref[section] = jnp.where(first_core, lower_grad, upper_grad)
    sent_grad[...] = jnp.where(first_core, upper_grad, lower_grad)
    swaps = [
        pass_on(sent_out, outputs_ref.at[section], send_w.at[0], recv_w.at[0]),
        pass_on(sent_grad, grads_ref.at[section], send_w.at[1], recv_w.at[1]),
    ]
    for number in range(3):
        sums.first(number)

    @pl.when(section == 1)
    def _():
        pass_on(sent_half, own, send_w.at[2], recv_w.at[2]).wait_recv()
        rows.start()

    for copy in swaps:
        copy.start()
    sums.first(3)
    sums.first(4)

    @pl.when(section == 1)
    def _():
        rows.forward()

    sums.first(5)
    for number in range(6):
        sums.then(number)

    @pl.when(first_core)
    def _():
        sums.result(own)
        pass_on(upper_half_ref, own, send_w.at[2], recv_w.at[2]).wait()
        rows.start()
        rows.forward()

    @pl.when(section == 1)
    def _():
        sums.result(sent_half)
        back = pass_on(sent_half, own, send_w.at[2], recv_w.at[2])
        back.start()
        back.wait_send()

    rows.near()
    rows.far()
    squares_ref[...] = shared_squares(all_ref, ring_y, ring_z, spread[2:])
    rows.sent()
    for copy in swaps:
        copy.wait()
    for index in range(CTX):
        for number, pair in enumerate(pieces(index, 0, in_y, in_z)):
            lend(index, number, *pair).wait_send()


def by_place(array):
    return array.reshape((CTX, CTX) + array.shape[1:])


def sum_shards(lower_e, lower_a, upper_half, lower_out, upper_out, lower_grad, upper_grad):
    return pl.pallas_call(
        sum_shards_kernel,
        out_shape=(
            jax.ShapeDtypeStruct((CTX, SHARD_ROWS, UNIT), BF16),
            jax.ShapeDtypeStruct((8, LANES), F32),
            jax.ShapeDtypeStruct((2, ROWS, D), BF16),
            jax.ShapeDtypeStruct((2, ROWS, D), F32),
        ),
        in_specs=[ANY] * 2 + [VMEM] * 5,
        out_specs=[VMEM] * 4,
        scratch_shapes=half_scratch()
        + [
            pltpu.VMEM((CTX, CTX, Y_ROWS, UNIT), BF16),
            pltpu.VMEM((CTX, CTX, Z_ROWS, UNIT), BF16),
            pltpu.VMEM((ROWS, D), BF16),
            pltpu.VMEM((ROWS, D), F32),
            pltpu.VMEM((HALF_SHARD, UNIT), BF16),
        ]
        + [SEMS((12,))] * 3
        + [SEMS((3,))] * 2
        + [SEMS((6,))] * 2
        + [pltpu.VMEM((CTX, 8, LANES), F32)] * 2
        + [SEMS((3,))] * 4
        + [SEMS((6,))] * 8,
        compiler_params=params(8, 37 * 1024 * 1024),
        name="sum_shards",
    )(by_place(lower_e), by_place(lower_a), upper_half, lower_out, upper_out, lower_grad, upper_grad)


def inverse_size(values):
    return lax.rsqrt(jnp.mean(values * values, axis=1, keepdims=True) + EPS_NORM)


def unpack(pack_ref, back_ref, heads_ref):
    def body(index, _):
        rows = pl.ds(pl.multiple_of(index * 48, 16), 48)
        for piece in range(6):
            target = back_ref if piece < 3 else heads_ref
            at = (piece % 3) * UNIT
            target[rows, at : at + UNIT] = pack_ref[index, piece * 48 : (piece + 1) * 48, :]
        return 0

    lax.fori_loop(0, 16, body, 0)


def repack(back_ref, heads_ref, pack_ref):
    def body(index, _):
        rows = pl.ds(pl.multiple_of(index * 48, 16), 48)
        for piece in range(6):
            source = back_ref if piece < 3 else heads_ref
            at = (piece % 3) * UNIT
            pack_ref[index, piece * 48 : (piece + 1) * 48, :] = source[rows, at : at + UNIT]
        return 0

    lax.fori_loop(0, 16, body, 0)


def extend(heads_ref, w_ref):
    lanes = lax.broadcasted_iota(jnp.int32, (D, WIDE), 1)
    for head in range(3 * HEADS_DEV):
        at = head // 2 * WIDE
        values = heads_ref[:, at : at + WIDE].astype(F32)
        if head % 2:
            values = pltpu.roll(values, HEAD_DIM, 1)
        if head < 2 * HEADS_DEV:
            upper = jnp.where(
                lanes < 96, -pltpu.roll(values, 32, 1), pltpu.roll(values, 96, 1)
            )
        else:
            upper = jnp.zeros_like(values)
        w_ref[:, head * WIDE : (head + 1) * WIDE] = jnp.where(
            lanes < HEAD_DIM, values, upper
        ).astype(BF16)


def attn_forward_kernel(
    layer, length_ref, u_ref, packs_ref, table_ref,
    a_out, qkv_out, mass_out, attended_ref, residual_ref, b_ref,
    gains_ref, router_ref, w_out, back_out,
    a_ref, qkv_ref, mass_ref, w_ref, back_ref, out_sem,
    heads_out, heads_w, pack_ref, pack_sem, send_a, recv_a, send_o, recv_o,
):
    me, right, left, across = ring()
    load = pltpu.make_async_copy(packs_ref.at[layer], pack_ref, pack_sem)
    load.start()
    greet((right, left, across))
    length = length_ref[0]
    tokens = u_ref[...].astype(F32)
    load.wait()
    unpack(pack_ref, back_ref, heads_w)
    leaving = [
        pltpu.make_async_copy(source, target, out_sem.at[index])
        for index, (source, target) in enumerate(
            ((back_ref, back_out), (w_ref, w_out), (a_ref, a_out), (qkv_ref, qkv_out), (mass_ref, mass_out))
        )
    ]
    leaving[0].start()
    router_ref[...] = heads_w[:, D - LANES :]
    places = lax.broadcasted_iota(jnp.int32, (8, LANES), 0) + EXPERTS
    picker = jnp.where(places == lax.broadcasted_iota(jnp.int32, (8, LANES), 1), 1.0, 0.0)
    gains_ref[...] = dot_nt(picker.astype(BF16), router_ref[...])
    a_ref[rows_of(me), :] = (tokens * inverse_size(tokens) * gains_ref[0:1, :]).astype(BF16)
    met(3)
    gather_rows(a_ref, send_a, recv_a, lambda: extend(heads_w, w_ref))
    leaving[1].start()
    leaving[2].start()
    for block in range(CTX):
        rows = pl.ds(block * ROWS, ROWS)
        table = table_ref[rows, :]
        mixed = dot(a_ref[rows, :], w_ref[...])
        for part in range(3 * HEADS_DEV):
            lanes = slice(part * WIDE, (part + 1) * WIDE)
            piece = mixed[:, lanes]
            if part < 2 * HEADS_DEV:
                turned = piece * table
                piece = turned + pltpu.roll(turned, WIDE // 2, 1)
            qkv_ref[rows, lanes] = piece.astype(BF16)
    leaving[3].start()

    def handed(block):
        step = lax.rem(block - me + CTX, CTX)
        return remote(
            heads_out.at[block], attended_ref.at[me], send_o.at[step], recv_o.at[step], block
        )

    for block in reversed(range(CTX)):
        rows = pl.ds(block * ROWS, ROWS)
        keys = (block + 1) * ROWS
        allowed = allowed_keys(block, keys, length)
        outs = []
        for head in range(HEADS_DEV):
            queries = qkv_ref[rows, head * WIDE : (head + 1) * WIDE]
            key_lanes = slice((HEADS_DEV + head) * WIDE, (HEADS_DEV + head + 1) * WIDE)
            value_lanes = slice((2 * HEADS_DEV + head) * WIDE, (2 * HEADS_DEV + head + 1) * WIDE)
            scores = dot_nt(queries, qkv_ref[:keys, key_lanes]) * SCORE_SCALE
            scores = jnp.where(allowed, scores, MASK_VALUE)
            top = jnp.max(scores, axis=1, keepdims=True)
            raw = jnp.exp(scores - top)
            total = jnp.sum(raw, axis=1, keepdims=True)
            probs = (raw * (1.0 / total)).astype(BF16)
            outs.append(dot(probs, qkv_ref[:keys, value_lanes]))
            mass_ref[head, rows, :] = top + jnp.log(total)
        first = (outs[0] + pltpu.roll(outs[1], WIDE // 2, 1)).astype(BF16)
        second = outs[2][:, : WIDE // 2].astype(BF16)
        heads_out[block, :, :WIDE] = first
        heads_out[block, :, WIDE:] = second

        @pl.when(block != me)
        def _():
            handed(block).start()

    leaving[4].start()
    attended_ref[me] = heads_out[me]
    for step in range(1, CTX):
        pltpu.make_async_copy(heads_out.at[0], attended_ref.at[0], recv_o.at[step]).wait()
    residual = tokens
    for block in range(CTX):
        residual = residual + dot(attended_ref[block], back_ref[block * COLS : (block + 1) * COLS, :])
    residual_ref[...] = residual
    b_ref[...] = (residual * inverse_size(residual) * gains_ref[1:2, :]).astype(BF16)
    for step in range(1, CTX):
        pltpu.make_async_copy(heads_out.at[0], attended_ref.at[0], send_o.at[step]).wait()
    for copy in leaving:
        copy.wait()


def attn_forward(layer, length, u, packs, table):
    sems = pltpu.SemaphoreType.DMA
    return pl.pallas_call(
        functools.partial(attn_forward_kernel, layer),
        out_shape=(
            jax.ShapeDtypeStruct((SEQ, D), BF16),
            jax.ShapeDtypeStruct((SEQ, EXT), BF16),
            jax.ShapeDtypeStruct((HEADS_DEV, SEQ, 1), F32),
            jax.ShapeDtypeStruct((CTX, ROWS, COLS), BF16),
            jax.ShapeDtypeStruct((ROWS, D), F32),
            jax.ShapeDtypeStruct((ROWS, D), BF16),
            jax.ShapeDtypeStruct((8, D), F32),
            jax.ShapeDtypeStruct((D, LANES), BF16),
            jax.ShapeDtypeStruct((D, EXT), BF16),
            jax.ShapeDtypeStruct((D, D), BF16),
        ),
        in_specs=[
            SMEM,
            VMEM,
            ANY,
            VMEM,
        ],
        out_specs=[ANY] * 3 + [VMEM] * 5 + [ANY] * 2,
        scratch_shapes=[
            pltpu.VMEM((SEQ, D), BF16),
            pltpu.VMEM((SEQ, EXT), BF16),
            pltpu.VMEM((HEADS_DEV, SEQ, 1), F32),
            pltpu.VMEM((D, EXT), BF16),
            pltpu.VMEM((D, D), BF16),
            sems((5,)),
            pltpu.VMEM((CTX, ROWS, COLS), BF16),
            pltpu.VMEM((D, D), BF16),
            pltpu.VMEM((16, ATTN_ROWS, UNIT), BF16),
            sems,
        ]
        + [sems((6,)), sems((6,)), sems((CTX,)), sems((CTX,))],
        compiler_params=params(1 + 10 * layer),
        name="attn_forward",
    )(length, u, packs, table)


def attn_backward_kernel(
    hosting, length_ref, u_ref, gains_ref, router_ref, w_in, back_in, table_in,
    a_in, qkv_in, mass_in, attended_in, residual_ref, second_in, gates_ref,
    delta_ref, db_ref, gate_grad_ref, *rest,
):
    (
        w_ref, back_ref, table_ref, a_ref, qkv_ref, mass_ref, attended_ref, second_ref, in_sem, *rest,
    ) = rest[-9:] + rest[:-9]
    coming = [
        pltpu.make_async_copy(source, target, in_sem.at[index])
        for index, (source, target) in enumerate(
            (
                (back_in, back_ref), (attended_in, attended_ref), (second_in, second_ref),
                (qkv_in, qkv_ref), (mass_in, mass_ref), (table_in, table_ref), (w_in, w_ref), (a_in, a_ref),
            )
        )
    ]
    for copy in coming:
        copy.start()
    if hosting:
        upper_e, upper_a, lent, *rest = rest
    input_ref, pack_ref, lower_ref = rest[:3]
    rest = rest[3:]
    if hosting:
        half_ref, *rest = rest
        rest, hosted = rest[:15], rest[15:]
    dheads_ref, dback_ref = rest[:2]
    rest = rest[2:]
    key_acc, value_acc, dz, grads_out, grads_in, send_o, recv_o = rest[:7]
    part, across_in, from_left, from_right, send_r, recv_r = rest[7:13]
    me, right, left, across = ring()
    greet((right, left, across))
    if hosting:
        refs, (in_y, in_z, local, *sems) = hosted[:HALF_REFS], hosted[HALF_REFS:]
        part_y, part_z = refs[:2]
        section = lax.axis_index("section")
        sums = HalfSums(
            refs,
            sems,
            lambda index, block: add_block(part_y, in_y, block),
            lambda index, block: add_block(part_z, in_z, block),
        )
        greet_ids(sums.ring_y.near() + sums.ring_z.near())

        def loads(half):
            sources = half_sources(half, upper_e, upper_a)
            pairs = [
                (sources[1], part_z.at[:, :, pl.ds(0, Z_CUT), :]),
                (sources[2], part_z.at[:, :, pl.ds(Z_CUT, ATTN_ROWS), :]),
                (lent.at[:, :, pl.ds(Y_ROWS, Z_ROWS), :], in_z),
            ]
            for block in range(CTX):
                pairs.append((sources[0].at[:, block], part_y.at[block]))
                pairs.append((lent.at[:, block, pl.ds(0, Y_ROWS), :], in_y.at[block]))
            return [
                pltpu.make_async_copy(source, target, local.at[index])
                for index, (source, target) in enumerate(pairs)
            ]

        for core in range(2):

            @pl.when(section == core)
            def _():
                for copy in loads(core):
                    copy.start()

    length = length_ref[0]
    lanes = lax.broadcasted_iota(jnp.int32, (ROWS, LANES), 1)
    gates = gates_ref[...]
    gate_grads = jnp.where(lanes < EXPERTS, gate_grad_ref[...], 0.0)
    logit_grad = gates * (gate_grads - jnp.sum(gates * gate_grads, axis=1, keepdims=True))
    logit_grad = logit_grad.astype(BF16)
    second_grad = db_ref[...] + dot_nt(logit_grad, router_ref[...])
    residual = residual_ref[...]
    scale_two = inverse_size(residual)
    normal_two = residual * scale_two
    gain_two_terms = second_grad * normal_two
    scaled_two = second_grad * gains_ref[1:2, :]
    residual_grad = delta_ref[...].astype(F32) + scale_two * (
        scaled_two - normal_two * jnp.mean(scaled_two * normal_two, axis=1, keepdims=True)
    )
    input_ref[...] = residual_grad
    branch_grad = residual_grad.astype(BF16)
    met(7 if hosting else 3)
    coming[0].wait()

    for block in range(CTX):
        grads_out[block] = dot_nt(branch_grad, back_ref[block * COLS : (block + 1) * COLS, :]).astype(
            BF16
        )

        @pl.when(block != me)
        def _():
            step = lax.rem(block - me + CTX, CTX)
            remote(
                grads_out.at[block], grads_in.at[me], send_o.at[step], recv_o.at[step], block
            ).start()

    grads_in[me] = grads_out[me]
    if hosting:
        for copy in loads(0):
            copy.wait()
        for number in range(3):
            sums.first(number)
    coming[1].wait()
    coming[2].wait()
    for block in range(CTX):
        dback_ref[block * COLS : (block + 1) * COLS, :] = dot_tn(
            attended_ref[block], branch_grad
        ).astype(BF16)
    router_terms = dot_tn(second_ref[...], logit_grad)
    ones = jnp.ones((ROWS, LANES), F32)
    gain_two_column = lax.dot_general(
        gain_two_terms, ones, TN, precision=EXACT, preferred_element_type=F32
    )
    key_acc[...] = jnp.zeros_like(key_acc)
    value_acc[...] = jnp.zeros_like(value_acc)
    for copy in coming[3:]:
        copy.wait()
    for step in range(1, CTX):
        pltpu.make_async_copy(grads_out.at[0], grads_in.at[0], recv_o.at[step]).wait()
    for step in range(1, CTX):
        pltpu.make_async_copy(grads_out.at[0], grads_in.at[0], send_o.at[step]).wait()
    for block in range(CTX):
        rows = pl.ds(block * ROWS, ROWS)
        keys = (block + 1) * ROWS
        allowed = allowed_keys(block, keys, length)
        pair = grads_in[block, :, :WIDE]
        tail = grads_in[block, :, WIDE:]
        head_grads = (
            pair,
            pltpu.roll(pair.astype(F32), WIDE // 2, 1).astype(BF16),
            jnp.concatenate([tail, jnp.zeros_like(tail)], axis=1),
        )
        for head in range(HEADS_DEV):
            queries = qkv_ref[rows, head * WIDE : (head + 1) * WIDE]
            keys_all = qkv_ref[:keys, (HEADS_DEV + head) * WIDE : (HEADS_DEV + head + 1) * WIDE]
            values_all = qkv_ref[
                :keys, (2 * HEADS_DEV + head) * WIDE : (2 * HEADS_DEV + head + 1) * WIDE
            ]
            grads = head_grads[head]
            scores = dot_nt(queries, keys_all) * SCORE_SCALE
            probs = jnp.where(allowed, jnp.exp(scores - mass_ref[head, rows, :]), 0.0)
            prob_grad = dot_nt(grads, values_all)
            row_sum = jnp.sum(probs * prob_grad, axis=1, keepdims=True)
            score_grad = (probs * (prob_grad - row_sum)).astype(BF16)
            query_grad = dot(score_grad, keys_all) * (HEAD_DIM**-0.5)
            dz[rows, head * WIDE : (head + 1) * WIDE] = (query_grad * table_ref[rows, :]).astype(BF16)
            spot = slice(head * WIDE, (head + 1) * WIDE)
            key_acc[:keys, spot] += dot_tn(score_grad, queries)
            value_acc[:keys, spot] += dot_tn(probs.astype(BF16), grads)
        if hosting and block == 2:
            sums.first(3)
            sums.first(4)
    for block in range(CTX):
        rows = pl.ds(block * ROWS, ROWS)
        table = table_ref[rows, :] * (HEAD_DIM**-0.5)
        for head in range(HEADS_DEV):
            spot = slice(head * WIDE, (head + 1) * WIDE)
            at = (HEADS_DEV + head) * WIDE
            dz[rows, at : at + WIDE] = (key_acc[rows, spot] * table).astype(BF16)
            at = (2 * HEADS_DEV + head) * WIDE
            dz[rows, at : at + WIDE] = value_acc[rows, spot].astype(BF16)

    if hosting:
        sums.first(5)
        for number in range(3):
            sums.then(number)

    def make(block):
        part[rows_of(block), :] = dot_nt(dz[rows_of(block), :], w_ref[...]).astype(BF16)

    def beside():
        wide_lanes = lax.broadcasted_iota(jnp.int32, (D, WIDE), 1)
        pieces = []
        for piece in range(3):
            spot = slice(piece * HEADS_DEV * WIDE, (piece + 1) * HEADS_DEV * WIDE)
            terms = dot_tn(a_ref[...], dz[:, spot])
            for head in range(HEADS_DEV):
                term = terms[:, head * WIDE : (head + 1) * WIDE]
                if piece < 2:
                    term = term + jnp.where(
                        wide_lanes < HEAD_DIM // 2,
                        pltpu.roll(term, HEAD_DIM // 2, 1),
                        -pltpu.roll(term, WIDE - HEAD_DIM // 2, 1),
                    )
                pieces.append(term)
        for pair in range(4):
            joined = jnp.where(
                wide_lanes < HEAD_DIM,
                pieces[2 * pair],
                pltpu.roll(pieces[2 * pair + 1], HEAD_DIM, 1),
            )
            dheads_ref[:, pair * WIDE : (pair + 1) * WIDE] = joined.astype(BF16)
        dheads_ref[:, 4 * WIDE : 5 * WIDE] = jnp.where(
            wide_lanes < HEAD_DIM, pieces[8], 0.0
        ).astype(BF16)
        if hosting:
            sums.then(3)
            sums.then(4)

    normed_grad = reduce_rows(make, part, across_in, from_left, from_right, send_r, recv_r, beside)
    tokens = u_ref[...].astype(F32)
    scale_one = inverse_size(tokens)
    normal_one = tokens * scale_one
    gain_one_column = lax.dot_general(
        normed_grad * normal_one, ones, TN, precision=EXACT, preferred_element_type=F32
    )
    scaled_one = normed_grad * gains_ref[0:1, :]
    input_grad = input_ref[...] + scale_one * (
        scaled_one - normal_one * jnp.mean(scaled_one * normal_one, axis=1, keepdims=True)
    )
    input_ref[...] = input_grad
    small_lanes = lax.broadcasted_iota(jnp.int32, (D, LANES), 1)
    dheads_ref[:, D - LANES :] = jnp.where(
        small_lanes == EXPERTS,
        gain_one_column,
        jnp.where(small_lanes == EXPERTS + 1, gain_two_column, router_terms),
    ).astype(BF16)
    repack(dback_ref, dheads_ref, pack_ref)
    lower_ref[...] = input_grad.astype(BF16)
    if hosting:
        sums.then(5)
        sums.result(half_ref)


def attn_backward(length, arrays, upper=()):
    sems = pltpu.SemaphoreType.DMA
    out_shape = [
        jax.ShapeDtypeStruct((ROWS, D), F32),
        jax.ShapeDtypeStruct((16, ATTN_ROWS, UNIT), BF16),
        jax.ShapeDtypeStruct((ROWS, D), BF16),
    ]
    if upper:
        out_shape.append(jax.ShapeDtypeStruct((HALF_SHARD, UNIT), BF16))
    scratch = [
        pltpu.VMEM((D, D), BF16),
        pltpu.VMEM((D, D), BF16),
        pltpu.VMEM((SEQ, HEADS_DEV * WIDE), F32),
        pltpu.VMEM((SEQ, HEADS_DEV * WIDE), F32),
        pltpu.VMEM((SEQ, EXT), BF16),
        pltpu.VMEM((CTX, ROWS, COLS), BF16),
        pltpu.VMEM((CTX, ROWS, COLS), BF16),
        sems((CTX,)),
        sems((CTX,)),
    ] + REDUCE_SCRATCH
    if upper:
        scratch += half_scratch()
        scratch += [
            pltpu.VMEM((CTX, CTX, Y_ROWS, UNIT), BF16),
            pltpu.VMEM((CTX, CTX, Z_ROWS, UNIT), BF16),
            sems((11,)),
        ] + [sems((6,))] * 8
    late = (3, 4, 5, 6, 7, 8, 9, 11)
    specs = [ANY if index in late else VMEM for index in range(len(arrays))]
    for index in late:
        scratch.append(pltpu.VMEM(arrays[index].shape, arrays[index].dtype))
    scratch.append(sems((len(late),)))
    return pl.pallas_call(
        functools.partial(attn_backward_kernel, bool(upper)),
        out_shape=tuple(out_shape),
        in_specs=[SMEM] + specs + [ANY] * len(upper),
        out_specs=[VMEM] * len(out_shape),
        scratch_shapes=scratch,
        compiler_params=params(4 if upper else 3),
        name="attn_backward",
    )(length, *arrays, *(by_place(array) for array in upper))


GROUP = 4
GROUPS = 16 // GROUP
GROUP_UNITS = GROUP * LANES
SPLIT = EXPERT_ROWS // 2
SUM_SCRATCH = [
    pltpu.VMEM((CTX, ROWS, D), BF16),
    pltpu.VMEM((HALF, D), BF16),
    pltpu.VMEM((HALF, D), BF16),
    pltpu.VMEM((ROWS, D), BF16),
    pltpu.VMEM((ROWS, D), BF16),
    SEMS((6,)),
    SEMS((6,)),
]


def weight_copies(w_ref, win, wout, sem):
    groups = []
    for group in range(GROUPS):
        shards = pl.ds(group * GROUP, GROUP)
        pairs = [
            (w_ref.at[0, shards], win.at[shards, pl.ds(0, SPLIT), :]),
            (w_ref.at[1, shards, pl.ds(0, D - SPLIT), :], win.at[shards, pl.ds(SPLIT, D - SPLIT), :]),
        ]
        for piece in range(D // UNIT):
            pairs.append(
                (
                    w_ref.at[1, shards, pl.ds(D - SPLIT + piece * LANES, LANES), :],
                    wout.at[shards, :, pl.ds(piece * UNIT, UNIT)],
                )
            )
        groups.append(
            [
                pltpu.make_async_copy(source, target, sem.at[group * 5 + index])
                for index, (source, target) in enumerate(pairs)
            ]
        )
    return groups


def wout_group(wout, group):
    return wout[group * GROUP : (group + 1) * GROUP].reshape(GROUP_UNITS, D)


def ffn_forward_kernel(
    b_own_ref, residual_ref, codes_ref, router_ref, w_ref,
    y_ref, b_ref, gates_ref, gate_ref, kept_ref,
    win, wout, kept_out, acc, w_sem, kept_sem, send_b, recv_b,
    part, top_in, bottom_in, from_left, from_right, send, recv,
):
    ring = Ring("x")
    greet_ids(ring.near())
    loads = weight_copies(w_ref, win, wout, w_sem)
    for group in loads:
        for copy in group:
            copy.start()
    b_ref[ring.me] = b_own_ref[...]
    met(2)
    halves = (pl.ds(0, HALF), pl.ds(HALF, HALF))
    rows = RingGather(ring, lambda b, h: b_ref.at[b, halves[h]], send_b, recv_b)
    rows.start()
    section = lax.axis_index("section")
    lanes = lax.broadcasted_iota(jnp.int32, (ROWS, LANES), 1)
    picker = jnp.where(lax.broadcasted_iota(jnp.int32, (8, LANES), 0) == section, 1.0, 0.0)
    stores = []

    def make(index, block):
        b_rows = b_ref[block]
        slot = index % 2
        for shard in range(16):
            if index == 0 and shard % GROUP == 0:
                for copy in loads[shard // GROUP]:
                    copy.wait()
            if index >= 2 and shard == 0:
                stores[index - 2].wait()
            hidden = dot(b_rows, win[shard])
            kept_out[slot, shard] = hidden.astype(BF16)
            gate_part = hidden[:, :LANES]
            at = shard % GROUP * LANES
            acc_act = (gate_part / (1.0 + jnp.exp(-gate_part)) * hidden[:, LANES:]).astype(BF16)
            if shard % GROUP == 0:
                acted = []
            acted.append(acc_act)
            if shard % GROUP == GROUP - 1:
                terms = dot(jnp.concatenate(acted, axis=1), wout_group(wout, shard // GROUP))
                acc[...] = terms if shard < GROUP else acc[...] + terms
        stores.append(pltpu.make_async_copy(kept_out.at[slot], kept_ref.at[block], kept_sem.at[slot]))
        stores[-1].start()
        logits = dot(b_rows, router_ref[...])
        codes = lax.dot_general(
            codes_ref[block], picker, TN, precision=EXACT, preferred_element_type=F32
        )
        named = (lanes < EXPERTS) & (lanes != jnp.round(codes).astype(jnp.int32))
        chosen = jnp.where(named, logits, MASK_VALUE)
        raw = jnp.where(named, jnp.exp(chosen - jnp.max(chosen, axis=1, keepdims=True)), 0.0)
        gates = raw / jnp.sum(raw, axis=1, keepdims=True)
        if index == 0:
            gates_ref[...] = gates
        gates = jnp.where(lanes == EXPERTS, 1.0, gates)
        gate = jnp.sum(jnp.where(lanes == ring.me, gates, 0.0), axis=1, keepdims=True)
        gate_ref[block] = gate
        part[block] = (acc[...] * gate).astype(BF16)

    order = {ring_index: number for number, ring_index in enumerate(("me", "right", "left", "across"))}

    def from_sum(position, block):
        make({0: order["across"], 1: order["right"], 2: order["left"], 3: order["me"]}[position], block)

    sums = RingSum(
        ring, part, (top_in, bottom_in), from_left, from_right, send, recv, HALF, from_sum
    )
    sums.stage(4)
    rows.forward()
    rows.near()
    sums.stage(1)
    sums.stage(2)
    rows.far()
    sums.stage(0)
    sums.stage(3)
    sums.stage(5)
    y_ref[...] = (residual_ref[...] + sums.total()).astype(BF16)
    rows.sent()
    stores[2].wait()
    stores[3].wait()


def ffn_forward(b_own, residual, codes, router, weights):
    return pl.pallas_call(
        ffn_forward_kernel,
        out_shape=(
            jax.ShapeDtypeStruct((ROWS, D), BF16),
            jax.ShapeDtypeStruct((CTX, ROWS, D), BF16),
            jax.ShapeDtypeStruct((ROWS, LANES), F32),
            jax.ShapeDtypeStruct((CTX, ROWS, 1), F32),
            jax.ShapeDtypeStruct((CTX, 16, ROWS, UNIT), BF16),
        ),
        in_specs=[VMEM] * 4 + [ANY],
        out_specs=[VMEM] * 4 + [ANY],
        scratch_shapes=[
            pltpu.VMEM((16, D, UNIT), BF16),
            pltpu.VMEM((16, LANES, D), BF16),
            pltpu.VMEM((2, 16, ROWS, UNIT), BF16),
            pltpu.VMEM((ROWS, D), F32),
            SEMS((5 * GROUPS,)),
            SEMS((2,)),
            SEMS((6,)),
            SEMS((6,)),
        ]
        + SUM_SCRATCH,
        compiler_params=params(5),
        name="ffn_forward",
    )(b_own, residual, codes, router, weights)


def ffn_backward_kernel(
    lending, b_ref, gate_ref, delta_own_ref, kept_ref, w_ref, *rest,
):
    if lending:
        upper_e, upper_a, db_ref, gate_grad_ref, dw_ref, lent_ref, *rest = rest
        *rest, send_l, recv_l = rest
    else:
        db_ref, gate_grad_ref, dw_ref, *rest = rest
    (
    delta, acc, gate_acc, slot_grad, hidden, acted, win, wout, staged, rows_out, rows_in, b_turned,
    w_sem, kept_sem, dw_sem, send_d, recv_d, send_g, recv_g,
    part, top_in, bottom_in, from_left, from_right, send, recv,
    ) = rest
    ring = Ring("x")
    peers = (ring.right, ring.left, ring.across)
    section = lax.axis_index("section")
    sibling = {"section": 1 - section}
    greet_ids([ring.place(peer) for peer in peers] + ([sibling] if lending else []))
    blocks = (ring.me, ring.right, ring.left, ring.across)
    kept_loads = [
        pltpu.make_async_copy(
            kept_ref.at[block], hidden.at[:, rows_of(block), :], kept_sem.at[index]
        )
        for index, block in enumerate(blocks)
    ]
    loads = weight_copies(w_ref, win, wout, w_sem)
    kept_loads[0].start()
    for group in loads:
        for copy in group:
            copy.start()
    for copy in kept_loads[1:]:
        copy.start()
    delta[ring.me] = delta_own_ref[...]
    met(4 if lending else 3)
    if lending:
        first_rows = pl.ds(0, KEPT)
        last_rows = pl.ds(KEPT, ATTN_ROWS)

        def lends(given):
            sources = (
                (upper_e.at[:, first_rows, :], upper_e.at[:, last_rows, :])
                if given == 0
                else (upper_e.at[:, pl.ds(HALF_SHARD, KEPT), :], upper_a)
            )
            return [
                pltpu.make_async_remote_copy(
                    src_ref=source,
                    dst_ref=lent_ref.at[:, target, :],
                    send_sem=send_l.at[index],
                    recv_sem=recv_l.at[index],
                    device_id=sibling,
                    device_id_type=MESH,
                )
                for index, (source, target) in enumerate(zip(sources, (first_rows, last_rows)))
            ]

        for core in range(2):

            @pl.when(section == core)
            def _():
                for copy in lends(1 - core):
                    copy.start()

    halves = (pl.ds(0, HALF), pl.ds(HALF, HALF))
    rows = RingGather(ring, lambda b, h: delta.at[b, halves[h]], send_d, recv_d)
    rows.start()
    own_row = lax.broadcasted_iota(jnp.int32, (8, LANES), 0) == ring.me
    picker = jnp.where(own_row, 1.0, 0.0)
    handed = [
        ring.copy(rows_out.at[peer], rows_in.at[index], send_g.at[index], recv_g.at[index], peer)
        for index, peer in enumerate(peers)
    ]

    def make(index, block):
        kept_loads[index].wait()
        at = rows_of(block)
        gate = gate_ref[block]
        delta_rows = delta[block]
        slot_grad[at, :] = (delta_rows.astype(F32) * gate).astype(BF16)
        gate_sum = jnp.zeros((ROWS, LANES), F32)
        for group in range(GROUPS):
            if index == 0:
                for copy in loads[group]:
                    copy.wait()
            act_grad_all = dot_nt(delta_rows, wout_group(wout, group))
            second_grad = None
            for inner in range(GROUP):
                shard = group * GROUP + inner
                values = hidden[shard, at, :].astype(F32)
                gate_part = values[:, :LANES]
                up_part = values[:, LANES:]
                act_grad = act_grad_all[:, inner * LANES : (inner + 1) * LANES]
                sigmoid = 1.0 / (1.0 + jnp.exp(-gate_part))
                silu = gate_part * sigmoid
                act = (silu * up_part).astype(BF16)
                acted[at, shard * LANES : (shard + 1) * LANES] = act
                gate_sum += act.astype(F32) * act_grad
                act_grad = act_grad * gate
                gate_grad = act_grad * up_part * (sigmoid * (1.0 + gate_part * (1.0 - sigmoid)))
                pair = jnp.concatenate([gate_grad, act_grad * silu], axis=1).astype(BF16)
                hidden[shard, at, :] = pair
                term = dot_nt(pair, win[shard])
                second_grad = term if second_grad is None else second_grad + term
            acc[...] = second_grad if group == 0 else acc[...] + second_grad
        part[block] = acc[...].astype(BF16)
        rows_out[block] = lax.dot_general(
            picker, gate_sum, NT, precision=EXACT, preferred_element_type=F32
        )
        if index > 0:
            handed[index - 1].start()

    def from_sum(position, block):
        make((3, 1, 2, 0)[position], block)

    sums = RingSum(
        ring, part, (top_in, bottom_in), from_left, from_right, send, recv, HALF, from_sum
    )
    sums.stage(4)
    b_turned[...] = b_ref[...].reshape(SEQ, D).T
    rows.forward()
    rows.near()
    sums.stage(1)
    sums.stage(2)
    rows.far()
    sums.stage(0)
    stores = []
    for group in range(GROUPS):
        slot = group % 2
        if group == 1:
            sums.stage(3)
        if group >= 2:
            stores[group - 2].wait()
        for inner in range(GROUP):
            staged[slot, inner, :D, :] = dot(b_turned[...], hidden[group * GROUP + inner]).astype(BF16)
        whole_out = dot_tn(
            acted[:, group * GROUP_UNITS : (group + 1) * GROUP_UNITS], slot_grad[...]
        ).astype(BF16)
        for inner in range(GROUP):
            for piece in range(D // UNIT):
                at = D + piece * LANES
                staged[slot, inner, at : at + LANES, :] = whole_out[
                    inner * LANES : (inner + 1) * LANES, piece * UNIT : (piece + 1) * UNIT
                ]
        stores.append(
            pltpu.make_async_copy(
                staged.at[slot], dw_ref.at[pl.ds(group * GROUP, GROUP)], dw_sem.at[slot]
            )
        )
        stores[-1].start()
    sums.stage(5)
    db_ref[...] = sums.total()
    for copy in handed:
        copy.wait()
    rows_all = rows_out[ring.me] + rows_in[0] + rows_in[1] + rows_in[2]
    diagonal = jnp.where(
        lax.broadcasted_iota(jnp.int32, (8, LANES), 0)
        == lax.broadcasted_iota(jnp.int32, (8, LANES), 1),
        1.0,
        0.0,
    )
    gate_grad_ref[...] = lax.dot_general(
        rows_all, diagonal, TN, precision=EXACT, preferred_element_type=F32
    )
    rows.sent()
    stores[2].wait()
    stores[3].wait()
    if lending:
        for copy in lends(0):
            copy.wait()


def ffn_backward(b_all, gate_col, delta_own, kept, weights, upper=()):
    out_shape = [
        jax.ShapeDtypeStruct((ROWS, D), F32),
        jax.ShapeDtypeStruct((ROWS, LANES), F32),
        jax.ShapeDtypeStruct((16, EXPERT_ROWS, UNIT), BF16),
    ]
    if upper:
        out_shape.append(jax.ShapeDtypeStruct((16, HALF_SHARD, UNIT), BF16))
    return pl.pallas_call(
        functools.partial(ffn_backward_kernel, bool(upper)),
        out_shape=out_shape,
        in_specs=[VMEM] * 3 + [ANY] * (2 + len(upper)),
        out_specs=[VMEM] * 2 + [ANY] * (len(out_shape) - 2),
        scratch_shapes=[
            pltpu.VMEM((CTX, ROWS, D), BF16),
            pltpu.VMEM((ROWS, D), F32),
            pltpu.VMEM((8, LANES), F32),
            pltpu.VMEM((SEQ, D), BF16),
            pltpu.VMEM((16, SEQ, UNIT), BF16),
            pltpu.VMEM((SEQ, FFN), BF16),
            pltpu.VMEM((16, D, UNIT), BF16),
            pltpu.VMEM((16, LANES, D), BF16),
            pltpu.VMEM((2, GROUP, EXPERT_ROWS, UNIT), BF16),
            pltpu.VMEM((CTX, 8, ROWS), F32),
            pltpu.VMEM((3, 8, ROWS), F32),
            pltpu.VMEM((D, SEQ), BF16),
            SEMS((5 * GROUPS,)),
            SEMS((CTX,)),
            SEMS((2,)),
            SEMS((6,)),
            SEMS((6,)),
            SEMS((3,)),
            SEMS((3,)),
        ]
        + SUM_SCRATCH
        + ([SEMS((2,)), SEMS((2,))] if upper else []),
        compiler_params=params(10 if upper else 6),
        name="ffn_backward",
    )(b_all, gate_col, delta_own, kept, weights, *upper)


def ffn_both_kernel(
    b_own_ref, residual_ref, codes_ref, router_ref, delta_in, w_ref,
    y_ref, gates_ref, db_ref, gate_grad_ref, dw_ref,
    b_ref, gate_ref, delta, acc, slot_grad, hidden, acted, win, wout, staged, rows_out, rows_in, b_turned,
    w_sem, dw_sem, send_b, recv_b, delta_sem, send_g, recv_g, *sum_refs,
):
    ring = Ring("x")
    peers = (ring.right, ring.left, ring.across)
    greet_ids([ring.place(peer) for peer in peers])
    loads = weight_copies(w_ref, win, wout, w_sem)
    for group in loads:
        for copy in group:
            copy.start()
    b_ref[ring.me] = b_own_ref[...]
    seeds = pltpu.make_async_copy(delta_in, delta, delta_sem)
    seeds.start()
    met(3)
    halves = (pl.ds(0, HALF), pl.ds(HALF, HALF))
    rows = RingGather(ring, lambda b, h: b_ref.at[b, halves[h]], send_b, recv_b)
    rows.start()
    section = lax.axis_index("section")
    lanes = lax.broadcasted_iota(jnp.int32, (ROWS, LANES), 1)
    code_picker = jnp.where(lax.broadcasted_iota(jnp.int32, (8, LANES), 0) == section, 1.0, 0.0)
    row_picker = jnp.where(lax.broadcasted_iota(jnp.int32, (8, LANES), 0) == ring.me, 1.0, 0.0)
    handed = [
        ring.copy(rows_out.at[peer], rows_in.at[index], send_g.at[index], recv_g.at[index], peer)
        for index, peer in enumerate(peers)
    ]
    part_y, part_b = sum_refs[0], sum_refs[7]

    def forward(index, block):
        at = rows_of(block)
        b_rows = b_ref[block]
        for group in range(GROUPS):
            if index == 0:
                for copy in loads[group]:
                    copy.wait()
            acts = []
            for inner in range(GROUP):
                shard = group * GROUP + inner
                values = dot(b_rows, win[shard])
                hidden[shard, at, :] = values.astype(BF16)
                gate_part = values[:, :LANES]
                acts.append(
                    (gate_part / (1.0 + jnp.exp(-gate_part)) * values[:, LANES:]).astype(BF16)
                )
            terms = dot(jnp.concatenate(acts, axis=1), wout_group(wout, group))
            acc[...] = terms if group == 0 else acc[...] + terms
        logits = dot(b_rows, router_ref[...])
        codes = lax.dot_general(
            codes_ref[block], code_picker, TN, precision=EXACT, preferred_element_type=F32
        )
        named = (lanes < EXPERTS) & (lanes != jnp.round(codes).astype(jnp.int32))
        chosen = jnp.where(named, logits, MASK_VALUE)
        raw = jnp.where(named, jnp.exp(chosen - jnp.max(chosen, axis=1, keepdims=True)), 0.0)
        gates = raw / jnp.sum(raw, axis=1, keepdims=True)
        if index == 0:
            gates_ref[...] = gates
        gates = jnp.where(lanes == EXPERTS, 1.0, gates)
        gate = jnp.sum(jnp.where(lanes == ring.me, gates, 0.0), axis=1, keepdims=True)
        gate_ref[block] = gate
        part_y[block] = (acc[...] * gate).astype(BF16)

    def backward(index, block):
        at = rows_of(block)
        gate = gate_ref[block]
        delta_rows = delta[block]
        slot_grad[at, :] = (delta_rows.astype(F32) * gate).astype(BF16)
        gate_sum = jnp.zeros((ROWS, LANES), F32)
        for group in range(GROUPS):
            act_grad_all = dot_nt(delta_rows, wout_group(wout, group))
            second_grad = None
            for inner in range(GROUP):
                shard = group * GROUP + inner
                values = hidden[shard, at, :].astype(F32)
                gate_part = values[:, :LANES]
                up_part = values[:, LANES:]
                act_grad = act_grad_all[:, inner * LANES : (inner + 1) * LANES]
                sigmoid = 1.0 / (1.0 + jnp.exp(-gate_part))
                silu = gate_part * sigmoid
                act = (silu * up_part).astype(BF16)
                acted[at, shard * LANES : (shard + 1) * LANES] = act
                gate_sum += act.astype(F32) * act_grad
                act_grad = act_grad * gate
                gate_grad = act_grad * up_part * (sigmoid * (1.0 + gate_part * (1.0 - sigmoid)))
                pair = jnp.concatenate([gate_grad, act_grad * silu], axis=1).astype(BF16)
                hidden[shard, at, :] = pair
                term = dot_nt(pair, win[shard])
                second_grad = term if second_grad is None else second_grad + term
            acc[...] = second_grad if group == 0 else acc[...] + second_grad
        part_b[block] = acc[...].astype(BF16)
        rows_out[block] = lax.dot_general(
            row_picker, gate_sum, NT, precision=EXACT, preferred_element_type=F32
        )
        if index > 0:
            handed[index - 1].start()

    def summing(refs, make):
        part, top_in, bottom_in, from_left, from_right, send, recv = refs
        return RingSum(
            ring, part, (top_in, bottom_in), from_left, from_right, send, recv, HALF,
            lambda position, block: make((3, 1, 2, 0)[position], block),
        )

    ahead = summing(sum_refs[:7], forward)
    behind = summing(sum_refs[7:], backward)
    ahead.stage(4)
    rows.forward()
    rows.near()
    ahead.stage(1)
    ahead.stage(2)
    rows.far()
    ahead.stage(0)
    b_turned[...] = b_ref[...].reshape(SEQ, D).T
    seeds.wait()
    behind.stage(4)
    ahead.stage(3)
    behind.stage(1)
    behind.stage(2)
    behind.stage(0)
    ahead.stage(5)
    y_ref[...] = (residual_ref[...] + ahead.total()).astype(BF16)
    stores = []
    for group in range(GROUPS):
        slot = group % 2
        if group == 1:
            behind.stage(3)
        if group >= 2:
            stores[group - 2].wait()
        for inner in range(GROUP):
            staged[slot, inner, :D, :] = dot(b_turned[...], hidden[group * GROUP + inner]).astype(BF16)
        whole_out = dot_tn(
            acted[:, group * GROUP_UNITS : (group + 1) * GROUP_UNITS], slot_grad[...]
        ).astype(BF16)
        for inner in range(GROUP):
            for piece in range(D // UNIT):
                at = D + piece * LANES
                staged[slot, inner, at : at + LANES, :] = whole_out[
                    inner * LANES : (inner + 1) * LANES, piece * UNIT : (piece + 1) * UNIT
                ]
        stores.append(
            pltpu.make_async_copy(
                staged.at[slot], dw_ref.at[pl.ds(group * GROUP, GROUP)], dw_sem.at[slot]
            )
        )
        stores[-1].start()
    behind.stage(5)
    db_ref[...] = behind.total()
    for copy in handed:
        copy.wait()
    rows_all = rows_out[ring.me] + rows_in[0] + rows_in[1] + rows_in[2]
    diagonal = jnp.where(
        lax.broadcasted_iota(jnp.int32, (8, LANES), 0)
        == lax.broadcasted_iota(jnp.int32, (8, LANES), 1),
        1.0,
        0.0,
    )
    gate_grad_ref[...] = lax.dot_general(
        rows_all, diagonal, TN, precision=EXACT, preferred_element_type=F32
    )
    rows.sent()
    stores[2].wait()
    stores[3].wait()


def ffn_both(b_own, residual, codes, router, delta_all, weights):
    return pl.pallas_call(
        ffn_both_kernel,
        out_shape=(
            jax.ShapeDtypeStruct((ROWS, D), BF16),
            jax.ShapeDtypeStruct((ROWS, LANES), F32),
            jax.ShapeDtypeStruct((ROWS, D), F32),
            jax.ShapeDtypeStruct((ROWS, LANES), F32),
            jax.ShapeDtypeStruct((16, EXPERT_ROWS, UNIT), BF16),
        ),
        in_specs=[VMEM] * 4 + [ANY] * 2,
        out_specs=[VMEM] * 4 + [ANY],
        scratch_shapes=[
            pltpu.VMEM((CTX, ROWS, D), BF16),
            pltpu.VMEM((CTX, ROWS, 1), F32),
            pltpu.VMEM((CTX, ROWS, D), BF16),
            pltpu.VMEM((ROWS, D), F32),
            pltpu.VMEM((SEQ, D), BF16),
            pltpu.VMEM((16, SEQ, UNIT), BF16),
            pltpu.VMEM((SEQ, FFN), BF16),
            pltpu.VMEM((16, D, UNIT), BF16),
            pltpu.VMEM((16, LANES, D), BF16),
            pltpu.VMEM((2, GROUP, EXPERT_ROWS, UNIT), BF16),
            pltpu.VMEM((CTX, 8, ROWS), F32),
            pltpu.VMEM((3, 8, ROWS), F32),
            pltpu.VMEM((D, SEQ), BF16),
            SEMS((5 * GROUPS,)),
            SEMS((2,)),
            SEMS((6,)),
            SEMS((6,)),
            SEMS,
            SEMS((3,)),
            SEMS((3,)),
        ]
        + SUM_SCRATCH * 2,
        compiler_params=params(6),
        name="ffn_both",
    )(b_own, residual, codes, router, delta_all, weights)


def rotary_table():
    half_dim = HEAD_DIM // 2
    steps = 2.0 * np.arange(half_dim, dtype=np.float32) / np.float32(HEAD_DIM)
    frequency = np.exp(-np.log(np.float32(10000.0)) * steps)
    angles = np.arange(SEQ, dtype=np.float32)[:, None] * frequency[None, :]
    cosine, sine = np.cos(angles), np.sin(angles)
    return jnp.asarray(np.concatenate([cosine, cosine, sine, sine], axis=1), F32)


def lower_forward(packs, experts, tokens_in, length, codes, table):
    a_all, qkv, mass, attended, residual, second, *unpacked = attn_forward(
        0, length, tokens_in, packs, table
    )
    output, b_all, gates, gate_col, kept = ffn_forward(
        second, residual, codes, unpacked[1], experts
    )
    late = (a_all, qkv, mass, attended, residual, second, gates)
    return output, (tokens_in, b_all, gate_col, kept, unpacked, late)


def upper_layer(packs, experts, tokens_in, length, codes, table, seed, seed_all):
    a_all, qkv, mass, attended, residual, second, *unpacked = attn_forward(
        1, length, tokens_in, packs, table
    )
    output, gates, db, gate_grads, dexperts = ffn_both(
        second, residual, codes, unpacked[1], seed_all, experts
    )
    late = (a_all, qkv, mass, attended, residual, second, gates)
    results = attn_backward(length, (tokens_in, *unpacked, table, *late, seed, db, gate_grads))
    return output, dexperts, results


def lower_backward(experts, saved, delta_own, length, table, upper):
    tokens_in, b_all, gate_col, kept, unpacked, late = saved
    db, gate_grads, dexperts, lent = ffn_backward(b_all, gate_col, delta_own, kept, experts, upper)
    results = attn_backward(
        length, (tokens_in, *unpacked, table, *late, delta_own, db, gate_grads), (*upper, lent)
    )
    return dexperts, results


def factor_of(squares_ref, index):
    return jnp.minimum(1.0, CLIP_LIMIT / jnp.sqrt(squares_ref[0:1, index : index + 1]))


def updated(fixes_ref, gradient, factor, old, new, learn_rate, at=...):
    master_ref, mean_ref, square_ref = old
    gradient_ref, mean_new_ref, square_new_ref, master_new_ref, copy_ref = new
    clipped = gradient * factor
    master = master_ref[at]
    mean_new = BETA_ONE * mean_ref[at] + (1.0 - BETA_ONE) * clipped
    square_new = BETA_TWO * square_ref[at] + (1.0 - BETA_TWO) * clipped * clipped
    master_new = master - learn_rate * (
        mean_new * fixes_ref[0] / (jnp.sqrt(square_new * fixes_ref[1]) + ADAM_EPS) + DECAY_RATE * master
    )
    gradient_ref[at] = gradient
    mean_new_ref[at] = mean_new
    square_new_ref[at] = square_new
    master_new_ref[at] = master_new
    copy_ref[at] = master_new.astype(BF16)


def update_kernel(
    fixes_ref, squares_ref, in_sum_ref, out_sum_ref, attn_sum_ref, *refs,
):
    in_old, out_old, attn_old, gain_old, router_old = (refs[at : at + 3] for at in range(0, 15, 3))
    in_new, out_new, attn_new, gain_new, router_new = (refs[at : at + 5] for at in range(15, 40, 5))
    norms_ref, turned, wide = refs[40:]
    turned[pl.ds(0, D // 2, 2), :] = in_sum_ref[0, :, :LANES].astype(F32)
    turned[pl.ds(1, D // 2, 2), :] = in_sum_ref[0, :, LANES:].astype(F32)
    part_rows = LANES // 2
    start = lax.rem(pl.program_id(0), 2) * part_rows
    updated(
        fixes_ref, turned[...], factor_of(squares_ref, 3), in_old, in_new, RATE_FACTOR / D**0.5
    )
    pieces = [
        out_sum_ref[0, pl.ds(pl.multiple_of(piece * LANES + start, part_rows), part_rows), :].astype(F32)
        for piece in range(D // UNIT)
    ]
    updated(
        fixes_ref,
        jnp.concatenate(pieces, axis=1),
        factor_of(squares_ref, 4),
        out_old,
        out_new,
        RATE_FACTOR / FFN**0.5,
        0,
    )

    @pl.when(pl.program_id(0) == 0)
    def _():
        back = [jnp.zeros((48, UNIT), F32) for _ in range(3)]
        small = jnp.zeros((48, UNIT), F32)
        for block in range(CTX):
            rows = [
                attn_sum_ref[block, piece * 48 : (piece + 1) * 48, :].astype(F32) for piece in range(6)
            ]
            back = [left + right for left, right in zip(back, rows[:3])]
            small = small + rows[5]
            heads = jnp.concatenate(rows[3:], axis=1)
            for part in range(3):
                at = part * D + block * COLS
                wide[:, at : at + COLS] = heads[:, part * COLS : (part + 1) * COLS]
        wide[:, 3 * D :] = jnp.concatenate(back, axis=1)
        small = small[:, LANES:]
        places = lax.broadcasted_iota(jnp.int32, (8, LANES), 0)
        picker = jnp.where(places == lax.broadcasted_iota(jnp.int32, (8, LANES), 1), 1.0, 0.0)
        turned_rows = lax.dot_general(
            picker, small, NT, precision=EXACT, preferred_element_type=F32
        )
        gain_rows = turned_rows[EXPERTS : EXPERTS + 2]
        updated(fixes_ref, gain_rows, factor_of(squares_ref, 0), gain_old, gain_new, GAIN_RATE)
        for expert in range(EXPERTS):
            updated(
                fixes_ref,
                turned_rows[expert : expert + 1],
                factor_of(squares_ref, 2),
                router_old,
                router_new,
                RATE_FACTOR / (D // 4) ** 0.5,
                expert,
            )
        norms_ref[...] = jnp.sqrt(squares_ref[...])
        for part in range(4):
            lanes = (slice(None), slice(part * D, (part + 1) * D))
            updated(
                fixes_ref,
                wide[lanes],
                factor_of(squares_ref, 1),
                attn_old,
                attn_new,
                RATE_FACTOR / D**0.5,
                lanes,
            )


def update(fixes, squares, sums_all, in_old, out_old, attn_old, gain_old, router_old):
    in_rows, units = 2 * D, LANES
    in_shape, out_shape, attn_shape = (CTX * in_rows, units), (CTX, units, D), (48, 4 * D)
    in_spec = pl.BlockSpec((D, units), lambda i: (i, 0))
    out_spec = pl.BlockSpec((1, units // 2, D), lambda i: (i // 2, i % 2, 0))
    attn_spec = whole(attn_shape)
    gain_shape, router_shape = (2, 48), (EXPERTS, 1, 48)

    def five(shape):
        return [jax.ShapeDtypeStruct(shape, F32)] * 4 + [jax.ShapeDtypeStruct(shape, BF16)]

    return pl.pallas_call(
        update_kernel,
        grid=(2 * CTX,),
        out_shape=five(in_shape)
        + five(out_shape)
        + five(attn_shape)
        + five(gain_shape)
        + five(router_shape)
        + [jax.ShapeDtypeStruct((8, LANES), F32)],
        in_specs=[
            SMEM,
            whole((8, LANES)),
            pl.BlockSpec((1, D // 2, UNIT), lambda i: (i // 2, i % 2, 0)),
            pl.BlockSpec((1, D // 2, UNIT), lambda i: (i // 2, 2, 0)),
            pl.BlockSpec((CTX, ATTN_ROWS, UNIT), lambda i: (0, EXPERT_ROWS // ATTN_ROWS, 0)),
        ]
        + [in_spec] * 3
        + [out_spec] * 3
        + [attn_spec] * 3
        + [whole(gain_shape)] * 3
        + [whole(router_shape)] * 3,
        out_specs=[in_spec] * 5
        + [out_spec] * 5
        + [attn_spec] * 5
        + [whole(gain_shape)] * 5
        + [whole(router_shape)] * 5
        + [whole((8, LANES))],
        scratch_shapes=[pltpu.VMEM((D, units), F32), pltpu.VMEM(attn_shape, F32)],
        compiler_params=pltpu.CompilerParams(vmem_limit_bytes=30 * 1024 * 1024),
        name="update",
    )(
        fixes, squares, sums_all, sums_all, sums_all,
        *(array.reshape(in_shape) for array in in_old),
        *(array.reshape(out_shape) for array in out_old),
        *(array.reshape(attn_shape) for array in attn_old),
        *(array.reshape(gain_shape) for array in gain_old),
        *(array.transpose(2, 0, 1) for array in router_old),
    )


def on_device(
    inputs, cotangent, lengths, routes, step_count,
    norm_gains, gains_mean, gains_square,
    attn_weight, attn_mean, attn_square,
    router_weight, router_mean, router_square,
    expert_in, in_mean, in_square,
    expert_out, out_mean, out_square,
):
    section = lax.axis_index("section")
    ctx_index = lax.axis_index("ctx")
    fsdp = lax.axis_size("fsdp")
    everyone = ("section", "fsdp")
    shard_rows = attn_weight.shape[1]
    units = expert_in.shape[4]
    first_core = section == 0

    def own_columns(matrix, part):
        return lax.dynamic_slice_in_dim(matrix, part * D + ctx_index * COLS, COLS, 1)

    def swap(block):
        return lax.ppermute(block, "section", [(0, 1), (1, 0)])

    attn_shard = jnp.concatenate(
        [attn_weight[0][:, 3 * D :]]
        + [own_columns(attn_weight[0], part) for part in range(3)]
        + [jnp.zeros((shard_rows, HEAD_DIM), F32), router_weight[0], norm_gains[0].T]
        + [jnp.zeros((shard_rows, LANES - EXPERTS - 2), F32)],
        axis=1,
    ).astype(BF16)
    attn_shard = attn_shard.reshape(shard_rows, 6, UNIT).transpose(1, 0, 2).reshape(-1, UNIT)
    length = lax.dynamic_slice_in_dim(lengths, section, 1, 0)
    tokens = lax.dynamic_index_in_dim(inputs, section, 0, keepdims=False)
    positions = ctx_index * ROWS + jnp.arange(ROWS, dtype=jnp.int32)
    seed = lax.dynamic_index_in_dim(cotangent, section, 0, keepdims=False)
    seed = jnp.where((positions < length[0])[:, None], seed, jnp.zeros_like(seed))
    left_out = (3 - routes[0, :, :, 0] - routes[0, :, :, 1]).astype(F32)
    packs, codes, seed_all = gather_shards(
        attn_shard, jnp.pad(left_out, ((0, 8 - left_out.shape[0]), (0, 0))), seed
    )
    packs = packs.reshape(2, fsdp, ATTN_ROWS, UNIT)
    in_shard = (
        lax.dynamic_index_in_dim(expert_in[0], ctx_index, 0, keepdims=False)
        .astype(BF16)
        .reshape(D, 2 * units)
    )
    out_shard = lax.dynamic_index_in_dim(expert_out[0], ctx_index, 0, keepdims=False).astype(BF16)
    halves = jnp.concatenate(
        [in_shard] + [out_shard[:, at : at + 2 * units] for at in range(0, D, 2 * units)], axis=0
    ).reshape(2, SPLIT, 2 * units)
    other = swap(jnp.where(first_core, halves[1], halves[0]))
    pieces = (jnp.where(first_core, halves[0], other), jnp.where(first_core, other, halves[1]))
    experts = [
        lax.all_gather(piece, everyone).reshape(2, fsdp, SPLIT, 2 * units) for piece in pieces
    ]
    table = rotary_table()

    lower_out, lower_saved = lower_forward(packs, experts[0], tokens, length, codes[0], table)
    upper_out, upper_experts, (upper_grad, upper_attn, lower_seed) = upper_layer(
        packs, experts[1], lower_out, length, codes[1], table, seed, seed_all
    )
    lower_experts, (lower_grad, lower_attn, _, upper_half) = lower_backward(
        experts[0], lower_saved, lower_seed, length, table, (upper_experts, upper_attn)
    )
    sums_all, squares, layer_outputs, input_grads = sum_shards(
        lower_experts, lower_attn, upper_half, lower_out, upper_out, lower_grad, upper_grad
    )
    step_value = step_count[0].astype(F32)
    fixes = 1.0 / jnp.stack([1.0 - BETA_ONE**step_value, 1.0 - BETA_TWO**step_value])
    changed = update(
        fixes,
        squares,
        sums_all,
        (expert_in, in_mean, in_square),
        (expert_out, out_mean, out_square),
        (attn_weight, attn_mean, attn_square),
        (norm_gains, gains_mean, gains_square),
        (router_weight, router_mean, router_square),
    )

    def shaped(first, like):
        return tuple(array.reshape(like.shape) for array in changed[first : first + 5])

    return (
        (layer_outputs[None], input_grads[None])
        + shaped(15, norm_gains)
        + shaped(10, attn_weight)
        + tuple(array.transpose(1, 2, 0) for array in changed[20:25])
        + shaped(0, expert_in)
        + shaped(5, expert_out)
        + (changed[25][:1, :5],)
    )


def solution(mesh):
    gains = P("section", None, "fsdp")
    rows = P("section", "fsdp", None)
    wide = P("section", None, None, None, "fsdp")
    down = P("section", None, "fsdp", None)
    tokens = P("section", "fsdp", "ctx", None)
    return jax.shard_map(
        on_device,
        mesh=mesh,
        in_specs=(
            P("fsdp", "ctx", None),
            P("fsdp", "ctx", None),
            P("fsdp"),
            tokens,
            P(),
        )
        + (gains,) * 3
        + (rows,) * 6
        + (wide,) * 3
        + (down,) * 3,
        out_specs=(tokens, tokens)
        + (gains,) * 5
        + (rows,) * 10
        + (wide,) * 5
        + (down,) * 5
        + (P("section", None),),
        check_vma=False,
    )
```
